32 devices in a mesh: slow: 8 (over y, x, core), fast: 4 (over z).
Axes of the slice: x: 2, y: 2, z: 4, core: 2. Of those that a mesh axis runs over, the one named last changes fastest.
Arguments:
- query_act: bfloat16 [4096, 512], P(('slow', 'fast')), may hold values from -6 to 6
- key_act: bfloat16 [4096, 512], P(('slow', 'fast')), may hold values from -6 to 6
- value_act: bfloat16 [4096, 512], P(('slow', 'fast')), may hold values from -6 to 6
- long_filter: bfloat16 [4096, 32], P(('slow', 'fast')), may hold values from -4 to 4
- out_grad: bfloat16 [4096, 512], P(('slow', 'fast')), may hold values from -6 to 6
Outputs:
- mixed_out: bfloat16 [4096, 512], P(('slow', 'fast'))
- query_grad: bfloat16 [4096, 512], P(('slow', 'fast'))
- key_grad: bfloat16 [4096, 512], P(('slow', 'fast'))
- value_grad: bfloat16 [4096, 512], P(('slow', 'fast'))
- filter_grad: float32 [4096, 32], P(('slow', 'fast'))
The draws below stay inside these ranges and needn't reach their ends.
All inputs are finite; a program needn't handle non-finite values.
Results may differ from the reference program's by a relative error of at most 0.0049.
Values may be sent and summed in bfloat16 or wider, within the bound.
No kernel may reach another device: no remote copies, remote signals or barrier semaphores. Data moves between devices by JAX's collectives and lax.ppermute only.
A program may use at most 64 MiB of HBM per device.

```python
import math
import jax
import jax.numpy as jnp
from jax import lax

SLAB = 512
GROUP_CH = 16
FILTER_GROUPS = 32
SEQUENCE_TOKENS = 4096


def draw_long_filter(key, part):
    random_keys = jax.random.split(key, 7)
    delay_index = jnp.arange(SEQUENCE_TOKENS, dtype=jnp.int32)[:, None]
    choose_slow = jax.random.uniform(random_keys[0], (FILTER_GROUPS,))
    is_slow = choose_slow < 0.5
    slow_rate = jnp.exp(jax.random.uniform(random_keys[1], (FILTER_GROUPS,), minval=math.log(0.3 / SEQUENCE_TOKENS), maxval=math.log(2.3 / SEQUENCE_TOKENS)))
    fast_rate = jax.random.uniform(random_keys[2], (FILTER_GROUPS,), minval=1.0 / 50.0, maxval=1.0 / 30.0)
    decay_rate = jnp.where(is_slow, slow_rate, fast_rate)
    spike_delays = jax.random.randint(random_keys[3], (3, FILTER_GROUPS), 1, SEQUENCE_TOKENS)
    spike_retained = jax.random.uniform(random_keys[4], (3, FILTER_GROUPS), minval=0.5, maxval=0.8)
    decay_profile = jnp.exp(-decay_rate[None, :] * delay_index.astype(jnp.float32))
    for spike_index in range(3):
        decay_profile = decay_profile * jnp.where(delay_index >= spike_delays[spike_index][None, :], spike_retained[spike_index][None, :], 1.0)
    factor_spread = jnp.exp(jax.random.uniform(random_keys[5], (SEQUENCE_TOKENS, FILTER_GROUPS), minval=-0.7, maxval=0.7))
    rough_part = jax.random.normal(random_keys[6], (SEQUENCE_TOKENS, FILTER_GROUPS))
    energy = -jnp.expm1(-2.0 * decay_rate) / -jnp.expm1(-2.0 * decay_rate * SEQUENCE_TOKENS)
    taps = rough_part * factor_spread * decay_profile * jnp.sqrt(energy / 1.36)[None, :]
    return taps.astype(jnp.bfloat16)


def steps_of(key, shape, shards, smallest, top_value):
    gain = 1.0
    for axis_at, blocks in shards:
        steps = jax.random.uniform(jax.random.fold_in(jax.random.fold_in(key, 6), axis_at), (blocks,), jnp.float32, smallest / len(shards), top_value / len(shards))
        gain = gain * jnp.repeat(jnp.exp(steps), shape[axis_at] // blocks).reshape((-1,) + (1,) * (len(shape) - 1 - axis_at))
    return gain


def bell_draw(stream_key, shape, scale, reach, shards=(), kind=jnp.bfloat16):
    entries = scale * jax.random.normal(stream_key, shape, jnp.float32)
    if shards:
        entries = entries * steps_of(stream_key, shape, shards, -0.22, 0.18)
    return jnp.clip(entries, -reach, reach).astype(kind)


def setup_inputs(seed: int = 0) -> dict:
    seeds = jax.random.split(jax.random.key(seed), 6)
    query_act = bell_draw(seeds[0], (SEQUENCE_TOKENS, SLAB), 1.0, 6.0, ((0, 32),))
    key_act = bell_draw(seeds[1], (SEQUENCE_TOKENS, SLAB), 1.0, 6.0, ((0, 32),))
    value_act = bell_draw(seeds[2], (SEQUENCE_TOKENS, SLAB), 1.0, 6.0, ((0, 32),))
    long_filter = draw_long_filter(jax.random.fold_in(seeds[5], 71), 0)
    out_grad = bell_draw(seeds[4], (SEQUENCE_TOKENS, SLAB), 1.0, 6.0, ((0, 32),))
    return {"query_act": query_act, "key_act": key_act, "value_act": value_act, "long_filter": long_filter, "out_grad": out_grad}


def group_terms(product, grad_in, filter_taps):
    points = 2 * SEQUENCE_TOKENS
    taps_spec = jnp.fft.rfft(filter_taps, points)
    prod_spec = jnp.fft.rfft(product, points, axis=0)
    grad_spec = jnp.fft.rfft(grad_in, points, axis=0)
    convolved = jnp.fft.irfft(prod_spec * taps_spec[:, None], points, axis=0)[:SEQUENCE_TOKENS]
    backward = jnp.fft.irfft(grad_spec * jnp.conj(taps_spec)[:, None], points, axis=0)[:SEQUENCE_TOKENS]
    correlation = jnp.fft.irfft(lax.optimization_barrier(jnp.sum(grad_spec * jnp.conj(prod_spec), axis=1)), points)[:SEQUENCE_TOKENS]
    return (convolved, backward, correlation)

def reference(query_act, key_act, value_act, long_filter, out_grad):
    scale = 1.0 / math.sqrt(SEQUENCE_TOKENS * GROUP_CH)

    def per_group(buffers, group_id):
        first_col = group_id * GROUP_CH

        def columns(values):
            return lax.dynamic_slice_in_dim(values, first_col, GROUP_CH, axis=1).astype(jnp.float32)
        query_cols = columns(query_act)
        key_cols = columns(key_act)
        value_cols = columns(value_act)
        grad_cols = columns(out_grad)
        product = lax.optimization_barrier((key_cols * value_cols).astype(jnp.bfloat16)).astype(jnp.float32)
        grad_in = lax.optimization_barrier((grad_cols * query_cols).astype(jnp.bfloat16)).astype(jnp.float32)
        filter_taps = lax.dynamic_slice_in_dim(long_filter, group_id, 1, axis=1)[:, 0].astype(jnp.float32)
        convolved, backward, correlation = group_terms(product, grad_in, filter_taps)
        results = (query_cols * convolved, grad_cols * convolved, backward * value_cols, backward * key_cols)
        updated = tuple((lax.dynamic_update_slice_in_dim(buffer_old, result_new.astype(jnp.bfloat16), first_col, axis=1) for buffer_old, result_new in zip(buffers, results)))
        return (updated, correlation * scale)
    empty = jnp.zeros((SEQUENCE_TOKENS, SLAB), jnp.bfloat16)
    buffers, correlations = lax.scan(per_group, (empty, empty, empty, empty), jnp.arange(FILTER_GROUPS, dtype=jnp.int32))
    return (buffers[0], buffers[1], buffers[2], buffers[3], jnp.transpose(correlations))
```

```python
import functools
import math

import jax
import jax.numpy as jnp
from jax import lax
from jax.experimental import pallas as pl
from jax.experimental.pallas import tpu as pltpu
from jax.sharding import PartitionSpec as P

highest = lax.Precision.HIGHEST


def index_ramp(points, along, ndim, offset):
    shape_list = [1] * ndim
    shape_list[along] = points
    return (jnp.arange(points, dtype=jnp.int32) + offset).reshape(shape_list)


def apply_dft(re_im, points, direction, along):
    index_row = jnp.arange(points, dtype=jnp.int32)
    phase_turns = index_row[:, None] * index_row[None, :] % points
    phases = 2.0 * math.pi / points * phase_turns.astype(jnp.float32)
    cosine = jnp.cos(phases)
    sine_part = direction * jnp.sin(phases)

    def contract(values, matrix):
        result = jnp.tensordot(values, matrix, axes=((along,), (1,)), precision=highest)
        return jnp.moveaxis(result, -1, along)

    return (
        contract(re_im[0], cosine) - contract(re_im[1], sine_part),
        contract(re_im[0], sine_part) + contract(re_im[1], cosine),
    )


def rotate(re_im, phase_turns, period, direction):
    phases = 2.0 * math.pi / period * (phase_turns % period).astype(jnp.float32)
    cosine = jnp.cos(phases)
    sine_part = direction * jnp.sin(phases)
    return (re_im[0] * cosine - re_im[1] * sine_part, re_im[0] * sine_part + re_im[1] * cosine)


def complex_times(left, right):
    return (left[0] * right[0] - left[1] * right[1], left[0] * right[1] + left[1] * right[0])


def conj_times(left, right):
    return (left[0] * right[0] + left[1] * right[1], left[0] * right[1] - left[1] * right[0])


def positions(grid_info, slow_points, slow_offset, fast_points, fast_offset):
    fast_count, tokens = (grid_info[1], grid_info[2])
    block_index = index_ramp(slow_points, 2, 5, slow_offset) * fast_count + index_ramp(
        fast_points, 3, 5, fast_offset
    )
    return block_index * tokens + index_ramp(tokens, 4, 5, 0)


def open_halves(re_im, grid_info, fast_offset):
    token_place = positions(grid_info, re_im[0].shape[1], 0, re_im[0].shape[2], fast_offset)
    return rotate(
        (re_im[0][None], re_im[1][None]),
        index_ramp(2, 0, 5, 0) * token_place,
        2 * grid_info[3],
        -1.0,
    )


def fold_halves(re_im, token_place, seq_length):
    turned = rotate(re_im, index_ramp(2, 0, 5, 0) * token_place, 2 * seq_length, 1.0)
    scale = 0.5 / seq_length
    return (jnp.sum(turned[0], axis=0) * scale, jnp.sum(turned[1], axis=0) * scale)


def front_forward(re_im, grid_info, fast_offset):
    slow_count, fast_count = (grid_info[0], grid_info[1])
    re_im = apply_dft(re_im, slow_count, -1.0, 2)
    phase_turns = index_ramp(slow_count, 2, 5, 0) * index_ramp(re_im[0].shape[3], 3, 5, fast_offset)
    return rotate(re_im, phase_turns, slow_count * fast_count, -1.0)


def front_inverse(re_im, grid_info, fast_offset):
    slow_count, fast_count = (grid_info[0], grid_info[1])
    phase_turns = index_ramp(slow_count, 2, 5, 0) * index_ramp(re_im[0].shape[3], 3, 5, fast_offset)
    re_im = rotate(re_im, phase_turns, slow_count * fast_count, 1.0)
    return apply_dft(re_im, slow_count, 1.0, 2)


def lead_phase(re_im, grid_info, ka_offset):
    slow_count, fast_count, tokens = (grid_info[0], grid_info[1], grid_info[2])
    lead_index = index_ramp(re_im[0].shape[2], 2, 5, ka_offset) + slow_count * index_ramp(
        fast_count, 3, 5, 0
    )
    return lead_index * index_ramp(tokens, 4, 5, 0)


def back_forward(re_im, grid_info, ka_offset):
    re_im = apply_dft(re_im, grid_info[1], -1.0, 3)
    re_im = rotate(re_im, lead_phase(re_im, grid_info, ka_offset), grid_info[3], -1.0)
    return apply_dft(re_im, grid_info[2], -1.0, 4)


def back_inverse(re_im, grid_info, ka_offset):
    re_im = apply_dft(re_im, grid_info[2], 1.0, 4)
    re_im = rotate(re_im, lead_phase(re_im, grid_info, ka_offset), grid_info[3], 1.0)
    return apply_dft(re_im, grid_info[1], 1.0, 3)


def to_channels(seq_rows):
    return lax.all_to_all(
        seq_rows.reshape(1, seq_rows.shape[0], seq_rows.shape[1]),
        "slow",
        split_axis=2,
        concat_axis=0,
        tiled=True,
    )


def merge_blocks(arrays, block_count):
    tokens = arrays[0].shape[0]
    pieces = [item.reshape(tokens, block_count, item.shape[1] // block_count) for item in arrays]
    return jnp.concatenate(pieces, axis=2).reshape(tokens, -1)


def split_columns(rows_major, widths):
    tokens, block_count = (rows_major.shape[0], rows_major.shape[1])
    result = []
    offset = 0
    for length in widths:
        result.append(
            rows_major[:, :, offset : offset + length].reshape(tokens, block_count * length)
        )
        offset += length
    return result


def real_blocks(real_part, imag_part, segments):
    pieces = []
    offset = 0
    for output_kind, length in segments:
        real_seg = real_part[:, offset : offset + length]
        imag_seg = imag_part[:, offset : offset + length]
        offset += length
        if output_kind == "pairs":
            stacked = jnp.transpose(jnp.stack((real_seg, imag_seg), axis=-1), (0, 2, 1, 3))
            pieces.append(stacked.reshape(stacked.shape[0], stacked.shape[1], 2 * length))
        else:
            pieces.append(jnp.transpose(real_seg, (0, 2, 1)))
    return jnp.concatenate(pieces, axis=2)


def segment_widths(segments):
    return [2 * length if output_kind == "pairs" else length for output_kind, length in segments]


def spread_forward(seq_rows, grid_info, fast_rank, segments):
    slow_count, fast_count = (grid_info[0], grid_info[1])
    blocks = to_channels(seq_rows).astype(jnp.float32)
    real_list = []
    imag_list = []
    offset = 0
    for length, packed in segments:
        segment = blocks[:, :, offset : offset + length]
        offset += length
        if packed:
            halves = segment.reshape(segment.shape[0], segment.shape[1], length // 2, 2)
            real_seg, imag_seg = (halves[..., 0], halves[..., 1])
        else:
            real_seg, imag_seg = (segment, jnp.zeros_like(segment))
        real_list.append(jnp.transpose(real_seg, (2, 0, 1)))
        imag_list.append(jnp.transpose(imag_seg, (2, 0, 1)))
    re_im = (
        jnp.concatenate(real_list, 0)[:, :, None, :],
        jnp.concatenate(imag_list, 0)[:, :, None, :],
    )
    re_im = front_forward(open_halves(re_im, grid_info, fast_rank), grid_info, fast_rank)
    re_im = (
        lax.all_to_all(re_im[0], "fast", split_axis=2, concat_axis=3, tiled=True),
        lax.all_to_all(re_im[1], "fast", split_axis=2, concat_axis=3, tiled=True),
    )
    return back_forward(re_im, grid_info, fast_rank * (slow_count // fast_count))


def spread_inverse(re_im, grid_info, fast_rank, slow_rank, segments):
    slow_count, fast_count, tokens, seq_length = grid_info
    re_im = back_inverse(re_im, grid_info, fast_rank * (slow_count // fast_count))
    re_im = (
        lax.all_to_all(re_im[0], "fast", split_axis=3, concat_axis=2, tiled=True),
        lax.all_to_all(re_im[1], "fast", split_axis=3, concat_axis=2, tiled=True),
    )
    re_im = front_inverse(re_im, grid_info, fast_rank)
    re_im = (
        lax.all_to_all(re_im[0], "slow", split_axis=2, concat_axis=1, tiled=True),
        lax.all_to_all(re_im[1], "slow", split_axis=2, concat_axis=1, tiled=True),
    )
    real_part, imag_part = fold_halves(
        re_im, positions(grid_info, 1, slow_rank, 1, fast_rank), seq_length
    )
    length = real_part.shape[0] // slow_count
    blocks = real_blocks(
        real_part.reshape(slow_count, length, tokens),
        imag_part.reshape(slow_count, length, tokens),
        segments,
    )
    rows_major = jnp.transpose(blocks, (1, 0, 2))
    return split_columns(rows_major, segment_widths(segments))


def regroup(re_im, length, local_groups):

    def by_group(values):
        values = values[:, :length]
        return values.reshape(
            (values.shape[0], local_groups, length // local_groups) + values.shape[2:]
        )

    return (by_group(re_im[0]), by_group(re_im[1]))


def flatten_pairs(re_im):

    def merged(values):
        return values.reshape(
            (values.shape[0], values.shape[1] * values.shape[2]) + values.shape[3:]
        )

    return (merged(re_im[0]), merged(re_im[1]))


def by_spectra(query_act, key_act, value_act, long_filter, out_grad):
    tokens, channels = query_act.shape
    groups = long_filter.shape[1]
    slow_count = lax.axis_size("slow")
    fast_count = lax.axis_size("fast")
    seq_length = tokens * slow_count * fast_count
    grid_info = (slow_count, fast_count, tokens, seq_length)
    group_width = channels // groups
    product = (key_act.astype(jnp.float32) * value_act.astype(jnp.float32)).astype(jnp.bfloat16)
    grad_in = (out_grad.astype(jnp.float32) * query_act.astype(jnp.float32)).astype(jnp.bfloat16)
    fast_rank = lax.axis_index("fast")
    slow_rank = lax.axis_index("slow")
    data_pairs = channels // (2 * slow_count)
    local_groups = groups // slow_count
    block_width = channels // slow_count
    spectra = spread_forward(
        merge_blocks((product, long_filter), slow_count),
        grid_info,
        fast_rank,
        ((block_width, True), (local_groups, False)),
    )
    prod_spec = regroup(spectra, data_pairs, local_groups)
    filter_spec = (spectra[0][:, data_pairs:, None], spectra[1][:, data_pairs:, None])
    convolved = spread_inverse(
        flatten_pairs(complex_times(prod_spec, filter_spec)),
        grid_info,
        fast_rank,
        slow_rank,
        (("pairs", data_pairs),),
    )[0]
    grad_spec = regroup(
        spread_forward(grad_in, grid_info, fast_rank, ((block_width, True),)),
        data_pairs,
        local_groups,
    )
    back_spec = flatten_pairs(conj_times(filter_spec, grad_spec))
    corr_spec = conj_times(prod_spec, grad_spec)
    joined = (
        jnp.concatenate((back_spec[0], jnp.sum(corr_spec[0], axis=2)), axis=1),
        jnp.concatenate((back_spec[1], jnp.sum(corr_spec[1], axis=2)), axis=1),
    )
    backward, filter_sum = spread_inverse(
        joined, grid_info, fast_rank, slow_rank, (("pairs", data_pairs), ("real", local_groups))
    )
    scale = 1.0 / math.sqrt(seq_length * group_width)
    mixed_out = (query_act.astype(jnp.float32) * convolved).astype(jnp.bfloat16)
    query_grad = (out_grad.astype(jnp.float32) * convolved).astype(jnp.bfloat16)
    key_grad = (backward * value_act.astype(jnp.float32)).astype(jnp.bfloat16)
    value_grad = (backward * key_act.astype(jnp.float32)).astype(jnp.bfloat16)
    return (mixed_out, query_grad, key_grad, value_grad, filter_sum * scale)


f32 = jnp.float32
bf16 = jnp.bfloat16
EXTRA_ROWS = 8


def dot(left, right):
    return jnp.dot(left, right, preferred_element_type=f32)


def dot_nt(left, right):
    return lax.dot_general(left, right, (((1,), (1,)), ((), ())), preferred_element_type=f32)


def ramp(shape, dim):
    return lax.broadcasted_iota(jnp.int32, shape, dim)


def flip_matrix(size):
    return (ramp((size, size), 0) + ramp((size, size), 1) == size - 1).astype(bf16)


def eye_matrix(size):
    return (ramp((size, size), 0) == ramp((size, size), 1)).astype(bf16)


def gate_kernel(query, key, value, filt, grad, sent):
    tokens, channels = query.shape
    groups, width = filt.shape[1], channels // filt.shape[1]
    product = (key[...].astype(f32) * value[...].astype(f32)).astype(bf16)
    grad_in = (grad[...].astype(f32) * query[...].astype(f32)).astype(bf16)
    sent[:, 0:width, :] = (
        product.astype(f32).T.astype(bf16).reshape(groups, width, tokens)
    )
    flipped = dot(flip_matrix(tokens), grad_in)
    sent[:, width : 2 * width, :] = flipped.T.astype(bf16).reshape(groups, width, tokens)
    taps = filt[...].astype(f32).T
    for group in range(groups):
        sent[group, 2 * width :, :] = jnp.broadcast_to(
            taps[group : group + 1], (EXTRA_ROWS, tokens)
        ).astype(bf16)


def group_kernel(scale, got, sent, streams, padded, toeplitz):
    blocks, _, tokens = got.shape
    width = (got.shape[1] - EXTRA_ROWS) // 2
    pairs = blocks // 2
    row, lane = ramp((tokens, tokens), 0), ramp((tokens, tokens), 1)
    for pair in range(pairs):
        for half in range(2):
            block = 2 * pair + half
            lanes = slice(half * tokens, (half + 1) * tokens)
            at = 2 * width * pair
            streams[at : at + width, lanes] = got[block, 0:width, :]
            streams[at + width : at + 2 * width, lanes] = got[blocks - 1 - block, width : 2 * width, :]
    for block in range(blocks):
        padded[block * width : (block + 1) * width, :] = got[block, width : 2 * width, :]
    padded[blocks * width :, :] = jnp.zeros((blocks * width, tokens), bf16)

    before = jnp.zeros((tokens, tokens), f32)
    for block in range(blocks):
        taps = jnp.broadcast_to(got[block, 2 * width : 2 * width + 1, :].astype(f32), (tokens, tokens))
        turned = pltpu.roll(taps, 0, 1, stride=1, stride_axis=0)
        toeplitz[block] = jnp.where(lane >= row, turned, before).astype(bf16)
        before = turned

    total = None
    for pair in range(pairs):
        left = jnp.zeros((tokens, tokens), bf16) if pair == 0 else toeplitz[2 * pair - 1]
        weights = jnp.concatenate(
            (
                jnp.concatenate((toeplitz[2 * pair], toeplitz[2 * pair + 1]), axis=1),
                jnp.concatenate((left, toeplitz[2 * pair]), axis=1),
            ),
            axis=0,
        )
        skip = 2 * width * pair
        term = dot(streams[0 : 2 * width * pairs - skip, :], weights)
        total = term if pair == 0 else jnp.concatenate((total[:skip], total[skip:] + term), axis=0)
    for pair in range(pairs):
        for half in range(2):
            block = 2 * pair + half
            lanes = slice(half * tokens, (half + 1) * tokens)
            at = 2 * width * pair
            sent[block, 0:width, :] = total[at : at + width, lanes].astype(bf16)
            sent[blocks - 1 - block, width : 2 * width, :] = total[
                at + width : at + 2 * width, lanes
            ].astype(bf16)

    ordered = got[:, 0:width, :].reshape(blocks * width, tokens).astype(f32).T.astype(bf16)
    carry = jnp.zeros((8, tokens), f32)
    which = ramp((EXTRA_ROWS, tokens), 0)
    for pair in range(pairs):
        depth = blocks * width if 2 * pair + 2 > blocks // 2 else blocks * width // 2
        columns = [
            padded[pl.ds((blocks - 1 - lag) * width, depth), :] for lag in (2 * pair, 2 * pair + 1)
        ]
        outer = dot(ordered[:, :depth], jnp.concatenate(columns, axis=1))
        for half in range(2):
            block = 2 * pair + half
            turned = pltpu.roll(
                outer[:, half * tokens : (half + 1) * tokens], 0, 1, stride=1, stride_axis=0
            )
            here = jnp.where(lane >= row, turned, 0.0).reshape(tokens // 8, 8, tokens).sum(axis=0)
            later = jnp.where(lane >= row, 0.0, turned).reshape(tokens // 8, 8, tokens).sum(axis=0)
            value = jnp.sum(here + carry, axis=0, keepdims=True) * scale
            carry = later
            high = value.astype(bf16).astype(f32)
            pieces = jnp.where(which == 0, high, jnp.where(which == 1, value - high, 0.0))
            sent[blocks - 1 - block, 2 * width :, :] = pieces.astype(bf16)


def output_kernel(got, query, key, value, grad, mixed, query_grad, key_grad, value_grad, filter_grad):
    blocks, _, tokens = got.shape
    width = (got.shape[1] - EXTRA_ROWS) // 2
    flip = flip_matrix(tokens)
    convolved = dot_nt(eye_matrix(tokens), got[:, 0:width, :].reshape(blocks * width, tokens))
    mixed[...] = (query[...].astype(f32) * convolved).astype(bf16)
    query_grad[...] = (grad[...].astype(f32) * convolved).astype(bf16)
    backward = dot_nt(flip, got[:, width : 2 * width, :].reshape(blocks * width, tokens))
    key_grad[...] = (backward * value[...].astype(f32)).astype(bf16)
    value_grad[...] = (backward * key[...].astype(f32)).astype(bf16)
    extra = got[:, 2 * width :, :].astype(f32)
    high = jnp.concatenate([extra[block, 0:1] for block in range(blocks)], axis=0)
    low = jnp.concatenate([extra[block, 1:2] for block in range(blocks)], axis=0)
    filter_grad[...] = dot_nt(flip, high.astype(bf16)) + dot_nt(flip, low.astype(bf16))


def by_groups(query_act, key_act, value_act, long_filter, out_grad):
    tokens, channels = query_act.shape
    groups = long_filter.shape[1]
    width = channels // groups
    rows = 2 * width + EXTRA_ROWS
    scale = 1.0 / math.sqrt(tokens * groups * width)
    sent = pl.pallas_call(
        gate_kernel,
        out_shape=jax.ShapeDtypeStruct((groups, rows, tokens), bf16),
        name="gate",
    )(query_act, key_act, value_act, long_filter, out_grad)
    got = lax.all_to_all(sent, ("slow", "fast"), split_axis=0, concat_axis=0, tiled=True)
    sent = pl.pallas_call(
        functools.partial(group_kernel, scale),
        out_shape=jax.ShapeDtypeStruct((groups, rows, tokens), bf16),
        scratch_shapes=[
            pltpu.VMEM((channels, 2 * tokens), bf16),
            pltpu.VMEM((2 * channels, tokens), bf16),
            pltpu.VMEM((groups, tokens, tokens), bf16),
        ],
        compiler_params=pltpu.CompilerParams(vmem_limit_bytes=32 * 2**20),
        name="group",
    )(got)
    got = lax.all_to_all(sent, ("slow", "fast"), split_axis=0, concat_axis=0, tiled=True)
    like = jax.ShapeDtypeStruct((tokens, channels), bf16)
    return pl.pallas_call(
        output_kernel,
        out_shape=(like, like, like, like, jax.ShapeDtypeStruct((tokens, groups), f32)),
        name="outputs",
    )(got, query_act, key_act, value_act, out_grad)


def on_device(query_act, key_act, value_act, long_filter, out_grad):
    tokens, channels = query_act.shape
    groups = long_filter.shape[1]
    devices = lax.axis_size("slow") * lax.axis_size("fast")
    if devices == groups and tokens == 128 and channels == 16 * groups and groups % 4 == 0:
        return by_groups(query_act, key_act, value_act, long_filter, out_grad)
    return by_spectra(query_act, key_act, value_act, long_filter, out_grad)


def solution(mesh):
    placed = (
        P(("slow", "fast"), None),
        P(("slow", "fast"), None),
        P(("slow", "fast"), None),
        P(("slow", "fast"), None),
        P(("slow", "fast"), None),
    )
    return jax.shard_map(
        on_device,
        mesh=mesh,
        in_specs=placed,
        out_specs=(
            P(("slow", "fast"), None),
            P(("slow", "fast"), None),
            P(("slow", "fast"), None),
            P(("slow", "fast"), None),
            P(("slow", "fast"), None),
        ),
        check_vma=False,
    )
```

```python
import functools
import math

import jax
import jax.numpy as jnp
from jax import lax
from jax.experimental import pallas as pl
from jax.experimental.pallas import tpu as pltpu
from jax.sharding import PartitionSpec as P

highest = lax.Precision.HIGHEST


def index_ramp(points, along, ndim, offset):
    shape_list = [1] * ndim
    shape_list[along] = points
    return (jnp.arange(points, dtype=jnp.int32) + offset).reshape(shape_list)


def apply_dft(re_im, points, direction, along):
    index_row = jnp.arange(points, dtype=jnp.int32)
    phase_turns = index_row[:, None] * index_row[None, :] % points
    phases = 2.0 * math.pi / points * phase_turns.astype(jnp.float32)
    cosine = jnp.cos(phases)
    sine_part = direction * jnp.sin(phases)

    def contract(values, matrix):
        result = jnp.tensordot(values, matrix, axes=((along,), (1,)), precision=highest)
        return jnp.moveaxis(result, -1, along)

    return (
        contract(re_im[0], cosine) - contract(re_im[1], sine_part),
        contract(re_im[0], sine_part) + contract(re_im[1], cosine),
    )


def rotate(re_im, phase_turns, period, direction):
    phases = 2.0 * math.pi / period * (phase_turns % period).astype(jnp.float32)
    cosine = jnp.cos(phases)
    sine_part = direction * jnp.sin(phases)
    return (re_im[0] * cosine - re_im[1] * sine_part, re_im[0] * sine_part + re_im[1] * cosine)


def complex_times(left, right):
    return (left[0] * right[0] - left[1] * right[1], left[0] * right[1] + left[1] * right[0])


def conj_times(left, right):
    return (left[0] * right[0] + left[1] * right[1], left[0] * right[1] - left[1] * right[0])


def positions(grid_info, slow_points, slow_offset, fast_points, fast_offset):
    fast_count, tokens = (grid_info[1], grid_info[2])
    block_index = index_ramp(slow_points, 2, 5, slow_offset) * fast_count + index_ramp(
        fast_points, 3, 5, fast_offset
    )
    return block_index * tokens + index_ramp(tokens, 4, 5, 0)


def open_halves(re_im, grid_info, fast_offset):
    token_place = positions(grid_info, re_im[0].shape[1], 0, re_im[0].shape[2], fast_offset)
    return rotate(
        (re_im[0][None], re_im[1][None]),
        index_ramp(2, 0, 5, 0) * token_place,
        2 * grid_info[3],
        -1.0,
    )


def fold_halves(re_im, token_place, seq_length):
    turned = rotate(re_im, index_ramp(2, 0, 5, 0) * token_place, 2 * seq_length, 1.0)
    scale = 0.5 / seq_length
    return (jnp.sum(turned[0], axis=0) * scale, jnp.sum(turned[1], axis=0) * scale)


def front_forward(re_im, grid_info, fast_offset):
    slow_count, fast_count = (grid_info[0], grid_info[1])
    re_im = apply_dft(re_im, slow_count, -1.0, 2)
    phase_turns = index_ramp(slow_count, 2, 5, 0) * index_ramp(re_im[0].shape[3], 3, 5, fast_offset)
    return rotate(re_im, phase_turns, slow_count * fast_count, -1.0)


def front_inverse(re_im, grid_info, fast_offset):
    slow_count, fast_count = (grid_info[0], grid_info[1])
    phase_turns = index_ramp(slow_count, 2, 5, 0) * index_ramp(re_im[0].shape[3], 3, 5, fast_offset)
    re_im = rotate(re_im, phase_turns, slow_count * fast_count, 1.0)
    return apply_dft(re_im, slow_count, 1.0, 2)


def lead_phase(re_im, grid_info, ka_offset):
    slow_count, fast_count, tokens = (grid_info[0], grid_info[1], grid_info[2])
    lead_index = index_ramp(re_im[0].shape[2], 2, 5, ka_offset) + slow_count * index_ramp(
        fast_count, 3, 5, 0
    )
    return lead_index * index_ramp(tokens, 4, 5, 0)


def back_forward(re_im, grid_info, ka_offset):
    re_im = apply_dft(re_im, grid_info[1], -1.0, 3)
    re_im = rotate(re_im, lead_phase(re_im, grid_info, ka_offset), grid_info[3], -1.0)
    return apply_dft(re_im, grid_info[2], -1.0, 4)


def back_inverse(re_im, grid_info, ka_offset):
    re_im = apply_dft(re_im, grid_info[2], 1.0, 4)
    re_im = rotate(re_im, lead_phase(re_im, grid_info, ka_offset), grid_info[3], 1.0)
    return apply_dft(re_im, grid_info[1], 1.0, 3)


def to_channels(seq_rows):
    return lax.all_to_all(
        seq_rows.reshape(1, seq_rows.shape[0], seq_rows.shape[1]),
        "slow",
        split_axis=2,
        concat_axis=0,
        tiled=True,
    )


def merge_blocks(arrays, block_count):
    tokens = arrays[0].shape[0]
    pieces = [item.reshape(tokens, block_count, item.shape[1] // block_count) for item in arrays]
    return jnp.concatenate(pieces, axis=2).reshape(tokens, -1)


def split_columns(rows_major, widths):
    tokens, block_count = (rows_major.shape[0], rows_major.shape[1])
    result = []
    offset = 0
    for length in widths:
        result.append(
            rows_major[:, :, offset : offset + length].reshape(tokens, block_count * length)
        )
        offset += length
    return result


def real_blocks(real_part, imag_part, segments):
    pieces = []
    offset = 0
    for output_kind, length in segments:
        real_seg = real_part[:, offset : offset + length]
        imag_seg = imag_part[:, offset : offset + length]
        offset += length
        if output_kind == "pairs":
            stacked = jnp.transpose(jnp.stack((real_seg, imag_seg), axis=-1), (0, 2, 1, 3))
            pieces.append(stacked.reshape(stacked.shape[0], stacked.shape[1], 2 * length))
        else:
            pieces.append(jnp.transpose(real_seg, (0, 2, 1)))
    return jnp.concatenate(pieces, axis=2)


def segment_widths(segments):
    return [2 * length if output_kind == "pairs" else length for output_kind, length in segments]


def spread_forward(seq_rows, grid_info, fast_rank, segments):
    slow_count, fast_count = (grid_info[0], grid_info[1])
    blocks = to_channels(seq_rows).astype(jnp.float32)
    real_list = []
    imag_list = []
    offset = 0
    for length, packed in segments:
        segment = blocks[:, :, offset : offset + length]
        offset += length
        if packed:
            halves = segment.reshape(segment.shape[0], segment.shape[1], length // 2, 2)
            real_seg, imag_seg = (halves[..., 0], halves[..., 1])
        else:
            real_seg, imag_seg = (segment, jnp.zeros_like(segment))
        real_list.append(jnp.transpose(real_seg, (2, 0, 1)))
        imag_list.append(jnp.transpose(imag_seg, (2, 0, 1)))
    re_im = (
        jnp.concatenate(real_list, 0)[:, :, None, :],
        jnp.concatenate(imag_list, 0)[:, :, None, :],
    )
    re_im = front_forward(open_halves(re_im, grid_info, fast_rank), grid_info, fast_rank)
    re_im = (
        lax.all_to_all(re_im[0], "fast", split_axis=2, concat_axis=3, tiled=True),
        lax.all_to_all(re_im[1], "fast", split_axis=2, concat_axis=3, tiled=True),
    )
    return back_forward(re_im, grid_info, fast_rank * (slow_count // fast_count))


def spread_inverse(re_im, grid_info, fast_rank, slow_rank, segments):
    slow_count, fast_count, tokens, seq_length = grid_info
    re_im = back_inverse(re_im, grid_info, fast_rank * (slow_count // fast_count))
    re_im = (
        lax.all_to_all(re_im[0], "fast", split_axis=3, concat_axis=2, tiled=True),
        lax.all_to_all(re_im[1], "fast", split_axis=3, concat_axis=2, tiled=True),
    )
    re_im = front_inverse(re_im, grid_info, fast_rank)
    re_im = (
        lax.all_to_all(re_im[0], "slow", split_axis=2, concat_axis=1, tiled=True),
        lax.all_to_all(re_im[1], "slow", split_axis=2, concat_axis=1, tiled=True),
    )
    real_part, imag_part = fold_halves(
        re_im, positions(grid_info, 1, slow_rank, 1, fast_rank), seq_length
    )
    length = real_part.shape[0] // slow_count
    blocks = real_blocks(
        real_part.reshape(slow_count, length, tokens),
        imag_part.reshape(slow_count, length, tokens),
        segments,
    )
    rows_major = jnp.transpose(blocks, (1, 0, 2))
    return split_columns(rows_major, segment_widths(segments))


def regroup(re_im, length, local_groups):

    def by_group(values):
        values = values[:, :length]
        return values.reshape(
            (values.shape[0], local_groups, length // local_groups) + values.shape[2:]
        )

    return (by_group(re_im[0]), by_group(re_im[1]))


def flatten_pairs(re_im):

    def merged(values):
        return values.reshape(
            (values.shape[0], values.shape[1] * values.shape[2]) + values.shape[3:]
        )

    return (merged(re_im[0]), merged(re_im[1]))


def by_spectra(query_act, key_act, value_act, long_filter, out_grad):
    tokens, channels = query_act.shape
    groups = long_filter.shape[1]
    slow_count = lax.axis_size("slow")
    fast_count = lax.axis_size("fast")
    seq_length = tokens * slow_count * fast_count
    grid_info = (slow_count, fast_count, tokens, seq_length)
    group_width = channels // groups
    product = (key_act.astype(jnp.float32) * value_act.astype(jnp.float32)).astype(jnp.bfloat16)
    grad_in = (out_grad.astype(jnp.float32) * query_act.astype(jnp.float32)).astype(jnp.bfloat16)
    fast_rank = lax.axis_index("fast")
    slow_rank = lax.axis_index("slow")
    data_pairs = channels // (2 * slow_count)
    local_groups = groups // slow_count
    block_width = channels // slow_count
    spectra = spread_forward(
        merge_blocks((product, long_filter), slow_count),
        grid_info,
        fast_rank,
        ((block_width, True), (local_groups, False)),
    )
    prod_spec = regroup(spectra, data_pairs, local_groups)
    filter_spec = (spectra[0][:, data_pairs:, None], spectra[1][:, data_pairs:, None])
    convolved = spread_inverse(
        flatten_pairs(complex_times(prod_spec, filter_spec)),
        grid_info,
        fast_rank,
        slow_rank,
        (("pairs", data_pairs),),
    )[0]
    grad_spec = regroup(
        spread_forward(grad_in, grid_info, fast_rank, ((block_width, True),)),
        data_pairs,
        local_groups,
    )
    back_spec = flatten_pairs(conj_times(filter_spec, grad_spec))
    corr_spec = conj_times(prod_spec, grad_spec)
    joined = (
        jnp.concatenate((back_spec[0], jnp.sum(corr_spec[0], axis=2)), axis=1),
        jnp.concatenate((back_spec[1], jnp.sum(corr_spec[1], axis=2)), axis=1),
    )
    backward, filter_sum = spread_inverse(
        joined, grid_info, fast_rank, slow_rank, (("pairs", data_pairs), ("real", local_groups))
    )
    scale = 1.0 / math.sqrt(seq_length * group_width)
    mixed_out = (query_act.astype(jnp.float32) * convolved).astype(jnp.bfloat16)
    query_grad = (out_grad.astype(jnp.float32) * convolved).astype(jnp.bfloat16)
    key_grad = (backward * value_act.astype(jnp.float32)).astype(jnp.bfloat16)
    value_grad = (backward * key_act.astype(jnp.float32)).astype(jnp.bfloat16)
    return (mixed_out, query_grad, key_grad, value_grad, filter_sum * scale)


f32 = jnp.float32
bf16 = jnp.bfloat16
EXTRA_ROWS = 8


def dot(left, right):
    return jnp.dot(left, right, preferred_element_type=f32)


def dot_nt(left, right):
    return lax.dot_general(left, right, (((1,), (1,)), ((), ())), preferred_element_type=f32)


def ramp(shape, dim):
    return lax.broadcasted_iota(jnp.int32, shape, dim)


def flip_matrix(size):
    return (ramp((size, size), 0) + ramp((size, size), 1) == size - 1).astype(bf16)


def eye_matrix(size):
    return (ramp((size, size), 0) == ramp((size, size), 1)).astype(bf16)


def gate_kernel(query, key, value, filt, grad, sent):
    tokens, channels = query.shape
    groups, width = filt.shape[0], channels // filt.shape[0]
    product = (key[...].astype(f32) * value[...].astype(f32)).astype(bf16)
    grad_in = (grad[...].astype(f32) * query[...].astype(f32)).astype(bf16)
    sent[:, 0:width, :] = (
        product.astype(f32).T.astype(bf16).reshape(groups, width, tokens)
    )
    flipped = dot(flip_matrix(tokens), grad_in)
    sent[:, width : 2 * width, :] = flipped.T.astype(bf16).reshape(groups, width, tokens)
    taps = filt[...].astype(f32)
    for group in range(groups):
        sent[group, 2 * width :, :] = jnp.broadcast_to(
            taps[group : group + 1], (EXTRA_ROWS, tokens)
        ).astype(bf16)


def group_kernel(scale, got, sent, streams, padded, toeplitz):
    blocks, _, tokens = got.shape
    width = (got.shape[1] - EXTRA_ROWS) // 2
    pairs = blocks // 2
    row, lane = ramp((tokens, tokens), 0), ramp((tokens, tokens), 1)
    for pair in range(pairs):
        for half in range(2):
            block = 2 * pair + half
            lanes = slice(half * tokens, (half + 1) * tokens)
            at = 2 * width * pair
            streams[at : at + width, lanes] = got[block, 0:width, :]
            streams[at + width : at + 2 * width, lanes] = got[blocks - 1 - block, width : 2 * width, :]
    for block in range(blocks):
        padded[block * width : (block + 1) * width, :] = got[block, width : 2 * width, :]
    padded[blocks * width :, :] = jnp.zeros((blocks * width, tokens), bf16)

    before = jnp.zeros((tokens, tokens), f32)
    for block in range(blocks):
        taps = jnp.broadcast_to(got[block, 2 * width : 2 * width + 1, :].astype(f32), (tokens, tokens))
        turned = pltpu.roll(taps, 0, 1, stride=1, stride_axis=0)
        toeplitz[block] = jnp.where(lane >= row, turned, before).astype(bf16)
        before = turned

    total = None
    for pair in range(pairs):
        left = jnp.zeros((tokens, tokens), bf16) if pair == 0 else toeplitz[2 * pair - 1]
        weights = jnp.concatenate(
            (
                jnp.concatenate((toeplitz[2 * pair], toeplitz[2 * pair + 1]), axis=1),
                jnp.concatenate((left, toeplitz[2 * pair]), axis=1),
            ),
            axis=0,
        )
        skip = 2 * width * pair
        term = dot(streams[0 : 2 * width * pairs - skip, :], weights)
        total = term if pair == 0 else jnp.concatenate((total[:skip], total[skip:] + term), axis=0)
    for pair in range(pairs):
        for half in range(2):
            block = 2 * pair + half
            lanes = slice(half * tokens, (half + 1) * tokens)
            at = 2 * width * pair
            sent[block, 0:width, :] = total[at : at + width, lanes].astype(bf16)
            sent[blocks - 1 - block, width : 2 * width, :] = total[
                at + width : at + 2 * width, lanes
            ].astype(bf16)

    ordered = got[:, 0:width, :].reshape(blocks * width, tokens).astype(f32).T.astype(bf16)
    carry = jnp.zeros((8, tokens), f32)
    which = ramp((EXTRA_ROWS, tokens), 0)
    for pair in range(pairs):
        depth = blocks * width if 2 * pair + 2 > blocks // 2 else blocks * width // 2
        columns = [
            padded[pl.ds((blocks - 1 - lag) * width, depth), :] for lag in (2 * pair, 2 * pair + 1)
        ]
        outer = dot(ordered[:, :depth], jnp.concatenate(columns, axis=1))
        for half in range(2):
            block = 2 * pair + half
            turned = pltpu.roll(
                outer[:, half * tokens : (half + 1) * tokens], 0, 1, stride=1, stride_axis=0
            )
            here = jnp.where(lane >= row, turned, 0.0).reshape(tokens // 8, 8, tokens).sum(axis=0)
            later = jnp.where(lane >= row, 0.0, turned).reshape(tokens // 8, 8, tokens).sum(axis=0)
            value = jnp.sum(here + carry, axis=0, keepdims=True) * scale
            carry = later
            high = value.astype(bf16).astype(f32)
            pieces = jnp.where(which == 0, high, jnp.where(which == 1, value - high, 0.0))
            sent[blocks - 1 - block, 2 * width :, :] = pieces.astype(bf16)


def output_kernel(got, query, key, value, grad, mixed, query_grad, key_grad, value_grad, filter_grad):
    blocks, _, tokens = got.shape
    width = (got.shape[1] - EXTRA_ROWS) // 2
    flip = flip_matrix(tokens)
    convolved = dot_nt(eye_matrix(tokens), got[:, 0:width, :].reshape(blocks * width, tokens))
    mixed[...] = (query[...].astype(f32) * convolved).astype(bf16)
    query_grad[...] = (grad[...].astype(f32) * convolved).astype(bf16)
    backward = dot_nt(flip, got[:, width : 2 * width, :].reshape(blocks * width, tokens))
    key_grad[...] = (backward * value[...].astype(f32)).astype(bf16)
    value_grad[...] = (backward * key[...].astype(f32)).astype(bf16)
    extra = got[:, 2 * width :, :].astype(f32)
    high = jnp.concatenate([extra[block, 0:1] for block in range(blocks)], axis=0)
    low = jnp.concatenate([extra[block, 1:2] for block in range(blocks)], axis=0)
    filter_grad[...] = dot(high.astype(bf16), flip) + dot(low.astype(bf16), flip)


def by_groups(query_act, key_act, value_act, long_filter, out_grad):
    tokens, channels = query_act.shape
    groups = long_filter.shape[1]
    width = channels // groups
    rows = 2 * width + EXTRA_ROWS
    scale = 1.0 / math.sqrt(tokens * groups * width)
    sent = pl.pallas_call(
        gate_kernel,
        out_shape=jax.ShapeDtypeStruct((groups, rows, tokens), bf16),
        compiler_params=pltpu.CompilerParams(vmem_limit_bytes=8 * 2**20),
        name="gate",
    )(query_act, key_act, value_act, long_filter.T, out_grad)
    got = lax.all_to_all(sent, ("slow", "fast"), split_axis=0, concat_axis=0, tiled=True)
    sent = pl.pallas_call(
        functools.partial(group_kernel, scale),
        out_shape=jax.ShapeDtypeStruct((groups, rows, tokens), bf16),
        scratch_shapes=[
            pltpu.VMEM((channels, 2 * tokens), bf16),
            pltpu.VMEM((2 * channels, tokens), bf16),
            pltpu.VMEM((groups, tokens, tokens), bf16),
        ],
        compiler_params=pltpu.CompilerParams(vmem_limit_bytes=16 * 2**20),
        name="group",
    )(got)
    got = lax.all_to_all(sent, ("slow", "fast"), split_axis=0, concat_axis=0, tiled=True)
    like = jax.ShapeDtypeStruct((tokens, channels), bf16)
    *acts, filter_grad = pl.pallas_call(
        output_kernel,
        out_shape=(like, like, like, like, jax.ShapeDtypeStruct((groups, tokens), f32)),
        compiler_params=pltpu.CompilerParams(vmem_limit_bytes=8 * 2**20),
        name="outputs",
    )(got, query_act, key_act, value_act, out_grad)
    return (*acts, filter_grad.T)


def on_device(query_act, key_act, value_act, long_filter, out_grad):
    tokens, channels = query_act.shape
    groups = long_filter.shape[1]
    devices = lax.axis_size("slow") * lax.axis_size("fast")
    if devices == groups and tokens == 128 and channels == 16 * groups and groups % 4 == 0:
        return by_groups(query_act, key_act, value_act, long_filter, out_grad)
    return by_spectra(query_act, key_act, value_act, long_filter, out_grad)


def solution(mesh):
    placed = (
        P(("slow", "fast"), None),
        P(("slow", "fast"), None),
        P(("slow", "fast"), None),
        P(("slow", "fast"), None),
        P(("slow", "fast"), None),
    )
    return jax.shard_map(
        on_device,
        mesh=mesh,
        in_specs=placed,
        out_specs=(
            P(("slow", "fast"), None),
            P(("slow", "fast"), None),
            P(("slow", "fast"), None),
            P(("slow", "fast"), None),
            P(("slow", "fast"), None),
        ),
        check_vma=False,
    )
```

```python
import functools
import math

import jax
import jax.numpy as jnp
from jax import lax
from jax.experimental import pallas as pl
from jax.experimental.pallas import tpu as pltpu
from jax.sharding import PartitionSpec as P

highest = lax.Precision.HIGHEST


def index_ramp(points, along, ndim, offset):
    shape_list = [1] * ndim
    shape_list[along] = points
    return (jnp.arange(points, dtype=jnp.int32) + offset).reshape(shape_list)


def apply_dft(re_im, points, direction, along):
    index_row = jnp.arange(points, dtype=jnp.int32)
    phase_turns = index_row[:, None] * index_row[None, :] % points
    phases = 2.0 * math.pi / points * phase_turns.astype(jnp.float32)
    cosine = jnp.cos(phases)
    sine_part = direction * jnp.sin(phases)

    def contract(values, matrix):
        result = jnp.tensordot(values, matrix, axes=((along,), (1,)), precision=highest)
        return jnp.moveaxis(result, -1, along)

    return (
        contract(re_im[0], cosine) - contract(re_im[1], sine_part),
        contract(re_im[0], sine_part) + contract(re_im[1], cosine),
    )


def rotate(re_im, phase_turns, period, direction):
    phases = 2.0 * math.pi / period * (phase_turns % period).astype(jnp.float32)
    cosine = jnp.cos(phases)
    sine_part = direction * jnp.sin(phases)
    return (re_im[0] * cosine - re_im[1] * sine_part, re_im[0] * sine_part + re_im[1] * cosine)


def complex_times(left, right):
    return (left[0] * right[0] - left[1] * right[1], left[0] * right[1] + left[1] * right[0])


def conj_times(left, right):
    return (left[0] * right[0] + left[1] * right[1], left[0] * right[1] - left[1] * right[0])


def positions(grid_info, slow_points, slow_offset, fast_points, fast_offset):
    fast_count, tokens = (grid_info[1], grid_info[2])
    block_index = index_ramp(slow_points, 2, 5, slow_offset) * fast_count + index_ramp(
        fast_points, 3, 5, fast_offset
    )
    return block_index * tokens + index_ramp(tokens, 4, 5, 0)


def open_halves(re_im, grid_info, fast_offset):
    token_place = positions(grid_info, re_im[0].shape[1], 0, re_im[0].shape[2], fast_offset)
    return rotate(
        (re_im[0][None], re_im[1][None]),
        index_ramp(2, 0, 5, 0) * token_place,
        2 * grid_info[3],
        -1.0,
    )


def fold_halves(re_im, token_place, seq_length):
    turned = rotate(re_im, index_ramp(2, 0, 5, 0) * token_place, 2 * seq_length, 1.0)
    scale = 0.5 / seq_length
    return (jnp.sum(turned[0], axis=0) * scale, jnp.sum(turned[1], axis=0) * scale)


def front_forward(re_im, grid_info, fast_offset):
    slow_count, fast_count = (grid_info[0], grid_info[1])
    re_im = apply_dft(re_im, slow_count, -1.0, 2)
    phase_turns = index_ramp(slow_count, 2, 5, 0) * index_ramp(re_im[0].shape[3], 3, 5, fast_offset)
    return rotate(re_im, phase_turns, slow_count * fast_count, -1.0)


def front_inverse(re_im, grid_info, fast_offset):
    slow_count, fast_count = (grid_info[0], grid_info[1])
    phase_turns = index_ramp(slow_count, 2, 5, 0) * index_ramp(re_im[0].shape[3], 3, 5, fast_offset)
    re_im = rotate(re_im, phase_turns, slow_count * fast_count, 1.0)
    return apply_dft(re_im, slow_count, 1.0, 2)


def lead_phase(re_im, grid_info, ka_offset):
    slow_count, fast_count, tokens = (grid_info[0], grid_info[1], grid_info[2])
    lead_index = index_ramp(re_im[0].shape[2], 2, 5, ka_offset) + slow_count * index_ramp(
        fast_count, 3, 5, 0
    )
    return lead_index * index_ramp(tokens, 4, 5, 0)


def back_forward(re_im, grid_info, ka_offset):
    re_im = apply_dft(re_im, grid_info[1], -1.0, 3)
    re_im = rotate(re_im, lead_phase(re_im, grid_info, ka_offset), grid_info[3], -1.0)
    return apply_dft(re_im, grid_info[2], -1.0, 4)


def back_inverse(re_im, grid_info, ka_offset):
    re_im = apply_dft(re_im, grid_info[2], 1.0, 4)
    re_im = rotate(re_im, lead_phase(re_im, grid_info, ka_offset), grid_info[3], 1.0)
    return apply_dft(re_im, grid_info[1], 1.0, 3)


def to_channels(seq_rows):
    return lax.all_to_all(
        seq_rows.reshape(1, seq_rows.shape[0], seq_rows.shape[1]),
        "slow",
        split_axis=2,
        concat_axis=0,
        tiled=True,
    )


def merge_blocks(arrays, block_count):
    tokens = arrays[0].shape[0]
    pieces = [item.reshape(tokens, block_count, item.shape[1] // block_count) for item in arrays]
    return jnp.concatenate(pieces, axis=2).reshape(tokens, -1)


def split_columns(rows_major, widths):
    tokens, block_count = (rows_major.shape[0], rows_major.shape[1])
    result = []
    offset = 0
    for length in widths:
        result.append(
            rows_major[:, :, offset : offset + length].reshape(tokens, block_count * length)
        )
        offset += length
    return result


def real_blocks(real_part, imag_part, segments):
    pieces = []
    offset = 0
    for output_kind, length in segments:
        real_seg = real_part[:, offset : offset + length]
        imag_seg = imag_part[:, offset : offset + length]
        offset += length
        if output_kind == "pairs":
            stacked = jnp.transpose(jnp.stack((real_seg, imag_seg), axis=-1), (0, 2, 1, 3))
            pieces.append(stacked.reshape(stacked.shape[0], stacked.shape[1], 2 * length))
        else:
            pieces.append(jnp.transpose(real_seg, (0, 2, 1)))
    return jnp.concatenate(pieces, axis=2)


def segment_widths(segments):
    return [2 * length if output_kind == "pairs" else length for output_kind, length in segments]


def spread_forward(seq_rows, grid_info, fast_rank, segments):
    slow_count, fast_count = (grid_info[0], grid_info[1])
    blocks = to_channels(seq_rows).astype(jnp.float32)
    real_list = []
    imag_list = []
    offset = 0
    for length, packed in segments:
        segment = blocks[:, :, offset : offset + length]
        offset += length
        if packed:
            halves = segment.reshape(segment.shape[0], segment.shape[1], length // 2, 2)
            real_seg, imag_seg = (halves[..., 0], halves[..., 1])
        else:
            real_seg, imag_seg = (segment, jnp.zeros_like(segment))
        real_list.append(jnp.transpose(real_seg, (2, 0, 1)))
        imag_list.append(jnp.transpose(imag_seg, (2, 0, 1)))
    re_im = (
        jnp.concatenate(real_list, 0)[:, :, None, :],
        jnp.concatenate(imag_list, 0)[:, :, None, :],
    )
    re_im = front_forward(open_halves(re_im, grid_info, fast_rank), grid_info, fast_rank)
    re_im = (
        lax.all_to_all(re_im[0], "fast", split_axis=2, concat_axis=3, tiled=True),
        lax.all_to_all(re_im[1], "fast", split_axis=2, concat_axis=3, tiled=True),
    )
    return back_forward(re_im, grid_info, fast_rank * (slow_count // fast_count))


def spread_inverse(re_im, grid_info, fast_rank, slow_rank, segments):
    slow_count, fast_count, tokens, seq_length = grid_info
    re_im = back_inverse(re_im, grid_info, fast_rank * (slow_count // fast_count))
    re_im = (
        lax.all_to_all(re_im[0], "fast", split_axis=3, concat_axis=2, tiled=True),
        lax.all_to_all(re_im[1], "fast", split_axis=3, concat_axis=2, tiled=True),
    )
    re_im = front_inverse(re_im, grid_info, fast_rank)
    re_im = (
        lax.all_to_all(re_im[0], "slow", split_axis=2, concat_axis=1, tiled=True),
        lax.all_to_all(re_im[1], "slow", split_axis=2, concat_axis=1, tiled=True),
    )
    real_part, imag_part = fold_halves(
        re_im, positions(grid_info, 1, slow_rank, 1, fast_rank), seq_length
    )
    length = real_part.shape[0] // slow_count
    blocks = real_blocks(
        real_part.reshape(slow_count, length, tokens),
        imag_part.reshape(slow_count, length, tokens),
        segments,
    )
    rows_major = jnp.transpose(blocks, (1, 0, 2))
    return split_columns(rows_major, segment_widths(segments))


def regroup(re_im, length, local_groups):

    def by_group(values):
        values = values[:, :length]
        return values.reshape(
            (values.shape[0], local_groups, length // local_groups) + values.shape[2:]
        )

    return (by_group(re_im[0]), by_group(re_im[1]))


def flatten_pairs(re_im):

    def merged(values):
        return values.reshape(
            (values.shape[0], values.shape[1] * values.shape[2]) + values.shape[3:]
        )

    return (merged(re_im[0]), merged(re_im[1]))


def by_spectra(query_act, key_act, value_act, long_filter, out_grad):
    tokens, channels = query_act.shape
    groups = long_filter.shape[1]
    slow_count = lax.axis_size("slow")
    fast_count = lax.axis_size("fast")
    seq_length = tokens * slow_count * fast_count
    grid_info = (slow_count, fast_count, tokens, seq_length)
    group_width = channels // groups
    product = (key_act.astype(jnp.float32) * value_act.astype(jnp.float32)).astype(jnp.bfloat16)
    grad_in = (out_grad.astype(jnp.float32) * query_act.astype(jnp.float32)).astype(jnp.bfloat16)
    fast_rank = lax.axis_index("fast")
    slow_rank = lax.axis_index("slow")
    data_pairs = channels // (2 * slow_count)
    local_groups = groups // slow_count
    block_width = channels // slow_count
    spectra = spread_forward(
        merge_blocks((product, long_filter), slow_count),
        grid_info,
        fast_rank,
        ((block_width, True), (local_groups, False)),
    )
    prod_spec = regroup(spectra, data_pairs, local_groups)
    filter_spec = (spectra[0][:, data_pairs:, None], spectra[1][:, data_pairs:, None])
    convolved = spread_inverse(
        flatten_pairs(complex_times(prod_spec, filter_spec)),
        grid_info,
        fast_rank,
        slow_rank,
        (("pairs", data_pairs),),
    )[0]
    grad_spec = regroup(
        spread_forward(grad_in, grid_info, fast_rank, ((block_width, True),)),
        data_pairs,
        local_groups,
    )
    back_spec = flatten_pairs(conj_times(filter_spec, grad_spec))
    corr_spec = conj_times(prod_spec, grad_spec)
    joined = (
        jnp.concatenate((back_spec[0], jnp.sum(corr_spec[0], axis=2)), axis=1),
        jnp.concatenate((back_spec[1], jnp.sum(corr_spec[1], axis=2)), axis=1),
    )
    backward, filter_sum = spread_inverse(
        joined, grid_info, fast_rank, slow_rank, (("pairs", data_pairs), ("real", local_groups))
    )
    scale = 1.0 / math.sqrt(seq_length * group_width)
    mixed_out = (query_act.astype(jnp.float32) * convolved).astype(jnp.bfloat16)
    query_grad = (out_grad.astype(jnp.float32) * convolved).astype(jnp.bfloat16)
    key_grad = (backward * value_act.astype(jnp.float32)).astype(jnp.bfloat16)
    value_grad = (backward * key_act.astype(jnp.float32)).astype(jnp.bfloat16)
    return (mixed_out, query_grad, key_grad, value_grad, filter_sum * scale)


f32 = jnp.float32
bf16 = jnp.bfloat16
EXTRA_ROWS = 2


def dot(left, right):
    return jnp.dot(left, right, preferred_element_type=f32)


def dot_nt(left, right):
    return lax.dot_general(left, right, (((1,), (1,)), ((), ())), preferred_element_type=f32)


def ramp(shape, dim):
    return lax.broadcasted_iota(jnp.int32, shape, dim)


def flip_matrix(size):
    return (ramp((size, size), 0) + ramp((size, size), 1) == size - 1).astype(bf16)


def eye_matrix(size):
    return (ramp((size, size), 0) == ramp((size, size), 1)).astype(bf16)


def gate_kernel(query, key, value, filt, grad, sent, queries, keys, values, taps, grads, done):
    copies = [
        pltpu.make_async_copy(source, target, done.at[at])
        for at, (source, target) in enumerate(
            ((key, keys), (value, values), (grad, grads), (query, queries), (filt, taps))
        )
    ]
    for copy in copies:
        copy.start()
    tokens, channels = queries.shape
    groups = taps.shape[0]
    width = channels // groups
    rows = 2 * width + EXTRA_ROWS
    copies[0].wait()
    copies[1].wait()
    product = (keys[...].astype(f32) * values[...].astype(f32)).astype(bf16)
    columns = product.astype(f32).T.astype(bf16)
    for group in range(groups):
        sent[group * rows : group * rows + width, :] = columns[group * width : (group + 1) * width]
    copies[2].wait()
    copies[3].wait()
    grad_in = (grads[...].astype(f32) * queries[...].astype(f32)).astype(bf16)
    columns = dot(flip_matrix(tokens), grad_in).T.astype(bf16)
    for group in range(groups):
        at = group * rows + width
        sent[at : at + width, :] = columns[group * width : (group + 1) * width]
    copies[4].wait()
    for group in range(groups):
        at = group * rows + 2 * width
        sent[at : at + EXTRA_ROWS, :] = jnp.broadcast_to(
            taps[group : group + 1, :], (EXTRA_ROWS, tokens)
        )


def group_kernel(scale, width, got, sent, streams, padded, toeplitz):
    rows, tokens = 2 * width + EXTRA_ROWS, got.shape[1]
    blocks = got.shape[0] // rows
    pairs = blocks // 2
    row, lane = ramp((tokens, tokens), 0), ramp((tokens, tokens), 1)
    for pair in range(pairs):
        for half in range(2):
            block = 2 * pair + half
            lanes = slice(half * tokens, (half + 1) * tokens)
            at = 2 * width * pair
            streams[at : at + width, lanes] = got[block * rows : block * rows + width, :]
            streams[at + width : at + 2 * width, lanes] = got[
                (blocks - 1 - block) * rows + width : (blocks - 1 - block) * rows + 2 * width, :
            ]
    for block in range(blocks):
        padded[block * width : (block + 1) * width, :] = got[
            block * rows + width : block * rows + 2 * width, :
        ]
    padded[blocks * width :, :] = jnp.zeros((blocks * width, tokens), bf16)

    before = jnp.zeros((tokens, tokens), f32)
    for block in range(blocks):
        taps = jnp.broadcast_to(got[block * rows + 2 * width : block * rows + 2 * width + 1, :].astype(f32), (tokens, tokens))
        turned = pltpu.roll(taps, 0, 1, stride=1, stride_axis=0)
        toeplitz[block] = jnp.where(lane >= row, turned, before).astype(bf16)
        before = turned

    total = None
    for pair in range(pairs):
        left = jnp.zeros((tokens, tokens), bf16) if pair == 0 else toeplitz[2 * pair - 1]
        weights = jnp.concatenate(
            (
                jnp.concatenate((toeplitz[2 * pair], toeplitz[2 * pair + 1]), axis=1),
                jnp.concatenate((left, toeplitz[2 * pair]), axis=1),
            ),
            axis=0,
        )
        skip = 2 * width * pair
        term = dot(streams[0 : 2 * width * pairs - skip, :], weights)
        total = term if pair == 0 else jnp.concatenate((total[:skip], total[skip:] + term), axis=0)
    for pair in range(pairs):
        for half in range(2):
            block = 2 * pair + half
            lanes = slice(half * tokens, (half + 1) * tokens)
            at = 2 * width * pair
            sent[block * rows : block * rows + width, :] = total[at : at + width, lanes].astype(bf16)
            place = (blocks - 1 - block) * rows + width
            sent[place : place + width, :] = total[
                at + width : at + 2 * width, lanes
            ].astype(bf16)

    ordered = jnp.concatenate(
        [got[block * rows : block * rows + width, :] for block in range(blocks)], axis=0
    )
    ordered = ordered.astype(f32).T.astype(bf16)
    carry = jnp.zeros((8, tokens), f32)
    which = ramp((EXTRA_ROWS, tokens), 0)
    for pair in range(pairs):
        depth = blocks * width if 2 * pair + 2 > blocks // 2 else blocks * width // 2
        columns = [
            padded[pl.ds((blocks - 1 - lag) * width, depth), :] for lag in (2 * pair, 2 * pair + 1)
        ]
        outer = dot(ordered[:, :depth], jnp.concatenate(columns, axis=1))
        for half in range(2):
            block = 2 * pair + half
            turned = pltpu.roll(
                outer[:, half * tokens : (half + 1) * tokens], 0, 1, stride=1, stride_axis=0
            )
            here = jnp.where(lane >= row, turned, 0.0).reshape(tokens // 8, 8, tokens).sum(axis=0)
            later = jnp.where(lane >= row, 0.0, turned).reshape(tokens // 8, 8, tokens).sum(axis=0)
            value = jnp.sum(here + carry, axis=0, keepdims=True) * scale
            carry = later
            high = value.astype(bf16).astype(f32)
            pieces = jnp.where(which == 0, high, jnp.where(which == 1, value - high, 0.0))
            place = (blocks - 1 - block) * rows + 2 * width
            sent[place : place + EXTRA_ROWS, :] = pieces.astype(bf16)


def output_kernel(
    width, got, query, key, value, grad, mixed, query_grad, key_grad, value_grad, filter_grad
):
    rows, tokens = 2 * width + EXTRA_ROWS, got.shape[1]
    blocks = got.shape[0] // rows

    def collect(first, count):
        return jnp.concatenate(
            [got[at * rows + first : at * rows + first + count, :] for at in range(blocks)], axis=0
        )

    flip = flip_matrix(tokens)
    convolved = dot_nt(eye_matrix(tokens), collect(0, width))
    mixed[...] = (query[...].astype(f32) * convolved).astype(bf16)
    query_grad[...] = (grad[...].astype(f32) * convolved).astype(bf16)
    backward = dot_nt(flip, collect(width, width))
    key_grad[...] = (backward * value[...].astype(f32)).astype(bf16)
    value_grad[...] = (backward * key[...].astype(f32)).astype(bf16)
    high, low = collect(2 * width, 1), collect(2 * width + 1, 1)
    filter_grad[...] = dot(high, flip) + dot(low, flip)


def by_groups(query_act, key_act, value_act, long_filter, out_grad):
    tokens, channels = query_act.shape
    groups = long_filter.shape[1]
    width = channels // groups
    rows = 2 * width + EXTRA_ROWS
    scale = 1.0 / math.sqrt(tokens * groups * width)
    chunks = jax.ShapeDtypeStruct((groups * rows, tokens), bf16)

    def exchange(sent):
        pieces = sent.reshape(groups, rows // 2, 2, tokens)
        pieces = lax.all_to_all(pieces, ("slow", "fast"), split_axis=0, concat_axis=0, tiled=True)
        return pieces.reshape(groups * rows, tokens)

    act = pltpu.VMEM((tokens, channels), bf16)
    sent = pl.pallas_call(
        gate_kernel,
        out_shape=chunks,
        in_specs=[pl.BlockSpec(memory_space=pltpu.HBM)] * 5,
        scratch_shapes=[
            act,
            act,
            act,
            pltpu.VMEM((groups, tokens), bf16),
            act,
            pltpu.SemaphoreType.DMA((5,)),
        ],
        compiler_params=pltpu.CompilerParams(vmem_limit_bytes=8 * 2**20),
        name="gate",
    )(query_act, key_act, value_act, long_filter.T, out_grad)
    got = exchange(sent)
    sent = pl.pallas_call(
        functools.partial(group_kernel, scale, width),
        out_shape=chunks,
        scratch_shapes=[
            pltpu.VMEM((channels, 2 * tokens), bf16),
            pltpu.VMEM((2 * channels, tokens), bf16),
            pltpu.VMEM((groups, tokens, tokens), bf16),
        ],
        compiler_params=pltpu.CompilerParams(vmem_limit_bytes=16 * 2**20),
        name="group",
    )(got)
    got = exchange(sent)
    like = jax.ShapeDtypeStruct((tokens, channels), bf16)
    *acts, filter_grad = pl.pallas_call(
        functools.partial(output_kernel, width),
        out_shape=(like, like, like, like, jax.ShapeDtypeStruct((groups, tokens), f32)),
        compiler_params=pltpu.CompilerParams(vmem_limit_bytes=8 * 2**20),
        name="outputs",
    )(got, query_act, key_act, value_act, out_grad)
    return (*acts, filter_grad.T)


def on_device(query_act, key_act, value_act, long_filter, out_grad):
    tokens, channels = query_act.shape
    groups = long_filter.shape[1]
    devices = lax.axis_size("slow") * lax.axis_size("fast")
    if devices == groups and tokens == 128 and channels == 16 * groups and groups % 4 == 0:
        return by_groups(query_act, key_act, value_act, long_filter, out_grad)
    return by_spectra(query_act, key_act, value_act, long_filter, out_grad)


def solution(mesh):
    placed = (
        P(("slow", "fast"), None),
        P(("slow", "fast"), None),
        P(("slow", "fast"), None),
        P(("slow", "fast"), None),
        P(("slow", "fast"), None),
    )
    return jax.shard_map(
        on_device,
        mesh=mesh,
        in_specs=placed,
        out_specs=(
            P(("slow", "fast"), None),
            P(("slow", "fast"), None),
            P(("slow", "fast"), None),
            P(("slow", "fast"), None),
            P(("slow", "fast"), None),
        ),
        check_vma=False,
    )
```

```python
import functools
import math

import jax
import jax.numpy as jnp
from jax import lax
from jax.experimental import pallas as pl
from jax.experimental.pallas import tpu as pltpu
from jax.sharding import PartitionSpec as P

highest = lax.Precision.HIGHEST


def index_ramp(points, along, ndim, offset):
    shape_list = [1] * ndim
    shape_list[along] = points
    return (jnp.arange(points, dtype=jnp.int32) + offset).reshape(shape_list)


def apply_dft(re_im, points, direction, along):
    index_row = jnp.arange(points, dtype=jnp.int32)
    phase_turns = index_row[:, None] * index_row[None, :] % points
    phases = 2.0 * math.pi / points * phase_turns.astype(jnp.float32)
    cosine = jnp.cos(phases)
    sine_part = direction * jnp.sin(phases)

    def contract(values, matrix):
        result = jnp.tensordot(values, matrix, axes=((along,), (1,)), precision=highest)
        return jnp.moveaxis(result, -1, along)

    return (
        contract(re_im[0], cosine) - contract(re_im[1], sine_part),
        contract(re_im[0], sine_part) + contract(re_im[1], cosine),
    )


def rotate(re_im, phase_turns, period, direction):
    phases = 2.0 * math.pi / period * (phase_turns % period).astype(jnp.float32)
    cosine = jnp.cos(phases)
    sine_part = direction * jnp.sin(phases)
    return (re_im[0] * cosine - re_im[1] * sine_part, re_im[0] * sine_part + re_im[1] * cosine)


def complex_times(left, right):
    return (left[0] * right[0] - left[1] * right[1], left[0] * right[1] + left[1] * right[0])


def conj_times(left, right):
    return (left[0] * right[0] + left[1] * right[1], left[0] * right[1] - left[1] * right[0])


def positions(grid_info, slow_points, slow_offset, fast_points, fast_offset):
    fast_count, tokens = (grid_info[1], grid_info[2])
    block_index = index_ramp(slow_points, 2, 5, slow_offset) * fast_count + index_ramp(
        fast_points, 3, 5, fast_offset
    )
    return block_index * tokens + index_ramp(tokens, 4, 5, 0)


def open_halves(re_im, grid_info, fast_offset):
    token_place = positions(grid_info, re_im[0].shape[1], 0, re_im[0].shape[2], fast_offset)
    return rotate(
        (re_im[0][None], re_im[1][None]),
        index_ramp(2, 0, 5, 0) * token_place,
        2 * grid_info[3],
        -1.0,
    )


def fold_halves(re_im, token_place, seq_length):
    turned = rotate(re_im, index_ramp(2, 0, 5, 0) * token_place, 2 * seq_length, 1.0)
    scale = 0.5 / seq_length
    return (jnp.sum(turned[0], axis=0) * scale, jnp.sum(turned[1], axis=0) * scale)


def front_forward(re_im, grid_info, fast_offset):
    slow_count, fast_count = (grid_info[0], grid_info[1])
    re_im = apply_dft(re_im, slow_count, -1.0, 2)
    phase_turns = index_ramp(slow_count, 2, 5, 0) * index_ramp(re_im[0].shape[3], 3, 5, fast_offset)
    return rotate(re_im, phase_turns, slow_count * fast_count, -1.0)


def front_inverse(re_im, grid_info, fast_offset):
    slow_count, fast_count = (grid_info[0], grid_info[1])
    phase_turns = index_ramp(slow_count, 2, 5, 0) * index_ramp(re_im[0].shape[3], 3, 5, fast_offset)
    re_im = rotate(re_im, phase_turns, slow_count * fast_count, 1.0)
    return apply_dft(re_im, slow_count, 1.0, 2)


def lead_phase(re_im, grid_info, ka_offset):
    slow_count, fast_count, tokens = (grid_info[0], grid_info[1], grid_info[2])
    lead_index = index_ramp(re_im[0].shape[2], 2, 5, ka_offset) + slow_count * index_ramp(
        fast_count, 3, 5, 0
    )
    return lead_index * index_ramp(tokens, 4, 5, 0)


def back_forward(re_im, grid_info, ka_offset):
    re_im = apply_dft(re_im, grid_info[1], -1.0, 3)
    re_im = rotate(re_im, lead_phase(re_im, grid_info, ka_offset), grid_info[3], -1.0)
    return apply_dft(re_im, grid_info[2], -1.0, 4)


def back_inverse(re_im, grid_info, ka_offset):
    re_im = apply_dft(re_im, grid_info[2], 1.0, 4)
    re_im = rotate(re_im, lead_phase(re_im, grid_info, ka_offset), grid_info[3], 1.0)
    return apply_dft(re_im, grid_info[1], 1.0, 3)


def to_channels(seq_rows):
    return lax.all_to_all(
        seq_rows.reshape(1, seq_rows.shape[0], seq_rows.shape[1]),
        "slow",
        split_axis=2,
        concat_axis=0,
        tiled=True,
    )


def merge_blocks(arrays, block_count):
    tokens = arrays[0].shape[0]
    pieces = [item.reshape(tokens, block_count, item.shape[1] // block_count) for item in arrays]
    return jnp.concatenate(pieces, axis=2).reshape(tokens, -1)


def split_columns(rows_major, widths):
    tokens, block_count = (rows_major.shape[0], rows_major.shape[1])
    result = []
    offset = 0
    for length in widths:
        result.append(
            rows_major[:, :, offset : offset + length].reshape(tokens, block_count * length)
        )
        offset += length
    return result


def real_blocks(real_part, imag_part, segments):
    pieces = []
    offset = 0
    for output_kind, length in segments:
        real_seg = real_part[:, offset : offset + length]
        imag_seg = imag_part[:, offset : offset + length]
        offset += length
        if output_kind == "pairs":
            stacked = jnp.transpose(jnp.stack((real_seg, imag_seg), axis=-1), (0, 2, 1, 3))
            pieces.append(stacked.reshape(stacked.shape[0], stacked.shape[1], 2 * length))
        else:
            pieces.append(jnp.transpose(real_seg, (0, 2, 1)))
    return jnp.concatenate(pieces, axis=2)


def segment_widths(segments):
    return [2 * length if output_kind == "pairs" else length for output_kind, length in segments]


def spread_forward(seq_rows, grid_info, fast_rank, segments):
    slow_count, fast_count = (grid_info[0], grid_info[1])
    blocks = to_channels(seq_rows).astype(jnp.float32)
    real_list = []
    imag_list = []
    offset = 0
    for length, packed in segments:
        segment = blocks[:, :, offset : offset + length]
        offset += length
        if packed:
            halves = segment.reshape(segment.shape[0], segment.shape[1], length // 2, 2)
            real_seg, imag_seg = (halves[..., 0], halves[..., 1])
        else:
            real_seg, imag_seg = (segment, jnp.zeros_like(segment))
        real_list.append(jnp.transpose(real_seg, (2, 0, 1)))
        imag_list.append(jnp.transpose(imag_seg, (2, 0, 1)))
    re_im = (
        jnp.concatenate(real_list, 0)[:, :, None, :],
        jnp.concatenate(imag_list, 0)[:, :, None, :],
    )
    re_im = front_forward(open_halves(re_im, grid_info, fast_rank), grid_info, fast_rank)
    re_im = (
        lax.all_to_all(re_im[0], "fast", split_axis=2, concat_axis=3, tiled=True),
        lax.all_to_all(re_im[1], "fast", split_axis=2, concat_axis=3, tiled=True),
    )
    return back_forward(re_im, grid_info, fast_rank * (slow_count // fast_count))


def spread_inverse(re_im, grid_info, fast_rank, slow_rank, segments):
    slow_count, fast_count, tokens, seq_length = grid_info
    re_im = back_inverse(re_im, grid_info, fast_rank * (slow_count // fast_count))
    re_im = (
        lax.all_to_all(re_im[0], "fast", split_axis=3, concat_axis=2, tiled=True),
        lax.all_to_all(re_im[1], "fast", split_axis=3, concat_axis=2, tiled=True),
    )
    re_im = front_inverse(re_im, grid_info, fast_rank)
    re_im = (
        lax.all_to_all(re_im[0], "slow", split_axis=2, concat_axis=1, tiled=True),
        lax.all_to_all(re_im[1], "slow", split_axis=2, concat_axis=1, tiled=True),
    )
    real_part, imag_part = fold_halves(
        re_im, positions(grid_info, 1, slow_rank, 1, fast_rank), seq_length
    )
    length = real_part.shape[0] // slow_count
    blocks = real_blocks(
        real_part.reshape(slow_count, length, tokens),
        imag_part.reshape(slow_count, length, tokens),
        segments,
    )
    rows_major = jnp.transpose(blocks, (1, 0, 2))
    return split_columns(rows_major, segment_widths(segments))


def regroup(re_im, length, local_groups):

    def by_group(values):
        values = values[:, :length]
        return values.reshape(
            (values.shape[0], local_groups, length // local_groups) + values.shape[2:]
        )

    return (by_group(re_im[0]), by_group(re_im[1]))


def flatten_pairs(re_im):

    def merged(values):
        return values.reshape(
            (values.shape[0], values.shape[1] * values.shape[2]) + values.shape[3:]
        )

    return (merged(re_im[0]), merged(re_im[1]))


def by_spectra(query_act, key_act, value_act, long_filter, out_grad):
    tokens, channels = query_act.shape
    groups = long_filter.shape[1]
    slow_count = lax.axis_size("slow")
    fast_count = lax.axis_size("fast")
    seq_length = tokens * slow_count * fast_count
    grid_info = (slow_count, fast_count, tokens, seq_length)
    group_width = channels // groups
    product = (key_act.astype(jnp.float32) * value_act.astype(jnp.float32)).astype(jnp.bfloat16)
    grad_in = (out_grad.astype(jnp.float32) * query_act.astype(jnp.float32)).astype(jnp.bfloat16)
    fast_rank = lax.axis_index("fast")
    slow_rank = lax.axis_index("slow")
    data_pairs = channels // (2 * slow_count)
    local_groups = groups // slow_count
    block_width = channels // slow_count
    spectra = spread_forward(
        merge_blocks((product, long_filter), slow_count),
        grid_info,
        fast_rank,
        ((block_width, True), (local_groups, False)),
    )
    prod_spec = regroup(spectra, data_pairs, local_groups)
    filter_spec = (spectra[0][:, data_pairs:, None], spectra[1][:, data_pairs:, None])
    convolved = spread_inverse(
        flatten_pairs(complex_times(prod_spec, filter_spec)),
        grid_info,
        fast_rank,
        slow_rank,
        (("pairs", data_pairs),),
    )[0]
    grad_spec = regroup(
        spread_forward(grad_in, grid_info, fast_rank, ((block_width, True),)),
        data_pairs,
        local_groups,
    )
    back_spec = flatten_pairs(conj_times(filter_spec, grad_spec))
    corr_spec = conj_times(prod_spec, grad_spec)
    joined = (
        jnp.concatenate((back_spec[0], jnp.sum(corr_spec[0], axis=2)), axis=1),
        jnp.concatenate((back_spec[1], jnp.sum(corr_spec[1], axis=2)), axis=1),
    )
    backward, filter_sum = spread_inverse(
        joined, grid_info, fast_rank, slow_rank, (("pairs", data_pairs), ("real", local_groups))
    )
    scale = 1.0 / math.sqrt(seq_length * group_width)
    mixed_out = (query_act.astype(jnp.float32) * convolved).astype(jnp.bfloat16)
    query_grad = (out_grad.astype(jnp.float32) * convolved).astype(jnp.bfloat16)
    key_grad = (backward * value_act.astype(jnp.float32)).astype(jnp.bfloat16)
    value_grad = (backward * key_act.astype(jnp.float32)).astype(jnp.bfloat16)
    return (mixed_out, query_grad, key_grad, value_grad, filter_sum * scale)


f32 = jnp.float32
bf16 = jnp.bfloat16
EXTRA_ROWS = 2


def dot(left, right):
    return jnp.dot(left, right, preferred_element_type=f32)


def dot_nt(left, right):
    return lax.dot_general(left, right, (((1,), (1,)), ((), ())), preferred_element_type=f32)


def ramp(shape, dim):
    return lax.broadcasted_iota(jnp.int32, shape, dim)


def flip_matrix(size):
    return (ramp((size, size), 0) + ramp((size, size), 1) == size - 1).astype(bf16)


def eye_matrix(size):
    return (ramp((size, size), 0) == ramp((size, size), 1)).astype(bf16)


def gate_kernel(query, key, value, filt, grad, sent, queries, keys, values, taps, grads, done):
    copies = [
        pltpu.make_async_copy(source, target, done.at[at])
        for at, (source, target) in enumerate(
            ((key, keys), (value, values), (grad, grads), (query, queries), (filt, taps))
        )
    ]
    for copy in copies:
        copy.start()
    tokens, channels = queries.shape
    groups = taps.shape[0]
    width = channels // groups
    rows = 2 * width + EXTRA_ROWS
    copies[0].wait()
    copies[1].wait()
    product = (keys[...].astype(f32) * values[...].astype(f32)).astype(bf16)
    columns = product.astype(f32).T.astype(bf16)
    for group in range(groups):
        sent[group * rows : group * rows + width, :] = columns[group * width : (group + 1) * width]
    copies[2].wait()
    copies[3].wait()
    grad_in = (grads[...].astype(f32) * queries[...].astype(f32)).astype(bf16)
    columns = dot(flip_matrix(tokens), grad_in).T.astype(bf16)
    for group in range(groups):
        at = group * rows + width
        sent[at : at + width, :] = columns[group * width : (group + 1) * width]
    copies[4].wait()
    for group in range(groups):
        at = group * rows + 2 * width
        sent[at : at + EXTRA_ROWS, :] = jnp.broadcast_to(
            taps[group : group + 1, :], (EXTRA_ROWS, tokens)
        )


def group_kernel(scale, width, got, sent, streams, padded, toeplitz):
    rows, tokens = 2 * width + EXTRA_ROWS, got.shape[1]
    blocks = got.shape[0] // rows
    pairs = blocks // 2
    row, lane = ramp((tokens, tokens), 0), ramp((tokens, tokens), 1)
    for pair in range(pairs):
        for half in range(2):
            block = 2 * pair + half
            lanes = slice(half * tokens, (half + 1) * tokens)
            at = 2 * width * pair
            streams[at : at + width, lanes] = got[block * rows : block * rows + width, :]
            streams[at + width : at + 2 * width, lanes] = got[
                (blocks - 1 - block) * rows + width : (blocks - 1 - block) * rows + 2 * width, :
            ]
    for block in range(blocks):
        padded[block * width : (block + 1) * width, :] = got[
            block * rows + width : block * rows + 2 * width, :
        ]
    padded[blocks * width :, :] = jnp.zeros((blocks * width, tokens), bf16)

    before = jnp.zeros((tokens, tokens), f32)
    for block in range(blocks):
        taps = jnp.broadcast_to(got[block * rows + 2 * width : block * rows + 2 * width + 1, :].astype(f32), (tokens, tokens))
        turned = pltpu.roll(taps, 0, 1, stride=1, stride_axis=0)
        toeplitz[block] = jnp.where(lane >= row, turned, before).astype(bf16)
        before = turned

    total = None
    for pair in range(pairs):
        left = jnp.zeros((tokens, tokens), bf16) if pair == 0 else toeplitz[2 * pair - 1]
        weights = jnp.concatenate(
            (
                jnp.concatenate((toeplitz[2 * pair], toeplitz[2 * pair + 1]), axis=1),
                jnp.concatenate((left, toeplitz[2 * pair]), axis=1),
            ),
            axis=0,
        )
        skip = 2 * width * pair
        term = dot(streams[0 : 2 * width * pairs - skip, :], weights)
        total = term if pair == 0 else jnp.concatenate((total[:skip], total[skip:] + term), axis=0)
    for pair in range(pairs):
        for half in range(2):
            block = 2 * pair + half
            lanes = slice(half * tokens, (half + 1) * tokens)
            at = 2 * width * pair
            sent[block * rows : block * rows + width, :] = total[at : at + width, lanes].astype(bf16)
            place = (blocks - 1 - block) * rows + width
            sent[place : place + width, :] = total[
                at + width : at + 2 * width, lanes
            ].astype(bf16)

    ordered = jnp.concatenate(
        [got[block * rows : block * rows + width, :] for block in range(blocks)], axis=0
    )
    ordered = ordered.astype(f32).T.astype(bf16)
    carry = jnp.zeros((8, tokens), f32)
    which = ramp((EXTRA_ROWS, tokens), 0)
    for pair in range(pairs):
        depth = blocks * width if 2 * pair + 2 > blocks // 2 else blocks * width // 2
        columns = [
            padded[pl.ds((blocks - 1 - lag) * width, depth), :] for lag in (2 * pair, 2 * pair + 1)
        ]
        outer = dot(ordered[:, :depth], jnp.concatenate(columns, axis=1))
        for half in range(2):
            block = 2 * pair + half
            turned = pltpu.roll(
                outer[:, half * tokens : (half + 1) * tokens], 0, 1, stride=1, stride_axis=0
            )
            here = jnp.where(lane >= row, turned, 0.0).reshape(tokens // 8, 8, tokens).sum(axis=0)
            later = jnp.where(lane >= row, 0.0, turned).reshape(tokens // 8, 8, tokens).sum(axis=0)
            value = jnp.sum(here + carry, axis=0, keepdims=True) * scale
            carry = later
            high = value.astype(bf16).astype(f32)
            pieces = jnp.where(which == 0, high, jnp.where(which == 1, value - high, 0.0))
            place = (blocks - 1 - block) * rows + 2 * width
            sent[place : place + EXTRA_ROWS, :] = pieces.astype(bf16)


def output_kernel(
    width, got, query, key, value, grad, mixed, query_grad, key_grad, value_grad, filter_grad
):
    rows, tokens = 2 * width + EXTRA_ROWS, got.shape[1]
    blocks = got.shape[0] // rows

    def collect(first, count):
        return jnp.concatenate(
            [got[at * rows + first : at * rows + first + count, :] for at in range(blocks)], axis=0
        )

    flip = flip_matrix(tokens)
    convolved = dot_nt(eye_matrix(tokens), collect(0, width))
    mixed[...] = (query[...].astype(f32) * convolved).astype(bf16)
    query_grad[...] = (grad[...].astype(f32) * convolved).astype(bf16)
    backward = dot_nt(flip, collect(width, width))
    key_grad[...] = (backward * value[...].astype(f32)).astype(bf16)
    value_grad[...] = (backward * key[...].astype(f32)).astype(bf16)
    high, low = collect(2 * width, 1), collect(2 * width + 1, 1)
    filter_grad[...] = dot(high, flip) + dot(low, flip)


def by_groups(query_act, key_act, value_act, long_filter, out_grad):
    tokens, channels = query_act.shape
    groups = long_filter.shape[1]
    width = channels // groups
    rows = 2 * width + EXTRA_ROWS
    scale = 1.0 / math.sqrt(tokens * groups * width)
    chunks = jax.ShapeDtypeStruct((groups * rows, tokens), bf16)

    def exchange(sent):
        pieces = sent.reshape(groups, rows // 2, 2, tokens)
        pieces = lax.all_to_all(pieces, ("slow", "fast"), split_axis=0, concat_axis=0, tiled=True)
        return pieces.reshape(groups * rows, tokens)

    act = pltpu.VMEM((tokens, channels), bf16)
    sent = pl.pallas_call(
        gate_kernel,
        out_shape=chunks,
        in_specs=[pl.BlockSpec(memory_space=pltpu.HBM)] * 5,
        scratch_shapes=[
            act,
            act,
            act,
            pltpu.VMEM((groups, tokens), bf16),
            act,
            pltpu.SemaphoreType.DMA((5,)),
        ],
        compiler_params=pltpu.CompilerParams(vmem_limit_bytes=8 * 2**20),
        name="gate",
    )(
        *(
            pltpu.with_memory_space_constraint(array, pltpu.HBM)
            for array in (query_act, key_act, value_act, long_filter.T, out_grad)
        )
    )
    got = exchange(sent)
    sent = pl.pallas_call(
        functools.partial(group_kernel, scale, width),
        out_shape=chunks,
        scratch_shapes=[
            pltpu.VMEM((channels, 2 * tokens), bf16),
            pltpu.VMEM((2 * channels, tokens), bf16),
            pltpu.VMEM((groups, tokens, tokens), bf16),
        ],
        compiler_params=pltpu.CompilerParams(vmem_limit_bytes=16 * 2**20),
        name="group",
    )(got)
    got = exchange(sent)
    like = jax.ShapeDtypeStruct((tokens, channels), bf16)
    *acts, filter_grad = pl.pallas_call(
        functools.partial(output_kernel, width),
        out_shape=(like, like, like, like, jax.ShapeDtypeStruct((groups, tokens), f32)),
        compiler_params=pltpu.CompilerParams(vmem_limit_bytes=8 * 2**20),
        name="outputs",
    )(got, query_act, key_act, value_act, out_grad)
    return (*acts, filter_grad.T)


def on_device(query_act, key_act, value_act, long_filter, out_grad):
    tokens, channels = query_act.shape
    groups = long_filter.shape[1]
    devices = lax.axis_size("slow") * lax.axis_size("fast")
    if devices == groups and tokens == 128 and channels == 16 * groups and groups % 4 == 0:
        return by_groups(query_act, key_act, value_act, long_filter, out_grad)
    return by_spectra(query_act, key_act, value_act, long_filter, out_grad)


def solution(mesh):
    placed = (
        P(("slow", "fast"), None),
        P(("slow", "fast"), None),
        P(("slow", "fast"), None),
        P(("slow", "fast"), None),
        P(("slow", "fast"), None),
    )
    return jax.shard_map(
        on_device,
        mesh=mesh,
        in_specs=placed,
        out_specs=(
            P(("slow", "fast"), None),
            P(("slow", "fast"), None),
            P(("slow", "fast"), None),
            P(("slow", "fast"), None),
            P(("slow", "fast"), None),
        ),
        check_vma=False,
    )
```

```python
import functools
import math

import jax
import jax.numpy as jnp
from jax import lax
from jax.experimental import pallas as pl
from jax.experimental.pallas import tpu as pltpu
from jax.sharding import PartitionSpec as P

highest = lax.Precision.HIGHEST


def index_ramp(points, along, ndim, offset):
    shape_list = [1] * ndim
    shape_list[along] = points
    return (jnp.arange(points, dtype=jnp.int32) + offset).reshape(shape_list)


def apply_dft(re_im, points, direction, along):
    index_row = jnp.arange(points, dtype=jnp.int32)
    phase_turns = index_row[:, None] * index_row[None, :] % points
    phases = 2.0 * math.pi / points * phase_turns.astype(jnp.float32)
    cosine = jnp.cos(phases)
    sine_part = direction * jnp.sin(phases)

    def contract(values, matrix):
        result = jnp.tensordot(values, matrix, axes=((along,), (1,)), precision=highest)
        return jnp.moveaxis(result, -1, along)

    return (
        contract(re_im[0], cosine) - contract(re_im[1], sine_part),
        contract(re_im[0], sine_part) + contract(re_im[1], cosine),
    )


def rotate(re_im, phase_turns, period, direction):
    phases = 2.0 * math.pi / period * (phase_turns % period).astype(jnp.float32)
    cosine = jnp.cos(phases)
    sine_part = direction * jnp.sin(phases)
    return (re_im[0] * cosine - re_im[1] * sine_part, re_im[0] * sine_part + re_im[1] * cosine)


def complex_times(left, right):
    return (left[0] * right[0] - left[1] * right[1], left[0] * right[1] + left[1] * right[0])


def conj_times(left, right):
    return (left[0] * right[0] + left[1] * right[1], left[0] * right[1] - left[1] * right[0])


def positions(grid_info, slow_points, slow_offset, fast_points, fast_offset):
    fast_count, tokens = (grid_info[1], grid_info[2])
    block_index = index_ramp(slow_points, 2, 5, slow_offset) * fast_count + index_ramp(
        fast_points, 3, 5, fast_offset
    )
    return block_index * tokens + index_ramp(tokens, 4, 5, 0)


def open_halves(re_im, grid_info, fast_offset):
    token_place = positions(grid_info, re_im[0].shape[1], 0, re_im[0].shape[2], fast_offset)
    return rotate(
        (re_im[0][None], re_im[1][None]),
        index_ramp(2, 0, 5, 0) * token_place,
        2 * grid_info[3],
        -1.0,
    )


def fold_halves(re_im, token_place, seq_length):
    turned = rotate(re_im, index_ramp(2, 0, 5, 0) * token_place, 2 * seq_length, 1.0)
    scale = 0.5 / seq_length
    return (jnp.sum(turned[0], axis=0) * scale, jnp.sum(turned[1], axis=0) * scale)


def front_forward(re_im, grid_info, fast_offset):
    slow_count, fast_count = (grid_info[0], grid_info[1])
    re_im = apply_dft(re_im, slow_count, -1.0, 2)
    phase_turns = index_ramp(slow_count, 2, 5, 0) * index_ramp(re_im[0].shape[3], 3, 5, fast_offset)
    return rotate(re_im, phase_turns, slow_count * fast_count, -1.0)


def front_inverse(re_im, grid_info, fast_offset):
    slow_count, fast_count = (grid_info[0], grid_info[1])
    phase_turns = index_ramp(slow_count, 2, 5, 0) * index_ramp(re_im[0].shape[3], 3, 5, fast_offset)
    re_im = rotate(re_im, phase_turns, slow_count * fast_count, 1.0)
    return apply_dft(re_im, slow_count, 1.0, 2)


def lead_phase(re_im, grid_info, ka_offset):
    slow_count, fast_count, tokens = (grid_info[0], grid_info[1], grid_info[2])
    lead_index = index_ramp(re_im[0].shape[2], 2, 5, ka_offset) + slow_count * index_ramp(
        fast_count, 3, 5, 0
    )
    return lead_index * index_ramp(tokens, 4, 5, 0)


def back_forward(re_im, grid_info, ka_offset):
    re_im = apply_dft(re_im, grid_info[1], -1.0, 3)
    re_im = rotate(re_im, lead_phase(re_im, grid_info, ka_offset), grid_info[3], -1.0)
    return apply_dft(re_im, grid_info[2], -1.0, 4)


def back_inverse(re_im, grid_info, ka_offset):
    re_im = apply_dft(re_im, grid_info[2], 1.0, 4)
    re_im = rotate(re_im, lead_phase(re_im, grid_info, ka_offset), grid_info[3], 1.0)
    return apply_dft(re_im, grid_info[1], 1.0, 3)


def to_channels(seq_rows):
    return lax.all_to_all(
        seq_rows.reshape(1, seq_rows.shape[0], seq_rows.shape[1]),
        "slow",
        split_axis=2,
        concat_axis=0,
        tiled=True,
    )


def merge_blocks(arrays, block_count):
    tokens = arrays[0].shape[0]
    pieces = [item.reshape(tokens, block_count, item.shape[1] // block_count) for item in arrays]
    return jnp.concatenate(pieces, axis=2).reshape(tokens, -1)


def split_columns(rows_major, widths):
    tokens, block_count = (rows_major.shape[0], rows_major.shape[1])
    result = []
    offset = 0
    for length in widths:
        result.append(
            rows_major[:, :, offset : offset + length].reshape(tokens, block_count * length)
        )
        offset += length
    return result


def real_blocks(real_part, imag_part, segments):
    pieces = []
    offset = 0
    for output_kind, length in segments:
        real_seg = real_part[:, offset : offset + length]
        imag_seg = imag_part[:, offset : offset + length]
        offset += length
        if output_kind == "pairs":
            stacked = jnp.transpose(jnp.stack((real_seg, imag_seg), axis=-1), (0, 2, 1, 3))
            pieces.append(stacked.reshape(stacked.shape[0], stacked.shape[1], 2 * length))
        else:
            pieces.append(jnp.transpose(real_seg, (0, 2, 1)))
    return jnp.concatenate(pieces, axis=2)


def segment_widths(segments):
    return [2 * length if output_kind == "pairs" else length for output_kind, length in segments]


def spread_forward(seq_rows, grid_info, fast_rank, segments):
    slow_count, fast_count = (grid_info[0], grid_info[1])
    blocks = to_channels(seq_rows).astype(jnp.float32)
    real_list = []
    imag_list = []
    offset = 0
    for length, packed in segments:
        segment = blocks[:, :, offset : offset + length]
        offset += length
        if packed:
            halves = segment.reshape(segment.shape[0], segment.shape[1], length // 2, 2)
            real_seg, imag_seg = (halves[..., 0], halves[..., 1])
        else:
            real_seg, imag_seg = (segment, jnp.zeros_like(segment))
        real_list.append(jnp.transpose(real_seg, (2, 0, 1)))
        imag_list.append(jnp.transpose(imag_seg, (2, 0, 1)))
    re_im = (
        jnp.concatenate(real_list, 0)[:, :, None, :],
        jnp.concatenate(imag_list, 0)[:, :, None, :],
    )
    re_im = front_forward(open_halves(re_im, grid_info, fast_rank), grid_info, fast_rank)
    re_im = (
        lax.all_to_all(re_im[0], "fast", split_axis=2, concat_axis=3, tiled=True),
        lax.all_to_all(re_im[1], "fast", split_axis=2, concat_axis=3, tiled=True),
    )
    return back_forward(re_im, grid_info, fast_rank * (slow_count // fast_count))


def spread_inverse(re_im, grid_info, fast_rank, slow_rank, segments):
    slow_count, fast_count, tokens, seq_length = grid_info
    re_im = back_inverse(re_im, grid_info, fast_rank * (slow_count // fast_count))
    re_im = (
        lax.all_to_all(re_im[0], "fast", split_axis=3, concat_axis=2, tiled=True),
        lax.all_to_all(re_im[1], "fast", split_axis=3, concat_axis=2, tiled=True),
    )
    re_im = front_inverse(re_im, grid_info, fast_rank)
    re_im = (
        lax.all_to_all(re_im[0], "slow", split_axis=2, concat_axis=1, tiled=True),
        lax.all_to_all(re_im[1], "slow", split_axis=2, concat_axis=1, tiled=True),
    )
    real_part, imag_part = fold_halves(
        re_im, positions(grid_info, 1, slow_rank, 1, fast_rank), seq_length
    )
    length = real_part.shape[0] // slow_count
    blocks = real_blocks(
        real_part.reshape(slow_count, length, tokens),
        imag_part.reshape(slow_count, length, tokens),
        segments,
    )
    rows_major = jnp.transpose(blocks, (1, 0, 2))
    return split_columns(rows_major, segment_widths(segments))


def regroup(re_im, length, local_groups):

    def by_group(values):
        values = values[:, :length]
        return values.reshape(
            (values.shape[0], local_groups, length // local_groups) + values.shape[2:]
        )

    return (by_group(re_im[0]), by_group(re_im[1]))


def flatten_pairs(re_im):

    def merged(values):
        return values.reshape(
            (values.shape[0], values.shape[1] * values.shape[2]) + values.shape[3:]
        )

    return (merged(re_im[0]), merged(re_im[1]))


def by_spectra(query_act, key_act, value_act, long_filter, out_grad):
    tokens, channels = query_act.shape
    groups = long_filter.shape[1]
    slow_count = lax.axis_size("slow")
    fast_count = lax.axis_size("fast")
    seq_length = tokens * slow_count * fast_count
    grid_info = (slow_count, fast_count, tokens, seq_length)
    group_width = channels // groups
    product = (key_act.astype(jnp.float32) * value_act.astype(jnp.float32)).astype(jnp.bfloat16)
    grad_in = (out_grad.astype(jnp.float32) * query_act.astype(jnp.float32)).astype(jnp.bfloat16)
    fast_rank = lax.axis_index("fast")
    slow_rank = lax.axis_index("slow")
    data_pairs = channels // (2 * slow_count)
    local_groups = groups // slow_count
    block_width = channels // slow_count
    spectra = spread_forward(
        merge_blocks((product, long_filter), slow_count),
        grid_info,
        fast_rank,
        ((block_width, True), (local_groups, False)),
    )
    prod_spec = regroup(spectra, data_pairs, local_groups)
    filter_spec = (spectra[0][:, data_pairs:, None], spectra[1][:, data_pairs:, None])
    convolved = spread_inverse(
        flatten_pairs(complex_times(prod_spec, filter_spec)),
        grid_info,
        fast_rank,
        slow_rank,
        (("pairs", data_pairs),),
    )[0]
    grad_spec = regroup(
        spread_forward(grad_in, grid_info, fast_rank, ((block_width, True),)),
        data_pairs,
        local_groups,
    )
    back_spec = flatten_pairs(conj_times(filter_spec, grad_spec))
    corr_spec = conj_times(prod_spec, grad_spec)
    joined = (
        jnp.concatenate((back_spec[0], jnp.sum(corr_spec[0], axis=2)), axis=1),
        jnp.concatenate((back_spec[1], jnp.sum(corr_spec[1], axis=2)), axis=1),
    )
    backward, filter_sum = spread_inverse(
        joined, grid_info, fast_rank, slow_rank, (("pairs", data_pairs), ("real", local_groups))
    )
    scale = 1.0 / math.sqrt(seq_length * group_width)
    mixed_out = (query_act.astype(jnp.float32) * convolved).astype(jnp.bfloat16)
    query_grad = (out_grad.astype(jnp.float32) * convolved).astype(jnp.bfloat16)
    key_grad = (backward * value_act.astype(jnp.float32)).astype(jnp.bfloat16)
    value_grad = (backward * key_act.astype(jnp.float32)).astype(jnp.bfloat16)
    return (mixed_out, query_grad, key_grad, value_grad, filter_sum * scale)


f32 = jnp.float32
bf16 = jnp.bfloat16
EXTRA_ROWS = 2


def dot(left, right):
    return jnp.dot(left, right, preferred_element_type=f32)


def dot_nt(left, right):
    return lax.dot_general(left, right, (((1,), (1,)), ((), ())), preferred_element_type=f32)


def ramp(shape, dim):
    return lax.broadcasted_iota(jnp.int32, shape, dim)


def flip_matrix(size):
    return (ramp((size, size), 0) + ramp((size, size), 1) == size - 1).astype(bf16)


def eye_matrix(size):
    return (ramp((size, size), 0) == ramp((size, size), 1)).astype(bf16)


def store_chunks(place, sources, targets, rows):
    products, grads, extras, chips, aside = sources
    width = products.shape[1]
    for core, target in enumerate(targets):
        for at, chip in enumerate(chips):
            block = place ^ (chip ^ (aside if core else 0))
            target[at * rows : at * rows + width, :] = products[block]
            target[at * rows + width : at * rows + 2 * width, :] = grads[block]
            target[at * rows + 2 * width : (at + 1) * rows, :] = extras[block][0:EXTRA_ROWS].astype(bf16)


def load_chunks(place, got, stores, rows):
    own, other, *far = got
    products, grads, extras, chips, aside = stores
    width = products.shape[1]
    for core in range(2):
        for at, chip in enumerate(chips):
            block = place ^ (chip ^ (aside if core else 0))
            source, first = (far[at - 1], core * rows) if at else ((own, other)[core], 0)
            products[block] = source[first : first + width, :]
            grads[block] = source[first + width : first + 2 * width, :]
            extras[block, 0:EXTRA_ROWS] = source[first + 2 * width : first + rows, :].astype(f32)


def device_place():
    return lax.axis_index("slow") * lax.axis_size("fast") + lax.axis_index("fast")


def gate_kernel(plan, *refs):
    query, key, value, filt, grad, own, other = refs[:7]
    products, grads_in, extras, queries, keys, values, taps, grads, done = refs[7:]
    copies = [
        pltpu.make_async_copy(source, target, done.at[at])
        for at, (source, target) in enumerate(
            ((key, keys), (value, values), (grad, grads), (query, queries), (filt, taps))
        )
    ]
    for copy in copies:
        copy.start()
    tokens, channels = queries.shape
    groups = taps.shape[0]
    width = channels // groups
    copies[0].wait()
    copies[1].wait()
    product = (keys[...].astype(f32) * values[...].astype(f32)).astype(bf16)
    products[...] = product.astype(f32).T.astype(bf16).reshape(groups, width, tokens)
    copies[2].wait()
    copies[3].wait()
    grad_in = (grads[...].astype(f32) * queries[...].astype(f32)).astype(bf16)
    flipped = dot(flip_matrix(tokens), grad_in)
    grads_in[...] = flipped.T.astype(bf16).reshape(groups, width, tokens)
    copies[4].wait()
    for group in range(groups):
        extras[group, 0:EXTRA_ROWS] = jnp.broadcast_to(
            taps[group : group + 1, :].astype(f32), (EXTRA_ROWS, tokens)
        )
    sources = (products, grads_in, extras, *plan)
    store_chunks(device_place(), sources, (own, other), 2 * width + EXTRA_ROWS)


def join_kernel(rows, own, other, *joined):
    for at, target in enumerate(joined, start=1):
        target[0:rows, :] = own[at * rows : (at + 1) * rows, :]
        target[rows:, :] = other[at * rows : (at + 1) * rows, :]


def group_kernel(plan, scale, *refs):
    count = len(plan[0]) + 1
    got, (own, other) = refs[:count], refs[count : count + 2]
    products, grads, extras, streams, padded, toeplitz = refs[count + 2 :]
    blocks, width, tokens = products.shape
    rows = 2 * width + EXTRA_ROWS
    place = device_place()
    load_chunks(place, got, (products, grads, extras, *plan), rows)

    pairs = blocks // 2
    row, lane = ramp((tokens, tokens), 0), ramp((tokens, tokens), 1)
    for pair in range(pairs):
        for half in range(2):
            block = 2 * pair + half
            lanes = slice(half * tokens, (half + 1) * tokens)
            at = 2 * width * pair
            streams[at : at + width, lanes] = products[block]
            streams[at + width : at + 2 * width, lanes] = grads[blocks - 1 - block]
    padded[0 : blocks * width, :] = grads[...].reshape(blocks * width, tokens)
    padded[blocks * width :, :] = jnp.zeros((blocks * width, tokens), bf16)
    ordered = products[...].reshape(blocks * width, tokens).astype(f32).T.astype(bf16)

    before = jnp.zeros((tokens, tokens), f32)
    for block in range(blocks):
        taps = jnp.broadcast_to(extras[block, 0:1], (tokens, tokens))
        turned = pltpu.roll(taps, 0, 1, stride=1, stride_axis=0)
        toeplitz[block] = jnp.where(lane >= row, turned, before).astype(bf16)
        before = turned

    total = None
    for pair in range(pairs):
        left = jnp.zeros((tokens, tokens), bf16) if pair == 0 else toeplitz[2 * pair - 1]
        weights = jnp.concatenate(
            (
                jnp.concatenate((toeplitz[2 * pair], toeplitz[2 * pair + 1]), axis=1),
                jnp.concatenate((left, toeplitz[2 * pair]), axis=1),
            ),
            axis=0,
        )
        skip = 2 * width * pair
        term = dot(streams[0 : 2 * width * pairs - skip, :], weights)
        total = term if pair == 0 else jnp.concatenate((total[:skip], total[skip:] + term), axis=0)
    for pair in range(pairs):
        for half in range(2):
            block = 2 * pair + half
            lanes = slice(half * tokens, (half + 1) * tokens)
            at = 2 * width * pair
            products[block] = total[at : at + width, lanes].astype(bf16)
            grads[blocks - 1 - block] = total[at + width : at + 2 * width, lanes].astype(bf16)

    carry = jnp.zeros((8, tokens), f32)
    which = ramp((EXTRA_ROWS, tokens), 0)
    for pair in range(pairs):
        depth = blocks * width if 2 * pair + 2 > blocks // 2 else blocks * width // 2
        columns = [
            padded[pl.ds((blocks - 1 - lag) * width, depth), :] for lag in (2 * pair, 2 * pair + 1)
        ]
        outer = dot(ordered[:, :depth], jnp.concatenate(columns, axis=1))
        for half in range(2):
            block = 2 * pair + half
            turned = pltpu.roll(
                outer[:, half * tokens : (half + 1) * tokens], 0, 1, stride=1, stride_axis=0
            )
            here = jnp.where(lane >= row, turned, 0.0).reshape(tokens // 8, 8, tokens).sum(axis=0)
            later = jnp.where(lane >= row, 0.0, turned).reshape(tokens // 8, 8, tokens).sum(axis=0)
            value = jnp.sum(here + carry, axis=0, keepdims=True) * scale
            carry = later
            high = value.astype(bf16).astype(f32)
            extras[blocks - 1 - block, 0:EXTRA_ROWS] = jnp.where(which == 0, high, value - high)
    store_chunks(place, (products, grads, extras, *plan), (own, other), rows)


def output_kernel(plan, *refs):
    count = len(plan[0]) + 1
    got, (query, key, value, grad) = refs[:count], refs[count : count + 4]
    mixed, query_grad, key_grad, value_grad, filter_grad = refs[count + 4 : count + 9]
    products, grads, extras = refs[count + 9 :]
    blocks, width, tokens = products.shape
    load_chunks(
        device_place(), got, (products, grads, extras, *plan), 2 * width + EXTRA_ROWS
    )
    flip = flip_matrix(tokens)
    convolved = dot_nt(eye_matrix(tokens), products[...].reshape(blocks * width, tokens))
    mixed[...] = (query[...].astype(f32) * convolved).astype(bf16)
    query_grad[...] = (grad[...].astype(f32) * convolved).astype(bf16)
    backward = dot_nt(flip, grads[...].reshape(blocks * width, tokens))
    key_grad[...] = (backward * value[...].astype(f32)).astype(bf16)
    value_grad[...] = (backward * key[...].astype(f32)).astype(bf16)
    high, low = (
        jnp.concatenate([extras[block, at : at + 1] for block in range(blocks)], axis=0)
        for at in range(2)
    )
    filter_grad[...] = dot(high.astype(bf16), flip) + dot(low.astype(bf16), flip)


def by_groups(query_act, key_act, value_act, long_filter, out_grad):
    tokens, channels = query_act.shape
    groups = long_filter.shape[1]
    width = channels // groups
    rows = 2 * width + EXTRA_ROWS
    scale = 1.0 / math.sqrt(tokens * groups * width)
    aside = lax.axis_size("fast")
    chips = tuple(place for place in range(groups) if not place & aside)
    plan = (chips, aside)
    half = jax.ShapeDtypeStruct((len(chips) * rows, tokens), bf16)
    blocks = (
        pltpu.VMEM((groups, width, tokens), bf16),
        pltpu.VMEM((groups, width, tokens), bf16),
        pltpu.VMEM((groups, 8, tokens), f32),
    )

    def swap(array, difference):
        pairs = [(place, place ^ difference) for place in range(groups)]
        return lax.ppermute(array, ("slow", "fast"), pairs)

    def exchange(own, other):
        other = swap(other, aside)
        joined = pl.pallas_call(
            functools.partial(join_kernel, rows),
            out_shape=[jax.ShapeDtypeStruct((2 * rows, tokens), bf16)] * (len(chips) - 1),
            compiler_params=pltpu.CompilerParams(vmem_limit_bytes=8 * 2**20),
            name="join",
        )(own, other)
        return own, other, *(swap(array, chip) for array, chip in zip(joined, chips[1:]))

    act = pltpu.VMEM((tokens, channels), bf16)
    sent = pl.pallas_call(
        functools.partial(gate_kernel, plan),
        out_shape=(half, half),
        in_specs=[pl.BlockSpec(memory_space=pltpu.HBM)] * 5,
        scratch_shapes=[
            *blocks,
            act,
            act,
            act,
            pltpu.VMEM((groups, tokens), bf16),
            act,
            pltpu.SemaphoreType.DMA((5,)),
        ],
        compiler_params=pltpu.CompilerParams(vmem_limit_bytes=8 * 2**20),
        name="gate",
    )(
        *(
            pltpu.with_memory_space_constraint(array, pltpu.HBM)
            for array in (query_act, key_act, value_act, long_filter.T, out_grad)
        )
    )
    got = exchange(*sent)
    sent = pl.pallas_call(
        functools.partial(group_kernel, plan, scale),
        out_shape=(half, half),
        scratch_shapes=[
            *blocks,
            pltpu.VMEM((channels, 2 * tokens), bf16),
            pltpu.VMEM((2 * channels, tokens), bf16),
            pltpu.VMEM((groups, tokens, tokens), bf16),
        ],
        compiler_params=pltpu.CompilerParams(vmem_limit_bytes=16 * 2**20),
        name="group",
    )(*got)
    got = exchange(*sent)
    like = jax.ShapeDtypeStruct((tokens, channels), bf16)
    *acts, filter_grad = pl.pallas_call(
        functools.partial(output_kernel, plan),
        out_shape=(like, like, like, like, jax.ShapeDtypeStruct((groups, tokens), f32)),
        scratch_shapes=blocks,
        compiler_params=pltpu.CompilerParams(vmem_limit_bytes=8 * 2**20),
        name="outputs",
    )(*got, query_act, key_act, value_act, out_grad)
    return (*acts, filter_grad.T)


def on_device(query_act, key_act, value_act, long_filter, out_grad):
    tokens, channels = query_act.shape
    groups = long_filter.shape[1]
    devices = lax.axis_size("slow") * lax.axis_size("fast")
    if devices == groups and tokens == 128 and channels == 16 * groups and groups & (groups - 1) == 0:
        return by_groups(query_act, key_act, value_act, long_filter, out_grad)
    return by_spectra(query_act, key_act, value_act, long_filter, out_grad)


def solution(mesh):
    placed = (
        P(("slow", "fast"), None),
        P(("slow", "fast"), None),
        P(("slow", "fast"), None),
        P(("slow", "fast"), None),
        P(("slow", "fast"), None),
    )
    return jax.shard_map(
        on_device,
        mesh=mesh,
        in_specs=placed,
        out_specs=(
            P(("slow", "fast"), None),
            P(("slow", "fast"), None),
            P(("slow", "fast"), None),
            P(("slow", "fast"), None),
            P(("slow", "fast"), None),
        ),
        check_vma=False,
    )
```

```python
import functools
import math

import jax
import jax.numpy as jnp
from jax import lax
from jax.experimental import pallas as pl
from jax.experimental.pallas import tpu as pltpu
from jax.sharding import PartitionSpec as P

highest = lax.Precision.HIGHEST


def index_ramp(points, along, ndim, offset):
    shape_list = [1] * ndim
    shape_list[along] = points
    return (jnp.arange(points, dtype=jnp.int32) + offset).reshape(shape_list)


def apply_dft(re_im, points, direction, along):
    index_row = jnp.arange(points, dtype=jnp.int32)
    phase_turns = index_row[:, None] * index_row[None, :] % points
    phases = 2.0 * math.pi / points * phase_turns.astype(jnp.float32)
    cosine = jnp.cos(phases)
    sine_part = direction * jnp.sin(phases)

    def contract(values, matrix):
        result = jnp.tensordot(values, matrix, axes=((along,), (1,)), precision=highest)
        return jnp.moveaxis(result, -1, along)

    return (
        contract(re_im[0], cosine) - contract(re_im[1], sine_part),
        contract(re_im[0], sine_part) + contract(re_im[1], cosine),
    )


def rotate(re_im, phase_turns, period, direction):
    phases = 2.0 * math.pi / period * (phase_turns % period).astype(jnp.float32)
    cosine = jnp.cos(phases)
    sine_part = direction * jnp.sin(phases)
    return (re_im[0] * cosine - re_im[1] * sine_part, re_im[0] * sine_part + re_im[1] * cosine)


def complex_times(left, right):
    return (left[0] * right[0] - left[1] * right[1], left[0] * right[1] + left[1] * right[0])


def conj_times(left, right):
    return (left[0] * right[0] + left[1] * right[1], left[0] * right[1] - left[1] * right[0])


def positions(grid_info, slow_points, slow_offset, fast_points, fast_offset):
    fast_count, tokens = (grid_info[1], grid_info[2])
    block_index = index_ramp(slow_points, 2, 5, slow_offset) * fast_count + index_ramp(
        fast_points, 3, 5, fast_offset
    )
    return block_index * tokens + index_ramp(tokens, 4, 5, 0)


def open_halves(re_im, grid_info, fast_offset):
    token_place = positions(grid_info, re_im[0].shape[1], 0, re_im[0].shape[2], fast_offset)
    return rotate(
        (re_im[0][None], re_im[1][None]),
        index_ramp(2, 0, 5, 0) * token_place,
        2 * grid_info[3],
        -1.0,
    )


def fold_halves(re_im, token_place, seq_length):
    turned = rotate(re_im, index_ramp(2, 0, 5, 0) * token_place, 2 * seq_length, 1.0)
    scale = 0.5 / seq_length
    return (jnp.sum(turned[0], axis=0) * scale, jnp.sum(turned[1], axis=0) * scale)


def front_forward(re_im, grid_info, fast_offset):
    slow_count, fast_count = (grid_info[0], grid_info[1])
    re_im = apply_dft(re_im, slow_count, -1.0, 2)
    phase_turns = index_ramp(slow_count, 2, 5, 0) * index_ramp(re_im[0].shape[3], 3, 5, fast_offset)
    return rotate(re_im, phase_turns, slow_count * fast_count, -1.0)


def front_inverse(re_im, grid_info, fast_offset):
    slow_count, fast_count = (grid_info[0], grid_info[1])
    phase_turns = index_ramp(slow_count, 2, 5, 0) * index_ramp(re_im[0].shape[3], 3, 5, fast_offset)
    re_im = rotate(re_im, phase_turns, slow_count * fast_count, 1.0)
    return apply_dft(re_im, slow_count, 1.0, 2)


def lead_phase(re_im, grid_info, ka_offset):
    slow_count, fast_count, tokens = (grid_info[0], grid_info[1], grid_info[2])
    lead_index = index_ramp(re_im[0].shape[2], 2, 5, ka_offset) + slow_count * index_ramp(
        fast_count, 3, 5, 0
    )
    return lead_index * index_ramp(tokens, 4, 5, 0)


def back_forward(re_im, grid_info, ka_offset):
    re_im = apply_dft(re_im, grid_info[1], -1.0, 3)
    re_im = rotate(re_im, lead_phase(re_im, grid_info, ka_offset), grid_info[3], -1.0)
    return apply_dft(re_im, grid_info[2], -1.0, 4)


def back_inverse(re_im, grid_info, ka_offset):
    re_im = apply_dft(re_im, grid_info[2], 1.0, 4)
    re_im = rotate(re_im, lead_phase(re_im, grid_info, ka_offset), grid_info[3], 1.0)
    return apply_dft(re_im, grid_info[1], 1.0, 3)


def to_channels(seq_rows):
    return lax.all_to_all(
        seq_rows.reshape(1, seq_rows.shape[0], seq_rows.shape[1]),
        "slow",
        split_axis=2,
        concat_axis=0,
        tiled=True,
    )


def merge_blocks(arrays, block_count):
    tokens = arrays[0].shape[0]
    pieces = [item.reshape(tokens, block_count, item.shape[1] // block_count) for item in arrays]
    return jnp.concatenate(pieces, axis=2).reshape(tokens, -1)


def split_columns(rows_major, widths):
    tokens, block_count = (rows_major.shape[0], rows_major.shape[1])
    result = []
    offset = 0
    for length in widths:
        result.append(
            rows_major[:, :, offset : offset + length].reshape(tokens, block_count * length)
        )
        offset += length
    return result


def real_blocks(real_part, imag_part, segments):
    pieces = []
    offset = 0
    for output_kind, length in segments:
        real_seg = real_part[:, offset : offset + length]
        imag_seg = imag_part[:, offset : offset + length]
        offset += length
        if output_kind == "pairs":
            stacked = jnp.transpose(jnp.stack((real_seg, imag_seg), axis=-1), (0, 2, 1, 3))
            pieces.append(stacked.reshape(stacked.shape[0], stacked.shape[1], 2 * length))
        else:
            pieces.append(jnp.transpose(real_seg, (0, 2, 1)))
    return jnp.concatenate(pieces, axis=2)


def segment_widths(segments):
    return [2 * length if output_kind == "pairs" else length for output_kind, length in segments]


def spread_forward(seq_rows, grid_info, fast_rank, segments):
    slow_count, fast_count = (grid_info[0], grid_info[1])
    blocks = to_channels(seq_rows).astype(jnp.float32)
    real_list = []
    imag_list = []
    offset = 0
    for length, packed in segments:
        segment = blocks[:, :, offset : offset + length]
        offset += length
        if packed:
            halves = segment.reshape(segment.shape[0], segment.shape[1], length // 2, 2)
            real_seg, imag_seg = (halves[..., 0], halves[..., 1])
        else:
            real_seg, imag_seg = (segment, jnp.zeros_like(segment))
        real_list.append(jnp.transpose(real_seg, (2, 0, 1)))
        imag_list.append(jnp.transpose(imag_seg, (2, 0, 1)))
    re_im = (
        jnp.concatenate(real_list, 0)[:, :, None, :],
        jnp.concatenate(imag_list, 0)[:, :, None, :],
    )
    re_im = front_forward(open_halves(re_im, grid_info, fast_rank), grid_info, fast_rank)
    re_im = (
        lax.all_to_all(re_im[0], "fast", split_axis=2, concat_axis=3, tiled=True),
        lax.all_to_all(re_im[1], "fast", split_axis=2, concat_axis=3, tiled=True),
    )
    return back_forward(re_im, grid_info, fast_rank * (slow_count // fast_count))


def spread_inverse(re_im, grid_info, fast_rank, slow_rank, segments):
    slow_count, fast_count, tokens, seq_length = grid_info
    re_im = back_inverse(re_im, grid_info, fast_rank * (slow_count // fast_count))
    re_im = (
        lax.all_to_all(re_im[0], "fast", split_axis=3, concat_axis=2, tiled=True),
        lax.all_to_all(re_im[1], "fast", split_axis=3, concat_axis=2, tiled=True),
    )
    re_im = front_inverse(re_im, grid_info, fast_rank)
    re_im = (
        lax.all_to_all(re_im[0], "slow", split_axis=2, concat_axis=1, tiled=True),
        lax.all_to_all(re_im[1], "slow", split_axis=2, concat_axis=1, tiled=True),
    )
    real_part, imag_part = fold_halves(
        re_im, positions(grid_info, 1, slow_rank, 1, fast_rank), seq_length
    )
    length = real_part.shape[0] // slow_count
    blocks = real_blocks(
        real_part.reshape(slow_count, length, tokens),
        imag_part.reshape(slow_count, length, tokens),
        segments,
    )
    rows_major = jnp.transpose(blocks, (1, 0, 2))
    return split_columns(rows_major, segment_widths(segments))


def regroup(re_im, length, local_groups):

    def by_group(values):
        values = values[:, :length]
        return values.reshape(
            (values.shape[0], local_groups, length // local_groups) + values.shape[2:]
        )

    return (by_group(re_im[0]), by_group(re_im[1]))


def flatten_pairs(re_im):

    def merged(values):
        return values.reshape(
            (values.shape[0], values.shape[1] * values.shape[2]) + values.shape[3:]
        )

    return (merged(re_im[0]), merged(re_im[1]))


def by_spectra(query_act, key_act, value_act, long_filter, out_grad):
    tokens, channels = query_act.shape
    groups = long_filter.shape[1]
    slow_count = lax.axis_size("slow")
    fast_count = lax.axis_size("fast")
    seq_length = tokens * slow_count * fast_count
    grid_info = (slow_count, fast_count, tokens, seq_length)
    group_width = channels // groups
    product = (key_act.astype(jnp.float32) * value_act.astype(jnp.float32)).astype(jnp.bfloat16)
    grad_in = (out_grad.astype(jnp.float32) * query_act.astype(jnp.float32)).astype(jnp.bfloat16)
    fast_rank = lax.axis_index("fast")
    slow_rank = lax.axis_index("slow")
    data_pairs = channels // (2 * slow_count)
    local_groups = groups // slow_count
    block_width = channels // slow_count
    spectra = spread_forward(
        merge_blocks((product, long_filter), slow_count),
        grid_info,
        fast_rank,
        ((block_width, True), (local_groups, False)),
    )
    prod_spec = regroup(spectra, data_pairs, local_groups)
    filter_spec = (spectra[0][:, data_pairs:, None], spectra[1][:, data_pairs:, None])
    convolved = spread_inverse(
        flatten_pairs(complex_times(prod_spec, filter_spec)),
        grid_info,
        fast_rank,
        slow_rank,
        (("pairs", data_pairs),),
    )[0]
    grad_spec = regroup(
        spread_forward(grad_in, grid_info, fast_rank, ((block_width, True),)),
        data_pairs,
        local_groups,
    )
    back_spec = flatten_pairs(conj_times(filter_spec, grad_spec))
    corr_spec = conj_times(prod_spec, grad_spec)
    joined = (
        jnp.concatenate((back_spec[0], jnp.sum(corr_spec[0], axis=2)), axis=1),
        jnp.concatenate((back_spec[1], jnp.sum(corr_spec[1], axis=2)), axis=1),
    )
    backward, filter_sum = spread_inverse(
        joined, grid_info, fast_rank, slow_rank, (("pairs", data_pairs), ("real", local_groups))
    )
    scale = 1.0 / math.sqrt(seq_length * group_width)
    mixed_out = (query_act.astype(jnp.float32) * convolved).astype(jnp.bfloat16)
    query_grad = (out_grad.astype(jnp.float32) * convolved).astype(jnp.bfloat16)
    key_grad = (backward * value_act.astype(jnp.float32)).astype(jnp.bfloat16)
    value_grad = (backward * key_act.astype(jnp.float32)).astype(jnp.bfloat16)
    return (mixed_out, query_grad, key_grad, value_grad, filter_sum * scale)


f32 = jnp.float32
bf16 = jnp.bfloat16
EXTRA_ROWS = 2


def dot(left, right):
    return jnp.dot(left, right, preferred_element_type=f32)


def dot_nt(left, right):
    return lax.dot_general(left, right, (((1,), (1,)), ((), ())), preferred_element_type=f32)


def ramp(shape, dim):
    return lax.broadcasted_iota(jnp.int32, shape, dim)


def flip_matrix(size):
    return (ramp((size, size), 0) + ramp((size, size), 1) == size - 1).astype(bf16)


def eye_matrix(size):
    return (ramp((size, size), 0) == ramp((size, size), 1)).astype(bf16)


def chunk_rows(block, fast_count, blocks, rows):
    return (block % fast_count * (blocks // fast_count) + block // fast_count) * rows


def gate_kernel(fast_count, query, key, value, filt, grad, sent, queries, keys, values, taps, grads, done):
    copies = [
        pltpu.make_async_copy(source, target, done.at[at])
        for at, (source, target) in enumerate(
            ((key, keys), (value, values), (grad, grads), (query, queries), (filt, taps))
        )
    ]
    for copy in copies:
        copy.start()
    tokens, channels = queries.shape
    groups = taps.shape[0]
    width = channels // groups
    rows = 2 * width + EXTRA_ROWS
    copies[0].wait()
    copies[1].wait()
    product = (keys[...].astype(f32) * values[...].astype(f32)).astype(bf16)
    columns = product.astype(f32).T.astype(bf16)
    for group in range(groups):
        at = chunk_rows(group, fast_count, groups, rows)
        sent[at : at + width, :] = columns[group * width : (group + 1) * width]
    copies[2].wait()
    copies[3].wait()
    grad_in = (grads[...].astype(f32) * queries[...].astype(f32)).astype(bf16)
    columns = dot(flip_matrix(tokens), grad_in).T.astype(bf16)
    for group in range(groups):
        at = chunk_rows(group, fast_count, groups, rows) + width
        sent[at : at + width, :] = columns[group * width : (group + 1) * width]
    copies[4].wait()
    for group in range(groups):
        at = chunk_rows(group, fast_count, groups, rows) + 2 * width
        sent[at : at + EXTRA_ROWS, :] = jnp.broadcast_to(
            taps[group : group + 1, :], (EXTRA_ROWS, tokens)
        )


def group_kernel(fast_count, scale, width, got, sent, streams, padded, toeplitz):
    rows, tokens = 2 * width + EXTRA_ROWS, got.shape[1]
    blocks = got.shape[0] // rows
    first = [chunk_rows(block, fast_count, blocks, rows) for block in range(blocks)]
    pairs = blocks // 2
    row, lane = ramp((tokens, tokens), 0), ramp((tokens, tokens), 1)
    for pair in range(pairs):
        for half in range(2):
            block = 2 * pair + half
            lanes = slice(half * tokens, (half + 1) * tokens)
            at = 2 * width * pair
            streams[at : at + width, lanes] = got[first[block] : first[block] + width, :]
            streams[at + width : at + 2 * width, lanes] = got[
                first[blocks - 1 - block] + width : first[blocks - 1 - block] + 2 * width, :
            ]
    for block in range(blocks):
        padded[block * width : (block + 1) * width, :] = got[
            first[block] + width : first[block] + 2 * width, :
        ]
    padded[blocks * width :, :] = jnp.zeros((blocks * width, tokens), bf16)

    before = jnp.zeros((tokens, tokens), f32)
    for block in range(blocks):
        taps = jnp.broadcast_to(got[first[block] + 2 * width : first[block] + 2 * width + 1, :].astype(f32), (tokens, tokens))
        turned = pltpu.roll(taps, 0, 1, stride=1, stride_axis=0)
        toeplitz[block] = jnp.where(lane >= row, turned, before).astype(bf16)
        before = turned

    total = None
    for pair in range(pairs):
        left = jnp.zeros((tokens, tokens), bf16) if pair == 0 else toeplitz[2 * pair - 1]
        weights = jnp.concatenate(
            (
                jnp.concatenate((toeplitz[2 * pair], toeplitz[2 * pair + 1]), axis=1),
                jnp.concatenate((left, toeplitz[2 * pair]), axis=1),
            ),
            axis=0,
        )
        skip = 2 * width * pair
        term = dot(streams[0 : 2 * width * pairs - skip, :], weights)
        total = term if pair == 0 else jnp.concatenate((total[:skip], total[skip:] + term), axis=0)
    for pair in range(pairs):
        for half in range(2):
            block = 2 * pair + half
            lanes = slice(half * tokens, (half + 1) * tokens)
            at = 2 * width * pair
            sent[first[block] : first[block] + width, :] = total[at : at + width, lanes].astype(bf16)
            place = first[blocks - 1 - block] + width
            sent[place : place + width, :] = total[
                at + width : at + 2 * width, lanes
            ].astype(bf16)

    ordered = jnp.concatenate(
        [got[first[block] : first[block] + width, :] for block in range(blocks)], axis=0
    )
    ordered = ordered.astype(f32).T.astype(bf16)
    carry = jnp.zeros((8, tokens), f32)
    which = ramp((EXTRA_ROWS, tokens), 0)
    for pair in range(pairs):
        depth = blocks * width if 2 * pair + 2 > blocks // 2 else blocks * width // 2
        columns = [
            padded[pl.ds((blocks - 1 - lag) * width, depth), :] for lag in (2 * pair, 2 * pair + 1)
        ]
        outer = dot(ordered[:, :depth], jnp.concatenate(columns, axis=1))
        for half in range(2):
            block = 2 * pair + half
            turned = pltpu.roll(
                outer[:, half * tokens : (half + 1) * tokens], 0, 1, stride=1, stride_axis=0
            )
            here = jnp.where(lane >= row, turned, 0.0).reshape(tokens // 8, 8, tokens).sum(axis=0)
            later = jnp.where(lane >= row, 0.0, turned).reshape(tokens // 8, 8, tokens).sum(axis=0)
            value = jnp.sum(here + carry, axis=0, keepdims=True) * scale
            carry = later
            high = value.astype(bf16).astype(f32)
            pieces = jnp.where(which == 0, high, jnp.where(which == 1, value - high, 0.0))
            place = first[blocks - 1 - block] + 2 * width
            sent[place : place + EXTRA_ROWS, :] = pieces.astype(bf16)


def output_kernel(
    fast_count, width, got, query, key, value, grad, mixed, query_grad, key_grad, value_grad, filter_grad
):
    rows, tokens = 2 * width + EXTRA_ROWS, got.shape[1]
    blocks = got.shape[0] // rows
    starts = [chunk_rows(block, fast_count, blocks, rows) for block in range(blocks)]

    def collect(first, count):
        return jnp.concatenate(
            [got[at + first : at + first + count, :] for at in starts], axis=0
        )

    flip = flip_matrix(tokens)
    convolved = dot_nt(eye_matrix(tokens), collect(0, width))
    mixed[...] = (query[...].astype(f32) * convolved).astype(bf16)
    query_grad[...] = (grad[...].astype(f32) * convolved).astype(bf16)
    backward = dot_nt(flip, collect(width, width))
    key_grad[...] = (backward * value[...].astype(f32)).astype(bf16)
    value_grad[...] = (backward * key[...].astype(f32)).astype(bf16)
    high, low = collect(2 * width, 1), collect(2 * width + 1, 1)
    filter_grad[...] = dot(high, flip) + dot(low, flip)


def by_groups(query_act, key_act, value_act, long_filter, out_grad):
    tokens, channels = query_act.shape
    groups = long_filter.shape[1]
    width = channels // groups
    rows = 2 * width + EXTRA_ROWS
    scale = 1.0 / math.sqrt(tokens * groups * width)
    fast_count = lax.axis_size("fast")
    chunks = jax.ShapeDtypeStruct((groups * rows, tokens), bf16)

    def exchange(sent):
        pieces = sent.reshape(groups, rows // 2, 2, tokens)
        pieces = lax.all_to_all(pieces, ("fast", "slow"), split_axis=0, concat_axis=0, tiled=True)
        return pieces.reshape(groups * rows, tokens)

    act = pltpu.VMEM((tokens, channels), bf16)
    sent = pl.pallas_call(
        functools.partial(gate_kernel, fast_count),
        out_shape=chunks,
        in_specs=[pl.BlockSpec(memory_space=pltpu.HBM)] * 5,
        scratch_shapes=[
            act,
            act,
            act,
            pltpu.VMEM((groups, tokens), bf16),
            act,
            pltpu.SemaphoreType.DMA((5,)),
        ],
        compiler_params=pltpu.CompilerParams(vmem_limit_bytes=8 * 2**20),
        name="gate",
    )(
        *(
            pltpu.with_memory_space_constraint(array, pltpu.HBM)
            for array in (query_act, key_act, value_act, long_filter.T, out_grad)
        )
    )
    got = exchange(sent)
    sent = pl.pallas_call(
        functools.partial(group_kernel, fast_count, scale, width),
        out_shape=chunks,
        scratch_shapes=[
            pltpu.VMEM((channels, 2 * tokens), bf16),
            pltpu.VMEM((2 * channels, tokens), bf16),
            pltpu.VMEM((groups, tokens, tokens), bf16),
        ],
        compiler_params=pltpu.CompilerParams(vmem_limit_bytes=16 * 2**20),
        name="group",
    )(got)
    got = exchange(sent)
    like = jax.ShapeDtypeStruct((tokens, channels), bf16)
    *acts, filter_grad = pl.pallas_call(
        functools.partial(output_kernel, fast_count, width),
        out_shape=(like, like, like, like, jax.ShapeDtypeStruct((groups, tokens), f32)),
        compiler_params=pltpu.CompilerParams(vmem_limit_bytes=8 * 2**20),
        name="outputs",
    )(got, query_act, key_act, value_act, out_grad)
    return (*acts, filter_grad.T)


def on_device(query_act, key_act, value_act, long_filter, out_grad):
    tokens, channels = query_act.shape
    groups = long_filter.shape[1]
    devices = lax.axis_size("slow") * lax.axis_size("fast")
    if devices == groups and tokens == 128 and channels == 16 * groups and groups % 4 == 0:
        return by_groups(query_act, key_act, value_act, long_filter, out_grad)
    return by_spectra(query_act, key_act, value_act, long_filter, out_grad)


def solution(mesh):
    placed = (
        P(("slow", "fast"), None),
        P(("slow", "fast"), None),
        P(("slow", "fast"), None),
        P(("slow", "fast"), None),
        P(("slow", "fast"), None),
    )
    return jax.shard_map(
        on_device,
        mesh=mesh,
        in_specs=placed,
        out_specs=(
            P(("slow", "fast"), None),
            P(("slow", "fast"), None),
            P(("slow", "fast"), None),
            P(("slow", "fast"), None),
            P(("slow", "fast"), None),
        ),
        check_vma=False,
    )
```

```python
import functools
import math

import jax
import jax.numpy as jnp
from jax import lax
from jax.experimental import pallas as pl
from jax.experimental.pallas import tpu as pltpu
from jax.sharding import PartitionSpec as P

highest = lax.Precision.HIGHEST


def index_ramp(points, along, ndim, offset):
    shape_list = [1] * ndim
    shape_list[along] = points
    return (jnp.arange(points, dtype=jnp.int32) + offset).reshape(shape_list)


def apply_dft(re_im, points, direction, along):
    index_row = jnp.arange(points, dtype=jnp.int32)
    phase_turns = index_row[:, None] * index_row[None, :] % points
    phases = 2.0 * math.pi / points * phase_turns.astype(jnp.float32)
    cosine = jnp.cos(phases)
    sine_part = direction * jnp.sin(phases)

    def contract(values, matrix):
        result = jnp.tensordot(values, matrix, axes=((along,), (1,)), precision=highest)
        return jnp.moveaxis(result, -1, along)

    return (
        contract(re_im[0], cosine) - contract(re_im[1], sine_part),
        contract(re_im[0], sine_part) + contract(re_im[1], cosine),
    )


def rotate(re_im, phase_turns, period, direction):
    phases = 2.0 * math.pi / period * (phase_turns % period).astype(jnp.float32)
    cosine = jnp.cos(phases)
    sine_part = direction * jnp.sin(phases)
    return (re_im[0] * cosine - re_im[1] * sine_part, re_im[0] * sine_part + re_im[1] * cosine)


def complex_times(left, right):
    return (left[0] * right[0] - left[1] * right[1], left[0] * right[1] + left[1] * right[0])


def conj_times(left, right):
    return (left[0] * right[0] + left[1] * right[1], left[0] * right[1] - left[1] * right[0])


def positions(grid_info, slow_points, slow_offset, fast_points, fast_offset):
    fast_count, tokens = (grid_info[1], grid_info[2])
    block_index = index_ramp(slow_points, 2, 5, slow_offset) * fast_count + index_ramp(
        fast_points, 3, 5, fast_offset
    )
    return block_index * tokens + index_ramp(tokens, 4, 5, 0)


def open_halves(re_im, grid_info, fast_offset):
    token_place = positions(grid_info, re_im[0].shape[1], 0, re_im[0].shape[2], fast_offset)
    return rotate(
        (re_im[0][None], re_im[1][None]),
        index_ramp(2, 0, 5, 0) * token_place,
        2 * grid_info[3],
        -1.0,
    )


def fold_halves(re_im, token_place, seq_length):
    turned = rotate(re_im, index_ramp(2, 0, 5, 0) * token_place, 2 * seq_length, 1.0)
    scale = 0.5 / seq_length
    return (jnp.sum(turned[0], axis=0) * scale, jnp.sum(turned[1], axis=0) * scale)


def front_forward(re_im, grid_info, fast_offset):
    slow_count, fast_count = (grid_info[0], grid_info[1])
    re_im = apply_dft(re_im, slow_count, -1.0, 2)
    phase_turns = index_ramp(slow_count, 2, 5, 0) * index_ramp(re_im[0].shape[3], 3, 5, fast_offset)
    return rotate(re_im, phase_turns, slow_count * fast_count, -1.0)


def front_inverse(re_im, grid_info, fast_offset):
    slow_count, fast_count = (grid_info[0], grid_info[1])
    phase_turns = index_ramp(slow_count, 2, 5, 0) * index_ramp(re_im[0].shape[3], 3, 5, fast_offset)
    re_im = rotate(re_im, phase_turns, slow_count * fast_count, 1.0)
    return apply_dft(re_im, slow_count, 1.0, 2)


def lead_phase(re_im, grid_info, ka_offset):
    slow_count, fast_count, tokens = (grid_info[0], grid_info[1], grid_info[2])
    lead_index = index_ramp(re_im[0].shape[2], 2, 5, ka_offset) + slow_count * index_ramp(
        fast_count, 3, 5, 0
    )
    return lead_index * index_ramp(tokens, 4, 5, 0)


def back_forward(re_im, grid_info, ka_offset):
    re_im = apply_dft(re_im, grid_info[1], -1.0, 3)
    re_im = rotate(re_im, lead_phase(re_im, grid_info, ka_offset), grid_info[3], -1.0)
    return apply_dft(re_im, grid_info[2], -1.0, 4)


def back_inverse(re_im, grid_info, ka_offset):
    re_im = apply_dft(re_im, grid_info[2], 1.0, 4)
    re_im = rotate(re_im, lead_phase(re_im, grid_info, ka_offset), grid_info[3], 1.0)
    return apply_dft(re_im, grid_info[1], 1.0, 3)


def to_channels(seq_rows):
    return lax.all_to_all(
        seq_rows.reshape(1, seq_rows.shape[0], seq_rows.shape[1]),
        "slow",
        split_axis=2,
        concat_axis=0,
        tiled=True,
    )


def merge_blocks(arrays, block_count):
    tokens = arrays[0].shape[0]
    pieces = [item.reshape(tokens, block_count, item.shape[1] // block_count) for item in arrays]
    return jnp.concatenate(pieces, axis=2).reshape(tokens, -1)


def split_columns(rows_major, widths):
    tokens, block_count = (rows_major.shape[0], rows_major.shape[1])
    result = []
    offset = 0
    for length in widths:
        result.append(
            rows_major[:, :, offset : offset + length].reshape(tokens, block_count * length)
        )
        offset += length
    return result


def real_blocks(real_part, imag_part, segments):
    pieces = []
    offset = 0
    for output_kind, length in segments:
        real_seg = real_part[:, offset : offset + length]
        imag_seg = imag_part[:, offset : offset + length]
        offset += length
        if output_kind == "pairs":
            stacked = jnp.transpose(jnp.stack((real_seg, imag_seg), axis=-1), (0, 2, 1, 3))
            pieces.append(stacked.reshape(stacked.shape[0], stacked.shape[1], 2 * length))
        else:
            pieces.append(jnp.transpose(real_seg, (0, 2, 1)))
    return jnp.concatenate(pieces, axis=2)


def segment_widths(segments):
    return [2 * length if output_kind == "pairs" else length for output_kind, length in segments]


def spread_forward(seq_rows, grid_info, fast_rank, segments):
    slow_count, fast_count = (grid_info[0], grid_info[1])
    blocks = to_channels(seq_rows).astype(jnp.float32)
    real_list = []
    imag_list = []
    offset = 0
    for length, packed in segments:
        segment = blocks[:, :, offset : offset + length]
        offset += length
        if packed:
            halves = segment.reshape(segment.shape[0], segment.shape[1], length // 2, 2)
            real_seg, imag_seg = (halves[..., 0], halves[..., 1])
        else:
            real_seg, imag_seg = (segment, jnp.zeros_like(segment))
        real_list.append(jnp.transpose(real_seg, (2, 0, 1)))
        imag_list.append(jnp.transpose(imag_seg, (2, 0, 1)))
    re_im = (
        jnp.concatenate(real_list, 0)[:, :, None, :],
        jnp.concatenate(imag_list, 0)[:, :, None, :],
    )
    re_im = front_forward(open_halves(re_im, grid_info, fast_rank), grid_info, fast_rank)
    re_im = (
        lax.all_to_all(re_im[0], "fast", split_axis=2, concat_axis=3, tiled=True),
        lax.all_to_all(re_im[1], "fast", split_axis=2, concat_axis=3, tiled=True),
    )
    return back_forward(re_im, grid_info, fast_rank * (slow_count // fast_count))


def spread_inverse(re_im, grid_info, fast_rank, slow_rank, segments):
    slow_count, fast_count, tokens, seq_length = grid_info
    re_im = back_inverse(re_im, grid_info, fast_rank * (slow_count // fast_count))
    re_im = (
        lax.all_to_all(re_im[0], "fast", split_axis=3, concat_axis=2, tiled=True),
        lax.all_to_all(re_im[1], "fast", split_axis=3, concat_axis=2, tiled=True),
    )
    re_im = front_inverse(re_im, grid_info, fast_rank)
    re_im = (
        lax.all_to_all(re_im[0], "slow", split_axis=2, concat_axis=1, tiled=True),
        lax.all_to_all(re_im[1], "slow", split_axis=2, concat_axis=1, tiled=True),
    )
    real_part, imag_part = fold_halves(
        re_im, positions(grid_info, 1, slow_rank, 1, fast_rank), seq_length
    )
    length = real_part.shape[0] // slow_count
    blocks = real_blocks(
        real_part.reshape(slow_count, length, tokens),
        imag_part.reshape(slow_count, length, tokens),
        segments,
    )
    rows_major = jnp.transpose(blocks, (1, 0, 2))
    return split_columns(rows_major, segment_widths(segments))


def regroup(re_im, length, local_groups):

    def by_group(values):
        values = values[:, :length]
        return values.reshape(
            (values.shape[0], local_groups, length // local_groups) + values.shape[2:]
        )

    return (by_group(re_im[0]), by_group(re_im[1]))


def flatten_pairs(re_im):

    def merged(values):
        return values.reshape(
            (values.shape[0], values.shape[1] * values.shape[2]) + values.shape[3:]
        )

    return (merged(re_im[0]), merged(re_im[1]))


def by_spectra(query_act, key_act, value_act, long_filter, out_grad):
    tokens, channels = query_act.shape
    groups = long_filter.shape[1]
    slow_count = lax.axis_size("slow")
    fast_count = lax.axis_size("fast")
    seq_length = tokens * slow_count * fast_count
    grid_info = (slow_count, fast_count, tokens, seq_length)
    group_width = channels // groups
    product = (key_act.astype(jnp.float32) * value_act.astype(jnp.float32)).astype(jnp.bfloat16)
    grad_in = (out_grad.astype(jnp.float32) * query_act.astype(jnp.float32)).astype(jnp.bfloat16)
    fast_rank = lax.axis_index("fast")
    slow_rank = lax.axis_index("slow")
    data_pairs = channels // (2 * slow_count)
    local_groups = groups // slow_count
    block_width = channels // slow_count
    spectra = spread_forward(
        merge_blocks((product, long_filter), slow_count),
        grid_info,
        fast_rank,
        ((block_width, True), (local_groups, False)),
    )
    prod_spec = regroup(spectra, data_pairs, local_groups)
    filter_spec = (spectra[0][:, data_pairs:, None], spectra[1][:, data_pairs:, None])
    convolved = spread_inverse(
        flatten_pairs(complex_times(prod_spec, filter_spec)),
        grid_info,
        fast_rank,
        slow_rank,
        (("pairs", data_pairs),),
    )[0]
    grad_spec = regroup(
        spread_forward(grad_in, grid_info, fast_rank, ((block_width, True),)),
        data_pairs,
        local_groups,
    )
    back_spec = flatten_pairs(conj_times(filter_spec, grad_spec))
    corr_spec = conj_times(prod_spec, grad_spec)
    joined = (
        jnp.concatenate((back_spec[0], jnp.sum(corr_spec[0], axis=2)), axis=1),
        jnp.concatenate((back_spec[1], jnp.sum(corr_spec[1], axis=2)), axis=1),
    )
    backward, filter_sum = spread_inverse(
        joined, grid_info, fast_rank, slow_rank, (("pairs", data_pairs), ("real", local_groups))
    )
    scale = 1.0 / math.sqrt(seq_length * group_width)
    mixed_out = (query_act.astype(jnp.float32) * convolved).astype(jnp.bfloat16)
    query_grad = (out_grad.astype(jnp.float32) * convolved).astype(jnp.bfloat16)
    key_grad = (backward * value_act.astype(jnp.float32)).astype(jnp.bfloat16)
    value_grad = (backward * key_act.astype(jnp.float32)).astype(jnp.bfloat16)
    return (mixed_out, query_grad, key_grad, value_grad, filter_sum * scale)


f32 = jnp.float32
bf16 = jnp.bfloat16
EXTRA_ROWS = 2


def dot(left, right):
    return jnp.dot(left, right, preferred_element_type=f32)


def dot_nt(left, right):
    return lax.dot_general(left, right, (((1,), (1,)), ((), ())), preferred_element_type=f32)


def ramp(shape, dim):
    return lax.broadcasted_iota(jnp.int32, shape, dim)


def flip_matrix(size):
    return (ramp((size, size), 0) + ramp((size, size), 1) == size - 1).astype(bf16)


def eye_matrix(size):
    return (ramp((size, size), 0) == ramp((size, size), 1)).astype(bf16)


def gate_kernel(query, key, value, filt, grad, sent, queries, keys, values, taps, grads, done):
    tokens, channels = queries.shape
    groups = taps.shape[0]
    width = channels // groups
    rows = 2 * width + EXTRA_ROWS
    parts = 2
    span = channels // parts
    spread = ((key, keys), (value, values), (grad, grads), (query, queries))
    copies = [pltpu.make_async_copy(filt, taps, done.at[parts * len(spread)])]
    for first in (0, 2):
        for part in range(parts):
            columns = pl.ds(part * span, span)
            for at in (first, first + 1):
                source, target = spread[at]
                copies.append(
                    pltpu.make_async_copy(
                        source.at[:, columns], target.at[:, columns], done.at[parts * at + part]
                    )
                )
    for copy in copies:
        copy.start()
    copies[0].wait()
    for group in range(groups):
        at = group * rows + 2 * width
        sent[at : at + EXTRA_ROWS, :] = jnp.broadcast_to(
            taps[group : group + 1, :], (EXTRA_ROWS, tokens)
        )
    flip = flip_matrix(tokens)
    for step in range(2 * parts):
        copies[2 * step + 1].wait()
        copies[2 * step + 2].wait()
        stream, part = step // parts, step % parts
        columns = slice(part * span, (part + 1) * span)
        left, right = (keys, values) if stream == 0 else (grads, queries)
        gated = (left[:, columns].astype(f32) * right[:, columns].astype(f32)).astype(bf16)
        gated = gated.astype(f32) if stream == 0 else dot(flip, gated)
        turned = gated.T.astype(bf16)
        for group in range(groups // parts):
            at = (group + part * groups // parts) * rows + stream * width
            sent[at : at + width, :] = turned[group * width : (group + 1) * width]


def group_kernel(scale, width, got, sent, streams, padded, total):
    rows, tokens = 2 * width + EXTRA_ROWS, got.shape[1]
    blocks = got.shape[0] // rows
    pairs = blocks // 2
    row, lane = ramp((tokens, tokens), 0), ramp((tokens, tokens), 1)

    def load(block, first, count):
        return got[block * rows + first : block * rows + first + count, :]

    def turn(square):
        return pltpu.roll(square, 0, 1, stride=1, stride_axis=0)

    for block in range(blocks):
        lanes = slice(block % 2 * tokens, (block % 2 + 1) * tokens)
        at = 2 * width * (block // 2)
        streams[at : at + width, lanes] = load(block, 0, width)
        streams[at + width : at + 2 * width, lanes] = load(blocks - 1 - block, width, width)
        padded[block * width : (block + 1) * width, :] = load(block, width, width)
    padded[blocks * width :, :] = jnp.zeros((blocks * width, tokens), bf16)
    ordered = jnp.concatenate([load(block, 0, width) for block in range(blocks)], axis=0)
    ordered = ordered.astype(f32).T.astype(bf16)

    before = jnp.zeros((tokens, tokens), f32)
    left = jnp.zeros((tokens, tokens), bf16)
    carry = jnp.zeros((8, tokens), f32)
    which = ramp((EXTRA_ROWS, tokens), 0)
    for pair in range(pairs):
        bands = []
        for block in (2 * pair, 2 * pair + 1):
            taps = load(block, 2 * width, 1).astype(f32)
            turned = turn(jnp.broadcast_to(taps, (tokens, tokens)))
            bands.append(jnp.where(lane >= row, turned, before).astype(bf16))
            before = turned
        weights = jnp.concatenate(
            (
                jnp.concatenate((bands[0], bands[1]), axis=1),
                jnp.concatenate((left, bands[0]), axis=1),
            ),
            axis=0,
        )
        left = bands[1]
        skip = 2 * width * pair
        term = dot(streams[0 : 2 * width * pairs - skip, :], weights)
        if pair == 0:
            total[...] = term
        else:
            total[skip:, :] += term
        ready = total[skip : skip + 2 * width, :].astype(bf16)
        for half in range(2):
            block = 2 * pair + half
            lanes = slice(half * tokens, (half + 1) * tokens)
            sent[block * rows : block * rows + width, :] = ready[:width, lanes]
            at = (blocks - 1 - block) * rows + width
            sent[at : at + width, :] = ready[width:, lanes]

        depth = blocks * width if 2 * pair + 2 > blocks // 2 else blocks * width // 2
        columns = [
            padded[pl.ds((blocks - 1 - lag) * width, depth), :] for lag in (2 * pair, 2 * pair + 1)
        ]
        outer = dot(ordered[:, :depth], jnp.concatenate(columns, axis=1))
        for half in range(2):
            block = 2 * pair + half
            turned = turn(outer[:, half * tokens : (half + 1) * tokens])
            here = jnp.where(lane >= row, turned, 0.0).reshape(tokens // 8, 8, tokens).sum(axis=0)
            later = jnp.where(lane >= row, 0.0, turned).reshape(tokens // 8, 8, tokens).sum(axis=0)
            value = jnp.sum(here + carry, axis=0, keepdims=True) * scale
            carry = later
            high = value.astype(bf16).astype(f32)
            pieces = jnp.where(which == 0, high, value - high)
            at = (blocks - 1 - block) * rows + 2 * width
            sent[at : at + EXTRA_ROWS, :] = pieces.astype(bf16)


def output_kernel(width, got, query, key, value, grad, *refs):
    outs, (*held, done) = refs[:5], refs[5:]
    rows, tokens = 2 * width + EXTRA_ROWS, got.shape[1]
    blocks = got.shape[0] // rows
    channels = blocks * width
    parts = 2
    span = channels // parts
    copies = []

    def collect(first, count, blocks_here):
        return jnp.concatenate(
            [got[at * rows + first : at * rows + first + count, :] for at in blocks_here], axis=0
        )

    def leave(source, target):
        copies.append(pltpu.make_async_copy(source, target, done.at[len(copies)]))
        copies[-1].start()

    flip, eye = flip_matrix(tokens), eye_matrix(tokens)
    high, low = (collect(2 * width + at, 1, range(blocks)) for at in range(2))
    held[4][...] = dot(high, flip) + dot(low, flip)
    leave(held[4], outs[4])
    for stream, turn in enumerate((eye, flip)):
        for part in range(parts):
            blocks_here = range(part * blocks // parts, (part + 1) * blocks // parts)
            sums = dot_nt(turn, collect(stream * width, width, blocks_here))
            columns = pl.ds(part * span, span)
            for at, factor in enumerate((query, grad) if stream == 0 else (value, key)):
                store, out = held[2 * stream + at], outs[2 * stream + at]
                store[:, columns] = (sums * factor[:, columns].astype(f32)).astype(bf16)
                leave(store.at[:, columns], out.at[:, columns])
    for copy in copies:
        copy.wait()


def by_groups(query_act, key_act, value_act, long_filter, out_grad):
    tokens, channels = query_act.shape
    groups = long_filter.shape[1]
    width = channels // groups
    rows = 2 * width + EXTRA_ROWS
    scale = 1.0 / math.sqrt(tokens * groups * width)
    chunks = jax.ShapeDtypeStruct((groups * rows, tokens), bf16)

    def exchange(sent):
        pieces = sent.reshape(groups, rows // 2, 2, tokens)
        pieces = lax.all_to_all(pieces, ("slow", "fast"), split_axis=0, concat_axis=0, tiled=True)
        return pieces.reshape(groups * rows, tokens)

    act = pltpu.VMEM((tokens, channels), bf16)
    sent = pl.pallas_call(
        gate_kernel,
        out_shape=chunks,
        in_specs=[pl.BlockSpec(memory_space=pltpu.HBM)] * 5,
        scratch_shapes=[
            act,
            act,
            act,
            pltpu.VMEM((groups, tokens), bf16),
            act,
            pltpu.SemaphoreType.DMA((9,)),
        ],
        compiler_params=pltpu.CompilerParams(vmem_limit_bytes=8 * 2**20),
        name="gate",
    )(
        *(
            pltpu.with_memory_space_constraint(array, pltpu.HBM)
            for array in (query_act, key_act, value_act, long_filter.T, out_grad)
        )
    )
    got = exchange(sent)
    sent = pl.pallas_call(
        functools.partial(group_kernel, scale, width),
        out_shape=chunks,
        scratch_shapes=[
            pltpu.VMEM((channels, 2 * tokens), bf16),
            pltpu.VMEM((2 * channels, tokens), bf16),
            pltpu.VMEM((channels, 2 * tokens), f32),
        ],
        compiler_params=pltpu.CompilerParams(vmem_limit_bytes=16 * 2**20),
        name="group",
    )(got)
    got = exchange(sent)
    like = jax.ShapeDtypeStruct((tokens, channels), bf16)
    *acts, filter_grad = pl.pallas_call(
        functools.partial(output_kernel, width),
        out_shape=(like, like, like, like, jax.ShapeDtypeStruct((groups, tokens), f32)),
        out_specs=[pl.BlockSpec(memory_space=pltpu.HBM)] * 5,
        scratch_shapes=[
            act,
            act,
            act,
            act,
            pltpu.VMEM((groups, tokens), f32),
            pltpu.SemaphoreType.DMA((9,)),
        ],
        compiler_params=pltpu.CompilerParams(vmem_limit_bytes=8 * 2**20),
        name="outputs",
    )(got, query_act, key_act, value_act, out_grad)
    return (*acts, filter_grad.T)


def on_device(query_act, key_act, value_act, long_filter, out_grad):
    tokens, channels = query_act.shape
    groups = long_filter.shape[1]
    devices = lax.axis_size("slow") * lax.axis_size("fast")
    if devices == groups and tokens == 128 and channels == 16 * groups and groups % 4 == 0:
        return by_groups(query_act, key_act, value_act, long_filter, out_grad)
    return by_spectra(query_act, key_act, value_act, long_filter, out_grad)


def solution(mesh):
    placed = (
        P(("slow", "fast"), None),
        P(("slow", "fast"), None),
        P(("slow", "fast"), None),
        P(("slow", "fast"), None),
        P(("slow", "fast"), None),
    )
    return jax.shard_map(
        on_device,
        mesh=mesh,
        in_specs=placed,
        out_specs=(
            P(("slow", "fast"), None),
            P(("slow", "fast"), None),
            P(("slow", "fast"), None),
            P(("slow", "fast"), None),
            P(("slow", "fast"), None),
        ),
        check_vma=False,
    )
```

```python
import functools
import math

import jax
import jax.numpy as jnp
from jax import lax
from jax.experimental import pallas as pl
from jax.experimental.pallas import tpu as pltpu
from jax.sharding import PartitionSpec as P

highest = lax.Precision.HIGHEST


def index_ramp(points, along, ndim, offset):
    shape_list = [1] * ndim
    shape_list[along] = points
    return (jnp.arange(points, dtype=jnp.int32) + offset).reshape(shape_list)


def apply_dft(re_im, points, direction, along):
    index_row = jnp.arange(points, dtype=jnp.int32)
    phase_turns = index_row[:, None] * index_row[None, :] % points
    phases = 2.0 * math.pi / points * phase_turns.astype(jnp.float32)
    cosine = jnp.cos(phases)
    sine_part = direction * jnp.sin(phases)

    def contract(values, matrix):
        result = jnp.tensordot(values, matrix, axes=((along,), (1,)), precision=highest)
        return jnp.moveaxis(result, -1, along)

    return (
        contract(re_im[0], cosine) - contract(re_im[1], sine_part),
        contract(re_im[0], sine_part) + contract(re_im[1], cosine),
    )


def rotate(re_im, phase_turns, period, direction):
    phases = 2.0 * math.pi / period * (phase_turns % period).astype(jnp.float32)
    cosine = jnp.cos(phases)
    sine_part = direction * jnp.sin(phases)
    return (re_im[0] * cosine - re_im[1] * sine_part, re_im[0] * sine_part + re_im[1] * cosine)


def complex_times(left, right):
    return (left[0] * right[0] - left[1] * right[1], left[0] * right[1] + left[1] * right[0])


def conj_times(left, right):
    return (left[0] * right[0] + left[1] * right[1], left[0] * right[1] - left[1] * right[0])


def positions(grid_info, slow_points, slow_offset, fast_points, fast_offset):
    fast_count, tokens = (grid_info[1], grid_info[2])
    block_index = index_ramp(slow_points, 2, 5, slow_offset) * fast_count + index_ramp(
        fast_points, 3, 5, fast_offset
    )
    return block_index * tokens + index_ramp(tokens, 4, 5, 0)


def open_halves(re_im, grid_info, fast_offset):
    token_place = positions(grid_info, re_im[0].shape[1], 0, re_im[0].shape[2], fast_offset)
    return rotate(
        (re_im[0][None], re_im[1][None]),
        index_ramp(2, 0, 5, 0) * token_place,
        2 * grid_info[3],
        -1.0,
    )


def fold_halves(re_im, token_place, seq_length):
    turned = rotate(re_im, index_ramp(2, 0, 5, 0) * token_place, 2 * seq_length, 1.0)
    scale = 0.5 / seq_length
    return (jnp.sum(turned[0], axis=0) * scale, jnp.sum(turned[1], axis=0) * scale)


def front_forward(re_im, grid_info, fast_offset):
    slow_count, fast_count = (grid_info[0], grid_info[1])
    re_im = apply_dft(re_im, slow_count, -1.0, 2)
    phase_turns = index_ramp(slow_count, 2, 5, 0) * index_ramp(re_im[0].shape[3], 3, 5, fast_offset)
    return rotate(re_im, phase_turns, slow_count * fast_count, -1.0)


def front_inverse(re_im, grid_info, fast_offset):
    slow_count, fast_count = (grid_info[0], grid_info[1])
    phase_turns = index_ramp(slow_count, 2, 5, 0) * index_ramp(re_im[0].shape[3], 3, 5, fast_offset)
    re_im = rotate(re_im, phase_turns, slow_count * fast_count, 1.0)
    return apply_dft(re_im, slow_count, 1.0, 2)


def lead_phase(re_im, grid_info, ka_offset):
    slow_count, fast_count, tokens = (grid_info[0], grid_info[1], grid_info[2])
    lead_index = index_ramp(re_im[0].shape[2], 2, 5, ka_offset) + slow_count * index_ramp(
        fast_count, 3, 5, 0
    )
    return lead_index * index_ramp(tokens, 4, 5, 0)


def back_forward(re_im, grid_info, ka_offset):
    re_im = apply_dft(re_im, grid_info[1], -1.0, 3)
    re_im = rotate(re_im, lead_phase(re_im, grid_info, ka_offset), grid_info[3], -1.0)
    return apply_dft(re_im, grid_info[2], -1.0, 4)


def back_inverse(re_im, grid_info, ka_offset):
    re_im = apply_dft(re_im, grid_info[2], 1.0, 4)
    re_im = rotate(re_im, lead_phase(re_im, grid_info, ka_offset), grid_info[3], 1.0)
    return apply_dft(re_im, grid_info[1], 1.0, 3)


def to_channels(seq_rows):
    return lax.all_to_all(
        seq_rows.reshape(1, seq_rows.shape[0], seq_rows.shape[1]),
        "slow",
        split_axis=2,
        concat_axis=0,
        tiled=True,
    )


def merge_blocks(arrays, block_count):
    tokens = arrays[0].shape[0]
    pieces = [item.reshape(tokens, block_count, item.shape[1] // block_count) for item in arrays]
    return jnp.concatenate(pieces, axis=2).reshape(tokens, -1)


def split_columns(rows_major, widths):
    tokens, block_count = (rows_major.shape[0], rows_major.shape[1])
    result = []
    offset = 0
    for length in widths:
        result.append(
            rows_major[:, :, offset : offset + length].reshape(tokens, block_count * length)
        )
        offset += length
    return result


def real_blocks(real_part, imag_part, segments):
    pieces = []
    offset = 0
    for output_kind, length in segments:
        real_seg = real_part[:, offset : offset + length]
        imag_seg = imag_part[:, offset : offset + length]
        offset += length
        if output_kind == "pairs":
            stacked = jnp.transpose(jnp.stack((real_seg, imag_seg), axis=-1), (0, 2, 1, 3))
            pieces.append(stacked.reshape(stacked.shape[0], stacked.shape[1], 2 * length))
        else:
            pieces.append(jnp.transpose(real_seg, (0, 2, 1)))
    return jnp.concatenate(pieces, axis=2)


def segment_widths(segments):
    return [2 * length if output_kind == "pairs" else length for output_kind, length in segments]


def spread_forward(seq_rows, grid_info, fast_rank, segments):
    slow_count, fast_count = (grid_info[0], grid_info[1])
    blocks = to_channels(seq_rows).astype(jnp.float32)
    real_list = []
    imag_list = []
    offset = 0
    for length, packed in segments:
        segment = blocks[:, :, offset : offset + length]
        offset += length
        if packed:
            halves = segment.reshape(segment.shape[0], segment.shape[1], length // 2, 2)
            real_seg, imag_seg = (halves[..., 0], halves[..., 1])
        else:
            real_seg, imag_seg = (segment, jnp.zeros_like(segment))
        real_list.append(jnp.transpose(real_seg, (2, 0, 1)))
        imag_list.append(jnp.transpose(imag_seg, (2, 0, 1)))
    re_im = (
        jnp.concatenate(real_list, 0)[:, :, None, :],
        jnp.concatenate(imag_list, 0)[:, :, None, :],
    )
    re_im = front_forward(open_halves(re_im, grid_info, fast_rank), grid_info, fast_rank)
    re_im = (
        lax.all_to_all(re_im[0], "fast", split_axis=2, concat_axis=3, tiled=True),
        lax.all_to_all(re_im[1], "fast", split_axis=2, concat_axis=3, tiled=True),
    )
    return back_forward(re_im, grid_info, fast_rank * (slow_count // fast_count))


def spread_inverse(re_im, grid_info, fast_rank, slow_rank, segments):
    slow_count, fast_count, tokens, seq_length = grid_info
    re_im = back_inverse(re_im, grid_info, fast_rank * (slow_count // fast_count))
    re_im = (
        lax.all_to_all(re_im[0], "fast", split_axis=3, concat_axis=2, tiled=True),
        lax.all_to_all(re_im[1], "fast", split_axis=3, concat_axis=2, tiled=True),
    )
    re_im = front_inverse(re_im, grid_info, fast_rank)
    re_im = (
        lax.all_to_all(re_im[0], "slow", split_axis=2, concat_axis=1, tiled=True),
        lax.all_to_all(re_im[1], "slow", split_axis=2, concat_axis=1, tiled=True),
    )
    real_part, imag_part = fold_halves(
        re_im, positions(grid_info, 1, slow_rank, 1, fast_rank), seq_length
    )
    length = real_part.shape[0] // slow_count
    blocks = real_blocks(
        real_part.reshape(slow_count, length, tokens),
        imag_part.reshape(slow_count, length, tokens),
        segments,
    )
    rows_major = jnp.transpose(blocks, (1, 0, 2))
    return split_columns(rows_major, segment_widths(segments))


def regroup(re_im, length, local_groups):

    def by_group(values):
        values = values[:, :length]
        return values.reshape(
            (values.shape[0], local_groups, length // local_groups) + values.shape[2:]
        )

    return (by_group(re_im[0]), by_group(re_im[1]))


def flatten_pairs(re_im):

    def merged(values):
        return values.reshape(
            (values.shape[0], values.shape[1] * values.shape[2]) + values.shape[3:]
        )

    return (merged(re_im[0]), merged(re_im[1]))


def by_spectra(query_act, key_act, value_act, long_filter, out_grad):
    tokens, channels = query_act.shape
    groups = long_filter.shape[1]
    slow_count = lax.axis_size("slow")
    fast_count = lax.axis_size("fast")
    seq_length = tokens * slow_count * fast_count
    grid_info = (slow_count, fast_count, tokens, seq_length)
    group_width = channels // groups
    product = (key_act.astype(jnp.float32) * value_act.astype(jnp.float32)).astype(jnp.bfloat16)
    grad_in = (out_grad.astype(jnp.float32) * query_act.astype(jnp.float32)).astype(jnp.bfloat16)
    fast_rank = lax.axis_index("fast")
    slow_rank = lax.axis_index("slow")
    data_pairs = channels // (2 * slow_count)
    local_groups = groups // slow_count
    block_width = channels // slow_count
    spectra = spread_forward(
        merge_blocks((product, long_filter), slow_count),
        grid_info,
        fast_rank,
        ((block_width, True), (local_groups, False)),
    )
    prod_spec = regroup(spectra, data_pairs, local_groups)
    filter_spec = (spectra[0][:, data_pairs:, None], spectra[1][:, data_pairs:, None])
    convolved = spread_inverse(
        flatten_pairs(complex_times(prod_spec, filter_spec)),
        grid_info,
        fast_rank,
        slow_rank,
        (("pairs", data_pairs),),
    )[0]
    grad_spec = regroup(
        spread_forward(grad_in, grid_info, fast_rank, ((block_width, True),)),
        data_pairs,
        local_groups,
    )
    back_spec = flatten_pairs(conj_times(filter_spec, grad_spec))
    corr_spec = conj_times(prod_spec, grad_spec)
    joined = (
        jnp.concatenate((back_spec[0], jnp.sum(corr_spec[0], axis=2)), axis=1),
        jnp.concatenate((back_spec[1], jnp.sum(corr_spec[1], axis=2)), axis=1),
    )
    backward, filter_sum = spread_inverse(
        joined, grid_info, fast_rank, slow_rank, (("pairs", data_pairs), ("real", local_groups))
    )
    scale = 1.0 / math.sqrt(seq_length * group_width)
    mixed_out = (query_act.astype(jnp.float32) * convolved).astype(jnp.bfloat16)
    query_grad = (out_grad.astype(jnp.float32) * convolved).astype(jnp.bfloat16)
    key_grad = (backward * value_act.astype(jnp.float32)).astype(jnp.bfloat16)
    value_grad = (backward * key_act.astype(jnp.float32)).astype(jnp.bfloat16)
    return (mixed_out, query_grad, key_grad, value_grad, filter_sum * scale)


f32 = jnp.float32
bf16 = jnp.bfloat16
EXTRA_ROWS = 2


def dot(left, right):
    return jnp.dot(left, right, preferred_element_type=f32)


def dot_nt(left, right):
    return lax.dot_general(left, right, (((1,), (1,)), ((), ())), preferred_element_type=f32)


def ramp(shape, dim):
    return lax.broadcasted_iota(jnp.int32, shape, dim)


def flip_matrix(size):
    return (ramp((size, size), 0) + ramp((size, size), 1) == size - 1).astype(bf16)


def eye_matrix(size):
    return (ramp((size, size), 0) == ramp((size, size), 1)).astype(bf16)


def gate_kernel(query, key, value, filt, grad, sent, queries, keys, values, taps, grads, done):
    copies = [
        pltpu.make_async_copy(source, target, done.at[at])
        for at, (source, target) in enumerate(
            ((key, keys), (value, values), (grad, grads), (query, queries), (filt, taps))
        )
    ]
    for copy in copies:
        copy.start()
    tokens, channels = queries.shape
    groups = taps.shape[0]
    width = channels // groups
    rows = 2 * width + EXTRA_ROWS
    copies[0].wait()
    copies[1].wait()
    product = (keys[...].astype(f32) * values[...].astype(f32)).astype(bf16)
    columns = product.T
    for group in range(groups):
        sent[group * rows : group * rows + width, :] = columns[group * width : (group + 1) * width]
    copies[2].wait()
    copies[3].wait()
    grad_in = (grads[...].astype(f32) * queries[...].astype(f32)).astype(bf16)
    columns = dot(flip_matrix(tokens), grad_in).astype(bf16).T
    for group in range(groups):
        at = group * rows + width
        sent[at : at + width, :] = columns[group * width : (group + 1) * width]
    copies[4].wait()
    for group in range(groups):
        at = group * rows + 2 * width
        sent[at : at + EXTRA_ROWS, :] = jnp.broadcast_to(
            taps[group : group + 1, :], (EXTRA_ROWS, tokens)
        )


def group_kernel(scale, width, got, sent, streams, padded, toeplitz):
    rows, tokens = 2 * width + EXTRA_ROWS, got.shape[1]
    blocks = got.shape[0] // rows
    pairs = blocks // 2
    row, lane = ramp((tokens, tokens), 0), ramp((tokens, tokens), 1)
    for pair in range(pairs):
        for half in range(2):
            block = 2 * pair + half
            lanes = slice(half * tokens, (half + 1) * tokens)
            at = 2 * width * pair
            streams[at : at + width, lanes] = got[block * rows : block * rows + width, :]
            streams[at + width : at + 2 * width, lanes] = got[
                (blocks - 1 - block) * rows + width : (blocks - 1 - block) * rows + 2 * width, :
            ]
    for block in range(blocks):
        padded[block * width : (block + 1) * width, :] = got[
            block * rows + width : block * rows + 2 * width, :
        ]
    padded[blocks * width :, :] = jnp.zeros((blocks * width, tokens), bf16)

    before = jnp.zeros((tokens, tokens), f32)
    for block in range(blocks):
        taps = jnp.broadcast_to(got[block * rows + 2 * width : block * rows + 2 * width + 1, :].astype(f32), (tokens, tokens))
        turned = pltpu.roll(taps, 0, 1, stride=1, stride_axis=0)
        toeplitz[block] = jnp.where(lane >= row, turned, before).astype(bf16)
        before = turned

    total = None
    for pair in range(pairs):
        left = jnp.zeros((tokens, tokens), bf16) if pair == 0 else toeplitz[2 * pair - 1]
        weights = jnp.concatenate(
            (
                jnp.concatenate((toeplitz[2 * pair], toeplitz[2 * pair + 1]), axis=1),
                jnp.concatenate((left, toeplitz[2 * pair]), axis=1),
            ),
            axis=0,
        )
        skip = 2 * width * pair
        term = dot(streams[0 : 2 * width * pairs - skip, :], weights)
        total = term if pair == 0 else jnp.concatenate((total[:skip], total[skip:] + term), axis=0)
    for pair in range(pairs):
        for half in range(2):
            block = 2 * pair + half
            lanes = slice(half * tokens, (half + 1) * tokens)
            at = 2 * width * pair
            sent[block * rows : block * rows + width, :] = total[at : at + width, lanes].astype(bf16)
            place = (blocks - 1 - block) * rows + width
            sent[place : place + width, :] = total[
                at + width : at + 2 * width, lanes
            ].astype(bf16)

    ordered = jnp.concatenate(
        [got[block * rows : block * rows + width, :] for block in range(blocks)], axis=0
    )
    ordered = ordered.T
    carry = jnp.zeros((8, tokens), f32)
    which = ramp((EXTRA_ROWS, tokens), 0)
    for pair in range(pairs):
        depth = blocks * width if 2 * pair + 2 > blocks // 2 else blocks * width // 2
        columns = [
            padded[pl.ds((blocks - 1 - lag) * width, depth), :] for lag in (2 * pair, 2 * pair + 1)
        ]
        outer = dot(ordered[:, :depth], jnp.concatenate(columns, axis=1))
        for half in range(2):
            block = 2 * pair + half
            turned = pltpu.roll(
                outer[:, half * tokens : (half + 1) * tokens], 0, 1, stride=1, stride_axis=0
            )
            here = jnp.where(lane >= row, turned, 0.0).reshape(tokens // 8, 8, tokens).sum(axis=0)
            later = jnp.where(lane >= row, 0.0, turned).reshape(tokens // 8, 8, tokens).sum(axis=0)
            value = jnp.sum(here + carry, axis=0, keepdims=True) * scale
            carry = later
            high = value.astype(bf16).astype(f32)
            pieces = jnp.where(which == 0, high, jnp.where(which == 1, value - high, 0.0))
            place = (blocks - 1 - block) * rows + 2 * width
            sent[place : place + EXTRA_ROWS, :] = pieces.astype(bf16)


def output_kernel(width, got, query, key, value, grad, *refs):
    outs, (*held, done) = refs[:5], refs[5:]
    rows, tokens = 2 * width + EXTRA_ROWS, got.shape[1]
    blocks = got.shape[0] // rows
    copies = [
        pltpu.make_async_copy(store, out, done.at[at])
        for at, (store, out) in enumerate(zip(held, outs))
    ]

    def collect(first, count):
        return jnp.concatenate(
            [got[at * rows + first : at * rows + first + count, :] for at in range(blocks)], axis=0
        )

    flip = flip_matrix(tokens)
    convolved = dot_nt(eye_matrix(tokens), collect(0, width))
    held[0][...] = (query[...].astype(f32) * convolved).astype(bf16)
    copies[0].start()
    held[1][...] = (grad[...].astype(f32) * convolved).astype(bf16)
    copies[1].start()
    high, low = collect(2 * width, 1), collect(2 * width + 1, 1)
    held[4][...] = dot(high, flip) + dot(low, flip)
    copies[4].start()
    backward = dot_nt(flip, collect(width, width))
    held[2][...] = (backward * value[...].astype(f32)).astype(bf16)
    copies[2].start()
    held[3][...] = (backward * key[...].astype(f32)).astype(bf16)
    copies[3].start()
    for copy in copies:
        copy.wait()


def by_groups(query_act, key_act, value_act, long_filter, out_grad):
    tokens, channels = query_act.shape
    groups = long_filter.shape[1]
    width = channels // groups
    rows = 2 * width + EXTRA_ROWS
    scale = 1.0 / math.sqrt(tokens * groups * width)
    chunks = jax.ShapeDtypeStruct((groups * rows, tokens), bf16)

    def exchange(sent):
        pieces = sent.reshape(groups, rows // 2, 2, tokens)
        pieces = lax.all_to_all(pieces, ("slow", "fast"), split_axis=0, concat_axis=0, tiled=True)
        return pieces.reshape(groups * rows, tokens)

    act = pltpu.VMEM((tokens, channels), bf16)
    sent = pl.pallas_call(
        gate_kernel,
        out_shape=chunks,
        in_specs=[pl.BlockSpec(memory_space=pltpu.HBM)] * 5,
        scratch_shapes=[
            act,
            act,
            act,
            pltpu.VMEM((groups, tokens), bf16),
            act,
            pltpu.SemaphoreType.DMA((5,)),
        ],
        compiler_params=pltpu.CompilerParams(vmem_limit_bytes=8 * 2**20),
        name="gate",
    )(
        *(
            pltpu.with_memory_space_constraint(array, pltpu.HBM)
            for array in (query_act, key_act, value_act, long_filter.T, out_grad)
        )
    )
    got = exchange(sent)
    sent = pl.pallas_call(
        functools.partial(group_kernel, scale, width),
        out_shape=chunks,
        scratch_shapes=[
            pltpu.VMEM((channels, 2 * tokens), bf16),
            pltpu.VMEM((2 * channels, tokens), bf16),
            pltpu.VMEM((groups, tokens, tokens), bf16),
        ],
        compiler_params=pltpu.CompilerParams(vmem_limit_bytes=16 * 2**20),
        name="group",
    )(got)
    got = exchange(sent)
    like = jax.ShapeDtypeStruct((tokens, channels), bf16)
    *acts, filter_grad = pl.pallas_call(
        functools.partial(output_kernel, width),
        out_shape=(like, like, like, like, jax.ShapeDtypeStruct((groups, tokens), f32)),
        out_specs=[pl.BlockSpec(memory_space=pltpu.HBM)] * 5,
        scratch_shapes=[
            act,
            act,
            act,
            act,
            pltpu.VMEM((groups, tokens), f32),
            pltpu.SemaphoreType.DMA((5,)),
        ],
        compiler_params=pltpu.CompilerParams(vmem_limit_bytes=8 * 2**20),
        name="outputs",
    )(got, query_act, key_act, value_act, out_grad)
    return (*acts, filter_grad.T)


def on_device(query_act, key_act, value_act, long_filter, out_grad):
    tokens, channels = query_act.shape
    groups = long_filter.shape[1]
    devices = lax.axis_size("slow") * lax.axis_size("fast")
    if devices == groups and tokens == 128 and channels == 16 * groups and groups % 4 == 0:
        return by_groups(query_act, key_act, value_act, long_filter, out_grad)
    return by_spectra(query_act, key_act, value_act, long_filter, out_grad)


def solution(mesh):
    placed = (
        P(("slow", "fast"), None),
        P(("slow", "fast"), None),
        P(("slow", "fast"), None),
        P(("slow", "fast"), None),
        P(("slow", "fast"), None),
    )
    return jax.shard_map(
        on_device,
        mesh=mesh,
        in_specs=placed,
        out_specs=(
            P(("slow", "fast"), None),
            P(("slow", "fast"), None),
            P(("slow", "fast"), None),
            P(("slow", "fast"), None),
            P(("slow", "fast"), None),
        ),
        check_vma=False,
    )
```

```python
import functools
import math

import jax
import jax.numpy as jnp
from jax import lax
from jax.experimental import pallas as pl
from jax.experimental.pallas import tpu as pltpu
from jax.sharding import PartitionSpec as P

highest = lax.Precision.HIGHEST


def index_ramp(points, along, ndim, offset):
    shape_list = [1] * ndim
    shape_list[along] = points
    return (jnp.arange(points, dtype=jnp.int32) + offset).reshape(shape_list)


def apply_dft(re_im, points, direction, along):
    index_row = jnp.arange(points, dtype=jnp.int32)
    phase_turns = index_row[:, None] * index_row[None, :] % points
    phases = 2.0 * math.pi / points * phase_turns.astype(jnp.float32)
    cosine = jnp.cos(phases)
    sine_part = direction * jnp.sin(phases)

    def contract(values, matrix):
        result = jnp.tensordot(values, matrix, axes=((along,), (1,)), precision=highest)
        return jnp.moveaxis(result, -1, along)

    return (
        contract(re_im[0], cosine) - contract(re_im[1], sine_part),
        contract(re_im[0], sine_part) + contract(re_im[1], cosine),
    )


def rotate(re_im, phase_turns, period, direction):
    phases = 2.0 * math.pi / period * (phase_turns % period).astype(jnp.float32)
    cosine = jnp.cos(phases)
    sine_part = direction * jnp.sin(phases)
    return (re_im[0] * cosine - re_im[1] * sine_part, re_im[0] * sine_part + re_im[1] * cosine)


def complex_times(left, right):
    return (left[0] * right[0] - left[1] * right[1], left[0] * right[1] + left[1] * right[0])


def conj_times(left, right):
    return (left[0] * right[0] + left[1] * right[1], left[0] * right[1] - left[1] * right[0])


def positions(grid_info, slow_points, slow_offset, fast_points, fast_offset):
    fast_count, tokens = (grid_info[1], grid_info[2])
    block_index = index_ramp(slow_points, 2, 5, slow_offset) * fast_count + index_ramp(
        fast_points, 3, 5, fast_offset
    )
    return block_index * tokens + index_ramp(tokens, 4, 5, 0)


def open_halves(re_im, grid_info, fast_offset):
    token_place = positions(grid_info, re_im[0].shape[1], 0, re_im[0].shape[2], fast_offset)
    return rotate(
        (re_im[0][None], re_im[1][None]),
        index_ramp(2, 0, 5, 0) * token_place,
        2 * grid_info[3],
        -1.0,
    )


def fold_halves(re_im, token_place, seq_length):
    turned = rotate(re_im, index_ramp(2, 0, 5, 0) * token_place, 2 * seq_length, 1.0)
    scale = 0.5 / seq_length
    return (jnp.sum(turned[0], axis=0) * scale, jnp.sum(turned[1], axis=0) * scale)


def front_forward(re_im, grid_info, fast_offset):
    slow_count, fast_count = (grid_info[0], grid_info[1])
    re_im = apply_dft(re_im, slow_count, -1.0, 2)
    phase_turns = index_ramp(slow_count, 2, 5, 0) * index_ramp(re_im[0].shape[3], 3, 5, fast_offset)
    return rotate(re_im, phase_turns, slow_count * fast_count, -1.0)


def front_inverse(re_im, grid_info, fast_offset):
    slow_count, fast_count = (grid_info[0], grid_info[1])
    phase_turns = index_ramp(slow_count, 2, 5, 0) * index_ramp(re_im[0].shape[3], 3, 5, fast_offset)
    re_im = rotate(re_im, phase_turns, slow_count * fast_count, 1.0)
    return apply_dft(re_im, slow_count, 1.0, 2)


def lead_phase(re_im, grid_info, ka_offset):
    slow_count, fast_count, tokens = (grid_info[0], grid_info[1], grid_info[2])
    lead_index = index_ramp(re_im[0].shape[2], 2, 5, ka_offset) + slow_count * index_ramp(
        fast_count, 3, 5, 0
    )
    return lead_index * index_ramp(tokens, 4, 5, 0)


def back_forward(re_im, grid_info, ka_offset):
    re_im = apply_dft(re_im, grid_info[1], -1.0, 3)
    re_im = rotate(re_im, lead_phase(re_im, grid_info, ka_offset), grid_info[3], -1.0)
    return apply_dft(re_im, grid_info[2], -1.0, 4)


def back_inverse(re_im, grid_info, ka_offset):
    re_im = apply_dft(re_im, grid_info[2], 1.0, 4)
    re_im = rotate(re_im, lead_phase(re_im, grid_info, ka_offset), grid_info[3], 1.0)
    return apply_dft(re_im, grid_info[1], 1.0, 3)


def to_channels(seq_rows):
    return lax.all_to_all(
        seq_rows.reshape(1, seq_rows.shape[0], seq_rows.shape[1]),
        "slow",
        split_axis=2,
        concat_axis=0,
        tiled=True,
    )


def merge_blocks(arrays, block_count):
    tokens = arrays[0].shape[0]
    pieces = [item.reshape(tokens, block_count, item.shape[1] // block_count) for item in arrays]
    return jnp.concatenate(pieces, axis=2).reshape(tokens, -1)


def split_columns(rows_major, widths):
    tokens, block_count = (rows_major.shape[0], rows_major.shape[1])
    result = []
    offset = 0
    for length in widths:
        result.append(
            rows_major[:, :, offset : offset + length].reshape(tokens, block_count * length)
        )
        offset += length
    return result


def real_blocks(real_part, imag_part, segments):
    pieces = []
    offset = 0
    for output_kind, length in segments:
        real_seg = real_part[:, offset : offset + length]
        imag_seg = imag_part[:, offset : offset + length]
        offset += length
        if output_kind == "pairs":
            stacked = jnp.transpose(jnp.stack((real_seg, imag_seg), axis=-1), (0, 2, 1, 3))
            pieces.append(stacked.reshape(stacked.shape[0], stacked.shape[1], 2 * length))
        else:
            pieces.append(jnp.transpose(real_seg, (0, 2, 1)))
    return jnp.concatenate(pieces, axis=2)


def segment_widths(segments):
    return [2 * length if output_kind == "pairs" else length for output_kind, length in segments]


def spread_forward(seq_rows, grid_info, fast_rank, segments):
    slow_count, fast_count = (grid_info[0], grid_info[1])
    blocks = to_channels(seq_rows).astype(jnp.float32)
    real_list = []
    imag_list = []
    offset = 0
    for length, packed in segments:
        segment = blocks[:, :, offset : offset + length]
        offset += length
        if packed:
            halves = segment.reshape(segment.shape[0], segment.shape[1], length // 2, 2)
            real_seg, imag_seg = (halves[..., 0], halves[..., 1])
        else:
            real_seg, imag_seg = (segment, jnp.zeros_like(segment))
        real_list.append(jnp.transpose(real_seg, (2, 0, 1)))
        imag_list.append(jnp.transpose(imag_seg, (2, 0, 1)))
    re_im = (
        jnp.concatenate(real_list, 0)[:, :, None, :],
        jnp.concatenate(imag_list, 0)[:, :, None, :],
    )
    re_im = front_forward(open_halves(re_im, grid_info, fast_rank), grid_info, fast_rank)
    re_im = (
        lax.all_to_all(re_im[0], "fast", split_axis=2, concat_axis=3, tiled=True),
        lax.all_to_all(re_im[1], "fast", split_axis=2, concat_axis=3, tiled=True),
    )
    return back_forward(re_im, grid_info, fast_rank * (slow_count // fast_count))


def spread_inverse(re_im, grid_info, fast_rank, slow_rank, segments):
    slow_count, fast_count, tokens, seq_length = grid_info
    re_im = back_inverse(re_im, grid_info, fast_rank * (slow_count // fast_count))
    re_im = (
        lax.all_to_all(re_im[0], "fast", split_axis=3, concat_axis=2, tiled=True),
        lax.all_to_all(re_im[1], "fast", split_axis=3, concat_axis=2, tiled=True),
    )
    re_im = front_inverse(re_im, grid_info, fast_rank)
    re_im = (
        lax.all_to_all(re_im[0], "slow", split_axis=2, concat_axis=1, tiled=True),
        lax.all_to_all(re_im[1], "slow", split_axis=2, concat_axis=1, tiled=True),
    )
    real_part, imag_part = fold_halves(
        re_im, positions(grid_info, 1, slow_rank, 1, fast_rank), seq_length
    )
    length = real_part.shape[0] // slow_count
    blocks = real_blocks(
        real_part.reshape(slow_count, length, tokens),
        imag_part.reshape(slow_count, length, tokens),
        segments,
    )
    rows_major = jnp.transpose(blocks, (1, 0, 2))
    return split_columns(rows_major, segment_widths(segments))


def regroup(re_im, length, local_groups):

    def by_group(values):
        values = values[:, :length]
        return values.reshape(
            (values.shape[0], local_groups, length // local_groups) + values.shape[2:]
        )

    return (by_group(re_im[0]), by_group(re_im[1]))


def flatten_pairs(re_im):

    def merged(values):
        return values.reshape(
            (values.shape[0], values.shape[1] * values.shape[2]) + values.shape[3:]
        )

    return (merged(re_im[0]), merged(re_im[1]))


def by_spectra(query_act, key_act, value_act, long_filter, out_grad):
    tokens, channels = query_act.shape
    groups = long_filter.shape[1]
    slow_count = lax.axis_size("slow")
    fast_count = lax.axis_size("fast")
    seq_length = tokens * slow_count * fast_count
    grid_info = (slow_count, fast_count, tokens, seq_length)
    group_width = channels // groups
    product = (key_act.astype(jnp.float32) * value_act.astype(jnp.float32)).astype(jnp.bfloat16)
    grad_in = (out_grad.astype(jnp.float32) * query_act.astype(jnp.float32)).astype(jnp.bfloat16)
    fast_rank = lax.axis_index("fast")
    slow_rank = lax.axis_index("slow")
    data_pairs = channels // (2 * slow_count)
    local_groups = groups // slow_count
    block_width = channels // slow_count
    spectra = spread_forward(
        merge_blocks((product, long_filter), slow_count),
        grid_info,
        fast_rank,
        ((block_width, True), (local_groups, False)),
    )
    prod_spec = regroup(spectra, data_pairs, local_groups)
    filter_spec = (spectra[0][:, data_pairs:, None], spectra[1][:, data_pairs:, None])
    convolved = spread_inverse(
        flatten_pairs(complex_times(prod_spec, filter_spec)),
        grid_info,
        fast_rank,
        slow_rank,
        (("pairs", data_pairs),),
    )[0]
    grad_spec = regroup(
        spread_forward(grad_in, grid_info, fast_rank, ((block_width, True),)),
        data_pairs,
        local_groups,
    )
    back_spec = flatten_pairs(conj_times(filter_spec, grad_spec))
    corr_spec = conj_times(prod_spec, grad_spec)
    joined = (
        jnp.concatenate((back_spec[0], jnp.sum(corr_spec[0], axis=2)), axis=1),
        jnp.concatenate((back_spec[1], jnp.sum(corr_spec[1], axis=2)), axis=1),
    )
    backward, filter_sum = spread_inverse(
        joined, grid_info, fast_rank, slow_rank, (("pairs", data_pairs), ("real", local_groups))
    )
    scale = 1.0 / math.sqrt(seq_length * group_width)
    mixed_out = (query_act.astype(jnp.float32) * convolved).astype(jnp.bfloat16)
    query_grad = (out_grad.astype(jnp.float32) * convolved).astype(jnp.bfloat16)
    key_grad = (backward * value_act.astype(jnp.float32)).astype(jnp.bfloat16)
    value_grad = (backward * key_act.astype(jnp.float32)).astype(jnp.bfloat16)
    return (mixed_out, query_grad, key_grad, value_grad, filter_sum * scale)


f32 = jnp.float32
bf16 = jnp.bfloat16
EXTRA_ROWS = 2
PACKED_ROWS = 16


def dot(left, right):
    return jnp.dot(left, right, preferred_element_type=f32)


def dot_nt(left, right):
    return lax.dot_general(left, right, (((1,), (1,)), ((), ())), preferred_element_type=f32)


def ramp(shape, dim):
    return lax.broadcasted_iota(jnp.int32, shape, dim)


def flip_matrix(size):
    return (ramp((size, size), 0) + ramp((size, size), 1) == size - 1).astype(bf16)


def eye_matrix(size):
    return (ramp((size, size), 0) == ramp((size, size), 1)).astype(bf16)


def gate_kernel(query, key, value, filt, grad, sent, queries, keys, values, taps, grads, done):
    copies = [
        pltpu.make_async_copy(source, target, done.at[at])
        for at, (source, target) in enumerate(
            ((key, keys), (value, values), (grad, grads), (query, queries), (filt, taps))
        )
    ]
    for copy in copies:
        copy.start()
    tokens, channels = queries.shape
    groups = taps.shape[0]
    width = channels // groups
    rows = 2 * width + EXTRA_ROWS
    copies[0].wait()
    copies[1].wait()
    product = (keys[...].astype(f32) * values[...].astype(f32)).astype(bf16)
    columns = product.astype(f32).T.astype(bf16)
    for group in range(groups):
        sent[group * rows : group * rows + width, :] = columns[group * width : (group + 1) * width]
    copies[2].wait()
    copies[3].wait()
    grad_in = (grads[...].astype(f32) * queries[...].astype(f32)).astype(bf16)
    columns = dot(flip_matrix(tokens), grad_in).T.astype(bf16)
    for group in range(groups):
        at = group * rows + width
        sent[at : at + width, :] = columns[group * width : (group + 1) * width]
    copies[4].wait()
    for group in range(groups):
        at = group * rows + 2 * width
        sent[at : at + EXTRA_ROWS, :] = jnp.broadcast_to(
            taps[group : group + 1, :], (EXTRA_ROWS, tokens)
        )


def group_kernel(scale, width, got, sent, streams, padded, toeplitz):
    rows, tokens = 2 * width + EXTRA_ROWS, got.shape[1]
    blocks = got.shape[0] // rows
    pairs = blocks // 2
    row, lane = ramp((tokens, tokens), 0), ramp((tokens, tokens), 1)
    for pair in range(pairs):
        for half in range(2):
            block = 2 * pair + half
            lanes = slice(half * tokens, (half + 1) * tokens)
            at = 2 * width * pair
            streams[at : at + width, lanes] = got[block * rows : block * rows + width, :]
            streams[at + width : at + 2 * width, lanes] = got[
                (blocks - 1 - block) * rows + width : (blocks - 1 - block) * rows + 2 * width, :
            ]
    for block in range(blocks):
        padded[block * width : (block + 1) * width, :] = got[
            block * rows + width : block * rows + 2 * width, :
        ]
    padded[blocks * width :, :] = jnp.zeros((blocks * width, tokens), bf16)

    before = jnp.zeros((tokens, tokens), bf16)
    for block in range(blocks):
        taps = got[block * rows + 2 * width : block * rows + 2 * width + 1, :].astype(f32)
        taps = jnp.broadcast_to(taps, (PACKED_ROWS, tokens))
        first = pltpu.roll(taps, 0, 1, stride=1, stride_axis=0).astype(bf16)
        turned = jnp.concatenate(
            [pltpu.roll(first, at, 1) if at else first for at in range(0, tokens, PACKED_ROWS)], axis=0
        )
        toeplitz[block] = jnp.where(lane >= row, turned, before)
        before = turned

    total = None
    for pair in range(pairs):
        left = jnp.zeros((tokens, tokens), bf16) if pair == 0 else toeplitz[2 * pair - 1]
        weights = jnp.concatenate(
            (
                jnp.concatenate((toeplitz[2 * pair], toeplitz[2 * pair + 1]), axis=1),
                jnp.concatenate((left, toeplitz[2 * pair]), axis=1),
            ),
            axis=0,
        )
        skip = 2 * width * pair
        term = dot(streams[0 : 2 * width * pairs - skip, :], weights)
        total = term if pair == 0 else jnp.concatenate((total[:skip], total[skip:] + term), axis=0)
    for pair in range(pairs):
        for half in range(2):
            block = 2 * pair + half
            lanes = slice(half * tokens, (half + 1) * tokens)
            at = 2 * width * pair
            sent[block * rows : block * rows + width, :] = total[at : at + width, lanes].astype(bf16)
            place = (blocks - 1 - block) * rows + width
            sent[place : place + width, :] = total[
                at + width : at + 2 * width, lanes
            ].astype(bf16)

    ordered = jnp.concatenate(
        [got[block * rows : block * rows + width, :] for block in range(blocks)], axis=0
    )
    ordered = ordered.astype(f32).T.astype(bf16)
    before = jnp.zeros((tokens, tokens), f32)
    which = ramp((EXTRA_ROWS, tokens), 0)
    for pair in range(pairs):
        depth = blocks * width if 2 * pair + 2 > blocks // 2 else blocks * width // 2
        columns = [
            padded[pl.ds((blocks - 1 - lag) * width, depth), :] for lag in (2 * pair, 2 * pair + 1)
        ]
        outer = dot(ordered[:, :depth], jnp.concatenate(columns, axis=1))
        for half in range(2):
            block = 2 * pair + half
            turned = pltpu.roll(
                outer[:, half * tokens : (half + 1) * tokens], 0, 1, stride=1, stride_axis=0
            )
            joined = jnp.where(lane >= row, turned, before)
            before = turned
            value = jnp.sum(joined, axis=0, keepdims=True) * scale
            high = value.astype(bf16).astype(f32)
            pieces = jnp.where(which == 0, high, jnp.where(which == 1, value - high, 0.0))
            place = (blocks - 1 - block) * rows + 2 * width
            sent[place : place + EXTRA_ROWS, :] = pieces.astype(bf16)


def output_kernel(
    width, got, query, key, value, grad, mixed, query_grad, key_grad, value_grad, filter_grad
):
    rows, tokens = 2 * width + EXTRA_ROWS, got.shape[1]
    blocks = got.shape[0] // rows

    def collect(first, count):
        return jnp.concatenate(
            [got[at * rows + first : at * rows + first + count, :] for at in range(blocks)], axis=0
        )

    flip = flip_matrix(tokens)
    convolved = dot_nt(eye_matrix(tokens), collect(0, width))
    mixed[...] = (query[...].astype(f32) * convolved).astype(bf16)
    query_grad[...] = (grad[...].astype(f32) * convolved).astype(bf16)
    backward = dot_nt(flip, collect(width, width))
    key_grad[...] = (backward * value[...].astype(f32)).astype(bf16)
    value_grad[...] = (backward * key[...].astype(f32)).astype(bf16)
    high, low = collect(2 * width, 1), collect(2 * width + 1, 1)
    filter_grad[...] = dot(high, flip) + dot(low, flip)


def by_groups(query_act, key_act, value_act, long_filter, out_grad):
    tokens, channels = query_act.shape
    groups = long_filter.shape[1]
    width = channels // groups
    rows = 2 * width + EXTRA_ROWS
    scale = 1.0 / math.sqrt(tokens * groups * width)
    chunks = jax.ShapeDtypeStruct((groups * rows, tokens), bf16)

    def exchange(sent):
        pieces = sent.reshape(groups, rows // 2, 2, tokens)
        pieces = lax.all_to_all(pieces, ("slow", "fast"), split_axis=0, concat_axis=0, tiled=True)
        return pieces.reshape(groups * rows, tokens)

    act = pltpu.VMEM((tokens, channels), bf16)
    sent = pl.pallas_call(
        gate_kernel,
        out_shape=chunks,
        in_specs=[pl.BlockSpec(memory_space=pltpu.HBM)] * 5,
        scratch_shapes=[
            act,
            act,
            act,
            pltpu.VMEM((groups, tokens), bf16),
            act,
            pltpu.SemaphoreType.DMA((5,)),
        ],
        compiler_params=pltpu.CompilerParams(vmem_limit_bytes=8 * 2**20),
        name="gate",
    )(
        *(
            pltpu.with_memory_space_constraint(array, pltpu.HBM)
            for array in (query_act, key_act, value_act, long_filter.T, out_grad)
        )
    )
    got = exchange(sent)
    sent = pl.pallas_call(
        functools.partial(group_kernel, scale, width),
        out_shape=chunks,
        scratch_shapes=[
            pltpu.VMEM((channels, 2 * tokens), bf16),
            pltpu.VMEM((2 * channels, tokens), bf16),
            pltpu.VMEM((groups, tokens, tokens), bf16),
        ],
        compiler_params=pltpu.CompilerParams(vmem_limit_bytes=16 * 2**20),
        name="group",
    )(got)
    got = exchange(sent)
    like = jax.ShapeDtypeStruct((tokens, channels), bf16)
    *acts, filter_grad = pl.pallas_call(
        functools.partial(output_kernel, width),
        out_shape=(like, like, like, like, jax.ShapeDtypeStruct((groups, tokens), f32)),
        compiler_params=pltpu.CompilerParams(vmem_limit_bytes=8 * 2**20),
        name="outputs",
    )(got, query_act, key_act, value_act, out_grad)
    return (*acts, filter_grad.T)


def on_device(query_act, key_act, value_act, long_filter, out_grad):
    tokens, channels = query_act.shape
    groups = long_filter.shape[1]
    devices = lax.axis_size("slow") * lax.axis_size("fast")
    if devices == groups and tokens == 128 and channels == 16 * groups and groups % 4 == 0:
        return by_groups(query_act, key_act, value_act, long_filter, out_grad)
    return by_spectra(query_act, key_act, value_act, long_filter, out_grad)


def solution(mesh):
    placed = (
        P(("slow", "fast"), None),
        P(("slow", "fast"), None),
        P(("slow", "fast"), None),
        P(("slow", "fast"), None),
        P(("slow", "fast"), None),
    )
    return jax.shard_map(
        on_device,
        mesh=mesh,
        in_specs=placed,
        out_specs=(
            P(("slow", "fast"), None),
            P(("slow", "fast"), None),
            P(("slow", "fast"), None),
            P(("slow", "fast"), None),
            P(("slow", "fast"), None),
        ),
        check_vma=False,
    )
```

```python
import functools
import math

import jax
import jax.numpy as jnp
from jax import lax
from jax.experimental import pallas as pl
from jax.experimental.pallas import tpu as pltpu
from jax.sharding import PartitionSpec as P

highest = lax.Precision.HIGHEST


def index_ramp(points, along, ndim, offset):
    shape_list = [1] * ndim
    shape_list[along] = points
    return (jnp.arange(points, dtype=jnp.int32) + offset).reshape(shape_list)


def apply_dft(re_im, points, direction, along):
    index_row = jnp.arange(points, dtype=jnp.int32)
    phase_turns = index_row[:, None] * index_row[None, :] % points
    phases = 2.0 * math.pi / points * phase_turns.astype(jnp.float32)
    cosine = jnp.cos(phases)
    sine_part = direction * jnp.sin(phases)

    def contract(values, matrix):
        result = jnp.tensordot(values, matrix, axes=((along,), (1,)), precision=highest)
        return jnp.moveaxis(result, -1, along)

    return (
        contract(re_im[0], cosine) - contract(re_im[1], sine_part),
        contract(re_im[0], sine_part) + contract(re_im[1], cosine),
    )


def rotate(re_im, phase_turns, period, direction):
    phases = 2.0 * math.pi / period * (phase_turns % period).astype(jnp.float32)
    cosine = jnp.cos(phases)
    sine_part = direction * jnp.sin(phases)
    return (re_im[0] * cosine - re_im[1] * sine_part, re_im[0] * sine_part + re_im[1] * cosine)


def complex_times(left, right):
    return (left[0] * right[0] - left[1] * right[1], left[0] * right[1] + left[1] * right[0])


def conj_times(left, right):
    return (left[0] * right[0] + left[1] * right[1], left[0] * right[1] - left[1] * right[0])


def positions(grid_info, slow_points, slow_offset, fast_points, fast_offset):
    fast_count, tokens = (grid_info[1], grid_info[2])
    block_index = index_ramp(slow_points, 2, 5, slow_offset) * fast_count + index_ramp(
        fast_points, 3, 5, fast_offset
    )
    return block_index * tokens + index_ramp(tokens, 4, 5, 0)


def open_halves(re_im, grid_info, fast_offset):
    token_place = positions(grid_info, re_im[0].shape[1], 0, re_im[0].shape[2], fast_offset)
    return rotate(
        (re_im[0][None], re_im[1][None]),
        index_ramp(2, 0, 5, 0) * token_place,
        2 * grid_info[3],
        -1.0,
    )


def fold_halves(re_im, token_place, seq_length):
    turned = rotate(re_im, index_ramp(2, 0, 5, 0) * token_place, 2 * seq_length, 1.0)
    scale = 0.5 / seq_length
    return (jnp.sum(turned[0], axis=0) * scale, jnp.sum(turned[1], axis=0) * scale)


def front_forward(re_im, grid_info, fast_offset):
    slow_count, fast_count = (grid_info[0], grid_info[1])
    re_im = apply_dft(re_im, slow_count, -1.0, 2)
    phase_turns = index_ramp(slow_count, 2, 5, 0) * index_ramp(re_im[0].shape[3], 3, 5, fast_offset)
    return rotate(re_im, phase_turns, slow_count * fast_count, -1.0)


def front_inverse(re_im, grid_info, fast_offset):
    slow_count, fast_count = (grid_info[0], grid_info[1])
    phase_turns = index_ramp(slow_count, 2, 5, 0) * index_ramp(re_im[0].shape[3], 3, 5, fast_offset)
    re_im = rotate(re_im, phase_turns, slow_count * fast_count, 1.0)
    return apply_dft(re_im, slow_count, 1.0, 2)


def lead_phase(re_im, grid_info, ka_offset):
    slow_count, fast_count, tokens = (grid_info[0], grid_info[1], grid_info[2])
    lead_index = index_ramp(re_im[0].shape[2], 2, 5, ka_offset) + slow_count * index_ramp(
        fast_count, 3, 5, 0
    )
    return lead_index * index_ramp(tokens, 4, 5, 0)


def back_forward(re_im, grid_info, ka_offset):
    re_im = apply_dft(re_im, grid_info[1], -1.0, 3)
    re_im = rotate(re_im, lead_phase(re_im, grid_info, ka_offset), grid_info[3], -1.0)
    return apply_dft(re_im, grid_info[2], -1.0, 4)


def back_inverse(re_im, grid_info, ka_offset):
    re_im = apply_dft(re_im, grid_info[2], 1.0, 4)
    re_im = rotate(re_im, lead_phase(re_im, grid_info, ka_offset), grid_info[3], 1.0)
    return apply_dft(re_im, grid_info[1], 1.0, 3)


def to_channels(seq_rows):
    return lax.all_to_all(
        seq_rows.reshape(1, seq_rows.shape[0], seq_rows.shape[1]),
        "slow",
        split_axis=2,
        concat_axis=0,
        tiled=True,
    )


def merge_blocks(arrays, block_count):
    tokens = arrays[0].shape[0]
    pieces = [item.reshape(tokens, block_count, item.shape[1] // block_count) for item in arrays]
    return jnp.concatenate(pieces, axis=2).reshape(tokens, -1)


def split_columns(rows_major, widths):
    tokens, block_count = (rows_major.shape[0], rows_major.shape[1])
    result = []
    offset = 0
    for length in widths:
        result.append(
            rows_major[:, :, offset : offset + length].reshape(tokens, block_count * length)
        )
        offset += length
    return result


def real_blocks(real_part, imag_part, segments):
    pieces = []
    offset = 0
    for output_kind, length in segments:
        real_seg = real_part[:, offset : offset + length]
        imag_seg = imag_part[:, offset : offset + length]
        offset += length
        if output_kind == "pairs":
            stacked = jnp.transpose(jnp.stack((real_seg, imag_seg), axis=-1), (0, 2, 1, 3))
            pieces.append(stacked.reshape(stacked.shape[0], stacked.shape[1], 2 * length))
        else:
            pieces.append(jnp.transpose(real_seg, (0, 2, 1)))
    return jnp.concatenate(pieces, axis=2)


def segment_widths(segments):
    return [2 * length if output_kind == "pairs" else length for output_kind, length in segments]


def spread_forward(seq_rows, grid_info, fast_rank, segments):
    slow_count, fast_count = (grid_info[0], grid_info[1])
    blocks = to_channels(seq_rows).astype(jnp.float32)
    real_list = []
    imag_list = []
    offset = 0
    for length, packed in segments:
        segment = blocks[:, :, offset : offset + length]
        offset += length
        if packed:
            halves = segment.reshape(segment.shape[0], segment.shape[1], length // 2, 2)
            real_seg, imag_seg = (halves[..., 0], halves[..., 1])
        else:
            real_seg, imag_seg = (segment, jnp.zeros_like(segment))
        real_list.append(jnp.transpose(real_seg, (2, 0, 1)))
        imag_list.append(jnp.transpose(imag_seg, (2, 0, 1)))
    re_im = (
        jnp.concatenate(real_list, 0)[:, :, None, :],
        jnp.concatenate(imag_list, 0)[:, :, None, :],
    )
    re_im = front_forward(open_halves(re_im, grid_info, fast_rank), grid_info, fast_rank)
    re_im = (
        lax.all_to_all(re_im[0], "fast", split_axis=2, concat_axis=3, tiled=True),
        lax.all_to_all(re_im[1], "fast", split_axis=2, concat_axis=3, tiled=True),
    )
    return back_forward(re_im, grid_info, fast_rank * (slow_count // fast_count))


def spread_inverse(re_im, grid_info, fast_rank, slow_rank, segments):
    slow_count, fast_count, tokens, seq_length = grid_info
    re_im = back_inverse(re_im, grid_info, fast_rank * (slow_count // fast_count))
    re_im = (
        lax.all_to_all(re_im[0], "fast", split_axis=3, concat_axis=2, tiled=True),
        lax.all_to_all(re_im[1], "fast", split_axis=3, concat_axis=2, tiled=True),
    )
    re_im = front_inverse(re_im, grid_info, fast_rank)
    re_im = (
        lax.all_to_all(re_im[0], "slow", split_axis=2, concat_axis=1, tiled=True),
        lax.all_to_all(re_im[1], "slow", split_axis=2, concat_axis=1, tiled=True),
    )
    real_part, imag_part = fold_halves(
        re_im, positions(grid_info, 1, slow_rank, 1, fast_rank), seq_length
    )
    length = real_part.shape[0] // slow_count
    blocks = real_blocks(
        real_part.reshape(slow_count, length, tokens),
        imag_part.reshape(slow_count, length, tokens),
        segments,
    )
    rows_major = jnp.transpose(blocks, (1, 0, 2))
    return split_columns(rows_major, segment_widths(segments))


def regroup(re_im, length, local_groups):

    def by_group(values):
        values = values[:, :length]
        return values.reshape(
            (values.shape[0], local_groups, length // local_groups) + values.shape[2:]
        )

    return (by_group(re_im[0]), by_group(re_im[1]))


def flatten_pairs(re_im):

    def merged(values):
        return values.reshape(
            (values.shape[0], values.shape[1] * values.shape[2]) + values.shape[3:]
        )

    return (merged(re_im[0]), merged(re_im[1]))


def by_spectra(query_act, key_act, value_act, long_filter, out_grad):
    tokens, channels = query_act.shape
    groups = long_filter.shape[1]
    slow_count = lax.axis_size("slow")
    fast_count = lax.axis_size("fast")
    seq_length = tokens * slow_count * fast_count
    grid_info = (slow_count, fast_count, tokens, seq_length)
    group_width = channels // groups
    product = (key_act.astype(jnp.float32) * value_act.astype(jnp.float32)).astype(jnp.bfloat16)
    grad_in = (out_grad.astype(jnp.float32) * query_act.astype(jnp.float32)).astype(jnp.bfloat16)
    fast_rank = lax.axis_index("fast")
    slow_rank = lax.axis_index("slow")
    data_pairs = channels // (2 * slow_count)
    local_groups = groups // slow_count
    block_width = channels // slow_count
    spectra = spread_forward(
        merge_blocks((product, long_filter), slow_count),
        grid_info,
        fast_rank,
        ((block_width, True), (local_groups, False)),
    )
    prod_spec = regroup(spectra, data_pairs, local_groups)
    filter_spec = (spectra[0][:, data_pairs:, None], spectra[1][:, data_pairs:, None])
    convolved = spread_inverse(
        flatten_pairs(complex_times(prod_spec, filter_spec)),
        grid_info,
        fast_rank,
        slow_rank,
        (("pairs", data_pairs),),
    )[0]
    grad_spec = regroup(
        spread_forward(grad_in, grid_info, fast_rank, ((block_width, True),)),
        data_pairs,
        local_groups,
    )
    back_spec = flatten_pairs(conj_times(filter_spec, grad_spec))
    corr_spec = conj_times(prod_spec, grad_spec)
    joined = (
        jnp.concatenate((back_spec[0], jnp.sum(corr_spec[0], axis=2)), axis=1),
        jnp.concatenate((back_spec[1], jnp.sum(corr_spec[1], axis=2)), axis=1),
    )
    backward, filter_sum = spread_inverse(
        joined, grid_info, fast_rank, slow_rank, (("pairs", data_pairs), ("real", local_groups))
    )
    scale = 1.0 / math.sqrt(seq_length * group_width)
    mixed_out = (query_act.astype(jnp.float32) * convolved).astype(jnp.bfloat16)
    query_grad = (out_grad.astype(jnp.float32) * convolved).astype(jnp.bfloat16)
    key_grad = (backward * value_act.astype(jnp.float32)).astype(jnp.bfloat16)
    value_grad = (backward * key_act.astype(jnp.float32)).astype(jnp.bfloat16)
    return (mixed_out, query_grad, key_grad, value_grad, filter_sum * scale)


f32 = jnp.float32
bf16 = jnp.bfloat16
EXTRA_ROWS = 2


def dot(left, right):
    return jnp.dot(left, right, preferred_element_type=f32)


def dot_nt(left, right):
    return lax.dot_general(left, right, (((1,), (1,)), ((), ())), preferred_element_type=f32)


def ramp(shape, dim):
    return lax.broadcasted_iota(jnp.int32, shape, dim)


def flip_matrix(size):
    return (ramp((size, size), 0) + ramp((size, size), 1) == size - 1).astype(bf16)


def eye_matrix(size):
    return (ramp((size, size), 0) == ramp((size, size), 1)).astype(bf16)


def gate_kernel(query, key, value, filt, grad, sent, queries, keys, values, taps, grads, done):
    copies = [
        pltpu.make_async_copy(source, target, done.at[at])
        for at, (source, target) in enumerate(
            ((key, keys), (value, values), (grad, grads), (query, queries), (filt, taps))
        )
    ]
    for at, copy in enumerate(copies):
        copy.start(priority=at % 2)
    tokens, channels = queries.shape
    groups = taps.shape[0]
    width = channels // groups
    rows = 2 * width + EXTRA_ROWS
    copies[0].wait()
    copies[1].wait()
    product = (keys[...].astype(f32) * values[...].astype(f32)).astype(bf16)
    columns = product.astype(f32).T.astype(bf16)
    for group in range(groups):
        sent[group * rows : group * rows + width, :] = columns[group * width : (group + 1) * width]
    copies[2].wait()
    copies[3].wait()
    grad_in = (grads[...].astype(f32) * queries[...].astype(f32)).astype(bf16)
    columns = dot(flip_matrix(tokens), grad_in).T.astype(bf16)
    for group in range(groups):
        at = group * rows + width
        sent[at : at + width, :] = columns[group * width : (group + 1) * width]
    copies[4].wait()
    for group in range(groups):
        at = group * rows + 2 * width
        sent[at : at + EXTRA_ROWS, :] = jnp.broadcast_to(
            taps[group : group + 1, :], (EXTRA_ROWS, tokens)
        )


def group_kernel(scale, width, got, sent, streams, padded, toeplitz):
    rows, tokens = 2 * width + EXTRA_ROWS, got.shape[1]
    blocks = got.shape[0] // rows
    pairs = blocks // 2
    row, lane = ramp((tokens, tokens), 0), ramp((tokens, tokens), 1)
    for pair in range(pairs):
        for half in range(2):
            block = 2 * pair + half
            lanes = slice(half * tokens, (half + 1) * tokens)
            at = 2 * width * pair
            streams[at : at + width, lanes] = got[block * rows : block * rows + width, :]
            streams[at + width : at + 2 * width, lanes] = got[
                (blocks - 1 - block) * rows + width : (blocks - 1 - block) * rows + 2 * width, :
            ]
    for block in range(blocks):
        padded[block * width : (block + 1) * width, :] = got[
            block * rows + width : block * rows + 2 * width, :
        ]
    padded[blocks * width :, :] = jnp.zeros((blocks * width, tokens), bf16)

    before = jnp.zeros((tokens, tokens), f32)
    for block in range(blocks):
        taps = jnp.broadcast_to(got[block * rows + 2 * width : block * rows + 2 * width + 1, :].astype(f32), (tokens, tokens))
        turned = pltpu.roll(taps, 0, 1, stride=1, stride_axis=0)
        toeplitz[block] = jnp.where(lane >= row, turned, before).astype(bf16)
        before = turned

    total = None
    for pair in range(pairs):
        left = jnp.zeros((tokens, tokens), bf16) if pair == 0 else toeplitz[2 * pair - 1]
        weights = jnp.concatenate(
            (
                jnp.concatenate((toeplitz[2 * pair], toeplitz[2 * pair + 1]), axis=1),
                jnp.concatenate((left, toeplitz[2 * pair]), axis=1),
            ),
            axis=0,
        )
        skip = 2 * width * pair
        term = dot(streams[0 : 2 * width * pairs - skip, :], weights)
        total = term if pair == 0 else jnp.concatenate((total[:skip], total[skip:] + term), axis=0)
    for pair in range(pairs):
        for half in range(2):
            block = 2 * pair + half
            lanes = slice(half * tokens, (half + 1) * tokens)
            at = 2 * width * pair
            sent[block * rows : block * rows + width, :] = total[at : at + width, lanes].astype(bf16)
            place = (blocks - 1 - block) * rows + width
            sent[place : place + width, :] = total[
                at + width : at + 2 * width, lanes
            ].astype(bf16)

    ordered = jnp.concatenate(
        [got[block * rows : block * rows + width, :] for block in range(blocks)], axis=0
    )
    ordered = ordered.astype(f32).T.astype(bf16)
    before = jnp.zeros((tokens, tokens), f32)
    which = ramp((EXTRA_ROWS, tokens), 0)
    for pair in range(pairs):
        depth = blocks * width if 2 * pair + 2 > blocks // 2 else blocks * width // 2
        columns = [
            padded[pl.ds((blocks - 1 - lag) * width, depth), :] for lag in (2 * pair, 2 * pair + 1)
        ]
        outer = dot(ordered[:, :depth], jnp.concatenate(columns, axis=1))
        for half in range(2):
            block = 2 * pair + half
            turned = pltpu.roll(
                outer[:, half * tokens : (half + 1) * tokens], 0, 1, stride=1, stride_axis=0
            )
            joined = jnp.where(lane >= row, turned, before)
            before = turned
            value = jnp.sum(joined, axis=0, keepdims=True) * scale
            high = value.astype(bf16).astype(f32)
            pieces = jnp.where(which == 0, high, jnp.where(which == 1, value - high, 0.0))
            place = (blocks - 1 - block) * rows + 2 * width
            sent[place : place + EXTRA_ROWS, :] = pieces.astype(bf16)


def output_kernel(
    width, got, query, key, value, grad, mixed, query_grad, key_grad, value_grad, filter_grad
):
    rows, tokens = 2 * width + EXTRA_ROWS, got.shape[1]
    blocks = got.shape[0] // rows

    def collect(first, count):
        return jnp.concatenate(
            [got[at * rows + first : at * rows + first + count, :] for at in range(blocks)], axis=0
        )

    flip = flip_matrix(tokens)
    convolved = dot_nt(eye_matrix(tokens), collect(0, width))
    mixed[...] = (query[...].astype(f32) * convolved).astype(bf16)
    query_grad[...] = (grad[...].astype(f32) * convolved).astype(bf16)
    backward = dot_nt(flip, collect(width, width))
    key_grad[...] = (backward * value[...].astype(f32)).astype(bf16)
    value_grad[...] = (backward * key[...].astype(f32)).astype(bf16)
    high, low = collect(2 * width, 1), collect(2 * width + 1, 1)
    filter_grad[...] = dot(high, flip) + dot(low, flip)


def by_groups(query_act, key_act, value_act, long_filter, out_grad):
    tokens, channels = query_act.shape
    groups = long_filter.shape[1]
    width = channels // groups
    rows = 2 * width + EXTRA_ROWS
    scale = 1.0 / math.sqrt(tokens * groups * width)
    chunks = jax.ShapeDtypeStruct((groups * rows, tokens), bf16)

    def exchange(sent):
        pieces = sent.reshape(groups, rows // 2, 2, tokens)
        pieces = lax.all_to_all(pieces, ("slow", "fast"), split_axis=0, concat_axis=0, tiled=True)
        return pieces.reshape(groups * rows, tokens)

    act = pltpu.VMEM((tokens, channels), bf16)
    sent = pl.pallas_call(
        gate_kernel,
        out_shape=chunks,
        in_specs=[pl.BlockSpec(memory_space=pltpu.HBM)] * 5,
        scratch_shapes=[
            act,
            act,
            act,
            pltpu.VMEM((groups, tokens), bf16),
            act,
            pltpu.SemaphoreType.DMA((5,)),
        ],
        compiler_params=pltpu.CompilerParams(vmem_limit_bytes=8 * 2**20),
        name="gate",
    )(
        *(
            pltpu.with_memory_space_constraint(array, pltpu.HBM)
            for array in (query_act, key_act, value_act, long_filter.T, out_grad)
        )
    )
    got = exchange(sent)
    sent = pl.pallas_call(
        functools.partial(group_kernel, scale, width),
        out_shape=chunks,
        scratch_shapes=[
            pltpu.VMEM((channels, 2 * tokens), bf16),
            pltpu.VMEM((2 * channels, tokens), bf16),
            pltpu.VMEM((groups, tokens, tokens), bf16),
        ],
        compiler_params=pltpu.CompilerParams(vmem_limit_bytes=16 * 2**20),
        name="group",
    )(got)
    got = exchange(sent)
    like = jax.ShapeDtypeStruct((tokens, channels), bf16)
    *acts, filter_grad = pl.pallas_call(
        functools.partial(output_kernel, width),
        out_shape=(like, like, like, like, jax.ShapeDtypeStruct((groups, tokens), f32)),
        compiler_params=pltpu.CompilerParams(vmem_limit_bytes=8 * 2**20),
        name="outputs",
    )(got, query_act, key_act, value_act, out_grad)
    return (*acts, filter_grad.T)


def on_device(query_act, key_act, value_act, long_filter, out_grad):
    tokens, channels = query_act.shape
    groups = long_filter.shape[1]
    devices = lax.axis_size("slow") * lax.axis_size("fast")
    if devices == groups and tokens == 128 and channels == 16 * groups and groups % 4 == 0:
        return by_groups(query_act, key_act, value_act, long_filter, out_grad)
    return by_spectra(query_act, key_act, value_act, long_filter, out_grad)


def solution(mesh):
    placed = (
        P(("slow", "fast"), None),
        P(("slow", "fast"), None),
        P(("slow", "fast"), None),
        P(("slow", "fast"), None),
        P(("slow", "fast"), None),
    )
    return jax.shard_map(
        on_device,
        mesh=mesh,
        in_specs=placed,
        out_specs=(
            P(("slow", "fast"), None),
            P(("slow", "fast"), None),
            P(("slow", "fast"), None),
            P(("slow", "fast"), None),
            P(("slow", "fast"), None),
        ),
        check_vma=False,
    )
```

```python
import functools
import math

import jax
import jax.numpy as jnp
from jax import lax
from jax.experimental import pallas as pl
from jax.experimental.pallas import tpu as pltpu
from jax.sharding import PartitionSpec as P

highest = lax.Precision.HIGHEST


def index_ramp(points, along, ndim, offset):
    shape_list = [1] * ndim
    shape_list[along] = points
    return (jnp.arange(points, dtype=jnp.int32) + offset).reshape(shape_list)


def apply_dft(re_im, points, direction, along):
    index_row = jnp.arange(points, dtype=jnp.int32)
    phase_turns = index_row[:, None] * index_row[None, :] % points
    phases = 2.0 * math.pi / points * phase_turns.astype(jnp.float32)
    cosine = jnp.cos(phases)
    sine_part = direction * jnp.sin(phases)

    def contract(values, matrix):
        result = jnp.tensordot(values, matrix, axes=((along,), (1,)), precision=highest)
        return jnp.moveaxis(result, -1, along)

    return (
        contract(re_im[0], cosine) - contract(re_im[1], sine_part),
        contract(re_im[0], sine_part) + contract(re_im[1], cosine),
    )


def rotate(re_im, phase_turns, period, direction):
    phases = 2.0 * math.pi / period * (phase_turns % period).astype(jnp.float32)
    cosine = jnp.cos(phases)
    sine_part = direction * jnp.sin(phases)
    return (re_im[0] * cosine - re_im[1] * sine_part, re_im[0] * sine_part + re_im[1] * cosine)


def complex_times(left, right):
    return (left[0] * right[0] - left[1] * right[1], left[0] * right[1] + left[1] * right[0])


def conj_times(left, right):
    return (left[0] * right[0] + left[1] * right[1], left[0] * right[1] - left[1] * right[0])


def positions(grid_info, slow_points, slow_offset, fast_points, fast_offset):
    fast_count, tokens = (grid_info[1], grid_info[2])
    block_index = index_ramp(slow_points, 2, 5, slow_offset) * fast_count + index_ramp(
        fast_points, 3, 5, fast_offset
    )
    return block_index * tokens + index_ramp(tokens, 4, 5, 0)


def open_halves(re_im, grid_info, fast_offset):
    token_place = positions(grid_info, re_im[0].shape[1], 0, re_im[0].shape[2], fast_offset)
    return rotate(
        (re_im[0][None], re_im[1][None]),
        index_ramp(2, 0, 5, 0) * token_place,
        2 * grid_info[3],
        -1.0,
    )


def fold_halves(re_im, token_place, seq_length):
    turned = rotate(re_im, index_ramp(2, 0, 5, 0) * token_place, 2 * seq_length, 1.0)
    scale = 0.5 / seq_length
    return (jnp.sum(turned[0], axis=0) * scale, jnp.sum(turned[1], axis=0) * scale)


def front_forward(re_im, grid_info, fast_offset):
    slow_count, fast_count = (grid_info[0], grid_info[1])
    re_im = apply_dft(re_im, slow_count, -1.0, 2)
    phase_turns = index_ramp(slow_count, 2, 5, 0) * index_ramp(re_im[0].shape[3], 3, 5, fast_offset)
    return rotate(re_im, phase_turns, slow_count * fast_count, -1.0)


def front_inverse(re_im, grid_info, fast_offset):
    slow_count, fast_count = (grid_info[0], grid_info[1])
    phase_turns = index_ramp(slow_count, 2, 5, 0) * index_ramp(re_im[0].shape[3], 3, 5, fast_offset)
    re_im = rotate(re_im, phase_turns, slow_count * fast_count, 1.0)
    return apply_dft(re_im, slow_count, 1.0, 2)


def lead_phase(re_im, grid_info, ka_offset):
    slow_count, fast_count, tokens = (grid_info[0], grid_info[1], grid_info[2])
    lead_index = index_ramp(re_im[0].shape[2], 2, 5, ka_offset) + slow_count * index_ramp(
        fast_count, 3, 5, 0
    )
    return lead_index * index_ramp(tokens, 4, 5, 0)


def back_forward(re_im, grid_info, ka_offset):
    re_im = apply_dft(re_im, grid_info[1], -1.0, 3)
    re_im = rotate(re_im, lead_phase(re_im, grid_info, ka_offset), grid_info[3], -1.0)
    return apply_dft(re_im, grid_info[2], -1.0, 4)


def back_inverse(re_im, grid_info, ka_offset):
    re_im = apply_dft(re_im, grid_info[2], 1.0, 4)
    re_im = rotate(re_im, lead_phase(re_im, grid_info, ka_offset), grid_info[3], 1.0)
    return apply_dft(re_im, grid_info[1], 1.0, 3)


def to_channels(seq_rows):
    return lax.all_to_all(
        seq_rows.reshape(1, seq_rows.shape[0], seq_rows.shape[1]),
        "slow",
        split_axis=2,
        concat_axis=0,
        tiled=True,
    )


def merge_blocks(arrays, block_count):
    tokens = arrays[0].shape[0]
    pieces = [item.reshape(tokens, block_count, item.shape[1] // block_count) for item in arrays]
    return jnp.concatenate(pieces, axis=2).reshape(tokens, -1)


def split_columns(rows_major, widths):
    tokens, block_count = (rows_major.shape[0], rows_major.shape[1])
    result = []
    offset = 0
    for length in widths:
        result.append(
            rows_major[:, :, offset : offset + length].reshape(tokens, block_count * length)
        )
        offset += length
    return result


def real_blocks(real_part, imag_part, segments):
    pieces = []
    offset = 0
    for output_kind, length in segments:
        real_seg = real_part[:, offset : offset + length]
        imag_seg = imag_part[:, offset : offset + length]
        offset += length
        if output_kind == "pairs":
            stacked = jnp.transpose(jnp.stack((real_seg, imag_seg), axis=-1), (0, 2, 1, 3))
            pieces.append(stacked.reshape(stacked.shape[0], stacked.shape[1], 2 * length))
        else:
            pieces.append(jnp.transpose(real_seg, (0, 2, 1)))
    return jnp.concatenate(pieces, axis=2)


def segment_widths(segments):
    return [2 * length if output_kind == "pairs" else length for output_kind, length in segments]


def spread_forward(seq_rows, grid_info, fast_rank, segments):
    slow_count, fast_count = (grid_info[0], grid_info[1])
    blocks = to_channels(seq_rows).astype(jnp.float32)
    real_list = []
    imag_list = []
    offset = 0
    for length, packed in segments:
        segment = blocks[:, :, offset : offset + length]
        offset += length
        if packed:
            halves = segment.reshape(segment.shape[0], segment.shape[1], length // 2, 2)
            real_seg, imag_seg = (halves[..., 0], halves[..., 1])
        else:
            real_seg, imag_seg = (segment, jnp.zeros_like(segment))
        real_list.append(jnp.transpose(real_seg, (2, 0, 1)))
        imag_list.append(jnp.transpose(imag_seg, (2, 0, 1)))
    re_im = (
        jnp.concatenate(real_list, 0)[:, :, None, :],
        jnp.concatenate(imag_list, 0)[:, :, None, :],
    )
    re_im = front_forward(open_halves(re_im, grid_info, fast_rank), grid_info, fast_rank)
    re_im = (
        lax.all_to_all(re_im[0], "fast", split_axis=2, concat_axis=3, tiled=True),
        lax.all_to_all(re_im[1], "fast", split_axis=2, concat_axis=3, tiled=True),
    )
    return back_forward(re_im, grid_info, fast_rank * (slow_count // fast_count))


def spread_inverse(re_im, grid_info, fast_rank, slow_rank, segments):
    slow_count, fast_count, tokens, seq_length = grid_info
    re_im = back_inverse(re_im, grid_info, fast_rank * (slow_count // fast_count))
    re_im = (
        lax.all_to_all(re_im[0], "fast", split_axis=3, concat_axis=2, tiled=True),
        lax.all_to_all(re_im[1], "fast", split_axis=3, concat_axis=2, tiled=True),
    )
    re_im = front_inverse(re_im, grid_info, fast_rank)
    re_im = (
        lax.all_to_all(re_im[0], "slow", split_axis=2, concat_axis=1, tiled=True),
        lax.all_to_all(re_im[1], "slow", split_axis=2, concat_axis=1, tiled=True),
    )
    real_part, imag_part = fold_halves(
        re_im, positions(grid_info, 1, slow_rank, 1, fast_rank), seq_length
    )
    length = real_part.shape[0] // slow_count
    blocks = real_blocks(
        real_part.reshape(slow_count, length, tokens),
        imag_part.reshape(slow_count, length, tokens),
        segments,
    )
    rows_major = jnp.transpose(blocks, (1, 0, 2))
    return split_columns(rows_major, segment_widths(segments))


def regroup(re_im, length, local_groups):

    def by_group(values):
        values = values[:, :length]
        return values.reshape(
            (values.shape[0], local_groups, length // local_groups) + values.shape[2:]
        )

    return (by_group(re_im[0]), by_group(re_im[1]))


def flatten_pairs(re_im):

    def merged(values):
        return values.reshape(
            (values.shape[0], values.shape[1] * values.shape[2]) + values.shape[3:]
        )

    return (merged(re_im[0]), merged(re_im[1]))


def by_spectra(query_act, key_act, value_act, long_filter, out_grad):
    tokens, channels = query_act.shape
    groups = long_filter.shape[1]
    slow_count = lax.axis_size("slow")
    fast_count = lax.axis_size("fast")
    seq_length = tokens * slow_count * fast_count
    grid_info = (slow_count, fast_count, tokens, seq_length)
    group_width = channels // groups
    product = (key_act.astype(jnp.float32) * value_act.astype(jnp.float32)).astype(jnp.bfloat16)
    grad_in = (out_grad.astype(jnp.float32) * query_act.astype(jnp.float32)).astype(jnp.bfloat16)
    fast_rank = lax.axis_index("fast")
    slow_rank = lax.axis_index("slow")
    data_pairs = channels // (2 * slow_count)
    local_groups = groups // slow_count
    block_width = channels // slow_count
    spectra = spread_forward(
        merge_blocks((product, long_filter), slow_count),
        grid_info,
        fast_rank,
        ((block_width, True), (local_groups, False)),
    )
    prod_spec = regroup(spectra, data_pairs, local_groups)
    filter_spec = (spectra[0][:, data_pairs:, None], spectra[1][:, data_pairs:, None])
    convolved = spread_inverse(
        flatten_pairs(complex_times(prod_spec, filter_spec)),
        grid_info,
        fast_rank,
        slow_rank,
        (("pairs", data_pairs),),
    )[0]
    grad_spec = regroup(
        spread_forward(grad_in, grid_info, fast_rank, ((block_width, True),)),
        data_pairs,
        local_groups,
    )
    back_spec = flatten_pairs(conj_times(filter_spec, grad_spec))
    corr_spec = conj_times(prod_spec, grad_spec)
    joined = (
        jnp.concatenate((back_spec[0], jnp.sum(corr_spec[0], axis=2)), axis=1),
        jnp.concatenate((back_spec[1], jnp.sum(corr_spec[1], axis=2)), axis=1),
    )
    backward, filter_sum = spread_inverse(
        joined, grid_info, fast_rank, slow_rank, (("pairs", data_pairs), ("real", local_groups))
    )
    scale = 1.0 / math.sqrt(seq_length * group_width)
    mixed_out = (query_act.astype(jnp.float32) * convolved).astype(jnp.bfloat16)
    query_grad = (out_grad.astype(jnp.float32) * convolved).astype(jnp.bfloat16)
    key_grad = (backward * value_act.astype(jnp.float32)).astype(jnp.bfloat16)
    value_grad = (backward * key_act.astype(jnp.float32)).astype(jnp.bfloat16)
    return (mixed_out, query_grad, key_grad, value_grad, filter_sum * scale)


f32 = jnp.float32
bf16 = jnp.bfloat16
EXTRA_ROWS = 2


def dot(left, right):
    return jnp.dot(left, right, preferred_element_type=f32)


def dot_nt(left, right):
    return lax.dot_general(left, right, (((1,), (1,)), ((), ())), preferred_element_type=f32)


def ramp(shape, dim):
    return lax.broadcasted_iota(jnp.int32, shape, dim)


def flip_matrix(size):
    return (ramp((size, size), 0) + ramp((size, size), 1) == size - 1).astype(bf16)


def eye_matrix(size):
    return (ramp((size, size), 0) == ramp((size, size), 1)).astype(bf16)


def skew(eight):
    return pltpu.roll(eight, 0, 1, stride=1, stride_axis=0)


def gate_kernel(query, key, value, filt, grad, sent, queries, keys, values, taps, grads, done):
    copies = [
        pltpu.make_async_copy(source, target, done.at[at])
        for at, (source, target) in enumerate(
            ((key, keys), (value, values), (grad, grads), (query, queries), (filt, taps))
        )
    ]
    for copy in copies:
        copy.start()
    tokens, channels = queries.shape
    groups = taps.shape[0]
    width = channels // groups
    rows = 2 * width + EXTRA_ROWS
    copies[0].wait()
    copies[1].wait()
    product = (keys[...].astype(f32) * values[...].astype(f32)).astype(bf16)
    columns = product.astype(f32).T.astype(bf16)
    for group in range(groups):
        sent[group * rows : group * rows + width, :] = columns[group * width : (group + 1) * width]
    copies[2].wait()
    copies[3].wait()
    grad_in = (grads[...].astype(f32) * queries[...].astype(f32)).astype(bf16)
    columns = dot(flip_matrix(tokens), grad_in).T.astype(bf16)
    for group in range(groups):
        at = group * rows + width
        sent[at : at + width, :] = columns[group * width : (group + 1) * width]
    copies[4].wait()
    for group in range(groups):
        at = group * rows + 2 * width
        sent[at : at + EXTRA_ROWS, :] = jnp.broadcast_to(
            taps[group : group + 1, :], (EXTRA_ROWS, tokens)
        )


def group_kernel(scale, width, got, sent, streams, padded, toeplitz):
    rows, tokens = 2 * width + EXTRA_ROWS, got.shape[1]
    blocks = got.shape[0] // rows
    pairs = blocks // 2
    for pair in range(pairs):
        for half in range(2):
            block = 2 * pair + half
            lanes = slice(half * tokens, (half + 1) * tokens)
            at = 2 * width * pair
            streams[at : at + width, lanes] = got[block * rows : block * rows + width, :]
            streams[at + width : at + 2 * width, lanes] = got[
                (blocks - 1 - block) * rows + width : (blocks - 1 - block) * rows + 2 * width, :
            ]
    for block in range(blocks):
        padded[block * width : (block + 1) * width, :] = got[
            block * rows + width : block * rows + 2 * width, :
        ]
    padded[blocks * width :, :] = jnp.zeros((blocks * width, tokens), bf16)

    row8, lane8 = ramp((8, tokens), 0), ramp((8, tokens), 1)
    before = [jnp.zeros((8, tokens), f32)] * (tokens // 8)
    for block in range(blocks):
        taps = got[block * rows + 2 * width : block * rows + 2 * width + 1, :].astype(f32)
        first = skew(jnp.broadcast_to(taps, (8, tokens)))
        turned = [pltpu.roll(first, at, 1) if at else first for at in range(0, tokens, 8)]
        band = [
            jnp.where(lane8 >= row8 + 8 * at, here, earlier)
            for at, (here, earlier) in enumerate(zip(turned, before))
        ]
        toeplitz[block] = jnp.concatenate(band, axis=0).astype(bf16)
        before = turned

    total = None
    for pair in range(pairs):
        left = jnp.zeros((tokens, tokens), bf16) if pair == 0 else toeplitz[2 * pair - 1]
        weights = jnp.concatenate(
            (
                jnp.concatenate((toeplitz[2 * pair], toeplitz[2 * pair + 1]), axis=1),
                jnp.concatenate((left, toeplitz[2 * pair]), axis=1),
            ),
            axis=0,
        )
        skip = 2 * width * pair
        term = dot(streams[0 : 2 * width * pairs - skip, :], weights)
        total = term if pair == 0 else jnp.concatenate((total[:skip], total[skip:] + term), axis=0)
    for pair in range(pairs):
        for half in range(2):
            block = 2 * pair + half
            lanes = slice(half * tokens, (half + 1) * tokens)
            at = 2 * width * pair
            sent[block * rows : block * rows + width, :] = total[at : at + width, lanes].astype(bf16)
            place = (blocks - 1 - block) * rows + width
            sent[place : place + width, :] = total[
                at + width : at + 2 * width, lanes
            ].astype(bf16)

    ordered = jnp.concatenate(
        [got[block * rows : block * rows + width, :] for block in range(blocks)], axis=0
    )
    ordered = ordered.astype(f32).T.astype(bf16)
    before = [jnp.zeros((8, tokens), f32)] * (tokens // 8)
    skewed = jnp.zeros((8, tokens), f32)
    which = ramp((EXTRA_ROWS, tokens), 0)
    for pair in range(pairs):
        depth = blocks * width if 2 * pair + 2 > blocks // 2 else blocks * width // 2
        columns = [
            padded[pl.ds((blocks - 1 - lag) * width, depth), :] for lag in (2 * pair, 2 * pair + 1)
        ]
        outer = dot(ordered[:, :depth], jnp.concatenate(columns, axis=1))
        for half in range(2):
            block = 2 * pair + half
            square = outer[:, half * tokens : (half + 1) * tokens]
            turned = [
                pltpu.roll(square[at : at + 8], at, 1) if at else square[:8]
                for at in range(0, tokens, 8)
            ]
            folded = sum(
                jnp.where(lane8 >= 8 * at, here, earlier)
                for at, (here, earlier) in enumerate(zip(turned, before))
            )
            before, earlier, skewed = turned, skewed, skew(folded)
            joined = jnp.where(lane8 >= row8, skewed, earlier)
            value = jnp.sum(joined, axis=0, keepdims=True) * scale
            high = value.astype(bf16).astype(f32)
            pieces = jnp.where(which == 0, high, jnp.where(which == 1, value - high, 0.0))
            place = (blocks - 1 - block) * rows + 2 * width
            sent[place : place + EXTRA_ROWS, :] = pieces.astype(bf16)


def output_kernel(
    width, got, query, key, value, grad, mixed, query_grad, key_grad, value_grad, filter_grad
):
    rows, tokens = 2 * width + EXTRA_ROWS, got.shape[1]
    blocks = got.shape[0] // rows

    def collect(first, count):
        return jnp.concatenate(
            [got[at * rows + first : at * rows + first + count, :] for at in range(blocks)], axis=0
        )

    flip = flip_matrix(tokens)
    convolved = dot_nt(eye_matrix(tokens), collect(0, width))
    mixed[...] = (query[...].astype(f32) * convolved).astype(bf16)
    query_grad[...] = (grad[...].astype(f32) * convolved).astype(bf16)
    backward = dot_nt(flip, collect(width, width))
    key_grad[...] = (backward * value[...].astype(f32)).astype(bf16)
    value_grad[...] = (backward * key[...].astype(f32)).astype(bf16)
    high, low = collect(2 * width, 1), collect(2 * width + 1, 1)
    filter_grad[...] = dot(high, flip) + dot(low, flip)


def by_groups(query_act, key_act, value_act, long_filter, out_grad):
    tokens, channels = query_act.shape
    groups = long_filter.shape[1]
    width = channels // groups
    rows = 2 * width + EXTRA_ROWS
    scale = 1.0 / math.sqrt(tokens * groups * width)
    chunks = jax.ShapeDtypeStruct((groups * rows, tokens), bf16)

    def exchange(sent):
        pieces = sent.reshape(groups, rows // 2, 2, tokens)
        pieces = lax.all_to_all(pieces, ("slow", "fast"), split_axis=0, concat_axis=0, tiled=True)
        return pieces.reshape(groups * rows, tokens)

    act = pltpu.VMEM((tokens, channels), bf16)
    sent = pl.pallas_call(
        gate_kernel,
        out_shape=chunks,
        in_specs=[pl.BlockSpec(memory_space=pltpu.HBM)] * 5,
        scratch_shapes=[
            act,
            act,
            act,
            pltpu.VMEM((groups, tokens), bf16),
            act,
            pltpu.SemaphoreType.DMA((5,)),
        ],
        compiler_params=pltpu.CompilerParams(vmem_limit_bytes=8 * 2**20),
        name="gate",
    )(
        *(
            pltpu.with_memory_space_constraint(array, pltpu.HBM)
            for array in (query_act, key_act, value_act, long_filter.T, out_grad)
        )
    )
    got = exchange(sent)
    sent = pl.pallas_call(
        functools.partial(group_kernel, scale, width),
        out_shape=chunks,
        scratch_shapes=[
            pltpu.VMEM((channels, 2 * tokens), bf16),
            pltpu.VMEM((2 * channels, tokens), bf16),
            pltpu.VMEM((groups, tokens, tokens), bf16),
        ],
        compiler_params=pltpu.CompilerParams(vmem_limit_bytes=16 * 2**20),
        name="group",
    )(got)
    got = exchange(sent)
    like = jax.ShapeDtypeStruct((tokens, channels), bf16)
    *acts, filter_grad = pl.pallas_call(
        functools.partial(output_kernel, width),
        out_shape=(like, like, like, like, jax.ShapeDtypeStruct((groups, tokens), f32)),
        compiler_params=pltpu.CompilerParams(vmem_limit_bytes=8 * 2**20),
        name="outputs",
    )(got, query_act, key_act, value_act, out_grad)
    return (*acts, filter_grad.T)


def on_device(query_act, key_act, value_act, long_filter, out_grad):
    tokens, channels = query_act.shape
    groups = long_filter.shape[1]
    devices = lax.axis_size("slow") * lax.axis_size("fast")
    if devices == groups and tokens == 128 and channels == 16 * groups and groups % 4 == 0:
        return by_groups(query_act, key_act, value_act, long_filter, out_grad)
    return by_spectra(query_act, key_act, value_act, long_filter, out_grad)


def solution(mesh):
    placed = (
        P(("slow", "fast"), None),
        P(("slow", "fast"), None),
        P(("slow", "fast"), None),
        P(("slow", "fast"), None),
        P(("slow", "fast"), None),
    )
    return jax.shard_map(
        on_device,
        mesh=mesh,
        in_specs=placed,
        out_specs=(
            P(("slow", "fast"), None),
            P(("slow", "fast"), None),
            P(("slow", "fast"), None),
            P(("slow", "fast"), None),
            P(("slow", "fast"), None),
        ),
        check_vma=False,
    )
```

```python
import functools
import math

import jax
import jax.numpy as jnp
from jax import lax
from jax.experimental import pallas as pl
from jax.experimental.pallas import tpu as pltpu
from jax.sharding import PartitionSpec as P

highest = lax.Precision.HIGHEST


def index_ramp(points, along, ndim, offset):
    shape_list = [1] * ndim
    shape_list[along] = points
    return (jnp.arange(points, dtype=jnp.int32) + offset).reshape(shape_list)


def apply_dft(re_im, points, direction, along):
    index_row = jnp.arange(points, dtype=jnp.int32)
    phase_turns = index_row[:, None] * index_row[None, :] % points
    phases = 2.0 * math.pi / points * phase_turns.astype(jnp.float32)
    cosine = jnp.cos(phases)
    sine_part = direction * jnp.sin(phases)

    def contract(values, matrix):
        result = jnp.tensordot(values, matrix, axes=((along,), (1,)), precision=highest)
        return jnp.moveaxis(result, -1, along)

    return (
        contract(re_im[0], cosine) - contract(re_im[1], sine_part),
        contract(re_im[0], sine_part) + contract(re_im[1], cosine),
    )


def rotate(re_im, phase_turns, period, direction):
    phases = 2.0 * math.pi / period * (phase_turns % period).astype(jnp.float32)
    cosine = jnp.cos(phases)
    sine_part = direction * jnp.sin(phases)
    return (re_im[0] * cosine - re_im[1] * sine_part, re_im[0] * sine_part + re_im[1] * cosine)


def complex_times(left, right):
    return (left[0] * right[0] - left[1] * right[1], left[0] * right[1] + left[1] * right[0])


def conj_times(left, right):
    return (left[0] * right[0] + left[1] * right[1], left[0] * right[1] - left[1] * right[0])


def positions(grid_info, slow_points, slow_offset, fast_points, fast_offset):
    fast_count, tokens = (grid_info[1], grid_info[2])
    block_index = index_ramp(slow_points, 2, 5, slow_offset) * fast_count + index_ramp(
        fast_points, 3, 5, fast_offset
    )
    return block_index * tokens + index_ramp(tokens, 4, 5, 0)


def open_halves(re_im, grid_info, fast_offset):
    token_place = positions(grid_info, re_im[0].shape[1], 0, re_im[0].shape[2], fast_offset)
    return rotate(
        (re_im[0][None], re_im[1][None]),
        index_ramp(2, 0, 5, 0) * token_place,
        2 * grid_info[3],
        -1.0,
    )


def fold_halves(re_im, token_place, seq_length):
    turned = rotate(re_im, index_ramp(2, 0, 5, 0) * token_place, 2 * seq_length, 1.0)
    scale = 0.5 / seq_length
    return (jnp.sum(turned[0], axis=0) * scale, jnp.sum(turned[1], axis=0) * scale)


def front_forward(re_im, grid_info, fast_offset):
    slow_count, fast_count = (grid_info[0], grid_info[1])
    re_im = apply_dft(re_im, slow_count, -1.0, 2)
    phase_turns = index_ramp(slow_count, 2, 5, 0) * index_ramp(re_im[0].shape[3], 3, 5, fast_offset)
    return rotate(re_im, phase_turns, slow_count * fast_count, -1.0)


def front_inverse(re_im, grid_info, fast_offset):
    slow_count, fast_count = (grid_info[0], grid_info[1])
    phase_turns = index_ramp(slow_count, 2, 5, 0) * index_ramp(re_im[0].shape[3], 3, 5, fast_offset)
    re_im = rotate(re_im, phase_turns, slow_count * fast_count, 1.0)
    return apply_dft(re_im, slow_count, 1.0, 2)


def lead_phase(re_im, grid_info, ka_offset):
    slow_count, fast_count, tokens = (grid_info[0], grid_info[1], grid_info[2])
    lead_index = index_ramp(re_im[0].shape[2], 2, 5, ka_offset) + slow_count * index_ramp(
        fast_count, 3, 5, 0
    )
    return lead_index * index_ramp(tokens, 4, 5, 0)


def back_forward(re_im, grid_info, ka_offset):
    re_im = apply_dft(re_im, grid_info[1], -1.0, 3)
    re_im = rotate(re_im, lead_phase(re_im, grid_info, ka_offset), grid_info[3], -1.0)
    return apply_dft(re_im, grid_info[2], -1.0, 4)


def back_inverse(re_im, grid_info, ka_offset):
    re_im = apply_dft(re_im, grid_info[2], 1.0, 4)
    re_im = rotate(re_im, lead_phase(re_im, grid_info, ka_offset), grid_info[3], 1.0)
    return apply_dft(re_im, grid_info[1], 1.0, 3)


def to_channels(seq_rows):
    return lax.all_to_all(
        seq_rows.reshape(1, seq_rows.shape[0], seq_rows.shape[1]),
        "slow",
        split_axis=2,
        concat_axis=0,
        tiled=True,
    )


def merge_blocks(arrays, block_count):
    tokens = arrays[0].shape[0]
    pieces = [item.reshape(tokens, block_count, item.shape[1] // block_count) for item in arrays]
    return jnp.concatenate(pieces, axis=2).reshape(tokens, -1)


def split_columns(rows_major, widths):
    tokens, block_count = (rows_major.shape[0], rows_major.shape[1])
    result = []
    offset = 0
    for length in widths:
        result.append(
            rows_major[:, :, offset : offset + length].reshape(tokens, block_count * length)
        )
        offset += length
    return result


def real_blocks(real_part, imag_part, segments):
    pieces = []
    offset = 0
    for output_kind, length in segments:
        real_seg = real_part[:, offset : offset + length]
        imag_seg = imag_part[:, offset : offset + length]
        offset += length
        if output_kind == "pairs":
            stacked = jnp.transpose(jnp.stack((real_seg, imag_seg), axis=-1), (0, 2, 1, 3))
            pieces.append(stacked.reshape(stacked.shape[0], stacked.shape[1], 2 * length))
        else:
            pieces.append(jnp.transpose(real_seg, (0, 2, 1)))
    return jnp.concatenate(pieces, axis=2)


def segment_widths(segments):
    return [2 * length if output_kind == "pairs" else length for output_kind, length in segments]


def spread_forward(seq_rows, grid_info, fast_rank, segments):
    slow_count, fast_count = (grid_info[0], grid_info[1])
    blocks = to_channels(seq_rows).astype(jnp.float32)
    real_list = []
    imag_list = []
    offset = 0
    for length, packed in segments:
        segment = blocks[:, :, offset : offset + length]
        offset += length
        if packed:
            halves = segment.reshape(segment.shape[0], segment.shape[1], length // 2, 2)
            real_seg, imag_seg = (halves[..., 0], halves[..., 1])
        else:
            real_seg, imag_seg = (segment, jnp.zeros_like(segment))
        real_list.append(jnp.transpose(real_seg, (2, 0, 1)))
        imag_list.append(jnp.transpose(imag_seg, (2, 0, 1)))
    re_im = (
        jnp.concatenate(real_list, 0)[:, :, None, :],
        jnp.concatenate(imag_list, 0)[:, :, None, :],
    )
    re_im = front_forward(open_halves(re_im, grid_info, fast_rank), grid_info, fast_rank)
    re_im = (
        lax.all_to_all(re_im[0], "fast", split_axis=2, concat_axis=3, tiled=True),
        lax.all_to_all(re_im[1], "fast", split_axis=2, concat_axis=3, tiled=True),
    )
    return back_forward(re_im, grid_info, fast_rank * (slow_count // fast_count))


def spread_inverse(re_im, grid_info, fast_rank, slow_rank, segments):
    slow_count, fast_count, tokens, seq_length = grid_info
    re_im = back_inverse(re_im, grid_info, fast_rank * (slow_count // fast_count))
    re_im = (
        lax.all_to_all(re_im[0], "fast", split_axis=3, concat_axis=2, tiled=True),
        lax.all_to_all(re_im[1], "fast", split_axis=3, concat_axis=2, tiled=True),
    )
    re_im = front_inverse(re_im, grid_info, fast_rank)
    re_im = (
        lax.all_to_all(re_im[0], "slow", split_axis=2, concat_axis=1, tiled=True),
        lax.all_to_all(re_im[1], "slow", split_axis=2, concat_axis=1, tiled=True),
    )
    real_part, imag_part = fold_halves(
        re_im, positions(grid_info, 1, slow_rank, 1, fast_rank), seq_length
    )
    length = real_part.shape[0] // slow_count
    blocks = real_blocks(
        real_part.reshape(slow_count, length, tokens),
        imag_part.reshape(slow_count, length, tokens),
        segments,
    )
    rows_major = jnp.transpose(blocks, (1, 0, 2))
    return split_columns(rows_major, segment_widths(segments))


def regroup(re_im, length, local_groups):

    def by_group(values):
        values = values[:, :length]
        return values.reshape(
            (values.shape[0], local_groups, length // local_groups) + values.shape[2:]
        )

    return (by_group(re_im[0]), by_group(re_im[1]))


def flatten_pairs(re_im):

    def merged(values):
        return values.reshape(
            (values.shape[0], values.shape[1] * values.shape[2]) + values.shape[3:]
        )

    return (merged(re_im[0]), merged(re_im[1]))


def by_spectra(query_act, key_act, value_act, long_filter, out_grad):
    tokens, channels = query_act.shape
    groups = long_filter.shape[1]
    slow_count = lax.axis_size("slow")
    fast_count = lax.axis_size("fast")
    seq_length = tokens * slow_count * fast_count
    grid_info = (slow_count, fast_count, tokens, seq_length)
    group_width = channels // groups
    product = (key_act.astype(jnp.float32) * value_act.astype(jnp.float32)).astype(jnp.bfloat16)
    grad_in = (out_grad.astype(jnp.float32) * query_act.astype(jnp.float32)).astype(jnp.bfloat16)
    fast_rank = lax.axis_index("fast")
    slow_rank = lax.axis_index("slow")
    data_pairs = channels // (2 * slow_count)
    local_groups = groups // slow_count
    block_width = channels // slow_count
    spectra = spread_forward(
        merge_blocks((product, long_filter), slow_count),
        grid_info,
        fast_rank,
        ((block_width, True), (local_groups, False)),
    )
    prod_spec = regroup(spectra, data_pairs, local_groups)
    filter_spec = (spectra[0][:, data_pairs:, None], spectra[1][:, data_pairs:, None])
    convolved = spread_inverse(
        flatten_pairs(complex_times(prod_spec, filter_spec)),
        grid_info,
        fast_rank,
        slow_rank,
        (("pairs", data_pairs),),
    )[0]
    grad_spec = regroup(
        spread_forward(grad_in, grid_info, fast_rank, ((block_width, True),)),
        data_pairs,
        local_groups,
    )
    back_spec = flatten_pairs(conj_times(filter_spec, grad_spec))
    corr_spec = conj_times(prod_spec, grad_spec)
    joined = (
        jnp.concatenate((back_spec[0], jnp.sum(corr_spec[0], axis=2)), axis=1),
        jnp.concatenate((back_spec[1], jnp.sum(corr_spec[1], axis=2)), axis=1),
    )
    backward, filter_sum = spread_inverse(
        joined, grid_info, fast_rank, slow_rank, (("pairs", data_pairs), ("real", local_groups))
    )
    scale = 1.0 / math.sqrt(seq_length * group_width)
    mixed_out = (query_act.astype(jnp.float32) * convolved).astype(jnp.bfloat16)
    query_grad = (out_grad.astype(jnp.float32) * convolved).astype(jnp.bfloat16)
    key_grad = (backward * value_act.astype(jnp.float32)).astype(jnp.bfloat16)
    value_grad = (backward * key_act.astype(jnp.float32)).astype(jnp.bfloat16)
    return (mixed_out, query_grad, key_grad, value_grad, filter_sum * scale)


f32 = jnp.float32
bf16 = jnp.bfloat16
EXTRA_ROWS = 2


def dot(left, right):
    return jnp.dot(left, right, preferred_element_type=f32)


def dot_nt(left, right):
    return lax.dot_general(left, right, (((1,), (1,)), ((), ())), preferred_element_type=f32)


def ramp(shape, dim):
    return lax.broadcasted_iota(jnp.int32, shape, dim)


def flip_matrix(size):
    return (ramp((size, size), 0) + ramp((size, size), 1) == size - 1).astype(bf16)


def eye_matrix(size):
    return (ramp((size, size), 0) == ramp((size, size), 1)).astype(bf16)


def gate_kernel(query, key, value, filt, grad, sent, queries, keys, values, taps, grads, done):
    copies = [
        pltpu.make_async_copy(source, target, done.at[at])
        for at, (source, target) in enumerate(
            ((key, keys), (value, values), (grad, grads), (query, queries), (filt, taps))
        )
    ]
    for copy in copies:
        copy.start()
    tokens, channels = queries.shape
    groups = taps.shape[0]
    width = channels // groups
    rows = 2 * width + EXTRA_ROWS
    copies[0].wait()
    copies[1].wait()
    product = (keys[...].astype(f32) * values[...].astype(f32)).astype(bf16)
    columns = product.astype(f32).T.astype(bf16)
    for group in range(groups):
        sent[group * rows : group * rows + width, :] = columns[group * width : (group + 1) * width]
    copies[2].wait()
    copies[3].wait()
    grad_in = (grads[...].astype(f32) * queries[...].astype(f32)).astype(bf16)
    columns = dot(flip_matrix(tokens), grad_in).T.astype(bf16)
    for group in range(groups):
        at = group * rows + width
        sent[at : at + width, :] = columns[group * width : (group + 1) * width]
    copies[4].wait()
    for group in range(groups):
        at = group * rows + 2 * width
        sent[at : at + EXTRA_ROWS, :] = jnp.broadcast_to(
            taps[group : group + 1, :], (EXTRA_ROWS, tokens)
        )


def group_kernel(scale, width, got, sent, streams, padded, toeplitz):
    rows, tokens = 2 * width + EXTRA_ROWS, got.shape[1]
    blocks = got.shape[0] // rows
    pairs = blocks // 2
    row, lane = ramp((tokens, tokens), 0), ramp((tokens, tokens), 1)
    for pair in range(pairs):
        for half in range(2):
            block = 2 * pair + half
            lanes = slice(half * tokens, (half + 1) * tokens)
            at = 2 * width * pair
            streams[at : at + width, lanes] = got[block * rows : block * rows + width, :]
            streams[at + width : at + 2 * width, lanes] = got[
                (blocks - 1 - block) * rows + width : (blocks - 1 - block) * rows + 2 * width, :
            ]
    for block in range(blocks):
        lanes = slice((1 - block % 2) * tokens, (2 - block % 2) * tokens)
        padded[block // 2 * width : (block // 2 + 1) * width, lanes] = got[
            block * rows + width : block * rows + 2 * width, :
        ]
    padded[pairs * width :, :] = jnp.zeros((pairs * width, 2 * tokens), bf16)

    before = jnp.zeros((tokens, tokens), f32)
    for block in range(blocks):
        taps = jnp.broadcast_to(got[block * rows + 2 * width : block * rows + 2 * width + 1, :].astype(f32), (tokens, tokens))
        turned = pltpu.roll(taps, 0, 1, stride=1, stride_axis=0)
        toeplitz[block] = jnp.where(lane >= row, turned, before).astype(bf16)
        before = turned

    total = None
    for pair in range(pairs):
        left = jnp.zeros((tokens, tokens), bf16) if pair == 0 else toeplitz[2 * pair - 1]
        weights = jnp.concatenate(
            (
                jnp.concatenate((toeplitz[2 * pair], toeplitz[2 * pair + 1]), axis=1),
                jnp.concatenate((left, toeplitz[2 * pair]), axis=1),
            ),
            axis=0,
        )
        skip = 2 * width * pair
        term = dot(streams[0 : 2 * width * pairs - skip, :], weights)
        total = term if pair == 0 else jnp.concatenate((total[:skip], total[skip:] + term), axis=0)
    for pair in range(pairs):
        for half in range(2):
            block = 2 * pair + half
            lanes = slice(half * tokens, (half + 1) * tokens)
            at = 2 * width * pair
            sent[block * rows : block * rows + width, :] = total[at : at + width, lanes].astype(bf16)
            place = (blocks - 1 - block) * rows + width
            sent[place : place + width, :] = total[
                at + width : at + 2 * width, lanes
            ].astype(bf16)

    ordered = jnp.concatenate(
        [
            jnp.concatenate(
                [got[block * rows : block * rows + width, :] for block in range(half, blocks, 2)], axis=0
            ).astype(f32).T
            for half in range(2)
        ],
        axis=0,
    ).astype(bf16)
    before = jnp.zeros((tokens, tokens), f32)
    spill = jnp.zeros((tokens, tokens), f32)
    which = ramp((EXTRA_ROWS, tokens), 0)
    for pair in range(pairs):
        outer = dot(ordered, padded[pl.ds((pairs - 1 - pair) * width, pairs * width), :])
        squares = (
            outer[:tokens, :tokens] + spill,
            outer[:tokens, tokens:] + outer[tokens:, :tokens],
        )
        spill = outer[tokens:, tokens:]
        for half in range(2):
            block = 2 * pair + half
            turned = pltpu.roll(squares[half], 0, 1, stride=1, stride_axis=0)
            joined = jnp.where(lane >= row, turned, before)
            before = turned
            value = jnp.sum(joined, axis=0, keepdims=True) * scale
            high = value.astype(bf16).astype(f32)
            pieces = jnp.where(which == 0, high, value - high)
            place = (blocks - 1 - block) * rows + 2 * width
            sent[place : place + EXTRA_ROWS, :] = pieces.astype(bf16)


def output_kernel(
    width, got, query, key, value, grad, mixed, query_grad, key_grad, value_grad, filter_grad
):
    rows, tokens = 2 * width + EXTRA_ROWS, got.shape[1]
    blocks = got.shape[0] // rows

    def collect(first, count):
        return jnp.concatenate(
            [got[at * rows + first : at * rows + first + count, :] for at in range(blocks)], axis=0
        )

    flip = flip_matrix(tokens)
    convolved = dot_nt(eye_matrix(tokens), collect(0, width))
    mixed[...] = (query[...].astype(f32) * convolved).astype(bf16)
    query_grad[...] = (grad[...].astype(f32) * convolved).astype(bf16)
    backward = dot_nt(flip, collect(width, width))
    key_grad[...] = (backward * value[...].astype(f32)).astype(bf16)
    value_grad[...] = (backward * key[...].astype(f32)).astype(bf16)
    high, low = collect(2 * width, 1), collect(2 * width + 1, 1)
    filter_grad[...] = dot(high, flip) + dot(low, flip)


def by_groups(query_act, key_act, value_act, long_filter, out_grad):
    tokens, channels = query_act.shape
    groups = long_filter.shape[1]
    width = channels // groups
    rows = 2 * width + EXTRA_ROWS
    scale = 1.0 / math.sqrt(tokens * groups * width)
    chunks = jax.ShapeDtypeStruct((groups * rows, tokens), bf16)

    def exchange(sent):
        pieces = sent.reshape(groups, rows // 2, 2, tokens)
        pieces = lax.all_to_all(pieces, ("slow", "fast"), split_axis=0, concat_axis=0, tiled=True)
        return pieces.reshape(groups * rows, tokens)

    act = pltpu.VMEM((tokens, channels), bf16)
    sent = pl.pallas_call(
        gate_kernel,
        out_shape=chunks,
        in_specs=[pl.BlockSpec(memory_space=pltpu.HBM)] * 5,
        scratch_shapes=[
            act,
            act,
            act,
            pltpu.VMEM((groups, tokens), bf16),
            act,
            pltpu.SemaphoreType.DMA((5,)),
        ],
        compiler_params=pltpu.CompilerParams(vmem_limit_bytes=8 * 2**20),
        name="gate",
    )(
        *(
            pltpu.with_memory_space_constraint(array, pltpu.HBM)
            for array in (query_act, key_act, value_act, long_filter.T, out_grad)
        )
    )
    got = exchange(sent)
    sent = pl.pallas_call(
        functools.partial(group_kernel, scale, width),
        out_shape=chunks,
        scratch_shapes=[
            pltpu.VMEM((channels, 2 * tokens), bf16),
            pltpu.VMEM((channels, 2 * tokens), bf16),
            pltpu.VMEM((groups, tokens, tokens), bf16),
        ],
        compiler_params=pltpu.CompilerParams(vmem_limit_bytes=16 * 2**20),
        name="group",
    )(got)
    got = exchange(sent)
    like = jax.ShapeDtypeStruct((tokens, channels), bf16)
    *acts, filter_grad = pl.pallas_call(
        functools.partial(output_kernel, width),
        out_shape=(like, like, like, like, jax.ShapeDtypeStruct((groups, tokens), f32)),
        compiler_params=pltpu.CompilerParams(vmem_limit_bytes=8 * 2**20),
        name="outputs",
    )(got, query_act, key_act, value_act, out_grad)
    return (*acts, filter_grad.T)


def on_device(query_act, key_act, value_act, long_filter, out_grad):
    tokens, channels = query_act.shape
    groups = long_filter.shape[1]
    devices = lax.axis_size("slow") * lax.axis_size("fast")
    if devices == groups and tokens == 128 and channels == 16 * groups and groups % 4 == 0:
        return by_groups(query_act, key_act, value_act, long_filter, out_grad)
    return by_spectra(query_act, key_act, value_act, long_filter, out_grad)


def solution(mesh):
    placed = (
        P(("slow", "fast"), None),
        P(("slow", "fast"), None),
        P(("slow", "fast"), None),
        P(("slow", "fast"), None),
        P(("slow", "fast"), None),
    )
    return jax.shard_map(
        on_device,
        mesh=mesh,
        in_specs=placed,
        out_specs=(
            P(("slow", "fast"), None),
            P(("slow", "fast"), None),
            P(("slow", "fast"), None),
            P(("slow", "fast"), None),
            P(("slow", "fast"), None),
        ),
        check_vma=False,
    )
```

```python
import functools
import math

import jax
import jax.numpy as jnp
from jax import lax
from jax.experimental import pallas as pl
from jax.experimental.pallas import tpu as pltpu
from jax.sharding import PartitionSpec as P

highest = lax.Precision.HIGHEST


def index_ramp(points, along, ndim, offset):
    shape_list = [1] * ndim
    shape_list[along] = points
    return (jnp.arange(points, dtype=jnp.int32) + offset).reshape(shape_list)


def apply_dft(re_im, points, direction, along):
    index_row = jnp.arange(points, dtype=jnp.int32)
    phase_turns = index_row[:, None] * index_row[None, :] % points
    phases = 2.0 * math.pi / points * phase_turns.astype(jnp.float32)
    cosine = jnp.cos(phases)
    sine_part = direction * jnp.sin(phases)

    def contract(values, matrix):
        result = jnp.tensordot(values, matrix, axes=((along,), (1,)), precision=highest)
        return jnp.moveaxis(result, -1, along)

    return (
        contract(re_im[0], cosine) - contract(re_im[1], sine_part),
        contract(re_im[0], sine_part) + contract(re_im[1], cosine),
    )


def rotate(re_im, phase_turns, period, direction):
    phases = 2.0 * math.pi / period * (phase_turns % period).astype(jnp.float32)
    cosine = jnp.cos(phases)
    sine_part = direction * jnp.sin(phases)
    return (re_im[0] * cosine - re_im[1] * sine_part, re_im[0] * sine_part + re_im[1] * cosine)


def complex_times(left, right):
    return (left[0] * right[0] - left[1] * right[1], left[0] * right[1] + left[1] * right[0])


def conj_times(left, right):
    return (left[0] * right[0] + left[1] * right[1], left[0] * right[1] - left[1] * right[0])


def positions(grid_info, slow_points, slow_offset, fast_points, fast_offset):
    fast_count, tokens = (grid_info[1], grid_info[2])
    block_index = index_ramp(slow_points, 2, 5, slow_offset) * fast_count + index_ramp(
        fast_points, 3, 5, fast_offset
    )
    return block_index * tokens + index_ramp(tokens, 4, 5, 0)


def open_halves(re_im, grid_info, fast_offset):
    token_place = positions(grid_info, re_im[0].shape[1], 0, re_im[0].shape[2], fast_offset)
    return rotate(
        (re_im[0][None], re_im[1][None]),
        index_ramp(2, 0, 5, 0) * token_place,
        2 * grid_info[3],
        -1.0,
    )


def fold_halves(re_im, token_place, seq_length):
    turned = rotate(re_im, index_ramp(2, 0, 5, 0) * token_place, 2 * seq_length, 1.0)
    scale = 0.5 / seq_length
    return (jnp.sum(turned[0], axis=0) * scale, jnp.sum(turned[1], axis=0) * scale)


def front_forward(re_im, grid_info, fast_offset):
    slow_count, fast_count = (grid_info[0], grid_info[1])
    re_im = apply_dft(re_im, slow_count, -1.0, 2)
    phase_turns = index_ramp(slow_count, 2, 5, 0) * index_ramp(re_im[0].shape[3], 3, 5, fast_offset)
    return rotate(re_im, phase_turns, slow_count * fast_count, -1.0)


def front_inverse(re_im, grid_info, fast_offset):
    slow_count, fast_count = (grid_info[0], grid_info[1])
    phase_turns = index_ramp(slow_count, 2, 5, 0) * index_ramp(re_im[0].shape[3], 3, 5, fast_offset)
    re_im = rotate(re_im, phase_turns, slow_count * fast_count, 1.0)
    return apply_dft(re_im, slow_count, 1.0, 2)


def lead_phase(re_im, grid_info, ka_offset):
    slow_count, fast_count, tokens = (grid_info[0], grid_info[1], grid_info[2])
    lead_index = index_ramp(re_im[0].shape[2], 2, 5, ka_offset) + slow_count * index_ramp(
        fast_count, 3, 5, 0
    )
    return lead_index * index_ramp(tokens, 4, 5, 0)


def back_forward(re_im, grid_info, ka_offset):
    re_im = apply_dft(re_im, grid_info[1], -1.0, 3)
    re_im = rotate(re_im, lead_phase(re_im, grid_info, ka_offset), grid_info[3], -1.0)
    return apply_dft(re_im, grid_info[2], -1.0, 4)


def back_inverse(re_im, grid_info, ka_offset):
    re_im = apply_dft(re_im, grid_info[2], 1.0, 4)
    re_im = rotate(re_im, lead_phase(re_im, grid_info, ka_offset), grid_info[3], 1.0)
    return apply_dft(re_im, grid_info[1], 1.0, 3)


def to_channels(seq_rows):
    return lax.all_to_all(
        seq_rows.reshape(1, seq_rows.shape[0], seq_rows.shape[1]),
        "slow",
        split_axis=2,
        concat_axis=0,
        tiled=True,
    )


def merge_blocks(arrays, block_count):
    tokens = arrays[0].shape[0]
    pieces = [item.reshape(tokens, block_count, item.shape[1] // block_count) for item in arrays]
    return jnp.concatenate(pieces, axis=2).reshape(tokens, -1)


def split_columns(rows_major, widths):
    tokens, block_count = (rows_major.shape[0], rows_major.shape[1])
    result = []
    offset = 0
    for length in widths:
        result.append(
            rows_major[:, :, offset : offset + length].reshape(tokens, block_count * length)
        )
        offset += length
    return result


def real_blocks(real_part, imag_part, segments):
    pieces = []
    offset = 0
    for output_kind, length in segments:
        real_seg = real_part[:, offset : offset + length]
        imag_seg = imag_part[:, offset : offset + length]
        offset += length
        if output_kind == "pairs":
            stacked = jnp.transpose(jnp.stack((real_seg, imag_seg), axis=-1), (0, 2, 1, 3))
            pieces.append(stacked.reshape(stacked.shape[0], stacked.shape[1], 2 * length))
        else:
            pieces.append(jnp.transpose(real_seg, (0, 2, 1)))
    return jnp.concatenate(pieces, axis=2)


def segment_widths(segments):
    return [2 * length if output_kind == "pairs" else length for output_kind, length in segments]


def spread_forward(seq_rows, grid_info, fast_rank, segments):
    slow_count, fast_count = (grid_info[0], grid_info[1])
    blocks = to_channels(seq_rows).astype(jnp.float32)
    real_list = []
    imag_list = []
    offset = 0
    for length, packed in segments:
        segment = blocks[:, :, offset : offset + length]
        offset += length
        if packed:
            halves = segment.reshape(segment.shape[0], segment.shape[1], length // 2, 2)
            real_seg, imag_seg = (halves[..., 0], halves[..., 1])
        else:
            real_seg, imag_seg = (segment, jnp.zeros_like(segment))
        real_list.append(jnp.transpose(real_seg, (2, 0, 1)))
        imag_list.append(jnp.transpose(imag_seg, (2, 0, 1)))
    re_im = (
        jnp.concatenate(real_list, 0)[:, :, None, :],
        jnp.concatenate(imag_list, 0)[:, :, None, :],
    )
    re_im = front_forward(open_halves(re_im, grid_info, fast_rank), grid_info, fast_rank)
    re_im = (
        lax.all_to_all(re_im[0], "fast", split_axis=2, concat_axis=3, tiled=True),
        lax.all_to_all(re_im[1], "fast", split_axis=2, concat_axis=3, tiled=True),
    )
    return back_forward(re_im, grid_info, fast_rank * (slow_count // fast_count))


def spread_inverse(re_im, grid_info, fast_rank, slow_rank, segments):
    slow_count, fast_count, tokens, seq_length = grid_info
    re_im = back_inverse(re_im, grid_info, fast_rank * (slow_count // fast_count))
    re_im = (
        lax.all_to_all(re_im[0], "fast", split_axis=3, concat_axis=2, tiled=True),
        lax.all_to_all(re_im[1], "fast", split_axis=3, concat_axis=2, tiled=True),
    )
    re_im = front_inverse(re_im, grid_info, fast_rank)
    re_im = (
        lax.all_to_all(re_im[0], "slow", split_axis=2, concat_axis=1, tiled=True),
        lax.all_to_all(re_im[1], "slow", split_axis=2, concat_axis=1, tiled=True),
    )
    real_part, imag_part = fold_halves(
        re_im, positions(grid_info, 1, slow_rank, 1, fast_rank), seq_length
    )
    length = real_part.shape[0] // slow_count
    blocks = real_blocks(
        real_part.reshape(slow_count, length, tokens),
        imag_part.reshape(slow_count, length, tokens),
        segments,
    )
    rows_major = jnp.transpose(blocks, (1, 0, 2))
    return split_columns(rows_major, segment_widths(segments))


def regroup(re_im, length, local_groups):

    def by_group(values):
        values = values[:, :length]
        return values.reshape(
            (values.shape[0], local_groups, length // local_groups) + values.shape[2:]
        )

    return (by_group(re_im[0]), by_group(re_im[1]))


def flatten_pairs(re_im):

    def merged(values):
        return values.reshape(
            (values.shape[0], values.shape[1] * values.shape[2]) + values.shape[3:]
        )

    return (merged(re_im[0]), merged(re_im[1]))


def by_spectra(query_act, key_act, value_act, long_filter, out_grad):
    tokens, channels = query_act.shape
    groups = long_filter.shape[1]
    slow_count = lax.axis_size("slow")
    fast_count = lax.axis_size("fast")
    seq_length = tokens * slow_count * fast_count
    grid_info = (slow_count, fast_count, tokens, seq_length)
    group_width = channels // groups
    product = (key_act.astype(jnp.float32) * value_act.astype(jnp.float32)).astype(jnp.bfloat16)
    grad_in = (out_grad.astype(jnp.float32) * query_act.astype(jnp.float32)).astype(jnp.bfloat16)
    fast_rank = lax.axis_index("fast")
    slow_rank = lax.axis_index("slow")
    data_pairs = channels // (2 * slow_count)
    local_groups = groups // slow_count
    block_width = channels // slow_count
    spectra = spread_forward(
        merge_blocks((product, long_filter), slow_count),
        grid_info,
        fast_rank,
        ((block_width, True), (local_groups, False)),
    )
    prod_spec = regroup(spectra, data_pairs, local_groups)
    filter_spec = (spectra[0][:, data_pairs:, None], spectra[1][:, data_pairs:, None])
    convolved = spread_inverse(
        flatten_pairs(complex_times(prod_spec, filter_spec)),
        grid_info,
        fast_rank,
        slow_rank,
        (("pairs", data_pairs),),
    )[0]
    grad_spec = regroup(
        spread_forward(grad_in, grid_info, fast_rank, ((block_width, True),)),
        data_pairs,
        local_groups,
    )
    back_spec = flatten_pairs(conj_times(filter_spec, grad_spec))
    corr_spec = conj_times(prod_spec, grad_spec)
    joined = (
        jnp.concatenate((back_spec[0], jnp.sum(corr_spec[0], axis=2)), axis=1),
        jnp.concatenate((back_spec[1], jnp.sum(corr_spec[1], axis=2)), axis=1),
    )
    backward, filter_sum = spread_inverse(
        joined, grid_info, fast_rank, slow_rank, (("pairs", data_pairs), ("real", local_groups))
    )
    scale = 1.0 / math.sqrt(seq_length * group_width)
    mixed_out = (query_act.astype(jnp.float32) * convolved).astype(jnp.bfloat16)
    query_grad = (out_grad.astype(jnp.float32) * convolved).astype(jnp.bfloat16)
    key_grad = (backward * value_act.astype(jnp.float32)).astype(jnp.bfloat16)
    value_grad = (backward * key_act.astype(jnp.float32)).astype(jnp.bfloat16)
    return (mixed_out, query_grad, key_grad, value_grad, filter_sum * scale)


f32 = jnp.float32
bf16 = jnp.bfloat16
EXTRA_ROWS = 2


def dot(left, right):
    return jnp.dot(left, right, preferred_element_type=f32)


def dot_nt(left, right):
    return lax.dot_general(left, right, (((1,), (1,)), ((), ())), preferred_element_type=f32)


def ramp(shape, dim):
    return lax.broadcasted_iota(jnp.int32, shape, dim)


def flip_matrix(size):
    return (ramp((size, size), 0) + ramp((size, size), 1) == size - 1).astype(bf16)


def eye_matrix(size):
    return (ramp((size, size), 0) == ramp((size, size), 1)).astype(bf16)


def gate_kernel(query, key, value, filt, grad, sent, queries, keys, values, taps, grads, done):
    copies = [
        pltpu.make_async_copy(source, target, done.at[at])
        for at, (source, target) in enumerate(
            ((grad, grads), (query, queries), (key, keys), (value, values), (filt, taps))
        )
    ]
    for copy in copies:
        copy.start()
    tokens, channels = queries.shape
    groups = taps.shape[0]
    width = channels // groups
    rows = 2 * width + EXTRA_ROWS
    for copy in copies:
        copy.wait()
    grad_in = (grads[...].astype(f32) * queries[...].astype(f32)).astype(bf16)
    flipped = dot(flip_matrix(tokens), grad_in)
    product = (keys[...].astype(f32) * values[...].astype(f32)).astype(bf16)
    columns = product.astype(f32).T.astype(bf16)
    flipped = flipped.T.astype(bf16)
    for group in range(groups):
        at = group * rows
        part = slice(group * width, (group + 1) * width)
        sent[at : at + width, :] = columns[part]
        sent[at + width : at + 2 * width, :] = flipped[part]
        sent[at + 2 * width : at + rows, :] = jnp.broadcast_to(
            taps[group : group + 1, :], (EXTRA_ROWS, tokens)
        )


def group_kernel(scale, width, got, sent, streams, padded, toeplitz):
    rows, tokens = 2 * width + EXTRA_ROWS, got.shape[1]
    blocks = got.shape[0] // rows
    pairs = blocks // 2
    row, lane = ramp((tokens, tokens), 0), ramp((tokens, tokens), 1)
    for pair in range(pairs):
        for half in range(2):
            block = 2 * pair + half
            lanes = slice(half * tokens, (half + 1) * tokens)
            at = 2 * width * pair
            streams[at : at + width, lanes] = got[block * rows : block * rows + width, :]
            streams[at + width : at + 2 * width, lanes] = got[
                (blocks - 1 - block) * rows + width : (blocks - 1 - block) * rows + 2 * width, :
            ]
    for block in range(blocks):
        padded[block * width : (block + 1) * width, :] = got[
            block * rows + width : block * rows + 2 * width, :
        ]
    padded[blocks * width :, :] = jnp.zeros((blocks * width, tokens), bf16)

    before = jnp.zeros((tokens, tokens), f32)
    for block in range(blocks):
        taps = jnp.broadcast_to(got[block * rows + 2 * width : block * rows + 2 * width + 1, :].astype(f32), (tokens, tokens))
        turned = pltpu.roll(taps, 0, 1, stride=1, stride_axis=0)
        toeplitz[block] = jnp.where(lane >= row, turned, before).astype(bf16)
        before = turned

    total = None
    for pair in range(pairs):
        left = jnp.zeros((tokens, tokens), bf16) if pair == 0 else toeplitz[2 * pair - 1]
        weights = jnp.concatenate(
            (
                jnp.concatenate((toeplitz[2 * pair], toeplitz[2 * pair + 1]), axis=1),
                jnp.concatenate((left, toeplitz[2 * pair]), axis=1),
            ),
            axis=0,
        )
        skip = 2 * width * pair
        term = dot(streams[0 : 2 * width * pairs - skip, :], weights)
        total = term if pair == 0 else jnp.concatenate((total[:skip], total[skip:] + term), axis=0)
    for pair in range(pairs):
        for half in range(2):
            block = 2 * pair + half
            lanes = slice(half * tokens, (half + 1) * tokens)
            at = 2 * width * pair
            sent[block * rows : block * rows + width, :] = total[at : at + width, lanes].astype(bf16)
            place = (blocks - 1 - block) * rows + width
            sent[place : place + width, :] = total[
                at + width : at + 2 * width, lanes
            ].astype(bf16)

    ordered = jnp.concatenate(
        [got[block * rows : block * rows + width, :] for block in range(blocks)], axis=0
    )
    ordered = ordered.astype(f32).T.astype(bf16)
    carry = jnp.zeros((8, tokens), f32)
    which = ramp((EXTRA_ROWS, tokens), 0)
    for pair in range(pairs):
        depth = blocks * width if 2 * pair + 2 > blocks // 2 else blocks * width // 2
        columns = [
            padded[pl.ds((blocks - 1 - lag) * width, depth), :] for lag in (2 * pair, 2 * pair + 1)
        ]
        outer = dot(ordered[:, :depth], jnp.concatenate(columns, axis=1))
        for half in range(2):
            block = 2 * pair + half
            turned = pltpu.roll(
                outer[:, half * tokens : (half + 1) * tokens], 0, 1, stride=1, stride_axis=0
            )
            here = jnp.where(lane >= row, turned, 0.0).reshape(tokens // 8, 8, tokens).sum(axis=0)
            later = jnp.where(lane >= row, 0.0, turned).reshape(tokens // 8, 8, tokens).sum(axis=0)
            value = jnp.sum(here + carry, axis=0, keepdims=True) * scale
            carry = later
            high = value.astype(bf16).astype(f32)
            pieces = jnp.where(which == 0, high, jnp.where(which == 1, value - high, 0.0))
            place = (blocks - 1 - block) * rows + 2 * width
            sent[place : place + EXTRA_ROWS, :] = pieces.astype(bf16)


def output_kernel(
    width, got, query, key, value, grad, mixed, query_grad, key_grad, value_grad, filter_grad
):
    rows, tokens = 2 * width + EXTRA_ROWS, got.shape[1]
    blocks = got.shape[0] // rows

    def collect(first, count):
        return jnp.concatenate(
            [got[at * rows + first : at * rows + first + count, :] for at in range(blocks)], axis=0
        )

    flip = flip_matrix(tokens)
    convolved = dot_nt(eye_matrix(tokens), collect(0, width))
    mixed[...] = (query[...].astype(f32) * convolved).astype(bf16)
    query_grad[...] = (grad[...].astype(f32) * convolved).astype(bf16)
    backward = dot_nt(flip, collect(width, width))
    key_grad[...] = (backward * value[...].astype(f32)).astype(bf16)
    value_grad[...] = (backward * key[...].astype(f32)).astype(bf16)
    high, low = collect(2 * width, 1), collect(2 * width + 1, 1)
    filter_grad[...] = dot(high, flip) + dot(low, flip)


def by_groups(query_act, key_act, value_act, long_filter, out_grad):
    tokens, channels = query_act.shape
    groups = long_filter.shape[1]
    width = channels // groups
    rows = 2 * width + EXTRA_ROWS
    scale = 1.0 / math.sqrt(tokens * groups * width)
    chunks = jax.ShapeDtypeStruct((groups * rows, tokens), bf16)

    def exchange(sent):
        pieces = sent.reshape(groups, rows // 2, 2, tokens)
        pieces = lax.all_to_all(pieces, ("slow", "fast"), split_axis=0, concat_axis=0, tiled=True)
        return pieces.reshape(groups * rows, tokens)

    act = pltpu.VMEM((tokens, channels), bf16)
    sent = pl.pallas_call(
        gate_kernel,
        out_shape=chunks,
        in_specs=[pl.BlockSpec(memory_space=pltpu.HBM)] * 5,
        scratch_shapes=[
            act,
            act,
            act,
            pltpu.VMEM((groups, tokens), bf16),
            act,
            pltpu.SemaphoreType.DMA((5,)),
        ],
        compiler_params=pltpu.CompilerParams(vmem_limit_bytes=8 * 2**20),
        name="gate",
    )(
        *(
            pltpu.with_memory_space_constraint(array, pltpu.HBM)
            for array in (query_act, key_act, value_act, long_filter.T, out_grad)
        )
    )
    got = exchange(sent)
    sent = pl.pallas_call(
        functools.partial(group_kernel, scale, width),
        out_shape=chunks,
        scratch_shapes=[
            pltpu.VMEM((channels, 2 * tokens), bf16),
            pltpu.VMEM((2 * channels, tokens), bf16),
            pltpu.VMEM((groups, tokens, tokens), bf16),
        ],
        compiler_params=pltpu.CompilerParams(vmem_limit_bytes=16 * 2**20),
        name="group",
    )(got)
    got = exchange(sent)
    like = jax.ShapeDtypeStruct((tokens, channels), bf16)
    *acts, filter_grad = pl.pallas_call(
        functools.partial(output_kernel, width),
        out_shape=(like, like, like, like, jax.ShapeDtypeStruct((groups, tokens), f32)),
        compiler_params=pltpu.CompilerParams(vmem_limit_bytes=8 * 2**20),
        name="outputs",
    )(got, query_act, key_act, value_act, out_grad)
    return (*acts, filter_grad.T)


def on_device(query_act, key_act, value_act, long_filter, out_grad):
    tokens, channels = query_act.shape
    groups = long_filter.shape[1]
    devices = lax.axis_size("slow") * lax.axis_size("fast")
    if devices == groups and tokens == 128 and channels == 16 * groups and groups % 4 == 0:
        return by_groups(query_act, key_act, value_act, long_filter, out_grad)
    return by_spectra(query_act, key_act, value_act, long_filter, out_grad)


def solution(mesh):
    placed = (
        P(("slow", "fast"), None),
        P(("slow", "fast"), None),
        P(("slow", "fast"), None),
        P(("slow", "fast"), None),
        P(("slow", "fast"), None),
    )
    return jax.shard_map(
        on_device,
        mesh=mesh,
        in_specs=placed,
        out_specs=(
            P(("slow", "fast"), None),
            P(("slow", "fast"), None),
            P(("slow", "fast"), None),
            P(("slow", "fast"), None),
            P(("slow", "fast"), None),
        ),
        check_vma=False,
    )
```

```python
import functools
import math

import jax
import jax.numpy as jnp
from jax import lax
from jax.experimental import pallas as pl
from jax.experimental.pallas import tpu as pltpu
from jax.sharding import PartitionSpec as P

highest = lax.Precision.HIGHEST


def index_ramp(points, along, ndim, offset):
    shape_list = [1] * ndim
    shape_list[along] = points
    return (jnp.arange(points, dtype=jnp.int32) + offset).reshape(shape_list)


def apply_dft(re_im, points, direction, along):
    index_row = jnp.arange(points, dtype=jnp.int32)
    phase_turns = index_row[:, None] * index_row[None, :] % points
    phases = 2.0 * math.pi / points * phase_turns.astype(jnp.float32)
    cosine = jnp.cos(phases)
    sine_part = direction * jnp.sin(phases)

    def contract(values, matrix):
        result = jnp.tensordot(values, matrix, axes=((along,), (1,)), precision=highest)
        return jnp.moveaxis(result, -1, along)

    return (
        contract(re_im[0], cosine) - contract(re_im[1], sine_part),
        contract(re_im[0], sine_part) + contract(re_im[1], cosine),
    )


def rotate(re_im, phase_turns, period, direction):
    phases = 2.0 * math.pi / period * (phase_turns % period).astype(jnp.float32)
    cosine = jnp.cos(phases)
    sine_part = direction * jnp.sin(phases)
    return (re_im[0] * cosine - re_im[1] * sine_part, re_im[0] * sine_part + re_im[1] * cosine)


def complex_times(left, right):
    return (left[0] * right[0] - left[1] * right[1], left[0] * right[1] + left[1] * right[0])


def conj_times(left, right):
    return (left[0] * right[0] + left[1] * right[1], left[0] * right[1] - left[1] * right[0])


def positions(grid_info, slow_points, slow_offset, fast_points, fast_offset):
    fast_count, tokens = (grid_info[1], grid_info[2])
    block_index = index_ramp(slow_points, 2, 5, slow_offset) * fast_count + index_ramp(
        fast_points, 3, 5, fast_offset
    )
    return block_index * tokens + index_ramp(tokens, 4, 5, 0)


def open_halves(re_im, grid_info, fast_offset):
    token_place = positions(grid_info, re_im[0].shape[1], 0, re_im[0].shape[2], fast_offset)
    return rotate(
        (re_im[0][None], re_im[1][None]),
        index_ramp(2, 0, 5, 0) * token_place,
        2 * grid_info[3],
        -1.0,
    )


def fold_halves(re_im, token_place, seq_length):
    turned = rotate(re_im, index_ramp(2, 0, 5, 0) * token_place, 2 * seq_length, 1.0)
    scale = 0.5 / seq_length
    return (jnp.sum(turned[0], axis=0) * scale, jnp.sum(turned[1], axis=0) * scale)


def front_forward(re_im, grid_info, fast_offset):
    slow_count, fast_count = (grid_info[0], grid_info[1])
    re_im = apply_dft(re_im, slow_count, -1.0, 2)
    phase_turns = index_ramp(slow_count, 2, 5, 0) * index_ramp(re_im[0].shape[3], 3, 5, fast_offset)
    return rotate(re_im, phase_turns, slow_count * fast_count, -1.0)


def front_inverse(re_im, grid_info, fast_offset):
    slow_count, fast_count = (grid_info[0], grid_info[1])
    phase_turns = index_ramp(slow_count, 2, 5, 0) * index_ramp(re_im[0].shape[3], 3, 5, fast_offset)
    re_im = rotate(re_im, phase_turns, slow_count * fast_count, 1.0)
    return apply_dft(re_im, slow_count, 1.0, 2)


def lead_phase(re_im, grid_info, ka_offset):
    slow_count, fast_count, tokens = (grid_info[0], grid_info[1], grid_info[2])
    lead_index = index_ramp(re_im[0].shape[2], 2, 5, ka_offset) + slow_count * index_ramp(
        fast_count, 3, 5, 0
    )
    return lead_index * index_ramp(tokens, 4, 5, 0)


def back_forward(re_im, grid_info, ka_offset):
    re_im = apply_dft(re_im, grid_info[1], -1.0, 3)
    re_im = rotate(re_im, lead_phase(re_im, grid_info, ka_offset), grid_info[3], -1.0)
    return apply_dft(re_im, grid_info[2], -1.0, 4)


def back_inverse(re_im, grid_info, ka_offset):
    re_im = apply_dft(re_im, grid_info[2], 1.0, 4)
    re_im = rotate(re_im, lead_phase(re_im, grid_info, ka_offset), grid_info[3], 1.0)
    return apply_dft(re_im, grid_info[1], 1.0, 3)


def to_channels(seq_rows):
    return lax.all_to_all(
        seq_rows.reshape(1, seq_rows.shape[0], seq_rows.shape[1]),
        "slow",
        split_axis=2,
        concat_axis=0,
        tiled=True,
    )


def merge_blocks(arrays, block_count):
    tokens = arrays[0].shape[0]
    pieces = [item.reshape(tokens, block_count, item.shape[1] // block_count) for item in arrays]
    return jnp.concatenate(pieces, axis=2).reshape(tokens, -1)


def split_columns(rows_major, widths):
    tokens, block_count = (rows_major.shape[0], rows_major.shape[1])
    result = []
    offset = 0
    for length in widths:
        result.append(
            rows_major[:, :, offset : offset + length].reshape(tokens, block_count * length)
        )
        offset += length
    return result


def real_blocks(real_part, imag_part, segments):
    pieces = []
    offset = 0
    for output_kind, length in segments:
        real_seg = real_part[:, offset : offset + length]
        imag_seg = imag_part[:, offset : offset + length]
        offset += length
        if output_kind == "pairs":
            stacked = jnp.transpose(jnp.stack((real_seg, imag_seg), axis=-1), (0, 2, 1, 3))
            pieces.append(stacked.reshape(stacked.shape[0], stacked.shape[1], 2 * length))
        else:
            pieces.append(jnp.transpose(real_seg, (0, 2, 1)))
    return jnp.concatenate(pieces, axis=2)


def segment_widths(segments):
    return [2 * length if output_kind == "pairs" else length for output_kind, length in segments]


def spread_forward(seq_rows, grid_info, fast_rank, segments):
    slow_count, fast_count = (grid_info[0], grid_info[1])
    blocks = to_channels(seq_rows).astype(jnp.float32)
    real_list = []
    imag_list = []
    offset = 0
    for length, packed in segments:
        segment = blocks[:, :, offset : offset + length]
        offset += length
        if packed:
            halves = segment.reshape(segment.shape[0], segment.shape[1], length // 2, 2)
            real_seg, imag_seg = (halves[..., 0], halves[..., 1])
        else:
            real_seg, imag_seg = (segment, jnp.zeros_like(segment))
        real_list.append(jnp.transpose(real_seg, (2, 0, 1)))
        imag_list.append(jnp.transpose(imag_seg, (2, 0, 1)))
    re_im = (
        jnp.concatenate(real_list, 0)[:, :, None, :],
        jnp.concatenate(imag_list, 0)[:, :, None, :],
    )
    re_im = front_forward(open_halves(re_im, grid_info, fast_rank), grid_info, fast_rank)
    re_im = (
        lax.all_to_all(re_im[0], "fast", split_axis=2, concat_axis=3, tiled=True),
        lax.all_to_all(re_im[1], "fast", split_axis=2, concat_axis=3, tiled=True),
    )
    return back_forward(re_im, grid_info, fast_rank * (slow_count // fast_count))


def spread_inverse(re_im, grid_info, fast_rank, slow_rank, segments):
    slow_count, fast_count, tokens, seq_length = grid_info
    re_im = back_inverse(re_im, grid_info, fast_rank * (slow_count // fast_count))
    re_im = (
        lax.all_to_all(re_im[0], "fast", split_axis=3, concat_axis=2, tiled=True),
        lax.all_to_all(re_im[1], "fast", split_axis=3, concat_axis=2, tiled=True),
    )
    re_im = front_inverse(re_im, grid_info, fast_rank)
    re_im = (
        lax.all_to_all(re_im[0], "slow", split_axis=2, concat_axis=1, tiled=True),
        lax.all_to_all(re_im[1], "slow", split_axis=2, concat_axis=1, tiled=True),
    )
    real_part, imag_part = fold_halves(
        re_im, positions(grid_info, 1, slow_rank, 1, fast_rank), seq_length
    )
    length = real_part.shape[0] // slow_count
    blocks = real_blocks(
        real_part.reshape(slow_count, length, tokens),
        imag_part.reshape(slow_count, length, tokens),
        segments,
    )
    rows_major = jnp.transpose(blocks, (1, 0, 2))
    return split_columns(rows_major, segment_widths(segments))


def regroup(re_im, length, local_groups):

    def by_group(values):
        values = values[:, :length]
        return values.reshape(
            (values.shape[0], local_groups, length // local_groups) + values.shape[2:]
        )

    return (by_group(re_im[0]), by_group(re_im[1]))


def flatten_pairs(re_im):

    def merged(values):
        return values.reshape(
            (values.shape[0], values.shape[1] * values.shape[2]) + values.shape[3:]
        )

    return (merged(re_im[0]), merged(re_im[1]))


def by_spectra(query_act, key_act, value_act, long_filter, out_grad):
    tokens, channels = query_act.shape
    groups = long_filter.shape[1]
    slow_count = lax.axis_size("slow")
    fast_count = lax.axis_size("fast")
    seq_length = tokens * slow_count * fast_count
    grid_info = (slow_count, fast_count, tokens, seq_length)
    group_width = channels // groups
    product = (key_act.astype(jnp.float32) * value_act.astype(jnp.float32)).astype(jnp.bfloat16)
    grad_in = (out_grad.astype(jnp.float32) * query_act.astype(jnp.float32)).astype(jnp.bfloat16)
    fast_rank = lax.axis_index("fast")
    slow_rank = lax.axis_index("slow")
    data_pairs = channels // (2 * slow_count)
    local_groups = groups // slow_count
    block_width = channels // slow_count
    spectra = spread_forward(
        merge_blocks((product, long_filter), slow_count),
        grid_info,
        fast_rank,
        ((block_width, True), (local_groups, False)),
    )
    prod_spec = regroup(spectra, data_pairs, local_groups)
    filter_spec = (spectra[0][:, data_pairs:, None], spectra[1][:, data_pairs:, None])
    convolved = spread_inverse(
        flatten_pairs(complex_times(prod_spec, filter_spec)),
        grid_info,
        fast_rank,
        slow_rank,
        (("pairs", data_pairs),),
    )[0]
    grad_spec = regroup(
        spread_forward(grad_in, grid_info, fast_rank, ((block_width, True),)),
        data_pairs,
        local_groups,
    )
    back_spec = flatten_pairs(conj_times(filter_spec, grad_spec))
    corr_spec = conj_times(prod_spec, grad_spec)
    joined = (
        jnp.concatenate((back_spec[0], jnp.sum(corr_spec[0], axis=2)), axis=1),
        jnp.concatenate((back_spec[1], jnp.sum(corr_spec[1], axis=2)), axis=1),
    )
    backward, filter_sum = spread_inverse(
        joined, grid_info, fast_rank, slow_rank, (("pairs", data_pairs), ("real", local_groups))
    )
    scale = 1.0 / math.sqrt(seq_length * group_width)
    mixed_out = (query_act.astype(jnp.float32) * convolved).astype(jnp.bfloat16)
    query_grad = (out_grad.astype(jnp.float32) * convolved).astype(jnp.bfloat16)
    key_grad = (backward * value_act.astype(jnp.float32)).astype(jnp.bfloat16)
    value_grad = (backward * key_act.astype(jnp.float32)).astype(jnp.bfloat16)
    return (mixed_out, query_grad, key_grad, value_grad, filter_sum * scale)


f32 = jnp.float32
bf16 = jnp.bfloat16
EXTRA_ROWS = 2


def dot(left, right):
    return jnp.dot(left, right, preferred_element_type=f32)


def dot_nt(left, right):
    return lax.dot_general(left, right, (((1,), (1,)), ((), ())), preferred_element_type=f32)


def ramp(shape, dim):
    return lax.broadcasted_iota(jnp.int32, shape, dim)


def flip_matrix(size):
    return (ramp((size, size), 0) + ramp((size, size), 1) == size - 1).astype(bf16)


def eye_matrix(size):
    return (ramp((size, size), 0) == ramp((size, size), 1)).astype(bf16)


def store_chunks(place, sources, targets, rows):
    products, grads, extras, chips, aside = sources
    width = products.shape[1]
    for other, target in enumerate(targets):
        for at, chip in enumerate(chips):
            block = chip + ((place & aside) ^ (aside * other))
            target[at * rows : at * rows + width, :] = products[block]
            target[at * rows + width : at * rows + 2 * width, :] = grads[block]
            target[at * rows + 2 * width : (at + 1) * rows, :] = extras[block][0:EXTRA_ROWS].astype(bf16)


def load_chunks(place, got, stores, rows):
    products, grads, extras, chips, aside = stores
    width = products.shape[1]
    for at, chip in enumerate(chips):
        for other in range(2):
            block = chip + ((place & aside) ^ (aside * other))
            first = (2 * at + other) * rows
            products[block] = got[first : first + width, :]
            grads[block] = got[first + width : first + 2 * width, :]
            extras[block, 0:EXTRA_ROWS] = got[first + 2 * width : first + rows, :].astype(f32)


def device_place():
    return lax.axis_index("slow") * lax.axis_size("fast") + lax.axis_index("fast")


def gate_kernel(plan, *refs):
    query, key, value, filt, grad, own, other = refs[:7]
    products, grads_in, extras, queries, keys, values, taps, grads, done = refs[7:]
    copies = [
        pltpu.make_async_copy(source, target, done.at[at])
        for at, (source, target) in enumerate(
            ((key, keys), (value, values), (grad, grads), (query, queries), (filt, taps))
        )
    ]
    for copy in copies:
        copy.start()
    tokens, channels = queries.shape
    groups = taps.shape[0]
    width = channels // groups
    copies[0].wait()
    copies[1].wait()
    product = (keys[...].astype(f32) * values[...].astype(f32)).astype(bf16)
    products[...] = product.astype(f32).T.astype(bf16).reshape(groups, width, tokens)
    copies[2].wait()
    copies[3].wait()
    grad_in = (grads[...].astype(f32) * queries[...].astype(f32)).astype(bf16)
    flipped = dot(flip_matrix(tokens), grad_in)
    grads_in[...] = flipped.T.astype(bf16).reshape(groups, width, tokens)
    copies[4].wait()
    for group in range(groups):
        extras[group, 0:EXTRA_ROWS] = jnp.broadcast_to(
            taps[group : group + 1, :].astype(f32), (EXTRA_ROWS, tokens)
        )
    sources = (products, grads_in, extras, *plan)
    store_chunks(device_place(), sources, (own, other), 2 * width + EXTRA_ROWS)


def join_kernel(rows, own, other, joined):
    for at in range(own.shape[0] // rows):
        part = slice(at * rows, (at + 1) * rows)
        joined[2 * at * rows : (2 * at + 1) * rows, :] = own[part, :]
        joined[(2 * at + 1) * rows : (2 * at + 2) * rows, :] = other[part, :]


def group_kernel(plan, scale, *refs):
    got, own, other, products, grads, extras, streams, padded, toeplitz = refs
    blocks, width, tokens = products.shape
    rows = 2 * width + EXTRA_ROWS
    place = device_place()
    load_chunks(place, got, (products, grads, extras, *plan), rows)

    pairs = blocks // 2
    row, lane = ramp((tokens, tokens), 0), ramp((tokens, tokens), 1)
    for pair in range(pairs):
        for half in range(2):
            block = 2 * pair + half
            lanes = slice(half * tokens, (half + 1) * tokens)
            at = 2 * width * pair
            streams[at : at + width, lanes] = products[block]
            streams[at + width : at + 2 * width, lanes] = grads[blocks - 1 - block]
    padded[0 : blocks * width, :] = grads[...].reshape(blocks * width, tokens)
    padded[blocks * width :, :] = jnp.zeros((blocks * width, tokens), bf16)
    ordered = products[...].reshape(blocks * width, tokens).astype(f32).T.astype(bf16)

    before = jnp.zeros((tokens, tokens), f32)
    for block in range(blocks):
        taps = jnp.broadcast_to(extras[block, 0:1], (tokens, tokens))
        turned = pltpu.roll(taps, 0, 1, stride=1, stride_axis=0)
        toeplitz[block] = jnp.where(lane >= row, turned, before).astype(bf16)
        before = turned

    total = None
    for pair in range(pairs):
        left = jnp.zeros((tokens, tokens), bf16) if pair == 0 else toeplitz[2 * pair - 1]
        weights = jnp.concatenate(
            (
                jnp.concatenate((toeplitz[2 * pair], toeplitz[2 * pair + 1]), axis=1),
                jnp.concatenate((left, toeplitz[2 * pair]), axis=1),
            ),
            axis=0,
        )
        skip = 2 * width * pair
        term = dot(streams[0 : 2 * width * pairs - skip, :], weights)
        total = term if pair == 0 else jnp.concatenate((total[:skip], total[skip:] + term), axis=0)
    for pair in range(pairs):
        for half in range(2):
            block = 2 * pair + half
            lanes = slice(half * tokens, (half + 1) * tokens)
            at = 2 * width * pair
            products[block] = total[at : at + width, lanes].astype(bf16)
            grads[blocks - 1 - block] = total[at + width : at + 2 * width, lanes].astype(bf16)

    carry = jnp.zeros((8, tokens), f32)
    which = ramp((EXTRA_ROWS, tokens), 0)
    for pair in range(pairs):
        depth = blocks * width if 2 * pair + 2 > blocks // 2 else blocks * width // 2
        columns = [
            padded[pl.ds((blocks - 1 - lag) * width, depth), :] for lag in (2 * pair, 2 * pair + 1)
        ]
        outer = dot(ordered[:, :depth], jnp.concatenate(columns, axis=1))
        for half in range(2):
            block = 2 * pair + half
            turned = pltpu.roll(
                outer[:, half * tokens : (half + 1) * tokens], 0, 1, stride=1, stride_axis=0
            )
            here = jnp.where(lane >= row, turned, 0.0).reshape(tokens // 8, 8, tokens).sum(axis=0)
            later = jnp.where(lane >= row, 0.0, turned).reshape(tokens // 8, 8, tokens).sum(axis=0)
            value = jnp.sum(here + carry, axis=0, keepdims=True) * scale
            carry = later
            high = value.astype(bf16).astype(f32)
            extras[blocks - 1 - block, 0:EXTRA_ROWS] = jnp.where(which == 0, high, value - high)
    store_chunks(place, (products, grads, extras, *plan), (own, other), rows)


def output_kernel(plan, *refs):
    got, query, key, value, grad = refs[:5]
    mixed, query_grad, key_grad, value_grad, filter_grad = refs[5:10]
    products, grads, extras = refs[10:]
    blocks, width, tokens = products.shape
    load_chunks(
        device_place(), got, (products, grads, extras, *plan), 2 * width + EXTRA_ROWS
    )
    flip = flip_matrix(tokens)
    convolved = dot_nt(eye_matrix(tokens), products[...].reshape(blocks * width, tokens))
    mixed[...] = (query[...].astype(f32) * convolved).astype(bf16)
    query_grad[...] = (grad[...].astype(f32) * convolved).astype(bf16)
    backward = dot_nt(flip, grads[...].reshape(blocks * width, tokens))
    key_grad[...] = (backward * value[...].astype(f32)).astype(bf16)
    value_grad[...] = (backward * key[...].astype(f32)).astype(bf16)
    high, low = (
        jnp.concatenate([extras[block, at : at + 1] for block in range(blocks)], axis=0)
        for at in range(2)
    )
    filter_grad[...] = dot(high.astype(bf16), flip) + dot(low.astype(bf16), flip)


def by_groups(query_act, key_act, value_act, long_filter, out_grad):
    tokens, channels = query_act.shape
    groups = long_filter.shape[1]
    width = channels // groups
    rows = 2 * width + EXTRA_ROWS
    scale = 1.0 / math.sqrt(tokens * groups * width)
    aside = lax.axis_size("fast")
    chips = tuple(place for place in range(groups) if not place & aside)
    plan = (chips, aside)
    half = jax.ShapeDtypeStruct((len(chips) * rows, tokens), bf16)
    blocks = (
        pltpu.VMEM((groups, width, tokens), bf16),
        pltpu.VMEM((groups, width, tokens), bf16),
        pltpu.VMEM((groups, 8, tokens), f32),
    )

    cores = [[chip + core for chip in chips] for core in (0, aside)]
    pairs = [(place, place ^ aside) for place in range(groups)]

    def exchange(own, other):
        other = lax.ppermute(other, ("slow", "fast"), pairs)
        joined = pl.pallas_call(
            functools.partial(join_kernel, rows),
            out_shape=jax.ShapeDtypeStruct((groups * rows, tokens), bf16),
            compiler_params=pltpu.CompilerParams(vmem_limit_bytes=8 * 2**20),
            name="join",
        )(own, other)
        pieces = lax.all_to_all(
            joined.reshape(len(chips), rows, 2, tokens),
            ("slow", "fast"),
            split_axis=0,
            concat_axis=0,
            axis_index_groups=cores,
            tiled=True,
        )
        return pieces.reshape(groups * rows, tokens)

    act = pltpu.VMEM((tokens, channels), bf16)
    sent = pl.pallas_call(
        functools.partial(gate_kernel, plan),
        out_shape=(half, half),
        in_specs=[pl.BlockSpec(memory_space=pltpu.HBM)] * 5,
        scratch_shapes=[
            *blocks,
            act,
            act,
            act,
            pltpu.VMEM((groups, tokens), bf16),
            act,
            pltpu.SemaphoreType.DMA((5,)),
        ],
        compiler_params=pltpu.CompilerParams(vmem_limit_bytes=8 * 2**20),
        name="gate",
    )(
        *(
            pltpu.with_memory_space_constraint(array, pltpu.HBM)
            for array in (query_act, key_act, value_act, long_filter.T, out_grad)
        )
    )
    got = exchange(*sent)
    sent = pl.pallas_call(
        functools.partial(group_kernel, plan, scale),
        out_shape=(half, half),
        scratch_shapes=[
            *blocks,
            pltpu.VMEM((channels, 2 * tokens), bf16),
            pltpu.VMEM((2 * channels, tokens), bf16),
            pltpu.VMEM((groups, tokens, tokens), bf16),
        ],
        compiler_params=pltpu.CompilerParams(vmem_limit_bytes=16 * 2**20),
        name="group",
    )(got)
    got = exchange(*sent)
    like = jax.ShapeDtypeStruct((tokens, channels), bf16)
    *acts, filter_grad = pl.pallas_call(
        functools.partial(output_kernel, plan),
        out_shape=(like, like, like, like, jax.ShapeDtypeStruct((groups, tokens), f32)),
        scratch_shapes=blocks,
        compiler_params=pltpu.CompilerParams(vmem_limit_bytes=8 * 2**20),
        name="outputs",
    )(got, query_act, key_act, value_act, out_grad)
    return (*acts, filter_grad.T)


def on_device(query_act, key_act, value_act, long_filter, out_grad):
    tokens, channels = query_act.shape
    groups = long_filter.shape[1]
    devices = lax.axis_size("slow") * lax.axis_size("fast")
    if devices == groups and tokens == 128 and channels == 16 * groups and groups & (groups - 1) == 0:
        return by_groups(query_act, key_act, value_act, long_filter, out_grad)
    return by_spectra(query_act, key_act, value_act, long_filter, out_grad)


def solution(mesh):
    placed = (
        P(("slow", "fast"), None),
        P(("slow", "fast"), None),
        P(("slow", "fast"), None),
        P(("slow", "fast"), None),
        P(("slow", "fast"), None),
    )
    return jax.shard_map(
        on_device,
        mesh=mesh,
        in_specs=placed,
        out_specs=(
            P(("slow", "fast"), None),
            P(("slow", "fast"), None),
            P(("slow", "fast"), None),
            P(("slow", "fast"), None),
            P(("slow", "fast"), None),
        ),
        check_vma=False,
    )
```

```python
import functools
import math

import jax
import jax.numpy as jnp
from jax import lax
from jax.experimental import pallas as pl
from jax.experimental.pallas import tpu as pltpu
from jax.sharding import PartitionSpec as P

highest = lax.Precision.HIGHEST


def index_ramp(points, along, ndim, offset):
    shape_list = [1] * ndim
    shape_list[along] = points
    return (jnp.arange(points, dtype=jnp.int32) + offset).reshape(shape_list)


def apply_dft(re_im, points, direction, along):
    index_row = jnp.arange(points, dtype=jnp.int32)
    phase_turns = index_row[:, None] * index_row[None, :] % points
    phases = 2.0 * math.pi / points * phase_turns.astype(jnp.float32)
    cosine = jnp.cos(phases)
    sine_part = direction * jnp.sin(phases)

    def contract(values, matrix):
        result = jnp.tensordot(values, matrix, axes=((along,), (1,)), precision=highest)
        return jnp.moveaxis(result, -1, along)

    return (
        contract(re_im[0], cosine) - contract(re_im[1], sine_part),
        contract(re_im[0], sine_part) + contract(re_im[1], cosine),
    )


def rotate(re_im, phase_turns, period, direction):
    phases = 2.0 * math.pi / period * (phase_turns % period).astype(jnp.float32)
    cosine = jnp.cos(phases)
    sine_part = direction * jnp.sin(phases)
    return (re_im[0] * cosine - re_im[1] * sine_part, re_im[0] * sine_part + re_im[1] * cosine)


def complex_times(left, right):
    return (left[0] * right[0] - left[1] * right[1], left[0] * right[1] + left[1] * right[0])


def conj_times(left, right):
    return (left[0] * right[0] + left[1] * right[1], left[0] * right[1] - left[1] * right[0])


def positions(grid_info, slow_points, slow_offset, fast_points, fast_offset):
    fast_count, tokens = (grid_info[1], grid_info[2])
    block_index = index_ramp(slow_points, 2, 5, slow_offset) * fast_count + index_ramp(
        fast_points, 3, 5, fast_offset
    )
    return block_index * tokens + index_ramp(tokens, 4, 5, 0)


def open_halves(re_im, grid_info, fast_offset):
    token_place = positions(grid_info, re_im[0].shape[1], 0, re_im[0].shape[2], fast_offset)
    return rotate(
        (re_im[0][None], re_im[1][None]),
        index_ramp(2, 0, 5, 0) * token_place,
        2 * grid_info[3],
        -1.0,
    )


def fold_halves(re_im, token_place, seq_length):
    turned = rotate(re_im, index_ramp(2, 0, 5, 0) * token_place, 2 * seq_length, 1.0)
    scale = 0.5 / seq_length
    return (jnp.sum(turned[0], axis=0) * scale, jnp.sum(turned[1], axis=0) * scale)


def front_forward(re_im, grid_info, fast_offset):
    slow_count, fast_count = (grid_info[0], grid_info[1])
    re_im = apply_dft(re_im, slow_count, -1.0, 2)
    phase_turns = index_ramp(slow_count, 2, 5, 0) * index_ramp(re_im[0].shape[3], 3, 5, fast_offset)
    return rotate(re_im, phase_turns, slow_count * fast_count, -1.0)


def front_inverse(re_im, grid_info, fast_offset):
    slow_count, fast_count = (grid_info[0], grid_info[1])
    phase_turns = index_ramp(slow_count, 2, 5, 0) * index_ramp(re_im[0].shape[3], 3, 5, fast_offset)
    re_im = rotate(re_im, phase_turns, slow_count * fast_count, 1.0)
    return apply_dft(re_im, slow_count, 1.0, 2)


def lead_phase(re_im, grid_info, ka_offset):
    slow_count, fast_count, tokens = (grid_info[0], grid_info[1], grid_info[2])
    lead_index = index_ramp(re_im[0].shape[2], 2, 5, ka_offset) + slow_count * index_ramp(
        fast_count, 3, 5, 0
    )
    return lead_index * index_ramp(tokens, 4, 5, 0)


def back_forward(re_im, grid_info, ka_offset):
    re_im = apply_dft(re_im, grid_info[1], -1.0, 3)
    re_im = rotate(re_im, lead_phase(re_im, grid_info, ka_offset), grid_info[3], -1.0)
    return apply_dft(re_im, grid_info[2], -1.0, 4)


def back_inverse(re_im, grid_info, ka_offset):
    re_im = apply_dft(re_im, grid_info[2], 1.0, 4)
    re_im = rotate(re_im, lead_phase(re_im, grid_info, ka_offset), grid_info[3], 1.0)
    return apply_dft(re_im, grid_info[1], 1.0, 3)


def to_channels(seq_rows):
    return lax.all_to_all(
        seq_rows.reshape(1, seq_rows.shape[0], seq_rows.shape[1]),
        "slow",
        split_axis=2,
        concat_axis=0,
        tiled=True,
    )


def merge_blocks(arrays, block_count):
    tokens = arrays[0].shape[0]
    pieces = [item.reshape(tokens, block_count, item.shape[1] // block_count) for item in arrays]
    return jnp.concatenate(pieces, axis=2).reshape(tokens, -1)


def split_columns(rows_major, widths):
    tokens, block_count = (rows_major.shape[0], rows_major.shape[1])
    result = []
    offset = 0
    for length in widths:
        result.append(
            rows_major[:, :, offset : offset + length].reshape(tokens, block_count * length)
        )
        offset += length
    return result


def real_blocks(real_part, imag_part, segments):
    pieces = []
    offset = 0
    for output_kind, length in segments:
        real_seg = real_part[:, offset : offset + length]
        imag_seg = imag_part[:, offset : offset + length]
        offset += length
        if output_kind == "pairs":
            stacked = jnp.transpose(jnp.stack((real_seg, imag_seg), axis=-1), (0, 2, 1, 3))
            pieces.append(stacked.reshape(stacked.shape[0], stacked.shape[1], 2 * length))
        else:
            pieces.append(jnp.transpose(real_seg, (0, 2, 1)))
    return jnp.concatenate(pieces, axis=2)


def segment_widths(segments):
    return [2 * length if output_kind == "pairs" else length for output_kind, length in segments]


def spread_forward(seq_rows, grid_info, fast_rank, segments):
    slow_count, fast_count = (grid_info[0], grid_info[1])
    blocks = to_channels(seq_rows).astype(jnp.float32)
    real_list = []
    imag_list = []
    offset = 0
    for length, packed in segments:
        segment = blocks[:, :, offset : offset + length]
        offset += length
        if packed:
            halves = segment.reshape(segment.shape[0], segment.shape[1], length // 2, 2)
            real_seg, imag_seg = (halves[..., 0], halves[..., 1])
        else:
            real_seg, imag_seg = (segment, jnp.zeros_like(segment))
        real_list.append(jnp.transpose(real_seg, (2, 0, 1)))
        imag_list.append(jnp.transpose(imag_seg, (2, 0, 1)))
    re_im = (
        jnp.concatenate(real_list, 0)[:, :, None, :],
        jnp.concatenate(imag_list, 0)[:, :, None, :],
    )
    re_im = front_forward(open_halves(re_im, grid_info, fast_rank), grid_info, fast_rank)
    re_im = (
        lax.all_to_all(re_im[0], "fast", split_axis=2, concat_axis=3, tiled=True),
        lax.all_to_all(re_im[1], "fast", split_axis=2, concat_axis=3, tiled=True),
    )
    return back_forward(re_im, grid_info, fast_rank * (slow_count // fast_count))


def spread_inverse(re_im, grid_info, fast_rank, slow_rank, segments):
    slow_count, fast_count, tokens, seq_length = grid_info
    re_im = back_inverse(re_im, grid_info, fast_rank * (slow_count // fast_count))
    re_im = (
        lax.all_to_all(re_im[0], "fast", split_axis=3, concat_axis=2, tiled=True),
        lax.all_to_all(re_im[1], "fast", split_axis=3, concat_axis=2, tiled=True),
    )
    re_im = front_inverse(re_im, grid_info, fast_rank)
    re_im = (
        lax.all_to_all(re_im[0], "slow", split_axis=2, concat_axis=1, tiled=True),
        lax.all_to_all(re_im[1], "slow", split_axis=2, concat_axis=1, tiled=True),
    )
    real_part, imag_part = fold_halves(
        re_im, positions(grid_info, 1, slow_rank, 1, fast_rank), seq_length
    )
    length = real_part.shape[0] // slow_count
    blocks = real_blocks(
        real_part.reshape(slow_count, length, tokens),
        imag_part.reshape(slow_count, length, tokens),
        segments,
    )
    rows_major = jnp.transpose(blocks, (1, 0, 2))
    return split_columns(rows_major, segment_widths(segments))


def regroup(re_im, length, local_groups):

    def by_group(values):
        values = values[:, :length]
        return values.reshape(
            (values.shape[0], local_groups, length // local_groups) + values.shape[2:]
        )

    return (by_group(re_im[0]), by_group(re_im[1]))


def flatten_pairs(re_im):

    def merged(values):
        return values.reshape(
            (values.shape[0], values.shape[1] * values.shape[2]) + values.shape[3:]
        )

    return (merged(re_im[0]), merged(re_im[1]))


def by_spectra(query_act, key_act, value_act, long_filter, out_grad):
    tokens, channels = query_act.shape
    groups = long_filter.shape[1]
    slow_count = lax.axis_size("slow")
    fast_count = lax.axis_size("fast")
    seq_length = tokens * slow_count * fast_count
    grid_info = (slow_count, fast_count, tokens, seq_length)
    group_width = channels // groups
    product = (key_act.astype(jnp.float32) * value_act.astype(jnp.float32)).astype(jnp.bfloat16)
    grad_in = (out_grad.astype(jnp.float32) * query_act.astype(jnp.float32)).astype(jnp.bfloat16)
    fast_rank = lax.axis_index("fast")
    slow_rank = lax.axis_index("slow")
    data_pairs = channels // (2 * slow_count)
    local_groups = groups // slow_count
    block_width = channels // slow_count
    spectra = spread_forward(
        merge_blocks((product, long_filter), slow_count),
        grid_info,
        fast_rank,
        ((block_width, True), (local_groups, False)),
    )
    prod_spec = regroup(spectra, data_pairs, local_groups)
    filter_spec = (spectra[0][:, data_pairs:, None], spectra[1][:, data_pairs:, None])
    convolved = spread_inverse(
        flatten_pairs(complex_times(prod_spec, filter_spec)),
        grid_info,
        fast_rank,
        slow_rank,
        (("pairs", data_pairs),),
    )[0]
    grad_spec = regroup(
        spread_forward(grad_in, grid_info, fast_rank, ((block_width, True),)),
        data_pairs,
        local_groups,
    )
    back_spec = flatten_pairs(conj_times(filter_spec, grad_spec))
    corr_spec = conj_times(prod_spec, grad_spec)
    joined = (
        jnp.concatenate((back_spec[0], jnp.sum(corr_spec[0], axis=2)), axis=1),
        jnp.concatenate((back_spec[1], jnp.sum(corr_spec[1], axis=2)), axis=1),
    )
    backward, filter_sum = spread_inverse(
        joined, grid_info, fast_rank, slow_rank, (("pairs", data_pairs), ("real", local_groups))
    )
    scale = 1.0 / math.sqrt(seq_length * group_width)
    mixed_out = (query_act.astype(jnp.float32) * convolved).astype(jnp.bfloat16)
    query_grad = (out_grad.astype(jnp.float32) * convolved).astype(jnp.bfloat16)
    key_grad = (backward * value_act.astype(jnp.float32)).astype(jnp.bfloat16)
    value_grad = (backward * key_act.astype(jnp.float32)).astype(jnp.bfloat16)
    return (mixed_out, query_grad, key_grad, value_grad, filter_sum * scale)


f32 = jnp.float32
bf16 = jnp.bfloat16
EXTRA_ROWS = 2


def dot(left, right):
    return jnp.dot(left, right, preferred_element_type=f32)


def dot_nt(left, right):
    return lax.dot_general(left, right, (((1,), (1,)), ((), ())), preferred_element_type=f32)


def ramp(shape, dim):
    return lax.broadcasted_iota(jnp.int32, shape, dim)


def flip_matrix(size):
    return (ramp((size, size), 0) + ramp((size, size), 1) == size - 1).astype(bf16)


def eye_matrix(size):
    return (ramp((size, size), 0) == ramp((size, size), 1)).astype(bf16)


def gate_kernel(query, key, value, filt, grad, sent, queries, keys, values, taps, grads, done):
    parts = 2
    span = queries.shape[0] // parts
    copies = [
        pltpu.make_async_copy(
            source.at[pl.ds(part * span, span), :],
            target.at[pl.ds(part * span, span), :],
            done.at[parts * at + part],
        )
        for part in range(parts)
        for at, (source, target) in enumerate(
            ((grad, grads), (query, queries), (key, keys), (value, values))
        )
    ]
    copies.append(pltpu.make_async_copy(filt, taps, done.at[len(copies)]))
    for copy in copies:
        copy.start()
    tokens, channels = queries.shape
    groups = taps.shape[0]
    width = channels // groups
    rows = 2 * width + EXTRA_ROWS
    for copy in copies:
        copy.wait()
    grad_in = (grads[...].astype(f32) * queries[...].astype(f32)).astype(bf16)
    flipped = dot(flip_matrix(tokens), grad_in)
    product = (keys[...].astype(f32) * values[...].astype(f32)).astype(bf16)
    columns = product.astype(f32).T.astype(bf16)
    flipped = flipped.T.astype(bf16)
    for group in range(groups):
        at = group * rows
        part = slice(group * width, (group + 1) * width)
        sent[at : at + width, :] = columns[part]
        sent[at + width : at + 2 * width, :] = flipped[part]
        sent[at + 2 * width : at + rows, :] = jnp.broadcast_to(
            taps[group : group + 1, :], (EXTRA_ROWS, tokens)
        )


def group_kernel(scale, width, got, sent, streams, padded, toeplitz):
    rows, tokens = 2 * width + EXTRA_ROWS, got.shape[1]
    blocks = got.shape[0] // rows
    pairs = blocks // 2
    row, lane = ramp((tokens, tokens), 0), ramp((tokens, tokens), 1)
    for pair in range(pairs):
        for half in range(2):
            block = 2 * pair + half
            lanes = slice(half * tokens, (half + 1) * tokens)
            at = 2 * width * pair
            streams[at : at + width, lanes] = got[block * rows : block * rows + width, :]
            streams[at + width : at + 2 * width, lanes] = got[
                (blocks - 1 - block) * rows + width : (blocks - 1 - block) * rows + 2 * width, :
            ]
    for block in range(blocks):
        padded[block * width : (block + 1) * width, :] = got[
            block * rows + width : block * rows + 2 * width, :
        ]
    padded[blocks * width :, :] = jnp.zeros((blocks * width, tokens), bf16)

    before = jnp.zeros((tokens, tokens), f32)
    for block in range(blocks):
        taps = jnp.broadcast_to(got[block * rows + 2 * width : block * rows + 2 * width + 1, :].astype(f32), (tokens, tokens))
        turned = pltpu.roll(taps, 0, 1, stride=1, stride_axis=0)
        toeplitz[block] = jnp.where(lane >= row, turned, before).astype(bf16)
        before = turned

    total = None
    for pair in range(pairs):
        left = jnp.zeros((tokens, tokens), bf16) if pair == 0 else toeplitz[2 * pair - 1]
        weights = jnp.concatenate(
            (
                jnp.concatenate((toeplitz[2 * pair], toeplitz[2 * pair + 1]), axis=1),
                jnp.concatenate((left, toeplitz[2 * pair]), axis=1),
            ),
            axis=0,
        )
        skip = 2 * width * pair
        term = dot(streams[0 : 2 * width * pairs - skip, :], weights)
        total = term if pair == 0 else jnp.concatenate((total[:skip], total[skip:] + term), axis=0)
    for pair in range(pairs):
        for half in range(2):
            block = 2 * pair + half
            lanes = slice(half * tokens, (half + 1) * tokens)
            at = 2 * width * pair
            sent[block * rows : block * rows + width, :] = total[at : at + width, lanes].astype(bf16)
            place = (blocks - 1 - block) * rows + width
            sent[place : place + width, :] = total[
                at + width : at + 2 * width, lanes
            ].astype(bf16)

    ordered = jnp.concatenate(
        [got[block * rows : block * rows + width, :] for block in range(blocks)], axis=0
    )
    ordered = ordered.astype(f32).T.astype(bf16)
    carry = jnp.zeros((8, tokens), f32)
    which = ramp((EXTRA_ROWS, tokens), 0)
    for pair in range(pairs):
        depth = blocks * width if 2 * pair + 2 > blocks // 2 else blocks * width // 2
        columns = [
            padded[pl.ds((blocks - 1 - lag) * width, depth), :] for lag in (2 * pair, 2 * pair + 1)
        ]
        outer = dot(ordered[:, :depth], jnp.concatenate(columns, axis=1))
        for half in range(2):
            block = 2 * pair + half
            turned = pltpu.roll(
                outer[:, half * tokens : (half + 1) * tokens], 0, 1, stride=1, stride_axis=0
            )
            here = jnp.where(lane >= row, turned, 0.0).reshape(tokens // 8, 8, tokens).sum(axis=0)
            later = jnp.where(lane >= row, 0.0, turned).reshape(tokens // 8, 8, tokens).sum(axis=0)
            value = jnp.sum(here + carry, axis=0, keepdims=True) * scale
            carry = later
            high = value.astype(bf16).astype(f32)
            pieces = jnp.where(which == 0, high, jnp.where(which == 1, value - high, 0.0))
            place = (blocks - 1 - block) * rows + 2 * width
            sent[place : place + EXTRA_ROWS, :] = pieces.astype(bf16)


def output_kernel(
    width, got, query, key, value, grad, mixed, query_grad, key_grad, value_grad, filter_grad
):
    rows, tokens = 2 * width + EXTRA_ROWS, got.shape[1]
    blocks = got.shape[0] // rows

    def collect(first, count):
        return jnp.concatenate(
            [got[at * rows + first : at * rows + first + count, :] for at in range(blocks)], axis=0
        )

    flip = flip_matrix(tokens)
    convolved = dot_nt(eye_matrix(tokens), collect(0, width))
    mixed[...] = (query[...].astype(f32) * convolved).astype(bf16)
    query_grad[...] = (grad[...].astype(f32) * convolved).astype(bf16)
    backward = dot_nt(flip, collect(width, width))
    key_grad[...] = (backward * value[...].astype(f32)).astype(bf16)
    value_grad[...] = (backward * key[...].astype(f32)).astype(bf16)
    high, low = collect(2 * width, 1), collect(2 * width + 1, 1)
    filter_grad[...] = dot(high, flip) + dot(low, flip)


def by_groups(query_act, key_act, value_act, long_filter, out_grad):
    tokens, channels = query_act.shape
    groups = long_filter.shape[1]
    width = channels // groups
    rows = 2 * width + EXTRA_ROWS
    scale = 1.0 / math.sqrt(tokens * groups * width)
    chunks = jax.ShapeDtypeStruct((groups * rows, tokens), bf16)

    def exchange(sent):
        pieces = sent.reshape(groups, rows // 2, 2, tokens)
        pieces = lax.all_to_all(pieces, ("slow", "fast"), split_axis=0, concat_axis=0, tiled=True)
        return pieces.reshape(groups * rows, tokens)

    act = pltpu.VMEM((tokens, channels), bf16)
    sent = pl.pallas_call(
        gate_kernel,
        out_shape=chunks,
        in_specs=[pl.BlockSpec(memory_space=pltpu.HBM)] * 5,
        scratch_shapes=[
            act,
            act,
            act,
            pltpu.VMEM((groups, tokens), bf16),
            act,
            pltpu.SemaphoreType.DMA((9,)),
        ],
        compiler_params=pltpu.CompilerParams(vmem_limit_bytes=8 * 2**20),
        name="gate",
    )(
        *(
            pltpu.with_memory_space_constraint(array, pltpu.HBM)
            for array in (query_act, key_act, value_act, long_filter.T, out_grad)
        )
    )
    got = exchange(sent)
    sent = pl.pallas_call(
        functools.partial(group_kernel, scale, width),
        out_shape=chunks,
        scratch_shapes=[
            pltpu.VMEM((channels, 2 * tokens), bf16),
            pltpu.VMEM((2 * channels, tokens), bf16),
            pltpu.VMEM((groups, tokens, tokens), bf16),
        ],
        compiler_params=pltpu.CompilerParams(vmem_limit_bytes=16 * 2**20),
        name="group",
    )(got)
    got = exchange(sent)
    like = jax.ShapeDtypeStruct((tokens, channels), bf16)
    *acts, filter_grad = pl.pallas_call(
        functools.partial(output_kernel, width),
        out_shape=(like, like, like, like, jax.ShapeDtypeStruct((groups, tokens), f32)),
        compiler_params=pltpu.CompilerParams(vmem_limit_bytes=8 * 2**20),
        name="outputs",
    )(got, query_act, key_act, value_act, out_grad)
    return (*acts, filter_grad.T)


def on_device(query_act, key_act, value_act, long_filter, out_grad):
    tokens, channels = query_act.shape
    groups = long_filter.shape[1]
    devices = lax.axis_size("slow") * lax.axis_size("fast")
    if devices == groups and tokens == 128 and channels == 16 * groups and groups % 4 == 0:
        return by_groups(query_act, key_act, value_act, long_filter, out_grad)
    return by_spectra(query_act, key_act, value_act, long_filter, out_grad)


def solution(mesh):
    placed = (
        P(("slow", "fast"), None),
        P(("slow", "fast"), None),
        P(("slow", "fast"), None),
        P(("slow", "fast"), None),
        P(("slow", "fast"), None),
    )
    return jax.shard_map(
        on_device,
        mesh=mesh,
        in_specs=placed,
        out_specs=(
            P(("slow", "fast"), None),
            P(("slow", "fast"), None),
            P(("slow", "fast"), None),
            P(("slow", "fast"), None),
            P(("slow", "fast"), None),
        ),
        check_vma=False,
    )
```

```python
import functools
import math

import jax
import jax.numpy as jnp
from jax import lax
from jax.experimental import pallas as pl
from jax.experimental.pallas import tpu as pltpu
from jax.sharding import PartitionSpec as P

highest = lax.Precision.HIGHEST


def index_ramp(points, along, ndim, offset):
    shape_list = [1] * ndim
    shape_list[along] = points
    return (jnp.arange(points, dtype=jnp.int32) + offset).reshape(shape_list)


def apply_dft(re_im, points, direction, along):
    index_row = jnp.arange(points, dtype=jnp.int32)
    phase_turns = index_row[:, None] * index_row[None, :] % points
    phases = 2.0 * math.pi / points * phase_turns.astype(jnp.float32)
    cosine = jnp.cos(phases)
    sine_part = direction * jnp.sin(phases)

    def contract(values, matrix):
        result = jnp.tensordot(values, matrix, axes=((along,), (1,)), precision=highest)
        return jnp.moveaxis(result, -1, along)

    return (
        contract(re_im[0], cosine) - contract(re_im[1], sine_part),
        contract(re_im[0], sine_part) + contract(re_im[1], cosine),
    )


def rotate(re_im, phase_turns, period, direction):
    phases = 2.0 * math.pi / period * (phase_turns % period).astype(jnp.float32)
    cosine = jnp.cos(phases)
    sine_part = direction * jnp.sin(phases)
    return (re_im[0] * cosine - re_im[1] * sine_part, re_im[0] * sine_part + re_im[1] * cosine)


def complex_times(left, right):
    return (left[0] * right[0] - left[1] * right[1], left[0] * right[1] + left[1] * right[0])


def conj_times(left, right):
    return (left[0] * right[0] + left[1] * right[1], left[0] * right[1] - left[1] * right[0])


def positions(grid_info, slow_points, slow_offset, fast_points, fast_offset):
    fast_count, tokens = (grid_info[1], grid_info[2])
    block_index = index_ramp(slow_points, 2, 5, slow_offset) * fast_count + index_ramp(
        fast_points, 3, 5, fast_offset
    )
    return block_index * tokens + index_ramp(tokens, 4, 5, 0)


def open_halves(re_im, grid_info, fast_offset):
    token_place = positions(grid_info, re_im[0].shape[1], 0, re_im[0].shape[2], fast_offset)
    return rotate(
        (re_im[0][None], re_im[1][None]),
        index_ramp(2, 0, 5, 0) * token_place,
        2 * grid_info[3],
        -1.0,
    )


def fold_halves(re_im, token_place, seq_length):
    turned = rotate(re_im, index_ramp(2, 0, 5, 0) * token_place, 2 * seq_length, 1.0)
    scale = 0.5 / seq_length
    return (jnp.sum(turned[0], axis=0) * scale, jnp.sum(turned[1], axis=0) * scale)


def front_forward(re_im, grid_info, fast_offset):
    slow_count, fast_count = (grid_info[0], grid_info[1])
    re_im = apply_dft(re_im, slow_count, -1.0, 2)
    phase_turns = index_ramp(slow_count, 2, 5, 0) * index_ramp(re_im[0].shape[3], 3, 5, fast_offset)
    return rotate(re_im, phase_turns, slow_count * fast_count, -1.0)


def front_inverse(re_im, grid_info, fast_offset):
    slow_count, fast_count = (grid_info[0], grid_info[1])
    phase_turns = index_ramp(slow_count, 2, 5, 0) * index_ramp(re_im[0].shape[3], 3, 5, fast_offset)
    re_im = rotate(re_im, phase_turns, slow_count * fast_count, 1.0)
    return apply_dft(re_im, slow_count, 1.0, 2)


def lead_phase(re_im, grid_info, ka_offset):
    slow_count, fast_count, tokens = (grid_info[0], grid_info[1], grid_info[2])
    lead_index = index_ramp(re_im[0].shape[2], 2, 5, ka_offset) + slow_count * index_ramp(
        fast_count, 3, 5, 0
    )
    return lead_index * index_ramp(tokens, 4, 5, 0)


def back_forward(re_im, grid_info, ka_offset):
    re_im = apply_dft(re_im, grid_info[1], -1.0, 3)
    re_im = rotate(re_im, lead_phase(re_im, grid_info, ka_offset), grid_info[3], -1.0)
    return apply_dft(re_im, grid_info[2], -1.0, 4)


def back_inverse(re_im, grid_info, ka_offset):
    re_im = apply_dft(re_im, grid_info[2], 1.0, 4)
    re_im = rotate(re_im, lead_phase(re_im, grid_info, ka_offset), grid_info[3], 1.0)
    return apply_dft(re_im, grid_info[1], 1.0, 3)


def to_channels(seq_rows):
    return lax.all_to_all(
        seq_rows.reshape(1, seq_rows.shape[0], seq_rows.shape[1]),
        "slow",
        split_axis=2,
        concat_axis=0,
        tiled=True,
    )


def merge_blocks(arrays, block_count):
    tokens = arrays[0].shape[0]
    pieces = [item.reshape(tokens, block_count, item.shape[1] // block_count) for item in arrays]
    return jnp.concatenate(pieces, axis=2).reshape(tokens, -1)


def split_columns(rows_major, widths):
    tokens, block_count = (rows_major.shape[0], rows_major.shape[1])
    result = []
    offset = 0
    for length in widths:
        result.append(
            rows_major[:, :, offset : offset + length].reshape(tokens, block_count * length)
        )
        offset += length
    return result


def real_blocks(real_part, imag_part, segments):
    pieces = []
    offset = 0
    for output_kind, length in segments:
        real_seg = real_part[:, offset : offset + length]
        imag_seg = imag_part[:, offset : offset + length]
        offset += length
        if output_kind == "pairs":
            stacked = jnp.transpose(jnp.stack((real_seg, imag_seg), axis=-1), (0, 2, 1, 3))
            pieces.append(stacked.reshape(stacked.shape[0], stacked.shape[1], 2 * length))
        else:
            pieces.append(jnp.transpose(real_seg, (0, 2, 1)))
    return jnp.concatenate(pieces, axis=2)


def segment_widths(segments):
    return [2 * length if output_kind == "pairs" else length for output_kind, length in segments]


def spread_forward(seq_rows, grid_info, fast_rank, segments):
    slow_count, fast_count = (grid_info[0], grid_info[1])
    blocks = to_channels(seq_rows).astype(jnp.float32)
    real_list = []
    imag_list = []
    offset = 0
    for length, packed in segments:
        segment = blocks[:, :, offset : offset + length]
        offset += length
        if packed:
            halves = segment.reshape(segment.shape[0], segment.shape[1], length // 2, 2)
            real_seg, imag_seg = (halves[..., 0], halves[..., 1])
        else:
            real_seg, imag_seg = (segment, jnp.zeros_like(segment))
        real_list.append(jnp.transpose(real_seg, (2, 0, 1)))
        imag_list.append(jnp.transpose(imag_seg, (2, 0, 1)))
    re_im = (
        jnp.concatenate(real_list, 0)[:, :, None, :],
        jnp.concatenate(imag_list, 0)[:, :, None, :],
    )
    re_im = front_forward(open_halves(re_im, grid_info, fast_rank), grid_info, fast_rank)
    re_im = (
        lax.all_to_all(re_im[0], "fast", split_axis=2, concat_axis=3, tiled=True),
        lax.all_to_all(re_im[1], "fast", split_axis=2, concat_axis=3, tiled=True),
    )
    return back_forward(re_im, grid_info, fast_rank * (slow_count // fast_count))


def spread_inverse(re_im, grid_info, fast_rank, slow_rank, segments):
    slow_count, fast_count, tokens, seq_length = grid_info
    re_im = back_inverse(re_im, grid_info, fast_rank * (slow_count // fast_count))
    re_im = (
        lax.all_to_all(re_im[0], "fast", split_axis=3, concat_axis=2, tiled=True),
        lax.all_to_all(re_im[1], "fast", split_axis=3, concat_axis=2, tiled=True),
    )
    re_im = front_inverse(re_im, grid_info, fast_rank)
    re_im = (
        lax.all_to_all(re_im[0], "slow", split_axis=2, concat_axis=1, tiled=True),
        lax.all_to_all(re_im[1], "slow", split_axis=2, concat_axis=1, tiled=True),
    )
    real_part, imag_part = fold_halves(
        re_im, positions(grid_info, 1, slow_rank, 1, fast_rank), seq_length
    )
    length = real_part.shape[0] // slow_count
    blocks = real_blocks(
        real_part.reshape(slow_count, length, tokens),
        imag_part.reshape(slow_count, length, tokens),
        segments,
    )
    rows_major = jnp.transpose(blocks, (1, 0, 2))
    return split_columns(rows_major, segment_widths(segments))


def regroup(re_im, length, local_groups):

    def by_group(values):
        values = values[:, :length]
        return values.reshape(
            (values.shape[0], local_groups, length // local_groups) + values.shape[2:]
        )

    return (by_group(re_im[0]), by_group(re_im[1]))


def flatten_pairs(re_im):

    def merged(values):
        return values.reshape(
            (values.shape[0], values.shape[1] * values.shape[2]) + values.shape[3:]
        )

    return (merged(re_im[0]), merged(re_im[1]))


def by_spectra(query_act, key_act, value_act, long_filter, out_grad):
    tokens, channels = query_act.shape
    groups = long_filter.shape[1]
    slow_count = lax.axis_size("slow")
    fast_count = lax.axis_size("fast")
    seq_length = tokens * slow_count * fast_count
    grid_info = (slow_count, fast_count, tokens, seq_length)
    group_width = channels // groups
    product = (key_act.astype(jnp.float32) * value_act.astype(jnp.float32)).astype(jnp.bfloat16)
    grad_in = (out_grad.astype(jnp.float32) * query_act.astype(jnp.float32)).astype(jnp.bfloat16)
    fast_rank = lax.axis_index("fast")
    slow_rank = lax.axis_index("slow")
    data_pairs = channels // (2 * slow_count)
    local_groups = groups // slow_count
    block_width = channels // slow_count
    spectra = spread_forward(
        merge_blocks((product, long_filter), slow_count),
        grid_info,
        fast_rank,
        ((block_width, True), (local_groups, False)),
    )
    prod_spec = regroup(spectra, data_pairs, local_groups)
    filter_spec = (spectra[0][:, data_pairs:, None], spectra[1][:, data_pairs:, None])
    convolved = spread_inverse(
        flatten_pairs(complex_times(prod_spec, filter_spec)),
        grid_info,
        fast_rank,
        slow_rank,
        (("pairs", data_pairs),),
    )[0]
    grad_spec = regroup(
        spread_forward(grad_in, grid_info, fast_rank, ((block_width, True),)),
        data_pairs,
        local_groups,
    )
    back_spec = flatten_pairs(conj_times(filter_spec, grad_spec))
    corr_spec = conj_times(prod_spec, grad_spec)
    joined = (
        jnp.concatenate((back_spec[0], jnp.sum(corr_spec[0], axis=2)), axis=1),
        jnp.concatenate((back_spec[1], jnp.sum(corr_spec[1], axis=2)), axis=1),
    )
    backward, filter_sum = spread_inverse(
        joined, grid_info, fast_rank, slow_rank, (("pairs", data_pairs), ("real", local_groups))
    )
    scale = 1.0 / math.sqrt(seq_length * group_width)
    mixed_out = (query_act.astype(jnp.float32) * convolved).astype(jnp.bfloat16)
    query_grad = (out_grad.astype(jnp.float32) * convolved).astype(jnp.bfloat16)
    key_grad = (backward * value_act.astype(jnp.float32)).astype(jnp.bfloat16)
    value_grad = (backward * key_act.astype(jnp.float32)).astype(jnp.bfloat16)
    return (mixed_out, query_grad, key_grad, value_grad, filter_sum * scale)


f32 = jnp.float32
bf16 = jnp.bfloat16
EXTRA_ROWS = 2


def dot(left, right):
    return jnp.dot(left, right, preferred_element_type=f32)


def dot_nt(left, right):
    return lax.dot_general(left, right, (((1,), (1,)), ((), ())), preferred_element_type=f32)


def ramp(shape, dim):
    return lax.broadcasted_iota(jnp.int32, shape, dim)


def flip_matrix(size):
    return (ramp((size, size), 0) + ramp((size, size), 1) == size - 1).astype(bf16)


def eye_matrix(size):
    return (ramp((size, size), 0) == ramp((size, size), 1)).astype(bf16)


def gate_kernel(query, key, value, filt, grad, sent, queries, keys, values, taps, grads, done):
    copies = [
        pltpu.make_async_copy(source, target, done.at[at])
        for at, (source, target) in enumerate(
            ((grad, grads), (query, queries), (key, keys), (value, values), (filt, taps))
        )
    ]
    for copy in copies:
        copy.start()
    tokens, channels = queries.shape
    groups = taps.shape[0]
    width = channels // groups
    rows = 2 * width + EXTRA_ROWS
    for copy in copies:
        copy.wait()
    grad_in = (grads[...].astype(f32) * queries[...].astype(f32)).astype(bf16)
    flipped = dot(flip_matrix(tokens), grad_in)
    product = (keys[...].astype(f32) * values[...].astype(f32)).astype(bf16)
    columns = product.astype(f32).T.astype(bf16)
    flipped = flipped.T.astype(bf16)
    for group in range(groups):
        at = group * rows
        part = slice(group * width, (group + 1) * width)
        sent[at : at + width, :] = columns[part]
        sent[at + width : at + 2 * width, :] = flipped[part]
        sent[at + 2 * width : at + rows, :] = jnp.broadcast_to(
            taps[group : group + 1, :], (EXTRA_ROWS, tokens)
        )


def turn(square):
    return pltpu.roll(square, 0, 1, stride=1, stride_axis=0)


def group_kernel(scale, width, got, sent, streams, padded, toeplitz):
    rows, tokens = 2 * width + EXTRA_ROWS, got.shape[1]
    blocks = got.shape[0] // rows
    pairs = blocks // 2
    row, lane = ramp((tokens, tokens), 0), ramp((tokens, tokens), 1)
    for pair in range(pairs):
        for half in range(2):
            block = 2 * pair + half
            lanes = slice(half * tokens, (half + 1) * tokens)
            at = 2 * width * pair
            streams[at : at + width, lanes] = got[block * rows : block * rows + width, :]
            streams[at + width : at + 2 * width, lanes] = got[
                (blocks - 1 - block) * rows + width : (blocks - 1 - block) * rows + 2 * width, :
            ]
    for block in range(blocks):
        padded[block * width : (block + 1) * width, :] = got[
            block * rows + width : block * rows + 2 * width, :
        ]
    padded[blocks * width :, :] = jnp.zeros((blocks * width, tokens), bf16)

    ordered = jnp.concatenate(
        [got[block * rows : block * rows + width, :] for block in range(blocks)], axis=0
    )
    ordered = ordered.astype(f32).T.astype(bf16)
    band = jnp.zeros((tokens, tokens), f32)
    before = jnp.zeros((tokens, tokens), f32)
    which = ramp((EXTRA_ROWS, tokens), 0)
    for pair in range(pairs):
        depth = -(-2 * (pair + 1) * width // tokens) * tokens
        columns = [
            padded[pl.ds((blocks - 1 - lag) * width, depth), :] for lag in (2 * pair, 2 * pair + 1)
        ]
        outer = dot(ordered[:, :depth], jnp.concatenate(columns, axis=1))
        for half in range(2):
            block = 2 * pair + half
            taps = got[block * rows + 2 * width : block * rows + 2 * width + 1, :].astype(f32)
            turned = turn(jnp.broadcast_to(taps, (tokens, tokens)))
            toeplitz[block] = jnp.where(lane >= row, turned, band).astype(bf16)
            band = turned
            turned = turn(outer[:, half * tokens : (half + 1) * tokens])
            joined = jnp.where(lane >= row, turned, before)
            before = turned
            value = jnp.sum(joined, axis=0, keepdims=True) * scale
            high = value.astype(bf16).astype(f32)
            pieces = jnp.where(which == 0, high, value - high)
            place = (blocks - 1 - block) * rows + 2 * width
            sent[place : place + EXTRA_ROWS, :] = pieces.astype(bf16)

    total = None
    for pair in range(pairs):
        left = jnp.zeros((tokens, tokens), bf16) if pair == 0 else toeplitz[2 * pair - 1]
        weights = jnp.concatenate(
            (
                jnp.concatenate((toeplitz[2 * pair], toeplitz[2 * pair + 1]), axis=1),
                jnp.concatenate((left, toeplitz[2 * pair]), axis=1),
            ),
            axis=0,
        )
        skip = 2 * width * pair
        term = dot(streams[0 : 2 * width * pairs - skip, :], weights)
        total = term if pair == 0 else jnp.concatenate((total[:skip], total[skip:] + term), axis=0)
    for pair in range(pairs):
        for half in range(2):
            block = 2 * pair + half
            lanes = slice(half * tokens, (half + 1) * tokens)
            at = 2 * width * pair
            sent[block * rows : block * rows + width, :] = total[at : at + width, lanes].astype(bf16)
            place = (blocks - 1 - block) * rows + width
            sent[place : place + width, :] = total[
                at + width : at + 2 * width, lanes
            ].astype(bf16)


def output_kernel(
    width, got, query, key, value, grad, mixed, query_grad, key_grad, value_grad, filter_grad
):
    rows, tokens = 2 * width + EXTRA_ROWS, got.shape[1]
    blocks = got.shape[0] // rows

    def collect(first, count):
        return jnp.concatenate(
            [got[at * rows + first : at * rows + first + count, :] for at in range(blocks)], axis=0
        )

    flip = flip_matrix(tokens)
    convolved = dot_nt(eye_matrix(tokens), collect(0, width))
    mixed[...] = (query[...].astype(f32) * convolved).astype(bf16)
    query_grad[...] = (grad[...].astype(f32) * convolved).astype(bf16)
    backward = dot_nt(flip, collect(width, width))
    key_grad[...] = (backward * value[...].astype(f32)).astype(bf16)
    value_grad[...] = (backward * key[...].astype(f32)).astype(bf16)
    high, low = collect(2 * width, 1), collect(2 * width + 1, 1)
    filter_grad[...] = dot(high, flip) + dot(low, flip)


def by_groups(query_act, key_act, value_act, long_filter, out_grad):
    tokens, channels = query_act.shape
    groups = long_filter.shape[1]
    width = channels // groups
    rows = 2 * width + EXTRA_ROWS
    scale = 1.0 / math.sqrt(tokens * groups * width)
    chunks = jax.ShapeDtypeStruct((groups * rows, tokens), bf16)

    def exchange(sent):
        pieces = sent.reshape(groups, rows // 2, 2, tokens)
        pieces = lax.all_to_all(pieces, ("slow", "fast"), split_axis=0, concat_axis=0, tiled=True)
        return pieces.reshape(groups * rows, tokens)

    act = pltpu.VMEM((tokens, channels), bf16)
    sent = pl.pallas_call(
        gate_kernel,
        out_shape=chunks,
        in_specs=[pl.BlockSpec(memory_space=pltpu.HBM)] * 5,
        scratch_shapes=[
            act,
            act,
            act,
            pltpu.VMEM((groups, tokens), bf16),
            act,
            pltpu.SemaphoreType.DMA((5,)),
        ],
        compiler_params=pltpu.CompilerParams(vmem_limit_bytes=8 * 2**20),
        name="gate",
    )(
        *(
            pltpu.with_memory_space_constraint(array, pltpu.HBM)
            for array in (query_act, key_act, value_act, long_filter.T, out_grad)
        )
    )
    got = exchange(sent)
    sent = pl.pallas_call(
        functools.partial(group_kernel, scale, width),
        out_shape=chunks,
        scratch_shapes=[
            pltpu.VMEM((channels, 2 * tokens), bf16),
            pltpu.VMEM((2 * channels, tokens), bf16),
            pltpu.VMEM((groups, tokens, tokens), bf16),
        ],
        compiler_params=pltpu.CompilerParams(vmem_limit_bytes=16 * 2**20),
        name="group",
    )(got)
    got = exchange(sent)
    like = jax.ShapeDtypeStruct((tokens, channels), bf16)
    *acts, filter_grad = pl.pallas_call(
        functools.partial(output_kernel, width),
        out_shape=(like, like, like, like, jax.ShapeDtypeStruct((groups, tokens), f32)),
        compiler_params=pltpu.CompilerParams(vmem_limit_bytes=8 * 2**20),
        name="outputs",
    )(got, query_act, key_act, value_act, out_grad)
    return (*acts, filter_grad.T)


def on_device(query_act, key_act, value_act, long_filter, out_grad):
    tokens, channels = query_act.shape
    groups = long_filter.shape[1]
    devices = lax.axis_size("slow") * lax.axis_size("fast")
    if devices == groups and tokens == 128 and channels == 16 * groups and groups % 4 == 0:
        return by_groups(query_act, key_act, value_act, long_filter, out_grad)
    return by_spectra(query_act, key_act, value_act, long_filter, out_grad)


def solution(mesh):
    placed = (
        P(("slow", "fast"), None),
        P(("slow", "fast"), None),
        P(("slow", "fast"), None),
        P(("slow", "fast"), None),
        P(("slow", "fast"), None),
    )
    return jax.shard_map(
        on_device,
        mesh=mesh,
        in_specs=placed,
        out_specs=(
            P(("slow", "fast"), None),
            P(("slow", "fast"), None),
            P(("slow", "fast"), None),
            P(("slow", "fast"), None),
            P(("slow", "fast"), None),
        ),
        check_vma=False,
    )
```

```python
import functools
import math

import jax
import jax.numpy as jnp
from jax import lax
from jax.experimental import pallas as pl
from jax.experimental.pallas import tpu as pltpu
from jax.sharding import PartitionSpec as P

highest = lax.Precision.HIGHEST


def index_ramp(points, along, ndim, offset):
    shape_list = [1] * ndim
    shape_list[along] = points
    return (jnp.arange(points, dtype=jnp.int32) + offset).reshape(shape_list)


def apply_dft(re_im, points, direction, along):
    index_row = jnp.arange(points, dtype=jnp.int32)
    phase_turns = index_row[:, None] * index_row[None, :] % points
    phases = 2.0 * math.pi / points * phase_turns.astype(jnp.float32)
    cosine = jnp.cos(phases)
    sine_part = direction * jnp.sin(phases)

    def contract(values, matrix):
        result = jnp.tensordot(values, matrix, axes=((along,), (1,)), precision=highest)
        return jnp.moveaxis(result, -1, along)

    return (
        contract(re_im[0], cosine) - contract(re_im[1], sine_part),
        contract(re_im[0], sine_part) + contract(re_im[1], cosine),
    )


def rotate(re_im, phase_turns, period, direction):
    phases = 2.0 * math.pi / period * (phase_turns % period).astype(jnp.float32)
    cosine = jnp.cos(phases)
    sine_part = direction * jnp.sin(phases)
    return (re_im[0] * cosine - re_im[1] * sine_part, re_im[0] * sine_part + re_im[1] * cosine)


def complex_times(left, right):
    return (left[0] * right[0] - left[1] * right[1], left[0] * right[1] + left[1] * right[0])


def conj_times(left, right):
    return (left[0] * right[0] + left[1] * right[1], left[0] * right[1] - left[1] * right[0])


def positions(grid_info, slow_points, slow_offset, fast_points, fast_offset):
    fast_count, tokens = (grid_info[1], grid_info[2])
    block_index = index_ramp(slow_points, 2, 5, slow_offset) * fast_count + index_ramp(
        fast_points, 3, 5, fast_offset
    )
    return block_index * tokens + index_ramp(tokens, 4, 5, 0)


def open_halves(re_im, grid_info, fast_offset):
    token_place = positions(grid_info, re_im[0].shape[1], 0, re_im[0].shape[2], fast_offset)
    return rotate(
        (re_im[0][None], re_im[1][None]),
        index_ramp(2, 0, 5, 0) * token_place,
        2 * grid_info[3],
        -1.0,
    )


def fold_halves(re_im, token_place, seq_length):
    turned = rotate(re_im, index_ramp(2, 0, 5, 0) * token_place, 2 * seq_length, 1.0)
    scale = 0.5 / seq_length
    return (jnp.sum(turned[0], axis=0) * scale, jnp.sum(turned[1], axis=0) * scale)


def front_forward(re_im, grid_info, fast_offset):
    slow_count, fast_count = (grid_info[0], grid_info[1])
    re_im = apply_dft(re_im, slow_count, -1.0, 2)
    phase_turns = index_ramp(slow_count, 2, 5, 0) * index_ramp(re_im[0].shape[3], 3, 5, fast_offset)
    return rotate(re_im, phase_turns, slow_count * fast_count, -1.0)


def front_inverse(re_im, grid_info, fast_offset):
    slow_count, fast_count = (grid_info[0], grid_info[1])
    phase_turns = index_ramp(slow_count, 2, 5, 0) * index_ramp(re_im[0].shape[3], 3, 5, fast_offset)
    re_im = rotate(re_im, phase_turns, slow_count * fast_count, 1.0)
    return apply_dft(re_im, slow_count, 1.0, 2)


def lead_phase(re_im, grid_info, ka_offset):
    slow_count, fast_count, tokens = (grid_info[0], grid_info[1], grid_info[2])
    lead_index = index_ramp(re_im[0].shape[2], 2, 5, ka_offset) + slow_count * index_ramp(
        fast_count, 3, 5, 0
    )
    return lead_index * index_ramp(tokens, 4, 5, 0)


def back_forward(re_im, grid_info, ka_offset):
    re_im = apply_dft(re_im, grid_info[1], -1.0, 3)
    re_im = rotate(re_im, lead_phase(re_im, grid_info, ka_offset), grid_info[3], -1.0)
    return apply_dft(re_im, grid_info[2], -1.0, 4)


def back_inverse(re_im, grid_info, ka_offset):
    re_im = apply_dft(re_im, grid_info[2], 1.0, 4)
    re_im = rotate(re_im, lead_phase(re_im, grid_info, ka_offset), grid_info[3], 1.0)
    return apply_dft(re_im, grid_info[1], 1.0, 3)


def to_channels(seq_rows):
    return lax.all_to_all(
        seq_rows.reshape(1, seq_rows.shape[0], seq_rows.shape[1]),
        "slow",
        split_axis=2,
        concat_axis=0,
        tiled=True,
    )


def merge_blocks(arrays, block_count):
    tokens = arrays[0].shape[0]
    pieces = [item.reshape(tokens, block_count, item.shape[1] // block_count) for item in arrays]
    return jnp.concatenate(pieces, axis=2).reshape(tokens, -1)


def split_columns(rows_major, widths):
    tokens, block_count = (rows_major.shape[0], rows_major.shape[1])
    result = []
    offset = 0
    for length in widths:
        result.append(
            rows_major[:, :, offset : offset + length].reshape(tokens, block_count * length)
        )
        offset += length
    return result


def real_blocks(real_part, imag_part, segments):
    pieces = []
    offset = 0
    for output_kind, length in segments:
        real_seg = real_part[:, offset : offset + length]
        imag_seg = imag_part[:, offset : offset + length]
        offset += length
        if output_kind == "pairs":
            stacked = jnp.transpose(jnp.stack((real_seg, imag_seg), axis=-1), (0, 2, 1, 3))
            pieces.append(stacked.reshape(stacked.shape[0], stacked.shape[1], 2 * length))
        else:
            pieces.append(jnp.transpose(real_seg, (0, 2, 1)))
    return jnp.concatenate(pieces, axis=2)


def segment_widths(segments):
    return [2 * length if output_kind == "pairs" else length for output_kind, length in segments]


def spread_forward(seq_rows, grid_info, fast_rank, segments):
    slow_count, fast_count = (grid_info[0], grid_info[1])
    blocks = to_channels(seq_rows).astype(jnp.float32)
    real_list = []
    imag_list = []
    offset = 0
    for length, packed in segments:
        segment = blocks[:, :, offset : offset + length]
        offset += length
        if packed:
            halves = segment.reshape(segment.shape[0], segment.shape[1], length // 2, 2)
            real_seg, imag_seg = (halves[..., 0], halves[..., 1])
        else:
            real_seg, imag_seg = (segment, jnp.zeros_like(segment))
        real_list.append(jnp.transpose(real_seg, (2, 0, 1)))
        imag_list.append(jnp.transpose(imag_seg, (2, 0, 1)))
    re_im = (
        jnp.concatenate(real_list, 0)[:, :, None, :],
        jnp.concatenate(imag_list, 0)[:, :, None, :],
    )
    re_im = front_forward(open_halves(re_im, grid_info, fast_rank), grid_info, fast_rank)
    re_im = (
        lax.all_to_all(re_im[0], "fast", split_axis=2, concat_axis=3, tiled=True),
        lax.all_to_all(re_im[1], "fast", split_axis=2, concat_axis=3, tiled=True),
    )
    return back_forward(re_im, grid_info, fast_rank * (slow_count // fast_count))


def spread_inverse(re_im, grid_info, fast_rank, slow_rank, segments):
    slow_count, fast_count, tokens, seq_length = grid_info
    re_im = back_inverse(re_im, grid_info, fast_rank * (slow_count // fast_count))
    re_im = (
        lax.all_to_all(re_im[0], "fast", split_axis=3, concat_axis=2, tiled=True),
        lax.all_to_all(re_im[1], "fast", split_axis=3, concat_axis=2, tiled=True),
    )
    re_im = front_inverse(re_im, grid_info, fast_rank)
    re_im = (
        lax.all_to_all(re_im[0], "slow", split_axis=2, concat_axis=1, tiled=True),
        lax.all_to_all(re_im[1], "slow", split_axis=2, concat_axis=1, tiled=True),
    )
    real_part, imag_part = fold_halves(
        re_im, positions(grid_info, 1, slow_rank, 1, fast_rank), seq_length
    )
    length = real_part.shape[0] // slow_count
    blocks = real_blocks(
        real_part.reshape(slow_count, length, tokens),
        imag_part.reshape(slow_count, length, tokens),
        segments,
    )
    rows_major = jnp.transpose(blocks, (1, 0, 2))
    return split_columns(rows_major, segment_widths(segments))


def regroup(re_im, length, local_groups):

    def by_group(values):
        values = values[:, :length]
        return values.reshape(
            (values.shape[0], local_groups, length // local_groups) + values.shape[2:]
        )

    return (by_group(re_im[0]), by_group(re_im[1]))


def flatten_pairs(re_im):

    def merged(values):
        return values.reshape(
            (values.shape[0], values.shape[1] * values.shape[2]) + values.shape[3:]
        )

    return (merged(re_im[0]), merged(re_im[1]))


def by_spectra(query_act, key_act, value_act, long_filter, out_grad):
    tokens, channels = query_act.shape
    groups = long_filter.shape[1]
    slow_count = lax.axis_size("slow")
    fast_count = lax.axis_size("fast")
    seq_length = tokens * slow_count * fast_count
    grid_info = (slow_count, fast_count, tokens, seq_length)
    group_width = channels // groups
    product = (key_act.astype(jnp.float32) * value_act.astype(jnp.float32)).astype(jnp.bfloat16)
    grad_in = (out_grad.astype(jnp.float32) * query_act.astype(jnp.float32)).astype(jnp.bfloat16)
    fast_rank = lax.axis_index("fast")
    slow_rank = lax.axis_index("slow")
    data_pairs = channels // (2 * slow_count)
    local_groups = groups // slow_count
    block_width = channels // slow_count
    spectra = spread_forward(
        merge_blocks((product, long_filter), slow_count),
        grid_info,
        fast_rank,
        ((block_width, True), (local_groups, False)),
    )
    prod_spec = regroup(spectra, data_pairs, local_groups)
    filter_spec = (spectra[0][:, data_pairs:, None], spectra[1][:, data_pairs:, None])
    convolved = spread_inverse(
        flatten_pairs(complex_times(prod_spec, filter_spec)),
        grid_info,
        fast_rank,
        slow_rank,
        (("pairs", data_pairs),),
    )[0]
    grad_spec = regroup(
        spread_forward(grad_in, grid_info, fast_rank, ((block_width, True),)),
        data_pairs,
        local_groups,
    )
    back_spec = flatten_pairs(conj_times(filter_spec, grad_spec))
    corr_spec = conj_times(prod_spec, grad_spec)
    joined = (
        jnp.concatenate((back_spec[0], jnp.sum(corr_spec[0], axis=2)), axis=1),
        jnp.concatenate((back_spec[1], jnp.sum(corr_spec[1], axis=2)), axis=1),
    )
    backward, filter_sum = spread_inverse(
        joined, grid_info, fast_rank, slow_rank, (("pairs", data_pairs), ("real", local_groups))
    )
    scale = 1.0 / math.sqrt(seq_length * group_width)
    mixed_out = (query_act.astype(jnp.float32) * convolved).astype(jnp.bfloat16)
    query_grad = (out_grad.astype(jnp.float32) * convolved).astype(jnp.bfloat16)
    key_grad = (backward * value_act.astype(jnp.float32)).astype(jnp.bfloat16)
    value_grad = (backward * key_act.astype(jnp.float32)).astype(jnp.bfloat16)
    return (mixed_out, query_grad, key_grad, value_grad, filter_sum * scale)


f32 = jnp.float32
bf16 = jnp.bfloat16
EXTRA_ROWS = 2


def dot(left, right):
    return jnp.dot(left, right, preferred_element_type=f32)


def dot_nt(left, right):
    return lax.dot_general(left, right, (((1,), (1,)), ((), ())), preferred_element_type=f32)


def ramp(shape, dim):
    return lax.broadcasted_iota(jnp.int32, shape, dim)


def flip_matrix(size):
    return (ramp((size, size), 0) + ramp((size, size), 1) == size - 1).astype(bf16)


def eye_matrix(size):
    return (ramp((size, size), 0) == ramp((size, size), 1)).astype(bf16)


def gate_kernel(query, key, value, filt, grad, sent, queries, keys, values, taps, grads, done):
    copies = [
        pltpu.make_async_copy(source, target, done.at[at])
        for at, (source, target) in enumerate(
            ((grad, grads), (query, queries), (key, keys), (value, values), (filt, taps))
        )
    ]
    for copy in copies:
        copy.start()
    tokens, channels = queries.shape
    groups = taps.shape[0]
    width = channels // groups
    rows = 2 * width + EXTRA_ROWS
    for copy in copies:
        copy.wait()
    grad_in = (grads[...].astype(f32) * queries[...].astype(f32)).astype(bf16)
    flipped = dot(flip_matrix(tokens), grad_in)
    product = (keys[...].astype(f32) * values[...].astype(f32)).astype(bf16)
    columns = product.astype(f32).T.astype(bf16)
    flipped = flipped.T.astype(bf16)
    for group in range(groups):
        at = group * rows
        part = slice(group * width, (group + 1) * width)
        sent[at : at + width, :] = columns[part]
        sent[at + width : at + 2 * width, :] = flipped[part]
        sent[at + 2 * width : at + rows, :] = jnp.broadcast_to(
            taps[group : group + 1, :], (EXTRA_ROWS, tokens)
        )


def turn(square):
    return pltpu.roll(square, 0, 1, stride=1, stride_axis=0)


def group_kernel(scale, width, got, sent, streams, padded, toeplitz):
    rows, tokens = 2 * width + EXTRA_ROWS, got.shape[1]
    blocks = got.shape[0] // rows
    pairs = blocks // 2
    row, lane = ramp((tokens, tokens), 0), ramp((tokens, tokens), 1)
    loaded = []
    for block in range(blocks):
        mirror = blocks - 1 - block
        here, there = (slice(half * tokens, (half + 1) * tokens) for half in (block % 2, mirror % 2))
        product = got[block * rows : block * rows + width, :]
        grad = got[block * rows + width : block * rows + 2 * width, :]
        at = 2 * width * (block // 2)
        streams[at : at + width, here] = product
        at = 2 * width * (mirror // 2) + width
        streams[at : at + width, there] = grad
        padded[block * width : (block + 1) * width, :] = grad
        loaded.append(product)
    padded[blocks * width :, :] = jnp.zeros((blocks * width, tokens), bf16)

    ordered = jnp.concatenate(loaded, axis=0)
    ordered = ordered.astype(f32).T.astype(bf16)
    band = jnp.zeros((tokens, tokens), f32)
    before = jnp.zeros((tokens, tokens), f32)
    which = ramp((EXTRA_ROWS, tokens), 0)
    for pair in range(pairs):
        depth = -(-2 * (pair + 1) * width // tokens) * tokens
        columns = [
            padded[pl.ds((blocks - 1 - lag) * width, depth), :] for lag in (2 * pair, 2 * pair + 1)
        ]
        outer = dot(ordered[:, :depth], jnp.concatenate(columns, axis=1))
        for half in range(2):
            block = 2 * pair + half
            taps = got[block * rows + 2 * width : block * rows + 2 * width + 1, :].astype(f32)
            turned = turn(jnp.broadcast_to(taps, (tokens, tokens)))
            toeplitz[block] = jnp.where(lane >= row, turned, band).astype(bf16)
            band = turned
            turned = turn(outer[:, half * tokens : (half + 1) * tokens])
            joined = jnp.where(lane >= row, turned, before)
            before = turned
            value = jnp.sum(joined, axis=0, keepdims=True) * scale
            high = value.astype(bf16).astype(f32)
            pieces = jnp.where(which == 0, high, value - high)
            place = (blocks - 1 - block) * rows + 2 * width
            sent[place : place + EXTRA_ROWS, :] = pieces.astype(bf16)

    total = None
    for pair in range(pairs):
        left = jnp.zeros((tokens, tokens), bf16) if pair == 0 else toeplitz[2 * pair - 1]
        weights = jnp.concatenate(
            (
                jnp.concatenate((toeplitz[2 * pair], toeplitz[2 * pair + 1]), axis=1),
                jnp.concatenate((left, toeplitz[2 * pair]), axis=1),
            ),
            axis=0,
        )
        skip = 2 * width * pair
        term = dot(streams[0 : 2 * width * pairs - skip, :], weights)
        total = term if pair == 0 else jnp.concatenate((total[:skip], total[skip:] + term), axis=0)
        ready = total[skip : skip + 2 * width].astype(bf16)
        for half in range(2):
            block = 2 * pair + half
            lanes = slice(half * tokens, (half + 1) * tokens)
            sent[block * rows : block * rows + width, :] = ready[:width, lanes]
            place = (blocks - 1 - block) * rows + width
            sent[place : place + width, :] = ready[width:, lanes]


def output_kernel(
    width, got, query, key, value, grad, mixed, query_grad, key_grad, value_grad, filter_grad
):
    rows, tokens = 2 * width + EXTRA_ROWS, got.shape[1]
    blocks = got.shape[0] // rows

    def collect(first, count):
        return jnp.concatenate(
            [got[at * rows + first : at * rows + first + count, :] for at in range(blocks)], axis=0
        )

    flip = flip_matrix(tokens)
    convolved = dot_nt(eye_matrix(tokens), collect(0, width))
    mixed[...] = (query[...].astype(f32) * convolved).astype(bf16)
    query_grad[...] = (grad[...].astype(f32) * convolved).astype(bf16)
    backward = dot_nt(flip, collect(width, width))
    key_grad[...] = (backward * value[...].astype(f32)).astype(bf16)
    value_grad[...] = (backward * key[...].astype(f32)).astype(bf16)
    high, low = collect(2 * width, 1), collect(2 * width + 1, 1)
    filter_grad[...] = dot(high, flip) + dot(low, flip)


def by_groups(query_act, key_act, value_act, long_filter, out_grad):
    tokens, channels = query_act.shape
    groups = long_filter.shape[1]
    width = channels // groups
    rows = 2 * width + EXTRA_ROWS
    scale = 1.0 / math.sqrt(tokens * groups * width)
    chunks = jax.ShapeDtypeStruct((groups * rows, tokens), bf16)

    def exchange(sent):
        pieces = sent.reshape(groups, rows // 2, 2, tokens)
        pieces = lax.all_to_all(pieces, ("slow", "fast"), split_axis=0, concat_axis=0, tiled=True)
        return pieces.reshape(groups * rows, tokens)

    act = pltpu.VMEM((tokens, channels), bf16)
    sent = pl.pallas_call(
        gate_kernel,
        out_shape=chunks,
        in_specs=[pl.BlockSpec(memory_space=pltpu.HBM)] * 5,
        scratch_shapes=[
            act,
            act,
            act,
            pltpu.VMEM((groups, tokens), bf16),
            act,
            pltpu.SemaphoreType.DMA((5,)),
        ],
        compiler_params=pltpu.CompilerParams(vmem_limit_bytes=8 * 2**20),
        name="gate",
    )(
        *(
            pltpu.with_memory_space_constraint(array, pltpu.HBM)
            for array in (query_act, key_act, value_act, long_filter.T, out_grad)
        )
    )
    got = exchange(sent)
    sent = pl.pallas_call(
        functools.partial(group_kernel, scale, width),
        out_shape=chunks,
        scratch_shapes=[
            pltpu.VMEM((channels, 2 * tokens), bf16),
            pltpu.VMEM((2 * channels, tokens), bf16),
            pltpu.VMEM((groups, tokens, tokens), bf16),
        ],
        compiler_params=pltpu.CompilerParams(vmem_limit_bytes=16 * 2**20),
        name="group",
    )(got)
    got = exchange(sent)
    like = jax.ShapeDtypeStruct((tokens, channels), bf16)
    *acts, filter_grad = pl.pallas_call(
        functools.partial(output_kernel, width),
        out_shape=(like, like, like, like, jax.ShapeDtypeStruct((groups, tokens), f32)),
        compiler_params=pltpu.CompilerParams(vmem_limit_bytes=8 * 2**20),
        name="outputs",
    )(got, query_act, key_act, value_act, out_grad)
    return (*acts, filter_grad.T)


def on_device(query_act, key_act, value_act, long_filter, out_grad):
    tokens, channels = query_act.shape
    groups = long_filter.shape[1]
    devices = lax.axis_size("slow") * lax.axis_size("fast")
    if devices == groups and tokens == 128 and channels == 16 * groups and groups % 4 == 0:
        return by_groups(query_act, key_act, value_act, long_filter, out_grad)
    return by_spectra(query_act, key_act, value_act, long_filter, out_grad)


def solution(mesh):
    placed = (
        P(("slow", "fast"), None),
        P(("slow", "fast"), None),
        P(("slow", "fast"), None),
        P(("slow", "fast"), None),
        P(("slow", "fast"), None),
    )
    return jax.shard_map(
        on_device,
        mesh=mesh,
        in_specs=placed,
        out_specs=(
            P(("slow", "fast"), None),
            P(("slow", "fast"), None),
            P(("slow", "fast"), None),
            P(("slow", "fast"), None),
            P(("slow", "fast"), None),
        ),
        check_vma=False,
    )
```

```python
import functools
import math

import jax
import jax.numpy as jnp
from jax import lax
from jax.experimental import pallas as pl
from jax.experimental.pallas import tpu as pltpu
from jax.sharding import PartitionSpec as P

highest = lax.Precision.HIGHEST


def index_ramp(points, along, ndim, offset):
    shape_list = [1] * ndim
    shape_list[along] = points
    return (jnp.arange(points, dtype=jnp.int32) + offset).reshape(shape_list)


def apply_dft(re_im, points, direction, along):
    index_row = jnp.arange(points, dtype=jnp.int32)
    phase_turns = index_row[:, None] * index_row[None, :] % points
    phases = 2.0 * math.pi / points * phase_turns.astype(jnp.float32)
    cosine = jnp.cos(phases)
    sine_part = direction * jnp.sin(phases)

    def contract(values, matrix):
        result = jnp.tensordot(values, matrix, axes=((along,), (1,)), precision=highest)
        return jnp.moveaxis(result, -1, along)

    return (
        contract(re_im[0], cosine) - contract(re_im[1], sine_part),
        contract(re_im[0], sine_part) + contract(re_im[1], cosine),
    )


def rotate(re_im, phase_turns, period, direction):
    phases = 2.0 * math.pi / period * (phase_turns % period).astype(jnp.float32)
    cosine = jnp.cos(phases)
    sine_part = direction * jnp.sin(phases)
    return (re_im[0] * cosine - re_im[1] * sine_part, re_im[0] * sine_part + re_im[1] * cosine)


def complex_times(left, right):
    return (left[0] * right[0] - left[1] * right[1], left[0] * right[1] + left[1] * right[0])


def conj_times(left, right):
    return (left[0] * right[0] + left[1] * right[1], left[0] * right[1] - left[1] * right[0])


def positions(grid_info, slow_points, slow_offset, fast_points, fast_offset):
    fast_count, tokens = (grid_info[1], grid_info[2])
    block_index = index_ramp(slow_points, 2, 5, slow_offset) * fast_count + index_ramp(
        fast_points, 3, 5, fast_offset
    )
    return block_index * tokens + index_ramp(tokens, 4, 5, 0)


def open_halves(re_im, grid_info, fast_offset):
    token_place = positions(grid_info, re_im[0].shape[1], 0, re_im[0].shape[2], fast_offset)
    return rotate(
        (re_im[0][None], re_im[1][None]),
        index_ramp(2, 0, 5, 0) * token_place,
        2 * grid_info[3],
        -1.0,
    )


def fold_halves(re_im, token_place, seq_length):
    turned = rotate(re_im, index_ramp(2, 0, 5, 0) * token_place, 2 * seq_length, 1.0)
    scale = 0.5 / seq_length
    return (jnp.sum(turned[0], axis=0) * scale, jnp.sum(turned[1], axis=0) * scale)


def front_forward(re_im, grid_info, fast_offset):
    slow_count, fast_count = (grid_info[0], grid_info[1])
    re_im = apply_dft(re_im, slow_count, -1.0, 2)
    phase_turns = index_ramp(slow_count, 2, 5, 0) * index_ramp(re_im[0].shape[3], 3, 5, fast_offset)
    return rotate(re_im, phase_turns, slow_count * fast_count, -1.0)


def front_inverse(re_im, grid_info, fast_offset):
    slow_count, fast_count = (grid_info[0], grid_info[1])
    phase_turns = index_ramp(slow_count, 2, 5, 0) * index_ramp(re_im[0].shape[3], 3, 5, fast_offset)
    re_im = rotate(re_im, phase_turns, slow_count * fast_count, 1.0)
    return apply_dft(re_im, slow_count, 1.0, 2)


def lead_phase(re_im, grid_info, ka_offset):
    slow_count, fast_count, tokens = (grid_info[0], grid_info[1], grid_info[2])
    lead_index = index_ramp(re_im[0].shape[2], 2, 5, ka_offset) + slow_count * index_ramp(
        fast_count, 3, 5, 0
    )
    return lead_index * index_ramp(tokens, 4, 5, 0)


def back_forward(re_im, grid_info, ka_offset):
    re_im = apply_dft(re_im, grid_info[1], -1.0, 3)
    re_im = rotate(re_im, lead_phase(re_im, grid_info, ka_offset), grid_info[3], -1.0)
    return apply_dft(re_im, grid_info[2], -1.0, 4)


def back_inverse(re_im, grid_info, ka_offset):
    re_im = apply_dft(re_im, grid_info[2], 1.0, 4)
    re_im = rotate(re_im, lead_phase(re_im, grid_info, ka_offset), grid_info[3], 1.0)
    return apply_dft(re_im, grid_info[1], 1.0, 3)


def to_channels(seq_rows):
    return lax.all_to_all(
        seq_rows.reshape(1, seq_rows.shape[0], seq_rows.shape[1]),
        "slow",
        split_axis=2,
        concat_axis=0,
        tiled=True,
    )


def merge_blocks(arrays, block_count):
    tokens = arrays[0].shape[0]
    pieces = [item.reshape(tokens, block_count, item.shape[1] // block_count) for item in arrays]
    return jnp.concatenate(pieces, axis=2).reshape(tokens, -1)


def split_columns(rows_major, widths):
    tokens, block_count = (rows_major.shape[0], rows_major.shape[1])
    result = []
    offset = 0
    for length in widths:
        result.append(
            rows_major[:, :, offset : offset + length].reshape(tokens, block_count * length)
        )
        offset += length
    return result


def real_blocks(real_part, imag_part, segments):
    pieces = []
    offset = 0
    for output_kind, length in segments:
        real_seg = real_part[:, offset : offset + length]
        imag_seg = imag_part[:, offset : offset + length]
        offset += length
        if output_kind == "pairs":
            stacked = jnp.transpose(jnp.stack((real_seg, imag_seg), axis=-1), (0, 2, 1, 3))
            pieces.append(stacked.reshape(stacked.shape[0], stacked.shape[1], 2 * length))
        else:
            pieces.append(jnp.transpose(real_seg, (0, 2, 1)))
    return jnp.concatenate(pieces, axis=2)


def segment_widths(segments):
    return [2 * length if output_kind == "pairs" else length for output_kind, length in segments]


def spread_forward(seq_rows, grid_info, fast_rank, segments):
    slow_count, fast_count = (grid_info[0], grid_info[1])
    blocks = to_channels(seq_rows).astype(jnp.float32)
    real_list = []
    imag_list = []
    offset = 0
    for length, packed in segments:
        segment = blocks[:, :, offset : offset + length]
        offset += length
        if packed:
            halves = segment.reshape(segment.shape[0], segment.shape[1], length // 2, 2)
            real_seg, imag_seg = (halves[..., 0], halves[..., 1])
        else:
            real_seg, imag_seg = (segment, jnp.zeros_like(segment))
        real_list.append(jnp.transpose(real_seg, (2, 0, 1)))
        imag_list.append(jnp.transpose(imag_seg, (2, 0, 1)))
    re_im = (
        jnp.concatenate(real_list, 0)[:, :, None, :],
        jnp.concatenate(imag_list, 0)[:, :, None, :],
    )
    re_im = front_forward(open_halves(re_im, grid_info, fast_rank), grid_info, fast_rank)
    re_im = (
        lax.all_to_all(re_im[0], "fast", split_axis=2, concat_axis=3, tiled=True),
        lax.all_to_all(re_im[1], "fast", split_axis=2, concat_axis=3, tiled=True),
    )
    return back_forward(re_im, grid_info, fast_rank * (slow_count // fast_count))


def spread_inverse(re_im, grid_info, fast_rank, slow_rank, segments):
    slow_count, fast_count, tokens, seq_length = grid_info
    re_im = back_inverse(re_im, grid_info, fast_rank * (slow_count // fast_count))
    re_im = (
        lax.all_to_all(re_im[0], "fast", split_axis=3, concat_axis=2, tiled=True),
        lax.all_to_all(re_im[1], "fast", split_axis=3, concat_axis=2, tiled=True),
    )
    re_im = front_inverse(re_im, grid_info, fast_rank)
    re_im = (
        lax.all_to_all(re_im[0], "slow", split_axis=2, concat_axis=1, tiled=True),
        lax.all_to_all(re_im[1], "slow", split_axis=2, concat_axis=1, tiled=True),
    )
    real_part, imag_part = fold_halves(
        re_im, positions(grid_info, 1, slow_rank, 1, fast_rank), seq_length
    )
    length = real_part.shape[0] // slow_count
    blocks = real_blocks(
        real_part.reshape(slow_count, length, tokens),
        imag_part.reshape(slow_count, length, tokens),
        segments,
    )
    rows_major = jnp.transpose(blocks, (1, 0, 2))
    return split_columns(rows_major, segment_widths(segments))


def regroup(re_im, length, local_groups):

    def by_group(values):
        values = values[:, :length]
        return values.reshape(
            (values.shape[0], local_groups, length // local_groups) + values.shape[2:]
        )

    return (by_group(re_im[0]), by_group(re_im[1]))


def flatten_pairs(re_im):

    def merged(values):
        return values.reshape(
            (values.shape[0], values.shape[1] * values.shape[2]) + values.shape[3:]
        )

    return (merged(re_im[0]), merged(re_im[1]))


def by_spectra(query_act, key_act, value_act, long_filter, out_grad):
    tokens, channels = query_act.shape
    groups = long_filter.shape[1]
    slow_count = lax.axis_size("slow")
    fast_count = lax.axis_size("fast")
    seq_length = tokens * slow_count * fast_count
    grid_info = (slow_count, fast_count, tokens, seq_length)
    group_width = channels // groups
    product = (key_act.astype(jnp.float32) * value_act.astype(jnp.float32)).astype(jnp.bfloat16)
    grad_in = (out_grad.astype(jnp.float32) * query_act.astype(jnp.float32)).astype(jnp.bfloat16)
    fast_rank = lax.axis_index("fast")
    slow_rank = lax.axis_index("slow")
    data_pairs = channels // (2 * slow_count)
    local_groups = groups // slow_count
    block_width = channels // slow_count
    spectra = spread_forward(
        merge_blocks((product, long_filter), slow_count),
        grid_info,
        fast_rank,
        ((block_width, True), (local_groups, False)),
    )
    prod_spec = regroup(spectra, data_pairs, local_groups)
    filter_spec = (spectra[0][:, data_pairs:, None], spectra[1][:, data_pairs:, None])
    convolved = spread_inverse(
        flatten_pairs(complex_times(prod_spec, filter_spec)),
        grid_info,
        fast_rank,
        slow_rank,
        (("pairs", data_pairs),),
    )[0]
    grad_spec = regroup(
        spread_forward(grad_in, grid_info, fast_rank, ((block_width, True),)),
        data_pairs,
        local_groups,
    )
    back_spec = flatten_pairs(conj_times(filter_spec, grad_spec))
    corr_spec = conj_times(prod_spec, grad_spec)
    joined = (
        jnp.concatenate((back_spec[0], jnp.sum(corr_spec[0], axis=2)), axis=1),
        jnp.concatenate((back_spec[1], jnp.sum(corr_spec[1], axis=2)), axis=1),
    )
    backward, filter_sum = spread_inverse(
        joined, grid_info, fast_rank, slow_rank, (("pairs", data_pairs), ("real", local_groups))
    )
    scale = 1.0 / math.sqrt(seq_length * group_width)
    mixed_out = (query_act.astype(jnp.float32) * convolved).astype(jnp.bfloat16)
    query_grad = (out_grad.astype(jnp.float32) * convolved).astype(jnp.bfloat16)
    key_grad = (backward * value_act.astype(jnp.float32)).astype(jnp.bfloat16)
    value_grad = (backward * key_act.astype(jnp.float32)).astype(jnp.bfloat16)
    return (mixed_out, query_grad, key_grad, value_grad, filter_sum * scale)


f32 = jnp.float32
bf16 = jnp.bfloat16
EXTRA_ROWS = 2


def dot(left, right):
    return jnp.dot(left, right, preferred_element_type=f32)


def dot_nt(left, right):
    return lax.dot_general(left, right, (((1,), (1,)), ((), ())), preferred_element_type=f32)


def dot_tn(left, right):
    return lax.dot_general(left, right, (((0,), (0,)), ((), ())), preferred_element_type=f32)


def ramp(shape, dim):
    return lax.broadcasted_iota(jnp.int32, shape, dim)


def flip_matrix(size):
    return (ramp((size, size), 0) + ramp((size, size), 1) == size - 1).astype(bf16)


def eye_matrix(size):
    return (ramp((size, size), 0) == ramp((size, size), 1)).astype(bf16)


def pair_matrix(count):
    shape = (count, EXTRA_ROWS * count)
    first = EXTRA_ROWS * ramp(shape, 0)
    return ((ramp(shape, 1) >= first) & (ramp(shape, 1) < first + EXTRA_ROWS)).astype(bf16)


def gate_kernel(query, key, value, filt, grad, sent, queries, keys, values, taps, grads, done):
    copies = [
        pltpu.make_async_copy(source, target, done.at[at])
        for at, (source, target) in enumerate(
            ((grad, grads), (query, queries), (key, keys), (value, values), (filt, taps))
        )
    ]
    for copy in copies:
        copy.start()
    tokens, channels = queries.shape
    groups = taps.shape[0]
    width = channels // groups
    rows = 2 * width + EXTRA_ROWS
    for copy in copies:
        copy.wait()
    grad_in = (grads[...].astype(f32) * queries[...].astype(f32)).astype(bf16)
    flipped = dot(flip_matrix(tokens), grad_in)
    product = (keys[...].astype(f32) * values[...].astype(f32)).astype(bf16)
    columns = product.astype(f32).T.astype(bf16)
    flipped = flipped.T.astype(bf16)
    doubled = dot_tn(pair_matrix(groups), taps[...]).astype(bf16)
    for group in range(groups):
        at = group * rows
        part = slice(group * width, (group + 1) * width)
        sent[at : at + width, :] = columns[part]
        sent[at + width : at + 2 * width, :] = flipped[part]
        sent[at + 2 * width : at + rows, :] = doubled[EXTRA_ROWS * group : EXTRA_ROWS * (group + 1)]


def turn(square):
    return pltpu.roll(square, 0, 1, stride=1, stride_axis=0)


def group_kernel(scale, width, got, sent, streams, padded, toeplitz):
    rows, tokens = 2 * width + EXTRA_ROWS, got.shape[1]
    blocks = got.shape[0] // rows
    pairs = blocks // 2
    row, lane = ramp((tokens, tokens), 0), ramp((tokens, tokens), 1)
    for pair in range(pairs):
        for half in range(2):
            block = 2 * pair + half
            lanes = slice(half * tokens, (half + 1) * tokens)
            at = 2 * width * pair
            streams[at : at + width, lanes] = got[block * rows : block * rows + width, :]
            streams[at + width : at + 2 * width, lanes] = got[
                (blocks - 1 - block) * rows + width : (blocks - 1 - block) * rows + 2 * width, :
            ]
    for block in range(blocks):
        padded[block * width : (block + 1) * width, :] = got[
            block * rows + width : block * rows + 2 * width, :
        ]
    padded[blocks * width :, :] = jnp.zeros((blocks * width, tokens), bf16)

    ordered = jnp.concatenate(
        [got[block * rows : block * rows + width, :] for block in range(blocks)], axis=0
    )
    ordered = ordered.astype(f32).T.astype(bf16)
    band = jnp.zeros((tokens, tokens), f32)
    before = jnp.zeros((tokens, tokens), f32)
    which = ramp((EXTRA_ROWS, tokens), 0)
    for pair in range(pairs):
        depth = -(-2 * (pair + 1) * width // tokens) * tokens
        columns = [
            padded[pl.ds((blocks - 1 - lag) * width, depth), :] for lag in (2 * pair, 2 * pair + 1)
        ]
        outer = dot(ordered[:, :depth], jnp.concatenate(columns, axis=1))
        for half in range(2):
            block = 2 * pair + half
            taps = got[block * rows + 2 * width : block * rows + 2 * width + 1, :].astype(f32)
            turned = turn(jnp.broadcast_to(taps, (tokens, tokens)))
            toeplitz[block] = jnp.where(lane >= row, turned, band).astype(bf16)
            band = turned
            turned = turn(outer[:, half * tokens : (half + 1) * tokens])
            joined = jnp.where(lane >= row, turned, before)
            before = turned
            value = jnp.sum(joined, axis=0, keepdims=True) * scale
            high = value.astype(bf16).astype(f32)
            pieces = jnp.where(which == 0, high, value - high)
            place = (blocks - 1 - block) * rows + 2 * width
            sent[place : place + EXTRA_ROWS, :] = pieces.astype(bf16)

    total = None
    for pair in range(pairs):
        left = jnp.zeros((tokens, tokens), bf16) if pair == 0 else toeplitz[2 * pair - 1]
        weights = jnp.concatenate(
            (
                jnp.concatenate((toeplitz[2 * pair], toeplitz[2 * pair + 1]), axis=1),
                jnp.concatenate((left, toeplitz[2 * pair]), axis=1),
            ),
            axis=0,
        )
        skip = 2 * width * pair
        term = dot(streams[0 : 2 * width * pairs - skip, :], weights)
        total = term if pair == 0 else jnp.concatenate((total[:skip], total[skip:] + term), axis=0)
    for pair in range(pairs):
        for half in range(2):
            block = 2 * pair + half
            lanes = slice(half * tokens, (half + 1) * tokens)
            at = 2 * width * pair
            sent[block * rows : block * rows + width, :] = total[at : at + width, lanes].astype(bf16)
            place = (blocks - 1 - block) * rows + width
            sent[place : place + width, :] = total[
                at + width : at + 2 * width, lanes
            ].astype(bf16)


def output_kernel(
    width, got, query, key, value, grad, mixed, query_grad, key_grad, value_grad, filter_grad
):
    rows, tokens = 2 * width + EXTRA_ROWS, got.shape[1]
    blocks = got.shape[0] // rows

    def collect(first, count):
        return jnp.concatenate(
            [got[at * rows + first : at * rows + first + count, :] for at in range(blocks)], axis=0
        )

    flip = flip_matrix(tokens)
    convolved = dot_nt(eye_matrix(tokens), collect(0, width))
    mixed[...] = (query[...].astype(f32) * convolved).astype(bf16)
    query_grad[...] = (grad[...].astype(f32) * convolved).astype(bf16)
    backward = dot_nt(flip, collect(width, width))
    key_grad[...] = (backward * value[...].astype(f32)).astype(bf16)
    value_grad[...] = (backward * key[...].astype(f32)).astype(bf16)
    turned = dot(collect(2 * width, EXTRA_ROWS), flip).astype(bf16)
    filter_grad[...] = dot(pair_matrix(blocks), turned)


def by_groups(query_act, key_act, value_act, long_filter, out_grad):
    tokens, channels = query_act.shape
    groups = long_filter.shape[1]
    width = channels // groups
    rows = 2 * width + EXTRA_ROWS
    scale = 1.0 / math.sqrt(tokens * groups * width)
    chunks = jax.ShapeDtypeStruct((groups * rows, tokens), bf16)

    def exchange(sent):
        pieces = sent.reshape(groups, rows // 2, 2, tokens)
        pieces = lax.all_to_all(pieces, ("slow", "fast"), split_axis=0, concat_axis=0, tiled=True)
        return pieces.reshape(groups * rows, tokens)

    act = pltpu.VMEM((tokens, channels), bf16)
    sent = pl.pallas_call(
        gate_kernel,
        out_shape=chunks,
        in_specs=[pl.BlockSpec(memory_space=pltpu.HBM)] * 5,
        scratch_shapes=[
            act,
            act,
            act,
            pltpu.VMEM((groups, tokens), bf16),
            act,
            pltpu.SemaphoreType.DMA((5,)),
        ],
        compiler_params=pltpu.CompilerParams(vmem_limit_bytes=8 * 2**20),
        name="gate",
    )(
        *(
            pltpu.with_memory_space_constraint(array, pltpu.HBM)
            for array in (query_act, key_act, value_act, long_filter.T, out_grad)
        )
    )
    got = exchange(sent)
    sent = pl.pallas_call(
        functools.partial(group_kernel, scale, width),
        out_shape=chunks,
        scratch_shapes=[
            pltpu.VMEM((channels, 2 * tokens), bf16),
            pltpu.VMEM((2 * channels, tokens), bf16),
            pltpu.VMEM((groups, tokens, tokens), bf16),
        ],
        compiler_params=pltpu.CompilerParams(vmem_limit_bytes=16 * 2**20),
        name="group",
    )(got)
    got = exchange(sent)
    like = jax.ShapeDtypeStruct((tokens, channels), bf16)
    *acts, filter_grad = pl.pallas_call(
        functools.partial(output_kernel, width),
        out_shape=(like, like, like, like, jax.ShapeDtypeStruct((groups, tokens), f32)),
        compiler_params=pltpu.CompilerParams(vmem_limit_bytes=8 * 2**20),
        name="outputs",
    )(got, query_act, key_act, value_act, out_grad)
    return (*acts, filter_grad.T)


def on_device(query_act, key_act, value_act, long_filter, out_grad):
    tokens, channels = query_act.shape
    groups = long_filter.shape[1]
    devices = lax.axis_size("slow") * lax.axis_size("fast")
    if devices == groups and tokens == 128 and channels == 16 * groups and groups % 4 == 0:
        return by_groups(query_act, key_act, value_act, long_filter, out_grad)
    return by_spectra(query_act, key_act, value_act, long_filter, out_grad)


def solution(mesh):
    placed = (
        P(("slow", "fast"), None),
        P(("slow", "fast"), None),
        P(("slow", "fast"), None),
        P(("slow", "fast"), None),
        P(("slow", "fast"), None),
    )
    return jax.shard_map(
        on_device,
        mesh=mesh,
        in_specs=placed,
        out_specs=(
            P(("slow", "fast"), None),
            P(("slow", "fast"), None),
            P(("slow", "fast"), None),
            P(("slow", "fast"), None),
            P(("slow", "fast"), None),
        ),
        check_vma=False,
    )
```

```python
import functools
import math

import jax
import jax.numpy as jnp
from jax import lax
from jax.experimental import pallas as pl
from jax.experimental.pallas import tpu as pltpu
from jax.sharding import PartitionSpec as P

highest = lax.Precision.HIGHEST


def index_ramp(points, along, ndim, offset):
    shape_list = [1] * ndim
    shape_list[along] = points
    return (jnp.arange(points, dtype=jnp.int32) + offset).reshape(shape_list)


def apply_dft(re_im, points, direction, along):
    index_row = jnp.arange(points, dtype=jnp.int32)
    phase_turns = index_row[:, None] * index_row[None, :] % points
    phases = 2.0 * math.pi / points * phase_turns.astype(jnp.float32)
    cosine = jnp.cos(phases)
    sine_part = direction * jnp.sin(phases)

    def contract(values, matrix):
        result = jnp.tensordot(values, matrix, axes=((along,), (1,)), precision=highest)
        return jnp.moveaxis(result, -1, along)

    return (
        contract(re_im[0], cosine) - contract(re_im[1], sine_part),
        contract(re_im[0], sine_part) + contract(re_im[1], cosine),
    )


def rotate(re_im, phase_turns, period, direction):
    phases = 2.0 * math.pi / period * (phase_turns % period).astype(jnp.float32)
    cosine = jnp.cos(phases)
    sine_part = direction * jnp.sin(phases)
    return (re_im[0] * cosine - re_im[1] * sine_part, re_im[0] * sine_part + re_im[1] * cosine)


def complex_times(left, right):
    return (left[0] * right[0] - left[1] * right[1], left[0] * right[1] + left[1] * right[0])


def conj_times(left, right):
    return (left[0] * right[0] + left[1] * right[1], left[0] * right[1] - left[1] * right[0])


def positions(grid_info, slow_points, slow_offset, fast_points, fast_offset):
    fast_count, tokens = (grid_info[1], grid_info[2])
    block_index = index_ramp(slow_points, 2, 5, slow_offset) * fast_count + index_ramp(
        fast_points, 3, 5, fast_offset
    )
    return block_index * tokens + index_ramp(tokens, 4, 5, 0)


def open_halves(re_im, grid_info, fast_offset):
    token_place = positions(grid_info, re_im[0].shape[1], 0, re_im[0].shape[2], fast_offset)
    return rotate(
        (re_im[0][None], re_im[1][None]),
        index_ramp(2, 0, 5, 0) * token_place,
        2 * grid_info[3],
        -1.0,
    )


def fold_halves(re_im, token_place, seq_length):
    turned = rotate(re_im, index_ramp(2, 0, 5, 0) * token_place, 2 * seq_length, 1.0)
    scale = 0.5 / seq_length
    return (jnp.sum(turned[0], axis=0) * scale, jnp.sum(turned[1], axis=0) * scale)


def front_forward(re_im, grid_info, fast_offset):
    slow_count, fast_count = (grid_info[0], grid_info[1])
    re_im = apply_dft(re_im, slow_count, -1.0, 2)
    phase_turns = index_ramp(slow_count, 2, 5, 0) * index_ramp(re_im[0].shape[3], 3, 5, fast_offset)
    return rotate(re_im, phase_turns, slow_count * fast_count, -1.0)


def front_inverse(re_im, grid_info, fast_offset):
    slow_count, fast_count = (grid_info[0], grid_info[1])
    phase_turns = index_ramp(slow_count, 2, 5, 0) * index_ramp(re_im[0].shape[3], 3, 5, fast_offset)
    re_im = rotate(re_im, phase_turns, slow_count * fast_count, 1.0)
    return apply_dft(re_im, slow_count, 1.0, 2)


def lead_phase(re_im, grid_info, ka_offset):
    slow_count, fast_count, tokens = (grid_info[0], grid_info[1], grid_info[2])
    lead_index = index_ramp(re_im[0].shape[2], 2, 5, ka_offset) + slow_count * index_ramp(
        fast_count, 3, 5, 0
    )
    return lead_index * index_ramp(tokens, 4, 5, 0)


def back_forward(re_im, grid_info, ka_offset):
    re_im = apply_dft(re_im, grid_info[1], -1.0, 3)
    re_im = rotate(re_im, lead_phase(re_im, grid_info, ka_offset), grid_info[3], -1.0)
    return apply_dft(re_im, grid_info[2], -1.0, 4)


def back_inverse(re_im, grid_info, ka_offset):
    re_im = apply_dft(re_im, grid_info[2], 1.0, 4)
    re_im = rotate(re_im, lead_phase(re_im, grid_info, ka_offset), grid_info[3], 1.0)
    return apply_dft(re_im, grid_info[1], 1.0, 3)


def to_channels(seq_rows):
    return lax.all_to_all(
        seq_rows.reshape(1, seq_rows.shape[0], seq_rows.shape[1]),
        "slow",
        split_axis=2,
        concat_axis=0,
        tiled=True,
    )


def merge_blocks(arrays, block_count):
    tokens = arrays[0].shape[0]
    pieces = [item.reshape(tokens, block_count, item.shape[1] // block_count) for item in arrays]
    return jnp.concatenate(pieces, axis=2).reshape(tokens, -1)


def split_columns(rows_major, widths):
    tokens, block_count = (rows_major.shape[0], rows_major.shape[1])
    result = []
    offset = 0
    for length in widths:
        result.append(
            rows_major[:, :, offset : offset + length].reshape(tokens, block_count * length)
        )
        offset += length
    return result


def real_blocks(real_part, imag_part, segments):
    pieces = []
    offset = 0
    for output_kind, length in segments:
        real_seg = real_part[:, offset : offset + length]
        imag_seg = imag_part[:, offset : offset + length]
        offset += length
        if output_kind == "pairs":
            stacked = jnp.transpose(jnp.stack((real_seg, imag_seg), axis=-1), (0, 2, 1, 3))
            pieces.append(stacked.reshape(stacked.shape[0], stacked.shape[1], 2 * length))
        else:
            pieces.append(jnp.transpose(real_seg, (0, 2, 1)))
    return jnp.concatenate(pieces, axis=2)


def segment_widths(segments):
    return [2 * length if output_kind == "pairs" else length for output_kind, length in segments]


def spread_forward(seq_rows, grid_info, fast_rank, segments):
    slow_count, fast_count = (grid_info[0], grid_info[1])
    blocks = to_channels(seq_rows).astype(jnp.float32)
    real_list = []
    imag_list = []
    offset = 0
    for length, packed in segments:
        segment = blocks[:, :, offset : offset + length]
        offset += length
        if packed:
            halves = segment.reshape(segment.shape[0], segment.shape[1], length // 2, 2)
            real_seg, imag_seg = (halves[..., 0], halves[..., 1])
        else:
            real_seg, imag_seg = (segment, jnp.zeros_like(segment))
        real_list.append(jnp.transpose(real_seg, (2, 0, 1)))
        imag_list.append(jnp.transpose(imag_seg, (2, 0, 1)))
    re_im = (
        jnp.concatenate(real_list, 0)[:, :, None, :],
        jnp.concatenate(imag_list, 0)[:, :, None, :],
    )
    re_im = front_forward(open_halves(re_im, grid_info, fast_rank), grid_info, fast_rank)
    re_im = (
        lax.all_to_all(re_im[0], "fast", split_axis=2, concat_axis=3, tiled=True),
        lax.all_to_all(re_im[1], "fast", split_axis=2, concat_axis=3, tiled=True),
    )
    return back_forward(re_im, grid_info, fast_rank * (slow_count // fast_count))


def spread_inverse(re_im, grid_info, fast_rank, slow_rank, segments):
    slow_count, fast_count, tokens, seq_length = grid_info
    re_im = back_inverse(re_im, grid_info, fast_rank * (slow_count // fast_count))
    re_im = (
        lax.all_to_all(re_im[0], "fast", split_axis=3, concat_axis=2, tiled=True),
        lax.all_to_all(re_im[1], "fast", split_axis=3, concat_axis=2, tiled=True),
    )
    re_im = front_inverse(re_im, grid_info, fast_rank)
    re_im = (
        lax.all_to_all(re_im[0], "slow", split_axis=2, concat_axis=1, tiled=True),
        lax.all_to_all(re_im[1], "slow", split_axis=2, concat_axis=1, tiled=True),
    )
    real_part, imag_part = fold_halves(
        re_im, positions(grid_info, 1, slow_rank, 1, fast_rank), seq_length
    )
    length = real_part.shape[0] // slow_count
    blocks = real_blocks(
        real_part.reshape(slow_count, length, tokens),
        imag_part.reshape(slow_count, length, tokens),
        segments,
    )
    rows_major = jnp.transpose(blocks, (1, 0, 2))
    return split_columns(rows_major, segment_widths(segments))


def regroup(re_im, length, local_groups):

    def by_group(values):
        values = values[:, :length]
        return values.reshape(
            (values.shape[0], local_groups, length // local_groups) + values.shape[2:]
        )

    return (by_group(re_im[0]), by_group(re_im[1]))


def flatten_pairs(re_im):

    def merged(values):
        return values.reshape(
            (values.shape[0], values.shape[1] * values.shape[2]) + values.shape[3:]
        )

    return (merged(re_im[0]), merged(re_im[1]))


def by_spectra(query_act, key_act, value_act, long_filter, out_grad):
    tokens, channels = query_act.shape
    groups = long_filter.shape[1]
    slow_count = lax.axis_size("slow")
    fast_count = lax.axis_size("fast")
    seq_length = tokens * slow_count * fast_count
    grid_info = (slow_count, fast_count, tokens, seq_length)
    group_width = channels // groups
    product = (key_act.astype(jnp.float32) * value_act.astype(jnp.float32)).astype(jnp.bfloat16)
    grad_in = (out_grad.astype(jnp.float32) * query_act.astype(jnp.float32)).astype(jnp.bfloat16)
    fast_rank = lax.axis_index("fast")
    slow_rank = lax.axis_index("slow")
    data_pairs = channels // (2 * slow_count)
    local_groups = groups // slow_count
    block_width = channels // slow_count
    spectra = spread_forward(
        merge_blocks((product, long_filter), slow_count),
        grid_info,
        fast_rank,
        ((block_width, True), (local_groups, False)),
    )
    prod_spec = regroup(spectra, data_pairs, local_groups)
    filter_spec = (spectra[0][:, data_pairs:, None], spectra[1][:, data_pairs:, None])
    convolved = spread_inverse(
        flatten_pairs(complex_times(prod_spec, filter_spec)),
        grid_info,
        fast_rank,
        slow_rank,
        (("pairs", data_pairs),),
    )[0]
    grad_spec = regroup(
        spread_forward(grad_in, grid_info, fast_rank, ((block_width, True),)),
        data_pairs,
        local_groups,
    )
    back_spec = flatten_pairs(conj_times(filter_spec, grad_spec))
    corr_spec = conj_times(prod_spec, grad_spec)
    joined = (
        jnp.concatenate((back_spec[0], jnp.sum(corr_spec[0], axis=2)), axis=1),
        jnp.concatenate((back_spec[1], jnp.sum(corr_spec[1], axis=2)), axis=1),
    )
    backward, filter_sum = spread_inverse(
        joined, grid_info, fast_rank, slow_rank, (("pairs", data_pairs), ("real", local_groups))
    )
    scale = 1.0 / math.sqrt(seq_length * group_width)
    mixed_out = (query_act.astype(jnp.float32) * convolved).astype(jnp.bfloat16)
    query_grad = (out_grad.astype(jnp.float32) * convolved).astype(jnp.bfloat16)
    key_grad = (backward * value_act.astype(jnp.float32)).astype(jnp.bfloat16)
    value_grad = (backward * key_act.astype(jnp.float32)).astype(jnp.bfloat16)
    return (mixed_out, query_grad, key_grad, value_grad, filter_sum * scale)


f32 = jnp.float32
bf16 = jnp.bfloat16
EXTRA_ROWS = 2


def dot(left, right):
    return jnp.dot(left, right, preferred_element_type=f32)


def dot_nt(left, right):
    return lax.dot_general(left, right, (((1,), (1,)), ((), ())), preferred_element_type=f32)


def ramp(shape, dim):
    return lax.broadcasted_iota(jnp.int32, shape, dim)


def flip_matrix(size):
    return (ramp((size, size), 0) + ramp((size, size), 1) == size - 1).astype(bf16)


def eye_matrix(size):
    return (ramp((size, size), 0) == ramp((size, size), 1)).astype(bf16)


def gate_kernel(query, key, value, filt, grad, sent, queries, keys, values, taps, grads, done):
    copies = [
        pltpu.make_async_copy(source, target, done.at[at])
        for at, (source, target) in enumerate(
            ((grad, grads), (query, queries), (key, keys), (value, values), (filt, taps))
        )
    ]
    for copy in copies:
        copy.start()
    tokens, channels = queries.shape
    groups = taps.shape[0]
    width = channels // groups
    rows = 2 * width + EXTRA_ROWS
    for copy in copies:
        copy.wait()
    grad_in = (grads[...].astype(f32) * queries[...].astype(f32)).astype(bf16)
    flipped = dot(flip_matrix(tokens), grad_in)
    product = (keys[...].astype(f32) * values[...].astype(f32)).astype(bf16)
    columns = product.astype(f32).T.astype(bf16)
    flipped = flipped.T.astype(bf16)
    for group in range(groups):
        at = group * rows
        part = slice(group * width, (group + 1) * width)
        sent[at : at + width, :] = columns[part]
        sent[at + width : at + 2 * width, :] = flipped[part]
        sent[at + 2 * width : at + rows, :] = jnp.broadcast_to(
            taps[group : group + 1, :], (EXTRA_ROWS, tokens)
        )


def turn(square):
    return pltpu.roll(square, 0, 1, stride=1, stride_axis=0)


def group_kernel(scale, width, got, sent, streams, padded, toeplitz):
    rows, tokens = 2 * width + EXTRA_ROWS, got.shape[1]
    blocks = got.shape[0] // rows
    pairs = blocks // 2
    row, lane = ramp((tokens, tokens), 0), ramp((tokens, tokens), 1)
    for pair in range(pairs):
        for half in range(2):
            block = 2 * pair + half
            lanes = slice(half * tokens, (half + 1) * tokens)
            at = 2 * width * pair
            streams[at : at + width, lanes] = got[block * rows : block * rows + width, :]
            streams[at + width : at + 2 * width, lanes] = got[
                (blocks - 1 - block) * rows + width : (blocks - 1 - block) * rows + 2 * width, :
            ]
    for block in range(blocks):
        padded[block * width : (block + 1) * width, :] = got[
            block * rows + width : block * rows + 2 * width, :
        ]
    padded[blocks * width :, :] = jnp.zeros((blocks * width, tokens), bf16)

    ordered = jnp.concatenate(
        [got[block * rows : block * rows + width, :] for block in range(blocks)], axis=0
    )
    ordered = ordered.astype(f32).T.astype(bf16)
    band = jnp.zeros((tokens, tokens), f32)
    before = jnp.zeros((tokens, tokens), f32)
    which = ramp((EXTRA_ROWS, tokens), 0)
    for pair in range(pairs):
        depth = -(-2 * (pair + 1) * width // tokens) * tokens
        columns = [
            padded[pl.ds((blocks - 1 - lag) * width, depth), :] for lag in (2 * pair, 2 * pair + 1)
        ]
        outer = dot(ordered[:, :depth], jnp.concatenate(columns, axis=1))
        for half in range(2):
            block = 2 * pair + half
            taps = got[block * rows + 2 * width : block * rows + 2 * width + 1, :].astype(f32)
            turned = turn(jnp.broadcast_to(taps, (tokens, tokens)))
            toeplitz[block] = jnp.where(lane >= row, turned, band).astype(bf16)
            band = turned
            turned = turn(outer[:, half * tokens : (half + 1) * tokens])
            joined = jnp.where(lane >= row, turned, before)
            before = turned
            value = jnp.sum(joined, axis=0, keepdims=True) * scale
            high = value.astype(bf16).astype(f32)
            pieces = jnp.where(which == 0, high, value - high)
            place = (blocks - 1 - block) * rows + 2 * width
            sent[place : place + EXTRA_ROWS, :] = pieces.astype(bf16)

    total = None
    for pair in range(pairs):
        left = jnp.zeros((tokens, tokens), bf16) if pair == 0 else toeplitz[2 * pair - 1]
        weights = jnp.concatenate(
            (
                jnp.concatenate((toeplitz[2 * pair], toeplitz[2 * pair + 1]), axis=1),
                jnp.concatenate((left, toeplitz[2 * pair]), axis=1),
            ),
            axis=0,
        )
        skip = 2 * width * pair
        term = dot(streams[0 : 2 * width * pairs - skip, :], weights)
        total = term if pair == 0 else jnp.concatenate((total[:skip], total[skip:] + term), axis=0)
    for pair in range(pairs):
        for half in range(2):
            block = 2 * pair + half
            lanes = slice(half * tokens, (half + 1) * tokens)
            at = 2 * width * pair
            sent[block * rows : block * rows + width, :] = total[at : at + width, lanes].astype(bf16)
            place = (blocks - 1 - block) * rows + width
            sent[place : place + width, :] = total[
                at + width : at + 2 * width, lanes
            ].astype(bf16)


def output_kernel(
    width, got, query, key, value, grad, mixed, query_grad, key_grad, value_grad, filter_grad
):
    rows, tokens = 2 * width + EXTRA_ROWS, got.shape[1]
    blocks = got.shape[0] // rows

    def collect(first, count):
        return jnp.concatenate(
            [got[at * rows + first : at * rows + first + count, :] for at in range(blocks)], axis=0
        )

    flip = flip_matrix(tokens)
    high, low = collect(2 * width, 1), collect(2 * width + 1, 1)
    filter_grad[...] = dot(high, flip) + dot(low, flip)
    convolved = dot_nt(eye_matrix(tokens), collect(0, width))
    mixed[...] = (query[...].astype(f32) * convolved).astype(bf16)
    query_grad[...] = (grad[...].astype(f32) * convolved).astype(bf16)
    backward = dot_nt(flip, collect(width, width))
    key_grad[...] = (backward * value[...].astype(f32)).astype(bf16)
    value_grad[...] = (backward * key[...].astype(f32)).astype(bf16)


def by_groups(query_act, key_act, value_act, long_filter, out_grad):
    tokens, channels = query_act.shape
    groups = long_filter.shape[1]
    width = channels // groups
    rows = 2 * width + EXTRA_ROWS
    scale = 1.0 / math.sqrt(tokens * groups * width)
    chunks = jax.ShapeDtypeStruct((groups * rows, tokens), bf16)

    def exchange(sent):
        pieces = sent.reshape(groups, rows // 2, 2, tokens)
        pieces = lax.all_to_all(pieces, ("slow", "fast"), split_axis=0, concat_axis=0, tiled=True)
        return pieces.reshape(groups * rows, tokens)

    act = pltpu.VMEM((tokens, channels), bf16)
    sent = pl.pallas_call(
        gate_kernel,
        out_shape=chunks,
        in_specs=[pl.BlockSpec(memory_space=pltpu.HBM)] * 5,
        scratch_shapes=[
            act,
            act,
            act,
            pltpu.VMEM((groups, tokens), bf16),
            act,
            pltpu.SemaphoreType.DMA((5,)),
        ],
        compiler_params=pltpu.CompilerParams(vmem_limit_bytes=8 * 2**20),
        name="gate",
    )(
        *(
            pltpu.with_memory_space_constraint(array, pltpu.HBM)
            for array in (query_act, key_act, value_act, long_filter.T, out_grad)
        )
    )
    got = exchange(sent)
    sent = pl.pallas_call(
        functools.partial(group_kernel, scale, width),
        out_shape=chunks,
        scratch_shapes=[
            pltpu.VMEM((channels, 2 * tokens), bf16),
            pltpu.VMEM((2 * channels, tokens), bf16),
            pltpu.VMEM((groups, tokens, tokens), bf16),
        ],
        compiler_params=pltpu.CompilerParams(vmem_limit_bytes=16 * 2**20),
        name="group",
    )(got)
    got = exchange(sent)
    like = jax.ShapeDtypeStruct((tokens, channels), bf16)
    *acts, filter_grad = pl.pallas_call(
        functools.partial(output_kernel, width),
        out_shape=(like, like, like, like, jax.ShapeDtypeStruct((groups, tokens), f32)),
        compiler_params=pltpu.CompilerParams(vmem_limit_bytes=8 * 2**20),
        name="outputs",
    )(got, query_act, key_act, value_act, out_grad)
    return (*acts, filter_grad.T)


def on_device(query_act, key_act, value_act, long_filter, out_grad):
    tokens, channels = query_act.shape
    groups = long_filter.shape[1]
    devices = lax.axis_size("slow") * lax.axis_size("fast")
    if devices == groups and tokens == 128 and channels == 16 * groups and groups % 4 == 0:
        return by_groups(query_act, key_act, value_act, long_filter, out_grad)
    return by_spectra(query_act, key_act, value_act, long_filter, out_grad)


def solution(mesh):
    placed = (
        P(("slow", "fast"), None),
        P(("slow", "fast"), None),
        P(("slow", "fast"), None),
        P(("slow", "fast"), None),
        P(("slow", "fast"), None),
    )
    return jax.shard_map(
        on_device,
        mesh=mesh,
        in_specs=placed,
        out_specs=(
            P(("slow", "fast"), None),
            P(("slow", "fast"), None),
            P(("slow", "fast"), None),
            P(("slow", "fast"), None),
            P(("slow", "fast"), None),
        ),
        check_vma=False,
    )
```

```python
import functools
import math

import jax
import jax.numpy as jnp
from jax import lax
from jax.experimental import pallas as pl
from jax.experimental.pallas import tpu as pltpu
from jax.sharding import PartitionSpec as P

highest = lax.Precision.HIGHEST


def index_ramp(points, along, ndim, offset):
    shape_list = [1] * ndim
    shape_list[along] = points
    return (jnp.arange(points, dtype=jnp.int32) + offset).reshape(shape_list)


def apply_dft(re_im, points, direction, along):
    index_row = jnp.arange(points, dtype=jnp.int32)
    phase_turns = index_row[:, None] * index_row[None, :] % points
    phases = 2.0 * math.pi / points * phase_turns.astype(jnp.float32)
    cosine = jnp.cos(phases)
    sine_part = direction * jnp.sin(phases)

    def contract(values, matrix):
        result = jnp.tensordot(values, matrix, axes=((along,), (1,)), precision=highest)
        return jnp.moveaxis(result, -1, along)

    return (
        contract(re_im[0], cosine) - contract(re_im[1], sine_part),
        contract(re_im[0], sine_part) + contract(re_im[1], cosine),
    )


def rotate(re_im, phase_turns, period, direction):
    phases = 2.0 * math.pi / period * (phase_turns % period).astype(jnp.float32)
    cosine = jnp.cos(phases)
    sine_part = direction * jnp.sin(phases)
    return (re_im[0] * cosine - re_im[1] * sine_part, re_im[0] * sine_part + re_im[1] * cosine)


def complex_times(left, right):
    return (left[0] * right[0] - left[1] * right[1], left[0] * right[1] + left[1] * right[0])


def conj_times(left, right):
    return (left[0] * right[0] + left[1] * right[1], left[0] * right[1] - left[1] * right[0])


def positions(grid_info, slow_points, slow_offset, fast_points, fast_offset):
    fast_count, tokens = (grid_info[1], grid_info[2])
    block_index = index_ramp(slow_points, 2, 5, slow_offset) * fast_count + index_ramp(
        fast_points, 3, 5, fast_offset
    )
    return block_index * tokens + index_ramp(tokens, 4, 5, 0)


def open_halves(re_im, grid_info, fast_offset):
    token_place = positions(grid_info, re_im[0].shape[1], 0, re_im[0].shape[2], fast_offset)
    return rotate(
        (re_im[0][None], re_im[1][None]),
        index_ramp(2, 0, 5, 0) * token_place,
        2 * grid_info[3],
        -1.0,
    )


def fold_halves(re_im, token_place, seq_length):
    turned = rotate(re_im, index_ramp(2, 0, 5, 0) * token_place, 2 * seq_length, 1.0)
    scale = 0.5 / seq_length
    return (jnp.sum(turned[0], axis=0) * scale, jnp.sum(turned[1], axis=0) * scale)


def front_forward(re_im, grid_info, fast_offset):
    slow_count, fast_count = (grid_info[0], grid_info[1])
    re_im = apply_dft(re_im, slow_count, -1.0, 2)
    phase_turns = index_ramp(slow_count, 2, 5, 0) * index_ramp(re_im[0].shape[3], 3, 5, fast_offset)
    return rotate(re_im, phase_turns, slow_count * fast_count, -1.0)


def front_inverse(re_im, grid_info, fast_offset):
    slow_count, fast_count = (grid_info[0], grid_info[1])
    phase_turns = index_ramp(slow_count, 2, 5, 0) * index_ramp(re_im[0].shape[3], 3, 5, fast_offset)
    re_im = rotate(re_im, phase_turns, slow_count * fast_count, 1.0)
    return apply_dft(re_im, slow_count, 1.0, 2)


def lead_phase(re_im, grid_info, ka_offset):
    slow_count, fast_count, tokens = (grid_info[0], grid_info[1], grid_info[2])
    lead_index = index_ramp(re_im[0].shape[2], 2, 5, ka_offset) + slow_count * index_ramp(
        fast_count, 3, 5, 0
    )
    return lead_index * index_ramp(tokens, 4, 5, 0)


def back_forward(re_im, grid_info, ka_offset):
    re_im = apply_dft(re_im, grid_info[1], -1.0, 3)
    re_im = rotate(re_im, lead_phase(re_im, grid_info, ka_offset), grid_info[3], -1.0)
    return apply_dft(re_im, grid_info[2], -1.0, 4)


def back_inverse(re_im, grid_info, ka_offset):
    re_im = apply_dft(re_im, grid_info[2], 1.0, 4)
    re_im = rotate(re_im, lead_phase(re_im, grid_info, ka_offset), grid_info[3], 1.0)
    return apply_dft(re_im, grid_info[1], 1.0, 3)


def to_channels(seq_rows):
    return lax.all_to_all(
        seq_rows.reshape(1, seq_rows.shape[0], seq_rows.shape[1]),
        "slow",
        split_axis=2,
        concat_axis=0,
        tiled=True,
    )


def merge_blocks(arrays, block_count):
    tokens = arrays[0].shape[0]
    pieces = [item.reshape(tokens, block_count, item.shape[1] // block_count) for item in arrays]
    return jnp.concatenate(pieces, axis=2).reshape(tokens, -1)


def split_columns(rows_major, widths):
    tokens, block_count = (rows_major.shape[0], rows_major.shape[1])
    result = []
    offset = 0
    for length in widths:
        result.append(
            rows_major[:, :, offset : offset + length].reshape(tokens, block_count * length)
        )
        offset += length
    return result


def real_blocks(real_part, imag_part, segments):
    pieces = []
    offset = 0
    for output_kind, length in segments:
        real_seg = real_part[:, offset : offset + length]
        imag_seg = imag_part[:, offset : offset + length]
        offset += length
        if output_kind == "pairs":
            stacked = jnp.transpose(jnp.stack((real_seg, imag_seg), axis=-1), (0, 2, 1, 3))
            pieces.append(stacked.reshape(stacked.shape[0], stacked.shape[1], 2 * length))
        else:
            pieces.append(jnp.transpose(real_seg, (0, 2, 1)))
    return jnp.concatenate(pieces, axis=2)


def segment_widths(segments):
    return [2 * length if output_kind == "pairs" else length for output_kind, length in segments]


def spread_forward(seq_rows, grid_info, fast_rank, segments):
    slow_count, fast_count = (grid_info[0], grid_info[1])
    blocks = to_channels(seq_rows).astype(jnp.float32)
    real_list = []
    imag_list = []
    offset = 0
    for length, packed in segments:
        segment = blocks[:, :, offset : offset + length]
        offset += length
        if packed:
            halves = segment.reshape(segment.shape[0], segment.shape[1], length // 2, 2)
            real_seg, imag_seg = (halves[..., 0], halves[..., 1])
        else:
            real_seg, imag_seg = (segment, jnp.zeros_like(segment))
        real_list.append(jnp.transpose(real_seg, (2, 0, 1)))
        imag_list.append(jnp.transpose(imag_seg, (2, 0, 1)))
    re_im = (
        jnp.concatenate(real_list, 0)[:, :, None, :],
        jnp.concatenate(imag_list, 0)[:, :, None, :],
    )
    re_im = front_forward(open_halves(re_im, grid_info, fast_rank), grid_info, fast_rank)
    re_im = (
        lax.all_to_all(re_im[0], "fast", split_axis=2, concat_axis=3, tiled=True),
        lax.all_to_all(re_im[1], "fast", split_axis=2, concat_axis=3, tiled=True),
    )
    return back_forward(re_im, grid_info, fast_rank * (slow_count // fast_count))


def spread_inverse(re_im, grid_info, fast_rank, slow_rank, segments):
    slow_count, fast_count, tokens, seq_length = grid_info
    re_im = back_inverse(re_im, grid_info, fast_rank * (slow_count // fast_count))
    re_im = (
        lax.all_to_all(re_im[0], "fast", split_axis=3, concat_axis=2, tiled=True),
        lax.all_to_all(re_im[1], "fast", split_axis=3, concat_axis=2, tiled=True),
    )
    re_im = front_inverse(re_im, grid_info, fast_rank)
    re_im = (
        lax.all_to_all(re_im[0], "slow", split_axis=2, concat_axis=1, tiled=True),
        lax.all_to_all(re_im[1], "slow", split_axis=2, concat_axis=1, tiled=True),
    )
    real_part, imag_part = fold_halves(
        re_im, positions(grid_info, 1, slow_rank, 1, fast_rank), seq_length
    )
    length = real_part.shape[0] // slow_count
    blocks = real_blocks(
        real_part.reshape(slow_count, length, tokens),
        imag_part.reshape(slow_count, length, tokens),
        segments,
    )
    rows_major = jnp.transpose(blocks, (1, 0, 2))
    return split_columns(rows_major, segment_widths(segments))


def regroup(re_im, length, local_groups):

    def by_group(values):
        values = values[:, :length]
        return values.reshape(
            (values.shape[0], local_groups, length // local_groups) + values.shape[2:]
        )

    return (by_group(re_im[0]), by_group(re_im[1]))


def flatten_pairs(re_im):

    def merged(values):
        return values.reshape(
            (values.shape[0], values.shape[1] * values.shape[2]) + values.shape[3:]
        )

    return (merged(re_im[0]), merged(re_im[1]))


def by_spectra(query_act, key_act, value_act, long_filter, out_grad):
    tokens, channels = query_act.shape
    groups = long_filter.shape[1]
    slow_count = lax.axis_size("slow")
    fast_count = lax.axis_size("fast")
    seq_length = tokens * slow_count * fast_count
    grid_info = (slow_count, fast_count, tokens, seq_length)
    group_width = channels // groups
    product = (key_act.astype(jnp.float32) * value_act.astype(jnp.float32)).astype(jnp.bfloat16)
    grad_in = (out_grad.astype(jnp.float32) * query_act.astype(jnp.float32)).astype(jnp.bfloat16)
    fast_rank = lax.axis_index("fast")
    slow_rank = lax.axis_index("slow")
    data_pairs = channels // (2 * slow_count)
    local_groups = groups // slow_count
    block_width = channels // slow_count
    spectra = spread_forward(
        merge_blocks((product, long_filter), slow_count),
        grid_info,
        fast_rank,
        ((block_width, True), (local_groups, False)),
    )
    prod_spec = regroup(spectra, data_pairs, local_groups)
    filter_spec = (spectra[0][:, data_pairs:, None], spectra[1][:, data_pairs:, None])
    convolved = spread_inverse(
        flatten_pairs(complex_times(prod_spec, filter_spec)),
        grid_info,
        fast_rank,
        slow_rank,
        (("pairs", data_pairs),),
    )[0]
    grad_spec = regroup(
        spread_forward(grad_in, grid_info, fast_rank, ((block_width, True),)),
        data_pairs,
        local_groups,
    )
    back_spec = flatten_pairs(conj_times(filter_spec, grad_spec))
    corr_spec = conj_times(prod_spec, grad_spec)
    joined = (
        jnp.concatenate((back_spec[0], jnp.sum(corr_spec[0], axis=2)), axis=1),
        jnp.concatenate((back_spec[1], jnp.sum(corr_spec[1], axis=2)), axis=1),
    )
    backward, filter_sum = spread_inverse(
        joined, grid_info, fast_rank, slow_rank, (("pairs", data_pairs), ("real", local_groups))
    )
    scale = 1.0 / math.sqrt(seq_length * group_width)
    mixed_out = (query_act.astype(jnp.float32) * convolved).astype(jnp.bfloat16)
    query_grad = (out_grad.astype(jnp.float32) * convolved).astype(jnp.bfloat16)
    key_grad = (backward * value_act.astype(jnp.float32)).astype(jnp.bfloat16)
    value_grad = (backward * key_act.astype(jnp.float32)).astype(jnp.bfloat16)
    return (mixed_out, query_grad, key_grad, value_grad, filter_sum * scale)


f32 = jnp.float32
bf16 = jnp.bfloat16
EXTRA_ROWS = 2


def dot(left, right):
    return jnp.dot(left, right, preferred_element_type=f32)


def dot_nt(left, right):
    return lax.dot_general(left, right, (((1,), (1,)), ((), ())), preferred_element_type=f32)


def ramp(shape, dim):
    return lax.broadcasted_iota(jnp.int32, shape, dim)


def flip_matrix(size):
    return (ramp((size, size), 0) + ramp((size, size), 1) == size - 1).astype(bf16)


def gate_kernel(query, key, value, filt, grad, sent, queries, keys, values, taps, grads, done):
    copies = [
        pltpu.make_async_copy(source, target, done.at[at])
        for at, (source, target) in enumerate(
            ((grad, grads), (query, queries), (key, keys), (value, values), (filt, taps))
        )
    ]
    for copy in copies:
        copy.start()
    tokens, channels = queries.shape
    groups = taps.shape[0]
    width = channels // groups
    rows = 2 * width + EXTRA_ROWS
    for copy in copies:
        copy.wait()
    grad_in = (grads[...].astype(f32) * queries[...].astype(f32)).astype(bf16)
    flipped = dot(flip_matrix(tokens), grad_in)
    product = (keys[...].astype(f32) * values[...].astype(f32)).astype(bf16)
    columns = product.astype(f32).T.astype(bf16)
    flipped = flipped.T.astype(bf16)
    for group in range(groups):
        at = group * rows
        part = slice(group * width, (group + 1) * width)
        sent[at : at + width, :] = columns[part]
        sent[at + width : at + 2 * width, :] = flipped[part]
        sent[at + 2 * width : at + rows, :] = jnp.broadcast_to(
            taps[group : group + 1, :], (EXTRA_ROWS, tokens)
        )


def turn(square):
    return pltpu.roll(square, 0, 1, stride=1, stride_axis=0)


def group_kernel(scale, width, got, sent, streams, padded, toeplitz):
    rows, tokens = 2 * width + EXTRA_ROWS, got.shape[1]
    blocks = got.shape[0] // rows
    pairs = blocks // 2
    row, lane = ramp((tokens, tokens), 0), ramp((tokens, tokens), 1)
    for pair in range(pairs):
        for half in range(2):
            block = 2 * pair + half
            lanes = slice(half * tokens, (half + 1) * tokens)
            at = 2 * width * pair
            streams[at : at + width, lanes] = got[block * rows : block * rows + width, :]
            streams[at + width : at + 2 * width, lanes] = got[
                (blocks - 1 - block) * rows + width : (blocks - 1 - block) * rows + 2 * width, :
            ]
    for block in range(blocks):
        padded[block * width : (block + 1) * width, :] = got[
            block * rows + width : block * rows + 2 * width, :
        ]
    padded[blocks * width :, :] = jnp.zeros((blocks * width, tokens), bf16)

    ordered = jnp.concatenate(
        [got[block * rows : block * rows + width, :] for block in range(blocks)], axis=0
    )
    ordered = ordered.astype(f32).T.astype(bf16)
    band = jnp.zeros((tokens, tokens), f32)
    before = jnp.zeros((tokens, tokens), f32)
    which = ramp((EXTRA_ROWS, tokens), 0)
    for pair in range(pairs):
        depth = -(-2 * (pair + 1) * width // tokens) * tokens
        columns = [
            padded[pl.ds((blocks - 1 - lag) * width, depth), :] for lag in (2 * pair, 2 * pair + 1)
        ]
        outer = dot(ordered[:, :depth], jnp.concatenate(columns, axis=1))
        for half in range(2):
            block = 2 * pair + half
            taps = got[block * rows + 2 * width : block * rows + 2 * width + 1, :].astype(f32)
            turned = turn(jnp.broadcast_to(taps, (tokens, tokens)))
            toeplitz[block] = jnp.where(lane >= row, turned, band).astype(bf16)
            band = turned
            turned = turn(outer[:, half * tokens : (half + 1) * tokens])
            joined = jnp.where(lane >= row, turned, before)
            before = turned
            value = jnp.sum(joined, axis=0, keepdims=True) * scale
            high = value.astype(bf16).astype(f32)
            pieces = jnp.where(which == 0, high, value - high)
            place = (blocks - 1 - block) * rows + 2 * width
            sent[place : place + EXTRA_ROWS, :] = pieces.astype(bf16)

    total = None
    for pair in range(pairs):
        left = jnp.zeros((tokens, tokens), bf16) if pair == 0 else toeplitz[2 * pair - 1]
        weights = jnp.concatenate(
            (
                jnp.concatenate((toeplitz[2 * pair], toeplitz[2 * pair + 1]), axis=1),
                jnp.concatenate((left, toeplitz[2 * pair]), axis=1),
            ),
            axis=0,
        )
        skip = 2 * width * pair
        term = dot(streams[0 : 2 * width * pairs - skip, :], weights)
        total = term if pair == 0 else jnp.concatenate((total[:skip], total[skip:] + term), axis=0)
    for pair in range(pairs):
        for half in range(2):
            block = 2 * pair + half
            lanes = slice(half * tokens, (half + 1) * tokens)
            at = 2 * width * pair
            sent[block * rows : block * rows + width, :] = total[at : at + width, lanes].astype(bf16)
            place = (blocks - 1 - block) * rows + width
            sent[place : place + width, :] = total[
                at + width : at + 2 * width, lanes
            ].astype(bf16)


def output_kernel(
    width, got, query, key, value, grad, mixed, query_grad, key_grad, value_grad, filter_grad
):
    rows, tokens = 2 * width + EXTRA_ROWS, got.shape[1]
    blocks = got.shape[0] // rows

    def collect(first, count):
        return jnp.concatenate(
            [got[at * rows + first : at * rows + first + count, :] for at in range(blocks)], axis=0
        )

    flip = flip_matrix(tokens)
    convolved = collect(0, width).astype(f32).T
    mixed[...] = (query[...].astype(f32) * convolved).astype(bf16)
    query_grad[...] = (grad[...].astype(f32) * convolved).astype(bf16)
    backward = dot_nt(flip, collect(width, width))
    key_grad[...] = (backward * value[...].astype(f32)).astype(bf16)
    value_grad[...] = (backward * key[...].astype(f32)).astype(bf16)
    high, low = collect(2 * width, 1), collect(2 * width + 1, 1)
    filter_grad[...] = dot(high, flip) + dot(low, flip)


def by_groups(query_act, key_act, value_act, long_filter, out_grad):
    tokens, channels = query_act.shape
    groups = long_filter.shape[1]
    width = channels // groups
    rows = 2 * width + EXTRA_ROWS
    scale = 1.0 / math.sqrt(tokens * groups * width)
    chunks = jax.ShapeDtypeStruct((groups * rows, tokens), bf16)

    def exchange(sent):
        pieces = sent.reshape(groups, rows // 2, 2, tokens)
        pieces = lax.all_to_all(pieces, ("slow", "fast"), split_axis=0, concat_axis=0, tiled=True)
        return pieces.reshape(groups * rows, tokens)

    act = pltpu.VMEM((tokens, channels), bf16)
    sent = pl.pallas_call(
        gate_kernel,
        out_shape=chunks,
        in_specs=[pl.BlockSpec(memory_space=pltpu.HBM)] * 5,
        scratch_shapes=[
            act,
            act,
            act,
            pltpu.VMEM((groups, tokens), bf16),
            act,
            pltpu.SemaphoreType.DMA((5,)),
        ],
        compiler_params=pltpu.CompilerParams(vmem_limit_bytes=8 * 2**20),
        name="gate",
    )(
        *(
            pltpu.with_memory_space_constraint(array, pltpu.HBM)
            for array in (query_act, key_act, value_act, long_filter.T, out_grad)
        )
    )
    got = exchange(sent)
    sent = pl.pallas_call(
        functools.partial(group_kernel, scale, width),
        out_shape=chunks,
        scratch_shapes=[
            pltpu.VMEM((channels, 2 * tokens), bf16),
            pltpu.VMEM((2 * channels, tokens), bf16),
            pltpu.VMEM((groups, tokens, tokens), bf16),
        ],
        compiler_params=pltpu.CompilerParams(vmem_limit_bytes=16 * 2**20),
        name="group",
    )(got)
    got = exchange(sent)
    like = jax.ShapeDtypeStruct((tokens, channels), bf16)
    *acts, filter_grad = pl.pallas_call(
        functools.partial(output_kernel, width),
        out_shape=(like, like, like, like, jax.ShapeDtypeStruct((groups, tokens), f32)),
        compiler_params=pltpu.CompilerParams(vmem_limit_bytes=8 * 2**20),
        name="outputs",
    )(got, query_act, key_act, value_act, out_grad)
    return (*acts, filter_grad.T)


def on_device(query_act, key_act, value_act, long_filter, out_grad):
    tokens, channels = query_act.shape
    groups = long_filter.shape[1]
    devices = lax.axis_size("slow") * lax.axis_size("fast")
    if devices == groups and tokens == 128 and channels == 16 * groups and groups % 4 == 0:
        return by_groups(query_act, key_act, value_act, long_filter, out_grad)
    return by_spectra(query_act, key_act, value_act, long_filter, out_grad)


def solution(mesh):
    placed = (
        P(("slow", "fast"), None),
        P(("slow", "fast"), None),
        P(("slow", "fast"), None),
        P(("slow", "fast"), None),
        P(("slow", "fast"), None),
    )
    return jax.shard_map(
        on_device,
        mesh=mesh,
        in_specs=placed,
        out_specs=(
            P(("slow", "fast"), None),
            P(("slow", "fast"), None),
            P(("slow", "fast"), None),
            P(("slow", "fast"), None),
            P(("slow", "fast"), None),
        ),
        check_vma=False,
    )
```

```python
import functools
import math

import jax
import jax.numpy as jnp
from jax import lax
from jax.experimental import pallas as pl
from jax.experimental.pallas import tpu as pltpu
from jax.sharding import PartitionSpec as P

highest = lax.Precision.HIGHEST


def index_ramp(points, along, ndim, offset):
    shape_list = [1] * ndim
    shape_list[along] = points
    return (jnp.arange(points, dtype=jnp.int32) + offset).reshape(shape_list)


def apply_dft(re_im, points, direction, along):
    index_row = jnp.arange(points, dtype=jnp.int32)
    phase_turns = index_row[:, None] * index_row[None, :] % points
    phases = 2.0 * math.pi / points * phase_turns.astype(jnp.float32)
    cosine = jnp.cos(phases)
    sine_part = direction * jnp.sin(phases)

    def contract(values, matrix):
        result = jnp.tensordot(values, matrix, axes=((along,), (1,)), precision=highest)
        return jnp.moveaxis(result, -1, along)

    return (
        contract(re_im[0], cosine) - contract(re_im[1], sine_part),
        contract(re_im[0], sine_part) + contract(re_im[1], cosine),
    )


def rotate(re_im, phase_turns, period, direction):
    phases = 2.0 * math.pi / period * (phase_turns % period).astype(jnp.float32)
    cosine = jnp.cos(phases)
    sine_part = direction * jnp.sin(phases)
    return (re_im[0] * cosine - re_im[1] * sine_part, re_im[0] * sine_part + re_im[1] * cosine)


def complex_times(left, right):
    return (left[0] * right[0] - left[1] * right[1], left[0] * right[1] + left[1] * right[0])


def conj_times(left, right):
    return (left[0] * right[0] + left[1] * right[1], left[0] * right[1] - left[1] * right[0])


def positions(grid_info, slow_points, slow_offset, fast_points, fast_offset):
    fast_count, tokens = (grid_info[1], grid_info[2])
    block_index = index_ramp(slow_points, 2, 5, slow_offset) * fast_count + index_ramp(
        fast_points, 3, 5, fast_offset
    )
    return block_index * tokens + index_ramp(tokens, 4, 5, 0)


def open_halves(re_im, grid_info, fast_offset):
    token_place = positions(grid_info, re_im[0].shape[1], 0, re_im[0].shape[2], fast_offset)
    return rotate(
        (re_im[0][None], re_im[1][None]),
        index_ramp(2, 0, 5, 0) * token_place,
        2 * grid_info[3],
        -1.0,
    )


def fold_halves(re_im, token_place, seq_length):
    turned = rotate(re_im, index_ramp(2, 0, 5, 0) * token_place, 2 * seq_length, 1.0)
    scale = 0.5 / seq_length
    return (jnp.sum(turned[0], axis=0) * scale, jnp.sum(turned[1], axis=0) * scale)


def front_forward(re_im, grid_info, fast_offset):
    slow_count, fast_count = (grid_info[0], grid_info[1])
    re_im = apply_dft(re_im, slow_count, -1.0, 2)
    phase_turns = index_ramp(slow_count, 2, 5, 0) * index_ramp(re_im[0].shape[3], 3, 5, fast_offset)
    return rotate(re_im, phase_turns, slow_count * fast_count, -1.0)


def front_inverse(re_im, grid_info, fast_offset):
    slow_count, fast_count = (grid_info[0], grid_info[1])
    phase_turns = index_ramp(slow_count, 2, 5, 0) * index_ramp(re_im[0].shape[3], 3, 5, fast_offset)
    re_im = rotate(re_im, phase_turns, slow_count * fast_count, 1.0)
    return apply_dft(re_im, slow_count, 1.0, 2)


def lead_phase(re_im, grid_info, ka_offset):
    slow_count, fast_count, tokens = (grid_info[0], grid_info[1], grid_info[2])
    lead_index = index_ramp(re_im[0].shape[2], 2, 5, ka_offset) + slow_count * index_ramp(
        fast_count, 3, 5, 0
    )
    return lead_index * index_ramp(tokens, 4, 5, 0)


def back_forward(re_im, grid_info, ka_offset):
    re_im = apply_dft(re_im, grid_info[1], -1.0, 3)
    re_im = rotate(re_im, lead_phase(re_im, grid_info, ka_offset), grid_info[3], -1.0)
    return apply_dft(re_im, grid_info[2], -1.0, 4)


def back_inverse(re_im, grid_info, ka_offset):
    re_im = apply_dft(re_im, grid_info[2], 1.0, 4)
    re_im = rotate(re_im, lead_phase(re_im, grid_info, ka_offset), grid_info[3], 1.0)
    return apply_dft(re_im, grid_info[1], 1.0, 3)


def to_channels(seq_rows):
    return lax.all_to_all(
        seq_rows.reshape(1, seq_rows.shape[0], seq_rows.shape[1]),
        "slow",
        split_axis=2,
        concat_axis=0,
        tiled=True,
    )


def merge_blocks(arrays, block_count):
    tokens = arrays[0].shape[0]
    pieces = [item.reshape(tokens, block_count, item.shape[1] // block_count) for item in arrays]
    return jnp.concatenate(pieces, axis=2).reshape(tokens, -1)


def split_columns(rows_major, widths):
    tokens, block_count = (rows_major.shape[0], rows_major.shape[1])
    result = []
    offset = 0
    for length in widths:
        result.append(
            rows_major[:, :, offset : offset + length].reshape(tokens, block_count * length)
        )
        offset += length
    return result


def real_blocks(real_part, imag_part, segments):
    pieces = []
    offset = 0
    for output_kind, length in segments:
        real_seg = real_part[:, offset : offset + length]
        imag_seg = imag_part[:, offset : offset + length]
        offset += length
        if output_kind == "pairs":
            stacked = jnp.transpose(jnp.stack((real_seg, imag_seg), axis=-1), (0, 2, 1, 3))
            pieces.append(stacked.reshape(stacked.shape[0], stacked.shape[1], 2 * length))
        else:
            pieces.append(jnp.transpose(real_seg, (0, 2, 1)))
    return jnp.concatenate(pieces, axis=2)


def segment_widths(segments):
    return [2 * length if output_kind == "pairs" else length for output_kind, length in segments]


def spread_forward(seq_rows, grid_info, fast_rank, segments):
    slow_count, fast_count = (grid_info[0], grid_info[1])
    blocks = to_channels(seq_rows).astype(jnp.float32)
    real_list = []
    imag_list = []
    offset = 0
    for length, packed in segments:
        segment = blocks[:, :, offset : offset + length]
        offset += length
        if packed:
            halves = segment.reshape(segment.shape[0], segment.shape[1], length // 2, 2)
            real_seg, imag_seg = (halves[..., 0], halves[..., 1])
        else:
            real_seg, imag_seg = (segment, jnp.zeros_like(segment))
        real_list.append(jnp.transpose(real_seg, (2, 0, 1)))
        imag_list.append(jnp.transpose(imag_seg, (2, 0, 1)))
    re_im = (
        jnp.concatenate(real_list, 0)[:, :, None, :],
        jnp.concatenate(imag_list, 0)[:, :, None, :],
    )
    re_im = front_forward(open_halves(re_im, grid_info, fast_rank), grid_info, fast_rank)
    re_im = (
        lax.all_to_all(re_im[0], "fast", split_axis=2, concat_axis=3, tiled=True),
        lax.all_to_all(re_im[1], "fast", split_axis=2, concat_axis=3, tiled=True),
    )
    return back_forward(re_im, grid_info, fast_rank * (slow_count // fast_count))


def spread_inverse(re_im, grid_info, fast_rank, slow_rank, segments):
    slow_count, fast_count, tokens, seq_length = grid_info
    re_im = back_inverse(re_im, grid_info, fast_rank * (slow_count // fast_count))
    re_im = (
        lax.all_to_all(re_im[0], "fast", split_axis=3, concat_axis=2, tiled=True),
        lax.all_to_all(re_im[1], "fast", split_axis=3, concat_axis=2, tiled=True),
    )
    re_im = front_inverse(re_im, grid_info, fast_rank)
    re_im = (
        lax.all_to_all(re_im[0], "slow", split_axis=2, concat_axis=1, tiled=True),
        lax.all_to_all(re_im[1], "slow", split_axis=2, concat_axis=1, tiled=True),
    )
    real_part, imag_part = fold_halves(
        re_im, positions(grid_info, 1, slow_rank, 1, fast_rank), seq_length
    )
    length = real_part.shape[0] // slow_count
    blocks = real_blocks(
        real_part.reshape(slow_count, length, tokens),
        imag_part.reshape(slow_count, length, tokens),
        segments,
    )
    rows_major = jnp.transpose(blocks, (1, 0, 2))
    return split_columns(rows_major, segment_widths(segments))


def regroup(re_im, length, local_groups):

    def by_group(values):
        values = values[:, :length]
        return values.reshape(
            (values.shape[0], local_groups, length // local_groups) + values.shape[2:]
        )

    return (by_group(re_im[0]), by_group(re_im[1]))


def flatten_pairs(re_im):

    def merged(values):
        return values.reshape(
            (values.shape[0], values.shape[1] * values.shape[2]) + values.shape[3:]
        )

    return (merged(re_im[0]), merged(re_im[1]))


def by_spectra(query_act, key_act, value_act, long_filter, out_grad):
    tokens, channels = query_act.shape
    groups = long_filter.shape[1]
    slow_count = lax.axis_size("slow")
    fast_count = lax.axis_size("fast")
    seq_length = tokens * slow_count * fast_count
    grid_info = (slow_count, fast_count, tokens, seq_length)
    group_width = channels // groups
    product = (key_act.astype(jnp.float32) * value_act.astype(jnp.float32)).astype(jnp.bfloat16)
    grad_in = (out_grad.astype(jnp.float32) * query_act.astype(jnp.float32)).astype(jnp.bfloat16)
    fast_rank = lax.axis_index("fast")
    slow_rank = lax.axis_index("slow")
    data_pairs = channels // (2 * slow_count)
    local_groups = groups // slow_count
    block_width = channels // slow_count
    spectra = spread_forward(
        merge_blocks((product, long_filter), slow_count),
        grid_info,
        fast_rank,
        ((block_width, True), (local_groups, False)),
    )
    prod_spec = regroup(spectra, data_pairs, local_groups)
    filter_spec = (spectra[0][:, data_pairs:, None], spectra[1][:, data_pairs:, None])
    convolved = spread_inverse(
        flatten_pairs(complex_times(prod_spec, filter_spec)),
        grid_info,
        fast_rank,
        slow_rank,
        (("pairs", data_pairs),),
    )[0]
    grad_spec = regroup(
        spread_forward(grad_in, grid_info, fast_rank, ((block_width, True),)),
        data_pairs,
        local_groups,
    )
    back_spec = flatten_pairs(conj_times(filter_spec, grad_spec))
    corr_spec = conj_times(prod_spec, grad_spec)
    joined = (
        jnp.concatenate((back_spec[0], jnp.sum(corr_spec[0], axis=2)), axis=1),
        jnp.concatenate((back_spec[1], jnp.sum(corr_spec[1], axis=2)), axis=1),
    )
    backward, filter_sum = spread_inverse(
        joined, grid_info, fast_rank, slow_rank, (("pairs", data_pairs), ("real", local_groups))
    )
    scale = 1.0 / math.sqrt(seq_length * group_width)
    mixed_out = (query_act.astype(jnp.float32) * convolved).astype(jnp.bfloat16)
    query_grad = (out_grad.astype(jnp.float32) * convolved).astype(jnp.bfloat16)
    key_grad = (backward * value_act.astype(jnp.float32)).astype(jnp.bfloat16)
    value_grad = (backward * key_act.astype(jnp.float32)).astype(jnp.bfloat16)
    return (mixed_out, query_grad, key_grad, value_grad, filter_sum * scale)


f32 = jnp.float32
bf16 = jnp.bfloat16
EXTRA_ROWS = 2


def dot(left, right):
    return jnp.dot(left, right, preferred_element_type=f32)


def dot_nt(left, right):
    return lax.dot_general(left, right, (((1,), (1,)), ((), ())), preferred_element_type=f32)


def ramp(shape, dim):
    return lax.broadcasted_iota(jnp.int32, shape, dim)


def flip_matrix(size):
    return (ramp((size, size), 0) + ramp((size, size), 1) == size - 1).astype(bf16)


def eye_matrix(size):
    return (ramp((size, size), 0) == ramp((size, size), 1)).astype(bf16)


def gate_kernel(query, key, value, filt, grad, sent, queries, keys, values, taps, grads, done):
    copies = [
        pltpu.make_async_copy(source, target, done.at[at])
        for at, (source, target) in enumerate(
            ((grad, grads), (query, queries), (key, keys), (value, values), (filt, taps))
        )
    ]
    for copy in copies:
        copy.start()
    tokens, channels = queries.shape
    groups = taps.shape[0]
    width = channels // groups
    rows = 2 * width + EXTRA_ROWS
    for copy in copies:
        copy.wait()
    grad_in = (grads[...].astype(f32) * queries[...].astype(f32)).astype(bf16)
    flipped = dot(flip_matrix(tokens), grad_in)
    product = (keys[...].astype(f32) * values[...].astype(f32)).astype(bf16)
    columns = product.astype(f32).T.astype(bf16)
    flipped = flipped.T.astype(bf16)
    for group in range(groups):
        at = group * rows
        part = slice(group * width, (group + 1) * width)
        sent[at : at + width, :] = columns[part]
        sent[at + width : at + 2 * width, :] = flipped[part]
        sent[at + 2 * width : at + rows, :] = jnp.broadcast_to(
            taps[group : group + 1, :], (EXTRA_ROWS, tokens)
        )


def turn(square):
    return pltpu.roll(square, 0, 1, stride=1, stride_axis=0)


def group_kernel(scale, width, got, sent, streams, padded):
    rows, tokens = 2 * width + EXTRA_ROWS, got.shape[1]
    blocks = got.shape[0] // rows
    pairs = blocks // 2
    row, lane = ramp((tokens, tokens), 0), ramp((tokens, tokens), 1)
    for pair in range(pairs):
        for half in range(2):
            block = 2 * pair + half
            lanes = slice(half * tokens, (half + 1) * tokens)
            at = 2 * width * pair
            streams[at : at + width, lanes] = got[block * rows : block * rows + width, :]
            streams[at + width : at + 2 * width, lanes] = got[
                (blocks - 1 - block) * rows + width : (blocks - 1 - block) * rows + 2 * width, :
            ]
    for block in range(blocks):
        padded[block * width : (block + 1) * width, :] = got[
            block * rows + width : block * rows + 2 * width, :
        ]
    padded[blocks * width :, :] = jnp.zeros((blocks * width, tokens), bf16)

    ordered = jnp.concatenate(
        [got[block * rows : block * rows + width, :] for block in range(blocks)], axis=0
    )
    ordered = ordered.astype(f32).T.astype(bf16)
    band = jnp.zeros((tokens, tokens), f32)
    left = jnp.zeros((tokens, tokens), bf16)
    before = jnp.zeros((tokens, tokens), f32)
    which = ramp((EXTRA_ROWS, tokens), 0)
    total = None
    for pair in range(pairs):
        bands = []
        for block in (2 * pair, 2 * pair + 1):
            taps = got[block * rows + 2 * width : block * rows + 2 * width + 1, :].astype(f32)
            turned = turn(jnp.broadcast_to(taps, (tokens, tokens)))
            bands.append(jnp.where(lane >= row, turned, band).astype(bf16))
            band = turned
        depth = -(-2 * (pair + 1) * width // tokens) * tokens
        columns = [
            padded[pl.ds((blocks - 1 - lag) * width, depth), :] for lag in (2 * pair, 2 * pair + 1)
        ]
        outer = dot(ordered[:, :depth], jnp.concatenate(columns, axis=1))
        for half in range(2):
            block = 2 * pair + half
            turned = turn(outer[:, half * tokens : (half + 1) * tokens])
            joined = jnp.where(lane >= row, turned, before)
            before = turned
            value = jnp.sum(joined, axis=0, keepdims=True) * scale
            high = value.astype(bf16).astype(f32)
            pieces = jnp.where(which == 0, high, value - high)
            place = (blocks - 1 - block) * rows + 2 * width
            sent[place : place + EXTRA_ROWS, :] = pieces.astype(bf16)
        weights = jnp.concatenate(
            (
                jnp.concatenate((bands[0], bands[1]), axis=1),
                jnp.concatenate((left, bands[0]), axis=1),
            ),
            axis=0,
        )
        left = bands[1]
        skip = 2 * width * pair
        term = dot(streams[0 : 2 * width * pairs - skip, :], weights)
        total = term if pair == 0 else jnp.concatenate((total[:skip], total[skip:] + term), axis=0)
    for pair in range(pairs):
        for half in range(2):
            block = 2 * pair + half
            lanes = slice(half * tokens, (half + 1) * tokens)
            at = 2 * width * pair
            sent[block * rows : block * rows + width, :] = total[at : at + width, lanes].astype(bf16)
            place = (blocks - 1 - block) * rows + width
            sent[place : place + width, :] = total[
                at + width : at + 2 * width, lanes
            ].astype(bf16)


def output_kernel(
    width, got, query, key, value, grad, mixed, query_grad, key_grad, value_grad, filter_grad
):
    rows, tokens = 2 * width + EXTRA_ROWS, got.shape[1]
    blocks = got.shape[0] // rows

    def collect(first, count):
        return jnp.concatenate(
            [got[at * rows + first : at * rows + first + count, :] for at in range(blocks)], axis=0
        )

    flip = flip_matrix(tokens)
    convolved = dot_nt(eye_matrix(tokens), collect(0, width))
    mixed[...] = (query[...].astype(f32) * convolved).astype(bf16)
    query_grad[...] = (grad[...].astype(f32) * convolved).astype(bf16)
    backward = dot_nt(flip, collect(width, width))
    key_grad[...] = (backward * value[...].astype(f32)).astype(bf16)
    value_grad[...] = (backward * key[...].astype(f32)).astype(bf16)
    high, low = collect(2 * width, 1), collect(2 * width + 1, 1)
    filter_grad[...] = dot(high, flip) + dot(low, flip)


def by_groups(query_act, key_act, value_act, long_filter, out_grad):
    tokens, channels = query_act.shape
    groups = long_filter.shape[1]
    width = channels // groups
    rows = 2 * width + EXTRA_ROWS
    scale = 1.0 / math.sqrt(tokens * groups * width)
    chunks = jax.ShapeDtypeStruct((groups * rows, tokens), bf16)

    def exchange(sent):
        pieces = sent.reshape(groups, rows // 2, 2, tokens)
        pieces = lax.all_to_all(pieces, ("slow", "fast"), split_axis=0, concat_axis=0, tiled=True)
        return pieces.reshape(groups * rows, tokens)

    act = pltpu.VMEM((tokens, channels), bf16)
    sent = pl.pallas_call(
        gate_kernel,
        out_shape=chunks,
        in_specs=[pl.BlockSpec(memory_space=pltpu.HBM)] * 5,
        scratch_shapes=[
            act,
            act,
            act,
            pltpu.VMEM((groups, tokens), bf16),
            act,
            pltpu.SemaphoreType.DMA((5,)),
        ],
        compiler_params=pltpu.CompilerParams(vmem_limit_bytes=8 * 2**20),
        name="gate",
    )(
        *(
            pltpu.with_memory_space_constraint(array, pltpu.HBM)
            for array in (query_act, key_act, value_act, long_filter.T, out_grad)
        )
    )
    got = exchange(sent)
    sent = pl.pallas_call(
        functools.partial(group_kernel, scale, width),
        out_shape=chunks,
        scratch_shapes=[
            pltpu.VMEM((channels, 2 * tokens), bf16),
            pltpu.VMEM((2 * channels, tokens), bf16),
        ],
        compiler_params=pltpu.CompilerParams(vmem_limit_bytes=16 * 2**20),
        name="group",
    )(got)
    got = exchange(sent)
    like = jax.ShapeDtypeStruct((tokens, channels), bf16)
    *acts, filter_grad = pl.pallas_call(
        functools.partial(output_kernel, width),
        out_shape=(like, like, like, like, jax.ShapeDtypeStruct((groups, tokens), f32)),
        compiler_params=pltpu.CompilerParams(vmem_limit_bytes=8 * 2**20),
        name="outputs",
    )(got, query_act, key_act, value_act, out_grad)
    return (*acts, filter_grad.T)


def on_device(query_act, key_act, value_act, long_filter, out_grad):
    tokens, channels = query_act.shape
    groups = long_filter.shape[1]
    devices = lax.axis_size("slow") * lax.axis_size("fast")
    if devices == groups and tokens == 128 and channels == 16 * groups and groups % 4 == 0:
        return by_groups(query_act, key_act, value_act, long_filter, out_grad)
    return by_spectra(query_act, key_act, value_act, long_filter, out_grad)


def solution(mesh):
    placed = (
        P(("slow", "fast"), None),
        P(("slow", "fast"), None),
        P(("slow", "fast"), None),
        P(("slow", "fast"), None),
        P(("slow", "fast"), None),
    )
    return jax.shard_map(
        on_device,
        mesh=mesh,
        in_specs=placed,
        out_specs=(
            P(("slow", "fast"), None),
            P(("slow", "fast"), None),
            P(("slow", "fast"), None),
            P(("slow", "fast"), None),
            P(("slow", "fast"), None),
        ),
        check_vma=False,
    )
```

```python
import functools
import math

import jax
import jax.numpy as jnp
from jax import lax
from jax.experimental import pallas as pl
from jax.experimental.pallas import tpu as pltpu
from jax.sharding import PartitionSpec as P

highest = lax.Precision.HIGHEST


def index_ramp(points, along, ndim, offset):
    shape_list = [1] * ndim
    shape_list[along] = points
    return (jnp.arange(points, dtype=jnp.int32) + offset).reshape(shape_list)


def apply_dft(re_im, points, direction, along):
    index_row = jnp.arange(points, dtype=jnp.int32)
    phase_turns = index_row[:, None] * index_row[None, :] % points
    phases = 2.0 * math.pi / points * phase_turns.astype(jnp.float32)
    cosine = jnp.cos(phases)
    sine_part = direction * jnp.sin(phases)

    def contract(values, matrix):
        result = jnp.tensordot(values, matrix, axes=((along,), (1,)), precision=highest)
        return jnp.moveaxis(result, -1, along)

    return (
        contract(re_im[0], cosine) - contract(re_im[1], sine_part),
        contract(re_im[0], sine_part) + contract(re_im[1], cosine),
    )


def rotate(re_im, phase_turns, period, direction):
    phases = 2.0 * math.pi / period * (phase_turns % period).astype(jnp.float32)
    cosine = jnp.cos(phases)
    sine_part = direction * jnp.sin(phases)
    return (re_im[0] * cosine - re_im[1] * sine_part, re_im[0] * sine_part + re_im[1] * cosine)


def complex_times(left, right):
    return (left[0] * right[0] - left[1] * right[1], left[0] * right[1] + left[1] * right[0])


def conj_times(left, right):
    return (left[0] * right[0] + left[1] * right[1], left[0] * right[1] - left[1] * right[0])


def positions(grid_info, slow_points, slow_offset, fast_points, fast_offset):
    fast_count, tokens = (grid_info[1], grid_info[2])
    block_index = index_ramp(slow_points, 2, 5, slow_offset) * fast_count + index_ramp(
        fast_points, 3, 5, fast_offset
    )
    return block_index * tokens + index_ramp(tokens, 4, 5, 0)


def open_halves(re_im, grid_info, fast_offset):
    token_place = positions(grid_info, re_im[0].shape[1], 0, re_im[0].shape[2], fast_offset)
    return rotate(
        (re_im[0][None], re_im[1][None]),
        index_ramp(2, 0, 5, 0) * token_place,
        2 * grid_info[3],
        -1.0,
    )


def fold_halves(re_im, token_place, seq_length):
    turned = rotate(re_im, index_ramp(2, 0, 5, 0) * token_place, 2 * seq_length, 1.0)
    scale = 0.5 / seq_length
    return (jnp.sum(turned[0], axis=0) * scale, jnp.sum(turned[1], axis=0) * scale)


def front_forward(re_im, grid_info, fast_offset):
    slow_count, fast_count = (grid_info[0], grid_info[1])
    re_im = apply_dft(re_im, slow_count, -1.0, 2)
    phase_turns = index_ramp(slow_count, 2, 5, 0) * index_ramp(re_im[0].shape[3], 3, 5, fast_offset)
    return rotate(re_im, phase_turns, slow_count * fast_count, -1.0)


def front_inverse(re_im, grid_info, fast_offset):
    slow_count, fast_count = (grid_info[0], grid_info[1])
    phase_turns = index_ramp(slow_count, 2, 5, 0) * index_ramp(re_im[0].shape[3], 3, 5, fast_offset)
    re_im = rotate(re_im, phase_turns, slow_count * fast_count, 1.0)
    return apply_dft(re_im, slow_count, 1.0, 2)


def lead_phase(re_im, grid_info, ka_offset):
    slow_count, fast_count, tokens = (grid_info[0], grid_info[1], grid_info[2])
    lead_index = index_ramp(re_im[0].shape[2], 2, 5, ka_offset) + slow_count * index_ramp(
        fast_count, 3, 5, 0
    )
    return lead_index * index_ramp(tokens, 4, 5, 0)


def back_forward(re_im, grid_info, ka_offset):
    re_im = apply_dft(re_im, grid_info[1], -1.0, 3)
    re_im = rotate(re_im, lead_phase(re_im, grid_info, ka_offset), grid_info[3], -1.0)
    return apply_dft(re_im, grid_info[2], -1.0, 4)


def back_inverse(re_im, grid_info, ka_offset):
    re_im = apply_dft(re_im, grid_info[2], 1.0, 4)
    re_im = rotate(re_im, lead_phase(re_im, grid_info, ka_offset), grid_info[3], 1.0)
    return apply_dft(re_im, grid_info[1], 1.0, 3)


def to_channels(seq_rows):
    return lax.all_to_all(
        seq_rows.reshape(1, seq_rows.shape[0], seq_rows.shape[1]),
        "slow",
        split_axis=2,
        concat_axis=0,
        tiled=True,
    )


def merge_blocks(arrays, block_count):
    tokens = arrays[0].shape[0]
    pieces = [item.reshape(tokens, block_count, item.shape[1] // block_count) for item in arrays]
    return jnp.concatenate(pieces, axis=2).reshape(tokens, -1)


def split_columns(rows_major, widths):
    tokens, block_count = (rows_major.shape[0], rows_major.shape[1])
    result = []
    offset = 0
    for length in widths:
        result.append(
            rows_major[:, :, offset : offset + length].reshape(tokens, block_count * length)
        )
        offset += length
    return result


def real_blocks(real_part, imag_part, segments):
    pieces = []
    offset = 0
    for output_kind, length in segments:
        real_seg = real_part[:, offset : offset + length]
        imag_seg = imag_part[:, offset : offset + length]
        offset += length
        if output_kind == "pairs":
            stacked = jnp.transpose(jnp.stack((real_seg, imag_seg), axis=-1), (0, 2, 1, 3))
            pieces.append(stacked.reshape(stacked.shape[0], stacked.shape[1], 2 * length))
        else:
            pieces.append(jnp.transpose(real_seg, (0, 2, 1)))
    return jnp.concatenate(pieces, axis=2)


def segment_widths(segments):
    return [2 * length if output_kind == "pairs" else length for output_kind, length in segments]


def spread_forward(seq_rows, grid_info, fast_rank, segments):
    slow_count, fast_count = (grid_info[0], grid_info[1])
    blocks = to_channels(seq_rows).astype(jnp.float32)
    real_list = []
    imag_list = []
    offset = 0
    for length, packed in segments:
        segment = blocks[:, :, offset : offset + length]
        offset += length
        if packed:
            halves = segment.reshape(segment.shape[0], segment.shape[1], length // 2, 2)
            real_seg, imag_seg = (halves[..., 0], halves[..., 1])
        else:
            real_seg, imag_seg = (segment, jnp.zeros_like(segment))
        real_list.append(jnp.transpose(real_seg, (2, 0, 1)))
        imag_list.append(jnp.transpose(imag_seg, (2, 0, 1)))
    re_im = (
        jnp.concatenate(real_list, 0)[:, :, None, :],
        jnp.concatenate(imag_list, 0)[:, :, None, :],
    )
    re_im = front_forward(open_halves(re_im, grid_info, fast_rank), grid_info, fast_rank)
    re_im = (
        lax.all_to_all(re_im[0], "fast", split_axis=2, concat_axis=3, tiled=True),
        lax.all_to_all(re_im[1], "fast", split_axis=2, concat_axis=3, tiled=True),
    )
    return back_forward(re_im, grid_info, fast_rank * (slow_count // fast_count))


def spread_inverse(re_im, grid_info, fast_rank, slow_rank, segments):
    slow_count, fast_count, tokens, seq_length = grid_info
    re_im = back_inverse(re_im, grid_info, fast_rank * (slow_count // fast_count))
    re_im = (
        lax.all_to_all(re_im[0], "fast", split_axis=3, concat_axis=2, tiled=True),
        lax.all_to_all(re_im[1], "fast", split_axis=3, concat_axis=2, tiled=True),
    )
    re_im = front_inverse(re_im, grid_info, fast_rank)
    re_im = (
        lax.all_to_all(re_im[0], "slow", split_axis=2, concat_axis=1, tiled=True),
        lax.all_to_all(re_im[1], "slow", split_axis=2, concat_axis=1, tiled=True),
    )
    real_part, imag_part = fold_halves(
        re_im, positions(grid_info, 1, slow_rank, 1, fast_rank), seq_length
    )
    length = real_part.shape[0] // slow_count
    blocks = real_blocks(
        real_part.reshape(slow_count, length, tokens),
        imag_part.reshape(slow_count, length, tokens),
        segments,
    )
    rows_major = jnp.transpose(blocks, (1, 0, 2))
    return split_columns(rows_major, segment_widths(segments))


def regroup(re_im, length, local_groups):

    def by_group(values):
        values = values[:, :length]
        return values.reshape(
            (values.shape[0], local_groups, length // local_groups) + values.shape[2:]
        )

    return (by_group(re_im[0]), by_group(re_im[1]))


def flatten_pairs(re_im):

    def merged(values):
        return values.reshape(
            (values.shape[0], values.shape[1] * values.shape[2]) + values.shape[3:]
        )

    return (merged(re_im[0]), merged(re_im[1]))


def by_spectra(query_act, key_act, value_act, long_filter, out_grad):
    tokens, channels = query_act.shape
    groups = long_filter.shape[1]
    slow_count = lax.axis_size("slow")
    fast_count = lax.axis_size("fast")
    seq_length = tokens * slow_count * fast_count
    grid_info = (slow_count, fast_count, tokens, seq_length)
    group_width = channels // groups
    product = (key_act.astype(jnp.float32) * value_act.astype(jnp.float32)).astype(jnp.bfloat16)
    grad_in = (out_grad.astype(jnp.float32) * query_act.astype(jnp.float32)).astype(jnp.bfloat16)
    fast_rank = lax.axis_index("fast")
    slow_rank = lax.axis_index("slow")
    data_pairs = channels // (2 * slow_count)
    local_groups = groups // slow_count
    block_width = channels // slow_count
    spectra = spread_forward(
        merge_blocks((product, long_filter), slow_count),
        grid_info,
        fast_rank,
        ((block_width, True), (local_groups, False)),
    )
    prod_spec = regroup(spectra, data_pairs, local_groups)
    filter_spec = (spectra[0][:, data_pairs:, None], spectra[1][:, data_pairs:, None])
    convolved = spread_inverse(
        flatten_pairs(complex_times(prod_spec, filter_spec)),
        grid_info,
        fast_rank,
        slow_rank,
        (("pairs", data_pairs),),
    )[0]
    grad_spec = regroup(
        spread_forward(grad_in, grid_info, fast_rank, ((block_width, True),)),
        data_pairs,
        local_groups,
    )
    back_spec = flatten_pairs(conj_times(filter_spec, grad_spec))
    corr_spec = conj_times(prod_spec, grad_spec)
    joined = (
        jnp.concatenate((back_spec[0], jnp.sum(corr_spec[0], axis=2)), axis=1),
        jnp.concatenate((back_spec[1], jnp.sum(corr_spec[1], axis=2)), axis=1),
    )
    backward, filter_sum = spread_inverse(
        joined, grid_info, fast_rank, slow_rank, (("pairs", data_pairs), ("real", local_groups))
    )
    scale = 1.0 / math.sqrt(seq_length * group_width)
    mixed_out = (query_act.astype(jnp.float32) * convolved).astype(jnp.bfloat16)
    query_grad = (out_grad.astype(jnp.float32) * convolved).astype(jnp.bfloat16)
    key_grad = (backward * value_act.astype(jnp.float32)).astype(jnp.bfloat16)
    value_grad = (backward * key_act.astype(jnp.float32)).astype(jnp.bfloat16)
    return (mixed_out, query_grad, key_grad, value_grad, filter_sum * scale)


f32 = jnp.float32
bf16 = jnp.bfloat16
EXTRA_ROWS = 2


def dot(left, right):
    return jnp.dot(left, right, preferred_element_type=f32)


def dot_nt(left, right):
    return lax.dot_general(left, right, (((1,), (1,)), ((), ())), preferred_element_type=f32)


def ramp(shape, dim):
    return lax.broadcasted_iota(jnp.int32, shape, dim)


def flip_matrix(size):
    return (ramp((size, size), 0) + ramp((size, size), 1) == size - 1).astype(bf16)


def eye_matrix(size):
    return (ramp((size, size), 0) == ramp((size, size), 1)).astype(bf16)


def gate_kernel(query, key, value, filt, grad, sent, queries, keys, values, taps, grads, done):
    copies = [
        pltpu.make_async_copy(source, target, done.at[at])
        for at, (source, target) in enumerate(
            ((grad, grads), (query, queries), (key, keys), (value, values), (filt, taps))
        )
    ]
    for copy in copies:
        copy.start()
    tokens, channels = queries.shape
    groups = taps.shape[0]
    width = channels // groups
    rows = 2 * width + EXTRA_ROWS
    for copy in copies:
        copy.wait()
    grad_in = (grads[...].astype(f32) * queries[...].astype(f32)).astype(bf16)
    flipped = dot(flip_matrix(tokens), grad_in)
    product = (keys[...].astype(f32) * values[...].astype(f32)).astype(bf16)
    columns = product.astype(f32).T.astype(bf16)
    flipped = flipped.T.astype(bf16)
    for group in range(groups):
        at = group * rows
        part = slice(group * width, (group + 1) * width)
        sent[at : at + width, :] = columns[part]
        sent[at + width : at + 2 * width, :] = flipped[part]
        sent[at + 2 * width : at + rows, :] = jnp.broadcast_to(
            taps[group : group + 1, :], (EXTRA_ROWS, tokens)
        )


def turn(square):
    return pltpu.roll(square, 0, 1, stride=1, stride_axis=0)


def group_kernel(scale, width, got, sent, streams, padded):
    rows, tokens = 2 * width + EXTRA_ROWS, got.shape[1]
    blocks = got.shape[0] // rows
    pairs = blocks // 2
    row, lane = ramp((tokens, tokens), 0), ramp((tokens, tokens), 1)
    for pair in range(pairs):
        for half in range(2):
            block = 2 * pair + half
            lanes = slice(half * tokens, (half + 1) * tokens)
            at = 2 * width * pair
            streams[at : at + width, lanes] = got[block * rows : block * rows + width, :]
            streams[at + width : at + 2 * width, lanes] = got[
                (blocks - 1 - block) * rows + width : (blocks - 1 - block) * rows + 2 * width, :
            ]
    for block in range(blocks):
        padded[block * width : (block + 1) * width, :] = got[
            block * rows + width : block * rows + 2 * width, :
        ]
    padded[blocks * width :, :] = jnp.zeros((blocks * width, tokens), bf16)

    ordered = jnp.concatenate(
        [got[block * rows : block * rows + width, :] for block in range(blocks)], axis=0
    )
    ordered = ordered.astype(f32).T.astype(bf16)
    band = jnp.zeros((tokens, tokens), f32)
    left = jnp.zeros((tokens, tokens), bf16)
    before = jnp.zeros((tokens, tokens), f32)
    which = ramp((EXTRA_ROWS, tokens), 0)
    for pair in range(pairs):
        depth = -(-2 * (pair + 1) * width // tokens) * tokens
        columns = [
            padded[pl.ds((blocks - 1 - lag) * width, depth), :] for lag in (2 * pair, 2 * pair + 1)
        ]
        outer = dot(ordered[:, :depth], jnp.concatenate(columns, axis=1))
        for half in range(2):
            block = 2 * pair + half
            turned = turn(outer[:, half * tokens : (half + 1) * tokens])
            joined = jnp.where(lane >= row, turned, before)
            before = turned
            value = jnp.sum(joined, axis=0, keepdims=True) * scale
            high = value.astype(bf16).astype(f32)
            pieces = jnp.where(which == 0, high, value - high)
            place = (blocks - 1 - block) * rows + 2 * width
            sent[place : place + EXTRA_ROWS, :] = pieces.astype(bf16)

    total = None
    for pair in range(pairs):
        bands = []
        for block in (2 * pair, 2 * pair + 1):
            taps = got[block * rows + 2 * width : block * rows + 2 * width + 1, :].astype(f32)
            turned = turn(jnp.broadcast_to(taps, (tokens, tokens)))
            bands.append(jnp.where(lane >= row, turned, band).astype(bf16))
            band = turned
        weights = jnp.concatenate(
            (
                jnp.concatenate((bands[0], bands[1]), axis=1),
                jnp.concatenate((left, bands[0]), axis=1),
            ),
            axis=0,
        )
        left = bands[1]
        skip = 2 * width * pair
        term = dot(streams[0 : 2 * width * pairs - skip, :], weights)
        total = term if pair == 0 else jnp.concatenate((total[:skip], total[skip:] + term), axis=0)
    for pair in range(pairs):
        for half in range(2):
            block = 2 * pair + half
            lanes = slice(half * tokens, (half + 1) * tokens)
            at = 2 * width * pair
            sent[block * rows : block * rows + width, :] = total[at : at + width, lanes].astype(bf16)
            place = (blocks - 1 - block) * rows + width
            sent[place : place + width, :] = total[
                at + width : at + 2 * width, lanes
            ].astype(bf16)


def output_kernel(
    width, got, query, key, value, grad, mixed, query_grad, key_grad, value_grad, filter_grad
):
    rows, tokens = 2 * width + EXTRA_ROWS, got.shape[1]
    blocks = got.shape[0] // rows

    def collect(first, count):
        return jnp.concatenate(
            [got[at * rows + first : at * rows + first + count, :] for at in range(blocks)], axis=0
        )

    flip = flip_matrix(tokens)
    convolved = dot_nt(eye_matrix(tokens), collect(0, width))
    mixed[...] = (query[...].astype(f32) * convolved).astype(bf16)
    query_grad[...] = (grad[...].astype(f32) * convolved).astype(bf16)
    backward = dot_nt(flip, collect(width, width))
    key_grad[...] = (backward * value[...].astype(f32)).astype(bf16)
    value_grad[...] = (backward * key[...].astype(f32)).astype(bf16)
    high, low = collect(2 * width, 1), collect(2 * width + 1, 1)
    filter_grad[...] = dot(high, flip) + dot(low, flip)


def by_groups(query_act, key_act, value_act, long_filter, out_grad):
    tokens, channels = query_act.shape
    groups = long_filter.shape[1]
    width = channels // groups
    rows = 2 * width + EXTRA_ROWS
    scale = 1.0 / math.sqrt(tokens * groups * width)
    chunks = jax.ShapeDtypeStruct((groups * rows, tokens), bf16)

    def exchange(sent):
        pieces = sent.reshape(groups, rows // 2, 2, tokens)
        pieces = lax.all_to_all(pieces, ("slow", "fast"), split_axis=0, concat_axis=0, tiled=True)
        return pieces.reshape(groups * rows, tokens)

    act = pltpu.VMEM((tokens, channels), bf16)
    sent = pl.pallas_call(
        gate_kernel,
        out_shape=chunks,
        in_specs=[pl.BlockSpec(memory_space=pltpu.HBM)] * 5,
        scratch_shapes=[
            act,
            act,
            act,
            pltpu.VMEM((groups, tokens), bf16),
            act,
            pltpu.SemaphoreType.DMA((5,)),
        ],
        compiler_params=pltpu.CompilerParams(vmem_limit_bytes=8 * 2**20),
        name="gate",
    )(
        *(
            pltpu.with_memory_space_constraint(array, pltpu.HBM)
            for array in (query_act, key_act, value_act, long_filter.T, out_grad)
        )
    )
    got = exchange(sent)
    sent = pl.pallas_call(
        functools.partial(group_kernel, scale, width),
        out_shape=chunks,
        scratch_shapes=[
            pltpu.VMEM((channels, 2 * tokens), bf16),
            pltpu.VMEM((2 * channels, tokens), bf16),
        ],
        compiler_params=pltpu.CompilerParams(vmem_limit_bytes=16 * 2**20),
        name="group",
    )(got)
    got = exchange(sent)
    like = jax.ShapeDtypeStruct((tokens, channels), bf16)
    *acts, filter_grad = pl.pallas_call(
        functools.partial(output_kernel, width),
        out_shape=(like, like, like, like, jax.ShapeDtypeStruct((groups, tokens), f32)),
        compiler_params=pltpu.CompilerParams(vmem_limit_bytes=8 * 2**20),
        name="outputs",
    )(got, query_act, key_act, value_act, out_grad)
    return (*acts, filter_grad.T)


def on_device(query_act, key_act, value_act, long_filter, out_grad):
    tokens, channels = query_act.shape
    groups = long_filter.shape[1]
    devices = lax.axis_size("slow") * lax.axis_size("fast")
    if devices == groups and tokens == 128 and channels == 16 * groups and groups % 4 == 0:
        return by_groups(query_act, key_act, value_act, long_filter, out_grad)
    return by_spectra(query_act, key_act, value_act, long_filter, out_grad)


def solution(mesh):
    placed = (
        P(("slow", "fast"), None),
        P(("slow", "fast"), None),
        P(("slow", "fast"), None),
        P(("slow", "fast"), None),
        P(("slow", "fast"), None),
    )
    return jax.shard_map(
        on_device,
        mesh=mesh,
        in_specs=placed,
        out_specs=(
            P(("slow", "fast"), None),
            P(("slow", "fast"), None),
            P(("slow", "fast"), None),
            P(("slow", "fast"), None),
            P(("slow", "fast"), None),
        ),
        check_vma=False,
    )
```
